128 devices in a mesh: seq: 64 (over x, z, y), head: 2 (over core).
Axes of the slice: x: 4, y: 4, z: 4, core: 2. Of those that a mesh axis runs over, the one named last changes fastest.
Arguments:
- layer_in: bfloat16 [16384, 1536], P('seq'), may hold values from -6 to 6
- norm_first: float32 [1536], replicated, may hold values from 0.5 to 1.5
- mixer_in: bfloat16 [1536, 2, 3072], P('seq', None, 'head'), may hold values from -0.15625 to 0.15625
- state_proj: bfloat16 [1536, 256], P('seq'), may hold values from -0.15625 to 0.15625
- step_proj: bfloat16 [1536, 48], P('seq', 'head'), may hold values from -0.15625 to 0.15625
- step_bias: float32 [48], P('head'), may hold values from -2 to 0
- conv_main: float32 [4, 3072], P(None, 'head'), may hold values from -3 to 3
- conv_state: float32 [4, 256], replicated, may hold values from -3 to 3
- decay_rate: float32 [48], P('head'), may hold values from 3.0517578e-05 to 0.05
- skip_gain: float32 [48], P('head'), may hold values from 0.25 to 1.75
- gate_gain: float32 [3072], P('head'), may hold values from 0.5 to 1.5
- mixer_out: bfloat16 [1536, 3072], P('seq', 'head'), may hold values from -0.109375 to 0.109375
- norm_second: float32 [1536], replicated, may hold values from 0.5 to 1.5
- shared_gate_up: bfloat16 [1536, 2, 1024], P('seq', None, 'head'), may hold values from -0.15625 to 0.15625
- shared_down: bfloat16 [1536, 1024], P('seq', 'head'), may hold values from -0.1875 to 0.1875
- expert_gate_up: bfloat16 [64, 1536, 2, 512], P('seq', None, None, 'head'), may hold values from -0.15625 to 0.15625
- expert_down: bfloat16 [64, 512, 1536], P('seq', 'head'), may hold values from -0.25 to 0.25
- routes: int32 [16384, 6], P('seq'), may hold values from 0 to 63, all different within a row; in each aligned block of 256 rows (0 to 255, 256 to 511, ...) at most 32 rows name the same one
- route_weights: float32 [16384, 6], P('seq'), may hold values from 0.3 to 0.9
- grad_out: bfloat16 [16384, 1536], P('seq'), may hold values from -6 to 6
Outputs:
- layer_out: bfloat16 [16384, 1536], P('seq')
- input_grad: float32 [16384, 1536], P('seq')
- norm_first_grad: float32 [1536], replicated
- mixer_in_grad: float32 [1536, 2, 3072], P('seq', None, 'head')
- state_proj_grad: float32 [1536, 256], P('seq')
- step_proj_grad: float32 [1536, 48], P('seq', 'head')
- step_bias_grad: float32 [48], P('head')
- conv_main_grad: float32 [4, 3072], P(None, 'head')
- conv_state_grad: float32 [4, 256], replicated
- decay_rate_grad: float32 [48], P('head')
- skip_gain_grad: float32 [48], P('head')
- gate_gain_grad: float32 [3072], P('head')
- mixer_out_grad: float32 [1536, 3072], P('seq', 'head')
- norm_second_grad: float32 [1536], replicated
- shared_gate_up_grad: float32 [1536, 2, 1024], P('seq', None, 'head')
- shared_down_grad: float32 [1536, 1024], P('seq', 'head')
- expert_gate_up_grad: float32 [64, 1536, 2, 512], P('seq', None, None, 'head')
- expert_down_grad: float32 [64, 512, 1536], P('seq', 'head')
The draws below stay inside these ranges and needn't reach their ends.
Inputs may be any that keep to these rules, and one draw needn't show every extreme that they name: `routes`: in each aligned block of 256 rows (the rows of one device) no expert is named in more than 32 rows; each row names 6 different experts.
All inputs are finite; a program needn't handle non-finite values.
Results may differ from the reference program's by a relative error of at most 0.015.
Values may be sent and summed in bfloat16 or wider, within the bound.
A program may use at most 320 MiB of HBM per device.

```python
import math
import jax
import jax.numpy as jnp
import numpy as np
from jax import lax

D = 1536
HEADS = 48
HEAD_DIM = 64
STATE = 128
CONV_K = 4
EXP_FF = 512
SHARED_FF = 1024
TOP = 6
TOK_DEV = 256
INNER = 3072
TOKENS = 16384
EXPERTS = 64
CAP = 32
N_SEQ = 64
N_HEAD = 2


def levels(key, shape, cuts, least, high):
    gain, own = 1.0, jax.random.fold_in(key, 6)
    for dim, parts in cuts:
        draws = jnp.exp(jax.random.uniform(jax.random.fold_in(own, dim), (parts,), jnp.float32, least / len(cuts), high / len(cuts)))
        gain = gain * jnp.repeat(draws, shape[dim] // parts).reshape([-1 if axis == dim else 1 for axis in range(len(shape))])
    return gain


def routed_block(stream_key, own, number, rows, amount, top, bound, skew):
    sequence = jax.random.permutation(stream_key, amount)
    packed, ordinary = shares(amount, rows * top, bound, skew, True), shares(amount, rows * top, bound, skew, False)
    places = jnp.arange(amount)

    def named(sizes, rotation):
        used = int((sizes > 0).sum())
        fixed = max(1, used // 4)
        passed = fixed + (places - fixed + rotation * (used - fixed)) % max(1, amount - fixed)
        return jnp.zeros((amount,), jnp.int32).at[sequence[jnp.where(places < fixed, places, passed)]].set(jnp.asarray(sizes, jnp.int32))

    sizes = jnp.where(number % 4 == 0, named(packed, number // 4), named(ordinary, number - number // 4 - 1))
    mixed = jax.random.permutation(jax.random.fold_in(own, 3), amount)
    donor, sink = mixed[0:amount // 2 * 2:2], mixed[1:amount // 2 * 2:2]
    margin = jnp.minimum(sizes[donor] - 1, bound - sizes[sink]) // 2
    margin = jnp.where((donor == sequence[0]) | (sink == sequence[0]) | (sizes[sink] == 0), 0, jnp.maximum(margin, 0))
    passed = jax.random.randint(jax.random.fold_in(own, 4), (amount // 2,), 0, 1 << 20) % (margin + 1)
    sizes = sizes.at[donor].add(-passed).at[sink].add(passed)
    members = jnp.searchsorted(jnp.cumsum(sizes), jnp.arange(rows * top), side="right").astype(jnp.int32)
    table = members.reshape(top, rows).T
    table = table[jax.random.permutation(jax.random.fold_in(own, 1), rows)]
    rotation = jax.random.randint(jax.random.fold_in(own, 2), (rows, 1), 0, top)
    return jnp.take_along_axis(table, (jnp.arange(top)[None, :] + rotation) % top, axis=1)


def shares(amount, total, bound, slope, full):
    portions = [(1 << 20) // math.isqrt(standing ** slope) + 1 for standing in range(1, amount + 1)]
    largest = bound if full else min(bound, max(-(-total // amount), total * portions[0] // sum(portions)))
    least = 1 if total - largest >= amount - 1 else 0
    holding, spare = [largest] + [least] * (amount - 1), total - largest - least * (amount - 1)
    while spare > 0:
        candidates = [i for i in range(1, amount) if holding[i] < largest] or [i for i in range(1, amount) if holding[i] < bound]
        whole, remaining = sum([portions[i] for i in candidates]), spare
        for i in candidates:
            more = min(bound - holding[i], max(1, remaining * portions[i] // whole), spare)
            holding[i] = holding[i] + more
            spare = spare - more
    return np.array(holding)


def scatter_about(key, dims, deviation, bound, cuts=(), kind=jnp.bfloat16):
    level = levels(key, dims, cuts, -0.22, 0.18) if cuts else 1.0
    array = jax.random.normal(key, dims, jnp.float32) * deviation * level
    return jnp.minimum(jnp.maximum(array, -bound), bound).astype(kind)


def setup_inputs(seed: int = 0) -> dict:
    splits = jax.random.split(jax.random.key(seed), 21)
    layer_in = scatter_about(splits[0], (TOKENS, D), 1.0, 6.0, ((0, 64),))
    norm_first = jnp.clip(1.0 + 0.1 * jax.random.normal(splits[1], (D,), jnp.float32), 0.5, 1.5)
    mixer_in = scatter_about(splits[2], (D, 2, INNER), D ** -0.5, 0.15625, ((0, 64), (2, 2)))
    state_proj = scatter_about(splits[3], (D, 2 * STATE), D ** -0.5, 0.15625, ((0, 64),))
    step_proj = scatter_about(splits[4], (D, HEADS), D ** -0.5, 0.15625, ((0, 64), (1, 2)))
    step_bias = jnp.clip(-2.0 + 2.0 * jax.random.uniform(splits[5], (HEADS,), jnp.float32) ** levels(splits[5], (HEADS,), ((0, 2),), -0.2, 0.2), -2.0, 0.0)
    conv_main = scatter_about(splits[6], (CONV_K, INNER), CONV_K ** -0.5, 3.0, ((1, 2),), jnp.float32)
    conv_state = scatter_about(splits[7], (CONV_K, 2 * STATE), CONV_K ** -0.5, 3.0, (), jnp.float32)
    decay_rate = jnp.clip(jnp.exp(math.log(0.05) - 7.4014754 * jax.random.uniform(splits[8], (HEADS,), jnp.float32) ** levels(splits[8], (HEADS,), ((0, 2),), -0.2, 0.2)), 3.0517578125e-05, 0.05)
    skip_gain = jnp.clip(1.0 + 0.15 * jax.random.normal(splits[9], (HEADS,), jnp.float32), 0.25, 1.75)
    gate_gain = jnp.clip(1.0 + 0.1 * jax.random.normal(splits[10], (INNER,), jnp.float32), 0.5, 1.5)
    mixer_out = scatter_about(splits[11], (D, INNER), INNER ** -0.5, 0.109375, ((0, 64), (1, 2)))
    norm_second = jnp.clip(1.0 + 0.1 * jax.random.normal(splits[12], (D,), jnp.float32), 0.5, 1.5)
    shared_gate_up = scatter_about(splits[13], (D, 2, SHARED_FF), D ** -0.5, 0.15625, ((0, 64), (2, 2)))
    shared_down = scatter_about(splits[14], (D, SHARED_FF), SHARED_FF ** -0.5, 0.1875, ((0, 64), (1, 2)))
    expert_gate_up = scatter_about(splits[15], (EXPERTS, D, 2, EXP_FF), D ** -0.5, 0.15625, ((0, 64), (3, 2)))
    expert_down = scatter_about(splits[16], (EXPERTS, EXP_FF, D), EXP_FF ** -0.5, 0.25, ((0, 64), (1, 2)))
    routes_keys = jax.random.split(jax.random.fold_in(splits[17], 1), TOKENS // TOK_DEV)
    routes_turns = jax.random.permutation(jax.random.fold_in(splits[17], 3), TOKENS // TOK_DEV)
    routes = jax.vmap(lambda own, number: routed_block(jax.random.fold_in(splits[17], 2), own, number, TOK_DEV, EXPERTS, TOP, CAP, 1))(routes_keys, routes_turns).reshape((TOKENS, TOP))
    route_weights = jnp.clip(0.3 + 0.59999996 * jax.random.uniform(splits[18], (TOKENS, TOP), jnp.float32) ** levels(splits[18], (TOKENS, TOP), ((0, 64),), -0.2, 0.2), 0.3, 0.9)
    grad_out = scatter_about(splits[19], (TOKENS, D), 1.0, 6.0, ((0, 64),))
    return {"layer_in": layer_in, "norm_first": norm_first, "mixer_in": mixer_in, "state_proj": state_proj, "step_proj": step_proj, "step_bias": step_bias, "conv_main": conv_main, "conv_state": conv_state, "decay_rate": decay_rate, "skip_gain": skip_gain, "gate_gain": gate_gain, "mixer_out": mixer_out, "norm_second": norm_second, "shared_gate_up": shared_gate_up, "shared_down": shared_down, "expert_gate_up": expert_gate_up, "expert_down": expert_down, "routes": routes, "route_weights": route_weights, "grad_out": grad_out}


HIGHEST = lax.Precision.HIGHEST
EPSILON = 1e-05

@jax.custom_vjp
def low(v):
    return lax.optimization_barrier(v.astype(jnp.bfloat16)).astype(jnp.float32)

@jax.custom_vjp
def low_back(v):
    return v

def low_keep(v):
    return (low(v), None)

def low_pass(kept, grad):
    return (grad,)

def back_keep(v):
    return (v, None)

def back_low(kept, grad):
    return (low(grad),)
low.defvjp(low_keep, low_pass)
low_back.defvjp(back_keep, back_low)

def matmul(left_side, right_side):
    return jnp.dot(left_side, right_side, precision=HIGHEST)

def silu(operand):
    return operand * jax.nn.sigmoid(operand)

def norm_rows(operand, gain_vec):
    return operand * lax.rsqrt(lax.optimization_barrier(jnp.mean(operand * operand, axis=-1, keepdims=True)) + EPSILON) * gain_vec

def group_state(heads_x, state_in, step_size, decay_rate):
    cum_decay = jnp.cumsum(-step_size * decay_rate[None, :], axis=0)
    tail_decay = cum_decay[-1]
    tok_weight = jnp.exp(tail_decay[None, :] - cum_decay) * step_size
    state_new = jnp.einsum('th,thp,tn->hpn', tok_weight, heads_x, state_in, precision=HIGHEST)
    return (jnp.exp(tail_decay), state_new)

def group_out(heads_x, state_in, state_read, step_size, decay_rate, state_start, skip_gain):
    length_rows = heads_x.shape[0]
    cum_decay = jnp.cumsum(-step_size * decay_rate[None, :], axis=0)
    causal = (jnp.arange(length_rows)[:, None] >= jnp.arange(length_rows)[None, :])[:, :, None]
    gap_decay = cum_decay[:, None, :] - cum_decay[None, :, :]
    decay_mat = jnp.where(causal, jnp.exp(jnp.where(causal, gap_decay, 0.0)), 0.0)
    scores = jnp.dot(state_read, state_in.T, precision=HIGHEST)
    mixing = decay_mat * scores[:, :, None] * step_size[None, :, :]
    within_part = jnp.einsum('tsh,shp->thp', mixing, heads_x, precision=HIGHEST)
    carried_part = jnp.exp(cum_decay)[:, :, None] * jnp.einsum('tn,hpn->thp', state_read, state_start, precision=HIGHEST)
    return within_part + carried_part + skip_gain[None, :, None] * heads_x

def slot_tables(routes):
    flat_routes = routes.reshape(N_SEQ, TOK_DEV * TOP)
    one_hot = (flat_routes[:, :, None] == jnp.arange(EXPERTS, dtype=jnp.int32)[None, None, :]).astype(jnp.int32)
    position = lax.optimization_barrier(jnp.sum((jnp.cumsum(one_hot, axis=1) - one_hot) * one_hot, axis=2))
    rows_expert = N_SEQ * CAP
    owner_base = jnp.arange(N_SEQ, dtype=jnp.int32)[:, None] * CAP
    slot_global = (flat_routes * rows_expert + owner_base + position).reshape(-1).astype(jnp.int32)
    token_of = jnp.repeat(jnp.arange(TOKENS, dtype=jnp.int32), TOP)
    slot_token = jnp.full((EXPERTS * rows_expert,), TOKENS, jnp.int32).at[slot_global].set(token_of)
    return (slot_token.reshape(EXPERTS, rows_expert), slot_global)

def layer(parameters, slot_token, slot_global, route_weights):
    layer_in, norm_first, mixer_in, state_proj, step_proj, step_bias, conv_main, conv_state, decay_rate, skip_gain, gate_gain, mixer_out, norm_second, shared_gate_up, shared_down, expert_gate_up, expert_down = parameters
    normed = low(norm_rows(layer_in, norm_first))
    zx_both = matmul(normed, mixer_in.reshape(D, 2 * INNER))
    gate_z = low_back(zx_both[:, :INNER])
    pre_x = low_back(zx_both[:, INNER:])
    pre_bc = low_back(matmul(normed, state_proj))
    step_raw = low_back(matmul(normed, step_proj)) + step_bias
    conv_input = jnp.concatenate([pre_x, pre_bc], axis=1)
    padded = jnp.concatenate([jnp.zeros((CONV_K - 1, INNER + 2 * STATE), jnp.float32), conv_input], axis=0)
    kernel = jnp.concatenate([conv_main, conv_state], axis=1)
    conv_sum = kernel[0] * padded[0:TOKENS]
    for tap_index in range(1, CONV_K):
        conv_sum = conv_sum + kernel[tap_index] * padded[tap_index:tap_index + TOKENS]
    active = silu(conv_sum)
    heads_x = active[:, :INNER].reshape(TOKENS, HEADS, HEAD_DIM)
    state_in = active[:, INNER:INNER + STATE]
    state_read = active[:, INNER + STATE:]
    step_size = jax.nn.softplus(step_raw)

    def group_step(state_carry, pieces):
        piece_x, piece_in, piece_read, piece_step = pieces
        outputs = group_out(piece_x, piece_in, piece_read, piece_step, decay_rate, state_carry, skip_gain)
        decay_end, state_local = group_state(piece_x, piece_in, piece_step, decay_rate)
        return (decay_end[:, None, None] * state_carry + state_local, outputs)
    start_state = jnp.zeros((HEADS, HEAD_DIM, STATE), jnp.float32)
    pieces = (heads_x.reshape(N_SEQ, TOK_DEV, HEADS, HEAD_DIM), state_in.reshape(N_SEQ, TOK_DEV, STATE), state_read.reshape(N_SEQ, TOK_DEV, STATE), step_size.reshape(N_SEQ, TOK_DEV, HEADS))
    _, ssd_blocks = lax.scan(jax.checkpoint(group_step), start_state, pieces)
    ssd = ssd_blocks.reshape(TOKENS, INNER)
    gated_ssd = ssd * silu(gate_z)
    normed_gate = low(norm_rows(gated_ssd, gate_gain))
    mixer_sum = low_back(jnp.dot(normed_gate, mixer_out.T, precision=HIGHEST))
    residual = layer_in + mixer_sum
    normed_second = low(norm_rows(residual, norm_second))
    shared_both = matmul(normed_second, shared_gate_up.reshape(D, 2 * SHARED_FF))
    shared_gate = low_back(shared_both[:, :SHARED_FF])
    shared_up = low_back(shared_both[:, SHARED_FF:])
    shared_hid = low(silu(shared_gate) * shared_up)
    shared_res = jnp.dot(shared_hid, shared_down.T, precision=HIGHEST)
    padded_rows = jnp.concatenate([normed_second, jnp.zeros((1, D), jnp.float32)], axis=0)
    part_width = EXP_FF // N_HEAD

    def expert_rows(pieces_e):
        token_ids, gate_up, down_proj = pieces_e
        slot_rows = padded_rows[token_ids]
        result = jnp.zeros((N_SEQ * CAP, D), jnp.float32)
        for part_index in range(N_HEAD):
            column_start = part_index * part_width
            inputs_part = low_back(slot_rows)
            expert_gate = low_back(matmul(inputs_part, gate_up[:, 0, column_start:column_start + part_width]))
            expert_up = low_back(matmul(inputs_part, gate_up[:, 1, column_start:column_start + part_width]))
            expert_hid = low(silu(expert_gate) * expert_up)
            result = result + low_back(low(matmul(expert_hid, down_proj[column_start:column_start + part_width])))
        return result
    expert_res = lax.map(jax.checkpoint(expert_rows), (slot_token, expert_gate_up, expert_down))
    picked = expert_res.reshape(EXPERTS * N_SEQ * CAP, D)[slot_global].reshape(TOKENS, TOP, D)
    expert_mix = lax.optimization_barrier(jnp.sum(picked * route_weights[:, :, None], axis=1))
    return residual + shared_res + expert_mix

def reference(layer_in, norm_first, mixer_in, state_proj, step_proj, step_bias, conv_main, conv_state, decay_rate, skip_gain, gate_gain, mixer_out, norm_second, shared_gate_up, shared_down, expert_gate_up, expert_down, routes, route_weights, grad_out):
    slot_token, slot_global = slot_tables(routes)
    parameters = (layer_in.astype(jnp.float32), norm_first.astype(jnp.float32), mixer_in.astype(jnp.float32), state_proj.astype(jnp.float32), step_proj.astype(jnp.float32), step_bias.astype(jnp.float32), conv_main.astype(jnp.float32), conv_state.astype(jnp.float32), decay_rate.astype(jnp.float32), skip_gain.astype(jnp.float32), gate_gain.astype(jnp.float32), mixer_out.astype(jnp.float32), norm_second.astype(jnp.float32), shared_gate_up.astype(jnp.float32), shared_down.astype(jnp.float32), expert_gate_up.astype(jnp.float32), expert_down.astype(jnp.float32))

    def forward(values_all):
        return layer(values_all, slot_token, slot_global, route_weights.astype(jnp.float32))
    layer_res, pullback = jax.vjp(forward, parameters)
    gradients = pullback(grad_out.astype(jnp.float32))[0]
    return (layer_res.astype(jnp.bfloat16), gradients[0], gradients[1], gradients[2], gradients[3], gradients[4], gradients[5], gradients[6], gradients[7], gradients[8], gradients[9], gradients[10], gradients[11], gradients[12], gradients[13], gradients[14], gradients[15], gradients[16])
```

```python
import functools
import jax
import jax.numpy as jnp
from jax import lax
from jax.experimental import pallas as pl
from jax.experimental.pallas import tpu as pltpu
from jax.sharding import PartitionSpec as P

ORDERS = ((0, 1, 2), (1, 2, 0), (2, 0, 1))
MIB = 1 << 20


def coordinates():
    me = lax.axis_index("seq")
    return me, [me // 16, (me // 4) % 4, me % 4]


def seq_of(at):
    return at[0] * 16 + at[1] * 4 + at[2]


def moved(at, axis, by):
    return [(c + by) % 4 if i == axis else c for i, c in enumerate(at)]


def greet_neighbours(at):
    barrier = pltpu.get_barrier_semaphore()
    for axis in range(3):
        for by in (1, 3):
            pl.semaphore_signal(barrier, inc=1, device_id={"seq": seq_of(moved(at, axis, by))})
    pl.semaphore_wait(barrier, 6)


def greet_all(me):
    barrier = pltpu.get_barrier_semaphore()

    @pl.loop(1, 64)
    def _(k):
        pl.semaphore_signal(barrier, inc=1, device_id={"seq": (me + k) % 64})

    pl.semaphore_wait(barrier, 63)


def parts_of(columns):
    third = columns // 3
    tiles = third // 128
    half = tiles // 2 * 128
    return third, half


def region(at, order, phase, value, cols):
    index = [None] * 3
    for i in range(3):
        if i < phase:
            index[order[i]] = slice(None)
        elif i == phase:
            index[order[i]] = value
        else:
            index[order[i]] = at[order[i]]
    return tuple(index) + (slice(None), cols)


def gather_kernel(columns, x_ref, out_ref, local_sem, send, recv):
    me, at = coordinates()
    third, half = parts_of(columns)
    own = pltpu.make_async_copy(x_ref, out_ref.at[at[0], at[1], at[2]], local_sem)
    own.start()
    greet_neighbours(at)
    for phase in range(3):
        firsts, seconds = [], []
        for p, order in enumerate(ORDERS):
            axis = order[phase]
            cols = pl.ds(p * third, third)
            here = region(at, order, phase, at[axis], cols)
            source = x_ref.at[:, cols] if phase == 0 else out_ref.at[here]
            for kind, by in enumerate((1, 3)):
                copy = pltpu.make_async_remote_copy(
                    src_ref=source,
                    dst_ref=out_ref.at[here],
                    send_sem=send.at[phase, p, kind],
                    recv_sem=recv.at[phase, p, kind],
                    device_id={"seq": seq_of(moved(at, axis, by))},
                )
                copy.start()
                firsts.append(copy)
        if phase == 0:
            own.wait()
        for p, order in enumerate(ORDERS):
            axis = order[phase]
            for kind, by in enumerate((1, 3)):
                cols = pl.ds(p * third, half) if kind == 0 else pl.ds(p * third + half, third - half)
                there = region(at, order, phase, (at[axis] - by) % 4, cols)
                firsts[p * 2 + kind].wait_recv()
                copy = pltpu.make_async_remote_copy(
                    src_ref=out_ref.at[there],
                    dst_ref=out_ref.at[there],
                    send_sem=send.at[phase, p, 2 + kind],
                    recv_sem=recv.at[phase, p, 2 + kind],
                    device_id={"seq": seq_of(moved(at, axis, by))},
                )
                copy.start()
                seconds.append(copy)
        for copy in seconds:
            copy.wait_recv()
        for copy in firsts + seconds:
            copy.wait_send()


def gather_rows(x, collective):
    rows, columns = x.shape
    out = pl.pallas_call(
        functools.partial(gather_kernel, columns),
        out_shape=jax.ShapeDtypeStruct((4, 4, 4, rows, columns), x.dtype),
        in_specs=[pl.BlockSpec(memory_space=pl.ANY)],
        out_specs=pl.BlockSpec(memory_space=pl.ANY),
        scratch_shapes=[
            pltpu.SemaphoreType.DMA,
            pltpu.SemaphoreType.DMA((3, 3, 4)),
            pltpu.SemaphoreType.DMA((3, 3, 4)),
        ],
        compiler_params=pltpu.CompilerParams(collective_id=collective, has_side_effects=True),
        name="gather_rows",
    )(x)
    return out


def exchange_kernel(x_ref, out_ref, local_sem, send, recv):
    me, at = coordinates()
    own = pltpu.make_async_copy(x_ref.at[me], out_ref.at[me], local_sem)
    own.start()
    greet_all(me)

    @pl.loop(1, 64)
    def _(k):
        target = ((at[0] + k // 16) % 4) * 16 + ((at[1] + k // 4) % 4) * 4 + (at[2] + k) % 4
        pltpu.make_async_remote_copy(
            src_ref=x_ref.at[target],
            dst_ref=out_ref.at[me],
            send_sem=send,
            recv_sem=recv,
            device_id={"seq": target},
        ).start()

    own.wait()
    whole = pltpu.make_async_copy(x_ref.at[pl.ds(0, 63)], out_ref.at[pl.ds(0, 63)], send)
    whole.wait()
    whole = pltpu.make_async_copy(x_ref.at[pl.ds(0, 63)], out_ref.at[pl.ds(0, 63)], recv)
    whole.wait()


def exchange(x, collective):
    return pl.pallas_call(
        exchange_kernel,
        out_shape=jax.ShapeDtypeStruct(x.shape, x.dtype),
        in_specs=[pl.BlockSpec(memory_space=pl.ANY)],
        out_specs=pl.BlockSpec(memory_space=pl.ANY),
        scratch_shapes=[pltpu.SemaphoreType.DMA] * 3,
        compiler_params=pltpu.CompilerParams(collective_id=collective, has_side_effects=True),
        name="exchange",
    )(x)


def scatter_kernel(columns, x_ref, out_ref, buf, rest, in_sem, send, recv):
    me, at = coordinates()
    third, half = parts_of(columns)
    loads = []
    for p in range(3):
        cols = pl.ds(p * third, third)
        load = pltpu.make_async_copy(
            x_ref.at[:, :, :, :, cols], buf.at[:, :, :, :, cols], in_sem.at[p]
        )
        load.start()
        loads.append(load)
    greet_neighbours(at)

    def spans(p):
        return pl.ds(p * third, half), pl.ds(p * third + half, third - half)

    for phase in (2, 1, 0):
        copies = {}
        room = rest[phase]

        def send_to(p, order, by, value, cols, slot, kind):
            axis = order[phase]
            lead = (slice(None),) * phase
            copy = pltpu.make_async_remote_copy(
                src_ref=buf.at[region(at, order, phase, value, cols)],
                dst_ref=room.at[(slot,) + lead + (slice(None), cols)],
                send_sem=send.at[phase, p, kind],
                recv_sem=recv.at[phase, p, kind],
                device_id={"seq": seq_of(moved(at, axis, by))},
            )
            copy.start()
            copies[p, kind] = copy

        def added(p, order, value, cols, slots):
            lead = 4**phase

            @pl.loop(0, lead)
            def _(i):
                free = ((), (i,), (i // 4, i % 4))[phase]
                index = list(region(at, order, phase, value, cols))
                for n, axis in enumerate(sorted(order[:phase])):
                    index[axis] = free[n]
                index = tuple(index)
                total = buf[index].astype(jnp.float32)
                for slot in slots:
                    total = total + room[(slot,) + free + (slice(None), cols)].astype(jnp.float32)
                if phase == 0 and len(slots) == 2:
                    out_ref[:, cols] = total
                else:
                    buf[index] = total.astype(jnp.bfloat16)

        for p, order in enumerate(ORDERS):
            if phase == 2:
                loads[p].wait()
            c = at[order[phase]]
            low, high = spans(p)
            send_to(p, order, 1, (c + 2) % 4, low, 2, 0)
            send_to(p, order, 3, (c + 2) % 4, high, 2, 1)
            send_to(p, order, 1, (c + 1) % 4, high, 0, 2)
            send_to(p, order, 3, (c + 3) % 4, low, 1, 3)
        for p, order in enumerate(ORDERS):
            c = at[order[phase]]
            low, high = spans(p)
            copies[p, 0].wait_recv()
            added(p, order, (c + 1) % 4, low, (2,))
            send_to(p, order, 1, (c + 1) % 4, low, 0, 4)
            copies[p, 1].wait_recv()
            added(p, order, (c + 3) % 4, high, (2,))
            send_to(p, order, 3, (c + 3) % 4, high, 1, 5)
        for p, order in enumerate(ORDERS):
            c = at[order[phase]]
            low, high = spans(p)
            copies[p, 2].wait_recv()
            copies[p, 5].wait_recv()
            added(p, order, c, high, (0, 1))
            copies[p, 3].wait_recv()
            copies[p, 4].wait_recv()
            added(p, order, c, low, (0, 1))
        for copy in copies.values():
            copy.wait_send()


def scatter_rows(x, collective):
    rows, columns = x.shape[3:]
    return pl.pallas_call(
        functools.partial(scatter_kernel, columns),
        out_shape=jax.ShapeDtypeStruct((rows, columns), jnp.float32),
        in_specs=[pl.BlockSpec(memory_space=pl.ANY)],
        out_specs=pl.BlockSpec(memory_space=pltpu.VMEM),
        scratch_shapes=[
            pltpu.VMEM((4, 4, 4, rows, columns), x.dtype),
            [
                pltpu.VMEM((3,) + (4,) * phase + (rows, columns), x.dtype)
                for phase in range(3)
            ],
            pltpu.SemaphoreType.DMA((3,)),
            pltpu.SemaphoreType.DMA((3, 3, 6)),
            pltpu.SemaphoreType.DMA((3, 3, 6)),
        ],
        compiler_params=pltpu.CompilerParams(
            collective_id=collective, has_side_effects=True, vmem_limit_bytes=60 * MIB
        ),
        name="scatter_rows",
    )(x)


def torus_target(at, k):
    return ((at[0] + k // 16) % 4) * 16 + ((at[1] + k // 4) % 4) * 4 + (at[2] + k) % 4


def params(collective, **more):
    return pltpu.CompilerParams(collective_id=collective, has_side_effects=True, **more)


def greet_all_and_sibling(me):
    barrier = pltpu.get_barrier_semaphore()

    @pl.loop(1, 64)
    def _(k):
        pl.semaphore_signal(barrier, inc=1, device_id={"seq": (me + k) % 64})

    pl.semaphore_signal(barrier, inc=1, device_id={"head": 1 - lax.axis_index("head")})
    pl.semaphore_wait(barrier, 64)


def greet_sibling():
    barrier = pltpu.get_barrier_semaphore()
    pl.semaphore_signal(barrier, inc=1, device_id={"head": 1 - lax.axis_index("head")})
    pl.semaphore_wait(barrier, 1)


def dispatch_kernel(x_ref, out_ref, local_sem, send, recv, pair_send, pair_recv):
    me, at = coordinates()
    head = lax.axis_index("head")
    own = pltpu.make_async_copy(x_ref.at[me], out_ref.at[me, head], local_sem)
    own.start()
    greet_all_and_sibling(me)

    @pl.loop(1, 64)
    def _(k):
        target = torus_target(at, k)
        pltpu.make_async_remote_copy(
            src_ref=x_ref.at[target],
            dst_ref=out_ref.at[me, head],
            send_sem=send,
            recv_sem=recv.at[me],
            device_id={"seq": target},
        ).start()

    def to_sibling(j):
        pltpu.make_async_remote_copy(
            src_ref=out_ref.at[j, head],
            dst_ref=out_ref.at[j, head],
            send_sem=pair_send,
            recv_sem=pair_recv,
            device_id={"head": 1 - head},
        ).start()

    own.wait()
    to_sibling(me)

    @pl.loop(1, 64)
    def _(k):
        source = torus_target(at, 64 - k)
        pltpu.make_async_copy(x_ref.at[0], out_ref.at[source, head], recv.at[source]).wait()
        to_sibling(source)

    pltpu.make_async_copy(x_ref.at[pl.ds(0, 63)], x_ref.at[pl.ds(0, 63)], send).wait()
    pltpu.make_async_copy(x_ref, x_ref, pair_send).wait()
    pltpu.make_async_copy(x_ref, x_ref, pair_recv).wait()


def dispatch(x, collective):
    return pl.pallas_call(
        dispatch_kernel,
        out_shape=jax.ShapeDtypeStruct((64, 2) + x.shape[1:], x.dtype),
        in_specs=[pl.BlockSpec(memory_space=pl.ANY)],
        out_specs=pl.BlockSpec(memory_space=pl.ANY),
        scratch_shapes=[
            pltpu.SemaphoreType.DMA,
            pltpu.SemaphoreType.DMA,
            pltpu.SemaphoreType.DMA((64,)),
            pltpu.SemaphoreType.DMA,
            pltpu.SemaphoreType.DMA,
        ],
        compiler_params=params(collective),
        name="dispatch",
    )(x)


def bring_home_kernel(x_ref, out_ref, theirs, sums, local_sem, send, recv, pair_send, pair_recv):
    me, at = coordinates()
    head = lax.axis_index("head")
    greet_all_and_sibling(me)

    @pl.loop(0, 64)
    def _(k):
        j = torus_target(at, k)
        pltpu.make_async_remote_copy(
            src_ref=x_ref.at[j, 1 - head],
            dst_ref=theirs.at[j],
            send_sem=pair_send,
            recv_sem=pair_recv.at[j],
            device_id={"head": 1 - head},
        ).start()

    def both(j):
        pltpu.make_async_copy(theirs.at[j], theirs.at[j], pair_recv.at[j]).wait()
        total = x_ref[j, head].astype(jnp.float32) + theirs[j].astype(jnp.float32)
        sums[j] = total.astype(sums.dtype)

    @pl.loop(1, 64)
    def _(k):
        j = torus_target(at, k)
        both(j)
        pltpu.make_async_remote_copy(
            src_ref=sums.at[j],
            dst_ref=out_ref.at[me],
            send_sem=send,
            recv_sem=recv,
            device_id={"seq": j},
        ).start()

    both(me)
    own = pltpu.make_async_copy(sums.at[me], out_ref.at[me], local_sem)
    own.start()
    own.wait()
    pltpu.make_async_copy(theirs, theirs, pair_send).wait()
    pltpu.make_async_copy(sums.at[pl.ds(0, 63)], sums.at[pl.ds(0, 63)], send).wait()
    pltpu.make_async_copy(sums.at[pl.ds(0, 63)], sums.at[pl.ds(0, 63)], recv).wait()


def bring_home(x, collective):
    shape = (x.shape[0],) + x.shape[2:]
    return pl.pallas_call(
        bring_home_kernel,
        out_shape=jax.ShapeDtypeStruct(shape, x.dtype),
        in_specs=[pl.BlockSpec(memory_space=pltpu.VMEM)],
        out_specs=pl.BlockSpec(memory_space=pl.ANY),
        scratch_shapes=[
            pltpu.VMEM(shape, x.dtype),
            pltpu.VMEM(shape, x.dtype),
            pltpu.SemaphoreType.DMA,
            pltpu.SemaphoreType.DMA,
            pltpu.SemaphoreType.DMA,
            pltpu.SemaphoreType.DMA,
            pltpu.SemaphoreType.DMA((64,)),
        ],
        compiler_params=params(collective, vmem_limit_bytes=40 * MIB),
        name="bring_home",
    )(x)


def scan_kernel(reverse, x_ref, out_ref, got, made, send, recv, back_send, back_recv):
    me, at = coordinates()
    greet_all(me)
    got[me] = x_ref[me]

    @pl.loop(1, 64)
    def _(k):
        target = torus_target(at, k)
        pltpu.make_async_remote_copy(
            src_ref=x_ref.at[target],
            dst_ref=got.at[me],
            send_sem=send,
            recv_sem=recv,
            device_id={"seq": target},
        ).start()

    some = pl.ds(0, 63)
    pltpu.make_async_copy(x_ref.at[some], x_ref.at[some], send).wait()
    pltpu.make_async_copy(got.at[some], got.at[some], recv).wait()
    heads, width = made.shape[1:]
    chosen = lax.broadcasted_iota(jnp.int32, (heads, width), 0) == lax.broadcasted_iota(
        jnp.int32, (heads, width), 1
    )

    def step(k, state):
        at_k = 63 - k if reverse else k
        made[at_k] = state
        row = got[at_k, heads : heads + 8, :][0:1, :]
        decay = jnp.sum(jnp.where(chosen, row, 0.0), axis=1, keepdims=True)
        return decay * state + got[at_k, 0:heads, :]

    lax.fori_loop(0, 64, step, jnp.zeros((heads, width), jnp.float32))
    out_ref[me] = made[me]

    @pl.loop(1, 64)
    def _(k):
        target = torus_target(at, k)
        pltpu.make_async_remote_copy(
            src_ref=made.at[target],
            dst_ref=out_ref.at[me],
            send_sem=back_send,
            recv_sem=back_recv,
            device_id={"seq": target},
        ).start()

    pltpu.make_async_copy(made.at[some], made.at[some], back_send).wait()
    pltpu.make_async_copy(made.at[some], made.at[some], back_recv).wait()


def carried(decay, state, reverse, collective):
    heads, size, width = state.shape
    rows = jnp.broadcast_to(jnp.pad(decay, (0, width - heads))[None, None, :], (size, 8, width))
    sent = jnp.concatenate([state.transpose(1, 0, 2), rows], axis=1)
    out = pl.pallas_call(
        functools.partial(scan_kernel, reverse),
        out_shape=jax.ShapeDtypeStruct((size, heads, width), jnp.float32),
        in_specs=[pl.BlockSpec(memory_space=pltpu.VMEM)],
        out_specs=pl.BlockSpec(memory_space=pltpu.VMEM),
        scratch_shapes=[
            pltpu.VMEM(sent.shape, jnp.float32),
            pltpu.VMEM((size, heads, width), jnp.float32),
        ]
        + [pltpu.SemaphoreType.DMA] * 4,
        compiler_params=params(collective),
        name="carried_back" if reverse else "carried",
    )(sent)
    return out.transpose(1, 0, 2)


def pair_kernel(x_ref, out_ref, theirs, send, recv):
    greet_sibling()
    copy = pltpu.make_async_remote_copy(
        src_ref=x_ref,
        dst_ref=theirs,
        send_sem=send,
        recv_sem=recv,
        device_id={"head": 1 - lax.axis_index("head")},
    )
    copy.start()
    copy.wait()
    rows = x_ref.shape[0]
    step = min(rows, 16)

    @pl.loop(0, rows // step)
    def _(i):
        here = pl.ds(pl.multiple_of(i * step, step), step)
        out_ref[here] = x_ref[here] + theirs[here]


def pair_total(x, collective):
    return pl.pallas_call(
        pair_kernel,
        out_shape=jax.ShapeDtypeStruct(x.shape, x.dtype),
        in_specs=[pl.BlockSpec(memory_space=pltpu.VMEM)],
        out_specs=pl.BlockSpec(memory_space=pltpu.VMEM),
        scratch_shapes=[
            pltpu.VMEM(x.shape, x.dtype),
            pltpu.SemaphoreType.DMA,
            pltpu.SemaphoreType.DMA,
        ],
        compiler_params=params(collective),
        name="pair_total",
    )(x)


def small_kernel(x_ref, out_ref, got, send, recv, back_send, back_recv):
    me, at = coordinates()
    greet_all(me)
    got[me] = x_ref[me]

    @pl.loop(1, 64)
    def _(k):
        target = torus_target(at, k)
        pltpu.make_async_remote_copy(
            src_ref=x_ref.at[target],
            dst_ref=got.at[me],
            send_sem=send,
            recv_sem=recv,
            device_id={"seq": target},
        ).start()

    some = pl.ds(0, 63)
    pltpu.make_async_copy(x_ref.at[some], x_ref.at[some], send).wait()
    pltpu.make_async_copy(got.at[some], got.at[some], recv).wait()
    out_ref[me] = lax.fori_loop(
        1, 64, lambda k, total: total + got[k], got[0]
    )

    @pl.loop(1, 64)
    def _(k):
        target = torus_target(at, k)
        pltpu.make_async_remote_copy(
            src_ref=out_ref.at[me],
            dst_ref=out_ref.at[me],
            send_sem=back_send,
            recv_sem=back_recv,
            device_id={"seq": target},
        ).start()

    pltpu.make_async_copy(got.at[some], got.at[some], back_send).wait()
    pltpu.make_async_copy(got.at[some], got.at[some], back_recv).wait()


def small_totals(parts, collective):
    flat = jnp.concatenate([part.reshape(-1) for part in parts])
    size = flat.shape[0]
    each = -(-size // (64 * 1024)) * 1024
    sent = jnp.pad(flat, (0, 64 * each - size)).reshape(64, each // 128, 128)
    out = pl.pallas_call(
        small_kernel,
        out_shape=jax.ShapeDtypeStruct(sent.shape, jnp.float32),
        in_specs=[pl.BlockSpec(memory_space=pltpu.VMEM)],
        out_specs=pl.BlockSpec(memory_space=pltpu.VMEM),
        scratch_shapes=[pltpu.VMEM(sent.shape, jnp.float32)] + [pltpu.SemaphoreType.DMA] * 4,
        compiler_params=params(collective),
        name="small_totals",
    )(sent).reshape(-1)
    result, start = [], 0
    for part in parts:
        result.append(out[start : start + part.size].reshape(part.shape))
        start += part.size
    return result


def routing_kernel(routes_ref, weights_ref, position_ref, weight_ref):
    experts, tokens = position_ref.shape
    expert = lax.broadcasted_iota(jnp.int32, (experts, tokens), 0)
    named = jnp.zeros((experts, tokens), jnp.float32)
    weight = jnp.zeros((experts, tokens), jnp.float32)
    for k in range(routes_ref.shape[0]):
        hit = expert == routes_ref[k : k + 1, :]
        named = named + jnp.where(hit, 1.0, 0.0)
        weight = weight + jnp.where(hit, weights_ref[k : k + 1, :], 0.0)
    earlier = jnp.where(
        lax.broadcasted_iota(jnp.int32, (tokens, tokens), 0)
        < lax.broadcasted_iota(jnp.int32, (tokens, tokens), 1),
        1.0,
        0.0,
    ).astype(jnp.bfloat16)
    count = jnp.dot(named.astype(jnp.bfloat16), earlier, preferred_element_type=jnp.float32)
    position_ref[...] = jnp.where(named > 0.0, count, -1.0)
    weight_ref[...] = weight


def routing(routes, route_weights, experts):
    tokens = routes.shape[0]
    return pl.pallas_call(
        routing_kernel,
        out_shape=[jax.ShapeDtypeStruct((experts, tokens), jnp.float32)] * 2,
        name="routing",
    )(routes.T, route_weights.T)


def chosen_slots(position, first, count, slots):
    tokens = position.shape[1]
    number = lax.broadcasted_iota(jnp.int32, (count, slots, tokens), 1)
    number = (number + slots * lax.axis_index("head")).astype(jnp.float32)
    return jnp.where(position[:, None, :] == number, 1.0, 0.0).reshape(count * slots, tokens)


def send_kernel(slots, position_ref, weight_ref, rows_ref, grads_ref, out_ref, grad_ref):
    position, weight = position_ref[...], weight_ref[...]
    count = position.shape[0]
    tokens = position.shape[1]
    chosen = chosen_slots(position, 0, count, slots)
    weighted = chosen.reshape(count, slots, tokens) * weight[:, None, :]
    slot_weight = jnp.sum(weighted.reshape(count * slots, tokens), axis=1, keepdims=True)
    chosen = chosen.astype(jnp.bfloat16)
    rows = jnp.dot(chosen, rows_ref[...], preferred_element_type=jnp.float32)
    out_ref[...] = rows.astype(jnp.bfloat16).reshape(out_ref.shape)
    grads = jnp.dot(chosen, grads_ref[...], preferred_element_type=jnp.float32) * slot_weight
    grad_ref[...] = grads.astype(jnp.bfloat16).reshape(grad_ref.shape)


def send_rows(position, weight, rows, grads, slots):
    experts, tokens = position.shape
    width = rows.shape[1]
    step = 8
    whole = pl.BlockSpec((tokens, width), lambda i: (0, 0))
    mine = pl.BlockSpec((step, tokens), lambda i: (i, 0))
    out = pl.BlockSpec((step, slots, width), lambda i: (i, 0, 0))
    return pl.pallas_call(
        functools.partial(send_kernel, slots),
        grid=(experts // step,),
        out_shape=[jax.ShapeDtypeStruct((experts, slots, width), jnp.bfloat16)] * 2,
        in_specs=[mine, mine, whole, whole],
        out_specs=[out, out],
        name="send_rows",
    )(position, weight, rows, grads)


def combine_kernel(slots, position_ref, weight_ref, res_ref, grad_ref, mix_ref, sum_ref):
    position, weight = position_ref[...], weight_ref[...]
    count, tokens = position.shape
    chosen = chosen_slots(position, 0, count, slots)
    weighted = (chosen.reshape(count, slots, tokens) * weight[:, None, :]).reshape(chosen.shape)
    high = weighted.astype(jnp.bfloat16)
    less = (weighted - high.astype(jnp.float32)).astype(jnp.bfloat16)
    rows = res_ref[...].reshape(count * slots, res_ref.shape[2])
    grads = grad_ref[...].reshape(count * slots, grad_ref.shape[2])

    def over_slots(picked, values):
        return lax.dot_general(
            picked, values, (((0,), (0,)), ((), ())), preferred_element_type=jnp.float32
        )

    @pl.when(pl.program_id(0) == 0)
    def _():
        mix_ref[...] = jnp.zeros_like(mix_ref)
        sum_ref[...] = jnp.zeros_like(sum_ref)

    mix_ref[...] += over_slots(high, rows) + over_slots(less, rows)
    sum_ref[...] += over_slots(chosen.astype(jnp.bfloat16), grads)


def combine(position, weight, res, grad):
    experts, tokens = position.shape
    _, slots, width = res.shape
    step = 16
    mine = pl.BlockSpec((step, tokens), lambda i: (i, 0))
    rows = pl.BlockSpec((step, slots, width), lambda i: (i, 0, 0))
    out = pl.BlockSpec((tokens, width), lambda i: (0, 0))
    return pl.pallas_call(
        functools.partial(combine_kernel, slots),
        grid=(experts // step,),
        out_shape=[jax.ShapeDtypeStruct((tokens, width), jnp.float32)] * 2,
        in_specs=[mine, mine, rows, rows],
        out_specs=[out, out],
        compiler_params=pltpu.CompilerParams(vmem_limit_bytes=40 * MIB),
        name="combine",
    )(position, weight, res, grad)


HIGHEST = lax.Precision.HIGHEST
EPSILON = 1e-05


def shifted(value, axis, steps):
    count = lax.axis_size(axis)
    leading, last = (max(0, -steps), min(count, count - steps))
    return lax.ppermute(value, axis, [(source, source + steps) for source in range(leading, last)])


def product(left_side, right_side):
    return jnp.dot(left_side, right_side, preferred_element_type=jnp.float32)


def product_nt(left_side, right_side):
    return lax.dot_general(
        left_side, right_side, (((1,), (1,)), ((), ())), preferred_element_type=jnp.float32
    )


def product_tn(left_side, right_side):
    return lax.dot_general(
        left_side, right_side, (((0,), (0,)), ((), ())), preferred_element_type=jnp.float32
    )


def silu(operand):
    return operand * jax.nn.sigmoid(operand)


def silu_slope(operand):
    sig_part = jax.nn.sigmoid(operand)
    return sig_part * (1.0 + operand * (1.0 - sig_part))


def rms_scale(operand):
    return lax.rsqrt(jnp.mean(operand * operand, axis=-1, keepdims=True) + EPSILON)


def norm_back(operand, row_scale, gain_vec, grad_rows):
    gain_grad = jnp.sum(grad_rows * operand * row_scale, axis=0)
    inner_mean = jnp.mean(operand * gain_vec * grad_rows, axis=-1, keepdims=True)
    return (gain_grad, row_scale * gain_vec * grad_rows - operand * row_scale**3 * inner_mean)


def group_state(heads_x, state_in, step_size, decay_rate):
    cum_decay = jnp.cumsum(-step_size * decay_rate[None, :], axis=0)
    tail_decay = cum_decay[-1]
    tok_weight = jnp.exp(tail_decay[None, :] - cum_decay) * step_size
    state_new = jnp.einsum("th,thp,tn->hpn", tok_weight, heads_x, state_in, precision=HIGHEST)
    return (jnp.exp(tail_decay), state_new)


def group_out(heads_x, state_in, state_read, step_size, decay_rate, state_start, skip_gain):
    length_rows = heads_x.shape[0]
    cum_decay = jnp.cumsum(-step_size * decay_rate[None, :], axis=0)
    causal = (jnp.arange(length_rows)[:, None] >= jnp.arange(length_rows)[None, :])[:, :, None]
    gap_decay = cum_decay[:, None, :] - cum_decay[None, :, :]
    decay_mat = jnp.where(causal, jnp.exp(jnp.where(causal, gap_decay, 0.0)), 0.0)
    scores = jnp.dot(state_read, state_in.T, precision=HIGHEST)
    mixing = decay_mat * scores[:, :, None] * step_size[None, :, :]
    within_part = jnp.einsum("tsh,shp->thp", mixing, heads_x, precision=HIGHEST)
    carried_part = jnp.exp(cum_decay)[:, :, None] * jnp.einsum(
        "tn,hpn->thp", state_read, state_start, precision=HIGHEST
    )
    return within_part + carried_part + skip_gain[None, :, None] * heads_x


def per_device(
    layer_in,
    norm_first,
    mixer_in,
    state_proj,
    step_proj,
    step_bias,
    conv_main,
    conv_state,
    decay_rate,
    skip_gain,
    gate_gain,
    mixer_out,
    norm_second,
    shared_gate_up,
    shared_down,
    expert_gate_up,
    expert_down,
    routes,
    route_weights,
    grad_out,
):
    tokens = layer_in.shape[0]
    model_width = layer_in.shape[1]
    inner_dev = mixer_in.shape[2]
    inner_all = inner_dev * lax.axis_size("head")
    state_size = state_proj.shape[1] // 2
    heads_dev = step_proj.shape[1]
    head_size = inner_dev // heads_dev
    conv_taps = conv_main.shape[0]
    shared_dev = shared_down.shape[1]
    local_experts = expert_gate_up.shape[0]
    seq_devices = lax.axis_size("seq")
    experts_all = local_experts * seq_devices
    choices_per = routes.shape[1]
    capacity = max(2, tokens * choices_per * 4 // (3 * experts_all))
    slot_count = local_experts * seq_devices * capacity
    gathered = gather_rows(
        jnp.concatenate(
            [
                mixer_in.reshape(-1, 2 * inner_dev),
                state_proj,
                jnp.pad(step_proj, ((0, 0), (0, 128 - heads_dev))),
            ],
            axis=1,
        ),
        0,
    ).reshape(model_width, -1)
    full_in = gathered[:, : 2 * inner_dev]
    full_state = gathered[:, 2 * inner_dev : 2 * inner_dev + 2 * state_size]
    full_step = gathered[:, 2 * inner_dev + 2 * state_size :][:, :heads_dev]
    gathered = gather_rows(
        jnp.concatenate(
            [mixer_out, shared_gate_up.reshape(-1, 2 * shared_dev), shared_down], axis=1
        ),
        1,
    ).reshape(model_width, -1)
    full_out = gathered[:, :inner_dev]
    shared_flat = gathered[:, inner_dev : inner_dev + 2 * shared_dev]
    full_down = gathered[:, inner_dev + 2 * shared_dev :]
    resid_in = layer_in.astype(jnp.float32)
    scale_first = rms_scale(resid_in)
    normed = (resid_in * scale_first * norm_first).astype(jnp.bfloat16)
    zx_both = product(normed, full_in)
    gate_z = zx_both[:, :inner_dev]
    pre_x = zx_both[:, inner_dev:]
    pre_bc = product(normed, full_state)
    step_raw = product(normed, full_step) + step_bias
    conv_input = jnp.concatenate([pre_x, pre_bc], axis=1)
    edge_rows = shifted(conv_input[tokens - (conv_taps - 1) :], "seq", 1)
    padded = jnp.concatenate([edge_rows, conv_input], axis=0)
    kernel = jnp.concatenate([conv_main, conv_state], axis=1)
    conv_sum = kernel[0] * padded[0:tokens]
    for tap_index in range(1, conv_taps):
        conv_sum = conv_sum + kernel[tap_index] * padded[tap_index : tap_index + tokens]
    active = silu(conv_sum)
    heads_x = active[:, :inner_dev].reshape(tokens, heads_dev, head_size)
    state_in = active[:, inner_dev : inner_dev + state_size]
    state_read = active[:, inner_dev + state_size :]
    step_size = jax.nn.softplus(step_raw)
    decay_total, state_local = group_state(heads_x, state_in, step_size, decay_rate)
    state_start = carried(decay_total, state_local, False, 2)
    ssd = group_out(
        heads_x, state_in, state_read, step_size, decay_rate, state_start, skip_gain
    ).reshape(tokens, inner_dev)
    gate_act = silu(gate_z)
    gated_ssd = ssd * gate_act
    gate_scale = lax.rsqrt(pair_total(jnp.sum(gated_ssd * gated_ssd, axis=1).reshape(-1, 128), 4).reshape(-1) / inner_all + EPSILON)[
        :, None
    ]
    normed_gate = (gated_ssd * gate_scale * gate_gain).astype(jnp.bfloat16)
    mixer_sum = pair_total(product_nt(normed_gate, full_out), 6)
    residual = resid_in + mixer_sum
    scale_second = rms_scale(residual)
    normed_second = (residual * scale_second * norm_second).astype(jnp.bfloat16)
    shared_both = product(normed_second, shared_flat)
    shared_gate = shared_both[:, :shared_dev]
    shared_up = shared_both[:, shared_dev:]
    shared_hid = (silu(shared_gate) * shared_up).astype(jnp.bfloat16)
    shared_part = product_nt(shared_hid, full_down)
    position, slot_weight = routing(routes, route_weights, experts_all)
    rows_out, grads_out = send_rows(
        position, slot_weight, normed_second, grad_out, capacity // lax.axis_size("head")
    )
    slot_shape = (local_experts, seq_devices * capacity, model_width)
    slot_in = dispatch(rows_out, 11).reshape(slot_shape)
    grad_slots = dispatch(grads_out, 12).reshape(slot_shape)
    gate_up_res = jnp.einsum(
        "erd,edkf->erkf", slot_in, expert_gate_up, preferred_element_type=jnp.float32
    )
    expert_gate = gate_up_res[:, :, 0]
    expert_up = gate_up_res[:, :, 1]
    expert_hid = (silu(expert_gate) * expert_up).astype(jnp.bfloat16)
    expert_res = jnp.einsum(
        "erf,efd->erd", expert_hid, expert_down, preferred_element_type=jnp.float32
    ).astype(jnp.bfloat16)
    home_shape = (seq_devices, 2, capacity // 2, model_width)
    home_rows = bring_home(expert_res.reshape(home_shape), 13)
    grad_float = grad_out.astype(jnp.float32)
    grad_hid = jnp.einsum(
        "erd,efd->erf", grad_slots, expert_down, preferred_element_type=jnp.float32
    )
    grad_expert_gate = grad_hid * expert_up * silu_slope(expert_gate)
    grad_expert_up = grad_hid * silu(expert_gate)
    grad_gate_up = jnp.stack([grad_expert_gate, grad_expert_up], axis=2).astype(jnp.bfloat16)
    expert_down_grad = jnp.einsum(
        "erf,erd->efd", expert_hid, grad_slots, preferred_element_type=jnp.float32
    )
    expert_gate_up_grad = jnp.einsum(
        "erd,erkf->edkf", slot_in, grad_gate_up, preferred_element_type=jnp.float32
    )
    grad_slot_in = jnp.einsum(
        "erkf,edkf->erd", grad_gate_up, expert_gate_up, preferred_element_type=jnp.float32
    ).astype(jnp.bfloat16)
    grad_home = bring_home(grad_slot_in.reshape(home_shape), 14)
    expert_mix, expert_grad_rows = combine(position, slot_weight, home_rows, grad_home)
    branch_sum = pair_total(shared_part + expert_mix, 7)
    layer_out = (residual + branch_sum).astype(jnp.bfloat16)
    grad_shared_hid = product(grad_out, full_down)
    grad_shared_gate = grad_shared_hid * shared_up * silu_slope(shared_gate)
    grad_shared_up = grad_shared_hid * silu(shared_gate)
    grad_shared_both = jnp.concatenate([grad_shared_gate, grad_shared_up], axis=1).astype(
        jnp.bfloat16
    )
    shared_down_grad = product_tn(grad_out, shared_hid)
    shared_gate_up_grad = product_tn(normed_second, grad_shared_both)
    grad_normed_second = pair_total(product_nt(grad_shared_both, shared_flat) + expert_grad_rows, 8)
    norm_second_grad, grad_resid_norm = norm_back(
        residual, scale_second, norm_second, grad_normed_second
    )
    grad_resid = grad_float + grad_resid_norm
    grad_mix = grad_resid.astype(jnp.bfloat16)
    mixer_out_grad = product_tn(grad_mix, normed_gate)
    grad_normed_gate = product(grad_mix, full_out)
    weighted = grad_normed_gate * gate_gain
    inner_dot = pair_total(jnp.sum(weighted * gated_ssd, axis=1).reshape(-1, 128), 5).reshape(-1)[:, None]
    grad_gated = gate_scale * weighted - gated_ssd * gate_scale**3 * inner_dot / inner_all
    gate_gain_grad = jnp.sum(grad_normed_gate * gated_ssd * gate_scale, axis=0)
    grad_ssd = grad_gated * gate_act
    grad_gate_z = grad_gated * ssd * silu_slope(gate_z)
    _, pull_out = jax.vjp(
        group_out, heads_x, state_in, state_read, step_size, decay_rate, state_start, skip_gain
    )
    (
        grad_x_first,
        grad_in_first,
        grad_read,
        grad_step_first,
        grad_rate_first,
        grad_start,
        skip_gain_grad,
    ) = pull_out(grad_ssd.reshape(tokens, heads_dev, head_size))
    grad_next = carried(decay_total, grad_start, True, 3)
    grad_decay = jnp.sum(grad_next * state_start, axis=(1, 2))
    _, pull_state = jax.vjp(group_state, heads_x, state_in, step_size, decay_rate)
    grad_x_second, grad_in_second, grad_step_second, grad_rate_second = pull_state(
        (grad_decay, grad_next)
    )
    decay_rate_grad = grad_rate_first + grad_rate_second
    grad_bc = pair_total(
        jnp.concatenate([grad_in_first + grad_in_second, grad_read], axis=1), 10
    )
    grad_active = jnp.concatenate(
        [(grad_x_first + grad_x_second).reshape(tokens, inner_dev), grad_bc], axis=1
    )
    grad_conv = grad_active * silu_slope(conv_sum)
    grad_padded = jnp.pad(kernel[0] * grad_conv, ((0, conv_taps - 1), (0, 0)))
    for tap_index in range(1, conv_taps):
        grad_padded = grad_padded + jnp.pad(
            kernel[tap_index] * grad_conv, ((tap_index, conv_taps - 1 - tap_index), (0, 0))
        )
    kernel_grad = jnp.stack(
        [
            jnp.sum(grad_conv * padded[tap_index : tap_index + tokens], axis=0)
            for tap_index in range(conv_taps)
        ]
    )
    spill_rows = shifted(grad_padded[: conv_taps - 1], "seq", -1)
    grad_pre = grad_padded[conv_taps - 1 :]
    grad_pre = jnp.concatenate(
        [grad_pre[: tokens - (conv_taps - 1)], grad_pre[tokens - (conv_taps - 1) :] + spill_rows],
        axis=0,
    )
    grad_step_raw = (grad_step_first + grad_step_second) * jax.nn.sigmoid(step_raw)
    step_bias_grad = jnp.sum(grad_step_raw, axis=0)
    grad_zx = jnp.concatenate([grad_gate_z, grad_pre[:, :inner_dev]], axis=1).astype(jnp.bfloat16)
    grad_bc_low = grad_pre[:, inner_dev:].astype(jnp.bfloat16)
    grad_step_low = grad_step_raw.astype(jnp.bfloat16)
    in_partial = product_nt(grad_zx, full_in) + product_nt(
        grad_step_low, full_step
    )
    grad_normed = pair_total(in_partial, 9) + product_nt(grad_bc_low, full_state)
    mixer_in_grad = product_tn(normed, grad_zx)
    state_proj_grad = product_tn(normed, grad_bc_low)
    step_proj_grad = product_tn(normed, grad_step_low)
    norm_first_grad, grad_in_norm = norm_back(resid_in, scale_first, norm_first, grad_normed)
    input_grad = grad_resid + grad_in_norm
    low = lambda *parts: jnp.concatenate(
        [part.astype(jnp.bfloat16) for part in parts], axis=1
    ).reshape(4, 4, 4, model_width // 64, -1)
    summed = scatter_rows(
        low(mixer_in_grad, state_proj_grad, jnp.pad(step_proj_grad, ((0, 0), (0, 128 - heads_dev)))),
        15,
    )
    summed_late = scatter_rows(low(mixer_out_grad, shared_gate_up_grad, shared_down_grad), 16)
    wide = 2 * inner_dev + 2 * state_size
    weight_sums = (
        summed[:, : 2 * inner_dev].reshape(-1, 2, inner_dev),
        summed[:, 2 * inner_dev : wide],
        summed[:, wide : wide + heads_dev],
        summed_late[:, :inner_dev],
        summed_late[:, inner_dev : inner_dev + 2 * shared_dev].reshape(-1, 2, shared_dev),
        summed_late[:, inner_dev + 2 * shared_dev :],
    )
    small_sums = small_totals(
        (
            norm_first_grad,
            norm_second_grad,
            step_bias_grad,
            kernel_grad[:, :inner_dev],
            kernel_grad[:, inner_dev:],
            decay_rate_grad,
            skip_gain_grad,
            gate_gain_grad,
        ),
        17,
    )
    return (
        layer_out,
        input_grad,
        small_sums[0],
        weight_sums[0],
        weight_sums[1],
        weight_sums[2],
        small_sums[2],
        small_sums[3],
        small_sums[4],
        small_sums[5],
        small_sums[6],
        small_sums[7],
        weight_sums[3],
        small_sums[1],
        weight_sums[4],
        weight_sums[5],
        expert_gate_up_grad,
        expert_down_grad,
    )


def solution(mesh):
    placed = (
        P("seq", None),
        P(),
        P("seq", None, "head"),
        P("seq", None),
        P("seq", "head"),
        P("head"),
        P(None, "head"),
        P(),
        P("head"),
        P("head"),
        P("head"),
        P("seq", "head"),
        P(),
        P("seq", None, "head"),
        P("seq", "head"),
        P("seq", None, None, "head"),
        P("seq", "head", None),
        P("seq", None),
        P("seq", None),
        P("seq", None),
    )
    return jax.shard_map(
        per_device,
        mesh=mesh,
        in_specs=placed,
        out_specs=(
            P("seq", None),
            P("seq", None),
            P(),
            P("seq", None, "head"),
            P("seq", None),
            P("seq", "head"),
            P("head"),
            P(None, "head"),
            P(),
            P("head"),
            P("head"),
            P("head"),
            P("seq", "head"),
            P(),
            P("seq", None, "head"),
            P("seq", "head"),
            P("seq", None, None, "head"),
            P("seq", "head", None),
        ),
        check_vma=False,
    )
```

```python
import functools
import jax
import jax.numpy as jnp
from jax import lax
from jax.experimental import pallas as pl
from jax.experimental.pallas import tpu as pltpu
from jax.sharding import PartitionSpec as P

ORDERS = ((0, 1, 2), (1, 2, 0), (2, 0, 1))
MIB = 1 << 20


def coordinates():
    me = lax.axis_index("seq")
    return me, [me // 16, (me // 4) % 4, me % 4]


def seq_of(at):
    return at[0] * 16 + at[1] * 4 + at[2]


def moved(at, axis, by):
    return [(c + by) % 4 if i == axis else c for i, c in enumerate(at)]


def greet_neighbours(at):
    barrier = pltpu.get_barrier_semaphore()
    for axis in range(3):
        for by in (1, 3):
            pl.semaphore_signal(barrier, inc=1, device_id={"seq": seq_of(moved(at, axis, by))})
    pl.semaphore_wait(barrier, 6)


def greet_all(me):
    barrier = pltpu.get_barrier_semaphore()

    @pl.loop(1, 64)
    def _(k):
        pl.semaphore_signal(barrier, inc=1, device_id={"seq": (me + k) % 64})

    pl.semaphore_wait(barrier, 63)


def parts_of(columns):
    third = columns // 3
    tiles = third // 128
    half = tiles // 2 * 128
    return third, half


def region(at, order, phase, value, cols):
    index = [None] * 3
    for i in range(3):
        if i < phase:
            index[order[i]] = slice(None)
        elif i == phase:
            index[order[i]] = value
        else:
            index[order[i]] = at[order[i]]
    return tuple(index) + (slice(None), cols)


def gather_kernel(columns, x_ref, out_ref, local_sem, send, recv):
    me, at = coordinates()
    third, half = parts_of(columns)
    own = pltpu.make_async_copy(x_ref, out_ref.at[at[0], at[1], at[2]], local_sem)
    own.start()
    greet_neighbours(at)
    for phase in range(3):
        firsts, seconds = [], []
        for p, order in enumerate(ORDERS):
            axis = order[phase]
            cols = pl.ds(p * third, third)
            here = region(at, order, phase, at[axis], cols)
            source = x_ref.at[:, cols] if phase == 0 else out_ref.at[here]
            for kind, by in enumerate((1, 3)):
                copy = pltpu.make_async_remote_copy(
                    src_ref=source,
                    dst_ref=out_ref.at[here],
                    send_sem=send.at[phase, p, kind],
                    recv_sem=recv.at[phase, p, kind],
                    device_id={"seq": seq_of(moved(at, axis, by))},
                )
                copy.start()
                firsts.append(copy)
        if phase == 0:
            own.wait()
        for p, order in enumerate(ORDERS):
            axis = order[phase]
            for kind, by in enumerate((1, 3)):
                cols = pl.ds(p * third, half) if kind == 0 else pl.ds(p * third + half, third - half)
                there = region(at, order, phase, (at[axis] - by) % 4, cols)
                firsts[p * 2 + kind].wait_recv()
                copy = pltpu.make_async_remote_copy(
                    src_ref=out_ref.at[there],
                    dst_ref=out_ref.at[there],
                    send_sem=send.at[phase, p, 2 + kind],
                    recv_sem=recv.at[phase, p, 2 + kind],
                    device_id={"seq": seq_of(moved(at, axis, by))},
                )
                copy.start()
                seconds.append(copy)
        for copy in seconds:
            copy.wait_recv()
        for copy in firsts + seconds:
            copy.wait_send()


def gather_rows(x, collective):
    rows, columns = x.shape
    out = pl.pallas_call(
        functools.partial(gather_kernel, columns),
        out_shape=jax.ShapeDtypeStruct((4, 4, 4, rows, columns), x.dtype),
        in_specs=[pl.BlockSpec(memory_space=pl.ANY)],
        out_specs=pl.BlockSpec(memory_space=pl.ANY),
        scratch_shapes=[
            pltpu.SemaphoreType.DMA,
            pltpu.SemaphoreType.DMA((3, 3, 4)),
            pltpu.SemaphoreType.DMA((3, 3, 4)),
        ],
        compiler_params=pltpu.CompilerParams(collective_id=collective, has_side_effects=True),
        name="gather_rows",
    )(x)
    return out


def torus_target(at, k):
    return ((at[0] + k // 16) % 4) * 16 + ((at[1] + k // 4) % 4) * 4 + (at[2] + k) % 4


def params(collective, **more):
    return pltpu.CompilerParams(collective_id=collective, has_side_effects=True, **more)


def greet_all_and_sibling(me):
    barrier = pltpu.get_barrier_semaphore()

    @pl.loop(1, 64)
    def _(k):
        pl.semaphore_signal(barrier, inc=1, device_id={"seq": (me + k) % 64})

    pl.semaphore_signal(barrier, inc=1, device_id={"head": 1 - lax.axis_index("head")})
    pl.semaphore_wait(barrier, 64)


def greet_sibling():
    barrier = pltpu.get_barrier_semaphore()
    pl.semaphore_signal(barrier, inc=1, device_id={"head": 1 - lax.axis_index("head")})
    pl.semaphore_wait(barrier, 1)


def experts_kernel(
    rows_ref,
    grads_ref,
    gate_up_ref,
    down_ref,
    home_ref,
    res_ref,
    gate_up_grad_ref,
    down_grad_ref,
    slot_in,
    grad_slots,
    theirs_x,
    theirs_y,
    sums,
    wide_grad,
    send,
    home_send,
    home_recv,
    sems,
):
    me, at = coordinates()
    head = lax.axis_index("head")
    sibling = {"head": 1 - head}
    mine, place = me // 8, me % 8
    names = ("recv", "fwd_send", "fwd_recv", "kept", "given_send", "given_recv")
    names += ("x_send", "x_recv", "y_send", "y_recv")
    sem = {name: sems.at[n] for n, name in enumerate(names)}
    greet_all_and_sibling(me)

    def group(c):
        return pl.ds(pl.multiple_of(c * 8, 8), 8)

    own = pltpu.make_async_copy(rows_ref.at[me], slot_in.at[me, head], sem["recv"].at[mine])
    own.start()

    @pl.loop(0, 64)
    def _(k):
        j = ((mine - k // 8) % 8) * 8 + (place + k) % 8

        @pl.when(k > 0)
        def _():
            pltpu.make_async_remote_copy(
                src_ref=rows_ref.at[j],
                dst_ref=slot_in.at[me, head],
                send_sem=send,
                recv_sem=sem["recv"].at[mine],
                device_id={"seq": j},
            ).start()

    def given(c):
        return pltpu.make_async_remote_copy(
            src_ref=grads_ref.at[group(c)],
            dst_ref=grad_slots.at[group(c), head],
            send_sem=sem["given_send"].at[c],
            recv_sem=sem["given_recv"].at[c],
            device_id=sibling,
        )

    def kept(c):
        return pltpu.make_async_copy(
            grads_ref.at[group(c)], grad_slots.at[group(c), head], sem["kept"].at[c]
        )

    def forward(c):
        return pltpu.make_async_remote_copy(
            src_ref=slot_in.at[group(c), head],
            dst_ref=slot_in.at[group(c), head],
            send_sem=sem["fwd_send"].at[c],
            recv_sem=sem["fwd_recv"].at[c],
            device_id=sibling,
        )

    def swap(c, source, target, name):
        return pltpu.make_async_remote_copy(
            src_ref=source.at[group(c), 1 - head],
            dst_ref=target.at[group(c)],
            send_sem=sem[name + "_send"].at[c],
            recv_sem=sem[name + "_recv"].at[c],
            device_id=sibling,
        )

    @pl.loop(0, 8)
    def _(i):
        c = (mine + i) % 8
        kept(c).start()
        given(c).start()

    wide_grad[...] = jnp.zeros_like(wide_grad)
    down_grad_ref[...] = jnp.zeros_like(down_grad_ref)
    hidden = down_ref.shape[0]
    width = down_ref.shape[1]

    def nt(left, right):
        return lax.dot_general(
            left, right, (((1,), (1,)), ((), ())), preferred_element_type=jnp.float32
        )

    def tn(left, right):
        return lax.dot_general(
            left, right, (((0,), (0,)), ((), ())), preferred_element_type=jnp.float32
        )

    @pl.loop(0, 10)
    def _(i):
        @pl.when(i < 8)
        def _():
            c = (mine + i) % 8
            pltpu.make_async_copy(
                rows_ref.at[group(c)], slot_in.at[group(c), head], sem["recv"].at[c]
            ).wait()
            forward(c).start()

        @pl.when((i >= 1) & (i < 9))
        def _():
            c = (mine + i + 7) % 8
            forward(c).wait()
            kept(c).wait()
            given(c).wait()
            rows = slot_in[group(c)].reshape(256, width)
            grads = grad_slots[group(c)].reshape(256, width)
            both = jnp.dot(rows, gate_up_ref[...], preferred_element_type=jnp.float32)
            gate, up = both[:, :hidden], both[:, hidden:]
            sig = jax.nn.sigmoid(gate)
            act = gate * sig
            hid = (act * up).astype(jnp.bfloat16)
            grad_hid = nt(grads, down_ref[...])
            grad_gate = grad_hid * up * (sig * (1.0 + gate * (1.0 - sig)))
            grad_both = jnp.concatenate([grad_gate, grad_hid * act], axis=1).astype(jnp.bfloat16)
            wide_grad[...] += tn(rows, grad_both)
            down_grad_ref[...] += tn(hid, grads)
            back = nt(grad_both, gate_up_ref[...]).astype(jnp.bfloat16)
            slot_in[group(c)] = back.reshape(8, 2, 16, width)
            res = jnp.dot(hid, down_ref[...], preferred_element_type=jnp.float32)
            grad_slots[group(c)] = res.astype(jnp.bfloat16).reshape(8, 2, 16, width)
            swap(c, slot_in, theirs_x, "x").start()
            swap(c, grad_slots, theirs_y, "y").start()

        @pl.when(i >= 2)
        def _():
            c = (mine + i + 6) % 8
            swap(c, slot_in, theirs_x, "x").wait()

            @pl.loop(0, 8)
            def _(n):
                j = c * 8 + (place + n) % 8
                total = slot_in[j, head].astype(jnp.float32) + theirs_x[j].astype(jnp.float32)
                sums[j] = total.astype(sums.dtype)

                @pl.when(j != me)
                def _():
                    pltpu.make_async_remote_copy(
                        src_ref=sums.at[j],
                        dst_ref=home_ref.at[me],
                        send_sem=home_send,
                        recv_sem=home_recv,
                        device_id={"seq": j},
                    ).start()

                @pl.when(j == me)
                def _():
                    pltpu.make_async_copy(sums.at[me], home_ref.at[me], home_recv).start()

            swap(c, grad_slots, theirs_y, "y").wait()

            @pl.loop(0, 8)
            def _(n):
                j = c * 8 + n
                total = grad_slots[j, head].astype(jnp.float32) + theirs_y[j].astype(jnp.float32)
                res_ref[j] = total.astype(res_ref.dtype)

    tiles = hidden // 128
    for tile in range(tiles):
        for which in range(2):
            start = which * hidden + tile * 128
            gate_up_grad_ref[pl.ds(tile * 2 + which, width, stride=2 * tiles), :] = wide_grad[
                :, start : start + 128
            ]
    some = pl.ds(0, 63)
    pltpu.make_async_copy(rows_ref.at[some], rows_ref.at[some], send).wait()
    pltpu.make_async_copy(sums.at[some], sums.at[some], home_send).wait()
    pltpu.make_async_copy(sums, home_ref, home_recv).wait()


def experts(rows, grads, gate_up, down, collective):
    hidden, width = down.shape
    half, bf16 = rows.shape, rows.dtype
    whole = (half[0], 2) + half[1:]
    vmem = pl.BlockSpec(memory_space=pltpu.VMEM)
    home, res, wide, down_grad = pl.pallas_call(
        experts_kernel,
        out_shape=[
            jax.ShapeDtypeStruct(half, bf16),
            jax.ShapeDtypeStruct(half, bf16),
            jax.ShapeDtypeStruct((width * 2 * hidden // 128, 128), jnp.float32),
            jax.ShapeDtypeStruct((hidden, width), jnp.float32),
        ],
        in_specs=[vmem] * 4,
        out_specs=[pl.BlockSpec(memory_space=pl.ANY)] + [vmem] * 3,
        scratch_shapes=[
            pltpu.VMEM(whole, bf16),
            pltpu.VMEM(whole, bf16),
            pltpu.VMEM(half, bf16),
            pltpu.VMEM(half, bf16),
            pltpu.VMEM(half, bf16),
            pltpu.VMEM((width, 2 * hidden), jnp.float32),
            pltpu.SemaphoreType.DMA,
            pltpu.SemaphoreType.DMA,
            pltpu.SemaphoreType.DMA,
            pltpu.SemaphoreType.DMA((10, 8)),
        ],
        compiler_params=params(collective, vmem_limit_bytes=58 * MIB),
        name="experts",
    )(rows, grads, gate_up, down)
    wide = wide.reshape(width, hidden // 128, 2, 128).transpose(0, 2, 1, 3)
    return home, res, wide.reshape(1, width, 2, hidden), down_grad[None]


class Scan:
    def __init__(self, reverse, at, me, x_ref, out_ref, got, made, sems):
        self.reverse, self.at, self.me = reverse, at, me
        self.x_ref, self.out_ref, self.got, self.made = x_ref, out_ref, got, made
        self.send, self.recv, self.back_send, self.back_recv = [sems.at[n] for n in range(4)]

    def spread(self, source, target_ref, send, recv):
        @pl.loop(1, 64)
        def _(k):
            target = torus_target(self.at, k)
            pltpu.make_async_remote_copy(
                src_ref=source.at[target],
                dst_ref=target_ref.at[self.me],
                send_sem=send,
                recv_sem=recv,
                device_id={"seq": target},
            ).start()

    def begin(self):
        self.got[self.me] = self.x_ref[self.me]
        self.spread(self.x_ref, self.got, self.send, self.recv)

    def middle(self):
        some = pl.ds(0, 63)
        x_ref, got, made = self.x_ref, self.got, self.made
        pltpu.make_async_copy(x_ref.at[some], x_ref.at[some], self.send).wait()
        pltpu.make_async_copy(got.at[some], got.at[some], self.recv).wait()
        heads, width = made.shape[1:]
        chosen = lax.broadcasted_iota(jnp.int32, (heads, width), 0) == lax.broadcasted_iota(
            jnp.int32, (heads, width), 1
        )

        def step(k, state):
            at_k = 63 - k if self.reverse else k
            made[at_k] = state
            row = got[at_k, heads : heads + 8, :][0:1, :]
            decay = jnp.sum(jnp.where(chosen, row, 0.0), axis=1, keepdims=True)
            return decay * state + got[at_k, 0:heads, :]

        lax.fori_loop(0, 64, step, jnp.zeros((heads, width), jnp.float32))
        self.out_ref[self.me] = made[self.me]
        self.spread(made, self.out_ref, self.back_send, self.back_recv)

    def end(self):
        some = pl.ds(0, 63)
        made = self.made
        pltpu.make_async_copy(made.at[some], made.at[some], self.back_send).wait()
        pltpu.make_async_copy(made.at[some], made.at[some], self.back_recv).wait()


def scan_shapes(size, heads, width):
    return [
        pltpu.VMEM((size, heads + 8, width), jnp.float32),
        pltpu.VMEM((size, heads, width), jnp.float32),
        pltpu.SemaphoreType.DMA((4,)),
    ]


def scan_kernel(reverse, x_ref, out_ref, got, made, sems):
    me, at = coordinates()
    greet_all(me)
    scan = Scan(reverse, at, me, x_ref, out_ref, got, made, sems)
    scan.begin()
    scan.middle()
    scan.end()


def scan_message(decay, state):
    heads, size, width = state.shape
    rows = jnp.broadcast_to(jnp.pad(decay, (0, width - heads))[None, None, :], (size, 8, width))
    return jnp.concatenate([state.transpose(1, 0, 2), rows], axis=1)


def carried(decay, state, collective):
    heads, size, width = state.shape
    out = pl.pallas_call(
        functools.partial(scan_kernel, False),
        out_shape=jax.ShapeDtypeStruct((size, heads, width), jnp.float32),
        in_specs=[pl.BlockSpec(memory_space=pltpu.VMEM)],
        out_specs=pl.BlockSpec(memory_space=pltpu.VMEM),
        scratch_shapes=scan_shapes(size, heads, width),
        compiler_params=params(collective),
        name="carried",
    )(scan_message(decay, state))
    return out.transpose(1, 0, 2)


class Small:
    def __init__(self, at, me, x_ref, out_ref, got, sems):
        self.at, self.me = at, me
        self.x_ref, self.out_ref, self.got = x_ref, out_ref, got
        self.send, self.recv, self.back_send, self.back_recv = [sems.at[n] for n in range(4)]

    def begin(self):
        self.got[self.me] = self.x_ref[self.me]

        @pl.loop(1, 64)
        def _(k):
            target = torus_target(self.at, k)
            pltpu.make_async_remote_copy(
                src_ref=self.x_ref.at[target],
                dst_ref=self.got.at[self.me],
                send_sem=self.send,
                recv_sem=self.recv,
                device_id={"seq": target},
            ).start()

    def middle(self):
        some = pl.ds(0, 63)
        x_ref, got, out_ref, me = self.x_ref, self.got, self.out_ref, self.me
        pltpu.make_async_copy(x_ref.at[some], x_ref.at[some], self.send).wait()
        pltpu.make_async_copy(got.at[some], got.at[some], self.recv).wait()
        out_ref[me] = lax.fori_loop(1, 64, lambda k, total: total + got[k], got[0])

        @pl.loop(1, 64)
        def _(k):
            target = torus_target(self.at, k)
            pltpu.make_async_remote_copy(
                src_ref=out_ref.at[me],
                dst_ref=out_ref.at[me],
                send_sem=self.back_send,
                recv_sem=self.back_recv,
                device_id={"seq": target},
            ).start()

    def end(self):
        some = pl.ds(0, 63)
        got = self.got
        pltpu.make_async_copy(got.at[some], got.at[some], self.back_send).wait()
        pltpu.make_async_copy(got.at[some], got.at[some], self.back_recv).wait()


class Scatter:
    def __init__(self, at, plan, lefts, right, out_ref, buf, rest, send, recv):
        self.at, self.plan, self.lefts, self.right = at, plan, lefts, right
        self.out_ref, self.buf, self.rest, self.send, self.recv = out_ref, buf, rest, send, recv
        self.third, self.half = parts_of(buf.shape[4])
        self.copies = {}

    def spans(self, p):
        start, third, half = p * self.third, self.third, self.half
        return pl.ds(start, half), pl.ds(start + half, third - half)

    def product(self, p):
        buf, right = self.buf, self.right
        rows = buf.shape[3]
        for which, start, length in self.plan[p]:
            left = self.lefts[which]

            @pl.loop(0, 4)
            def _(x):
                across = pl.ds(pl.multiple_of(x * 16 * rows, 128), 16 * rows)
                total = lax.dot_general(
                    left[:, across],
                    right[:, start : start + length],
                    (((0,), (0,)), ((), ())),
                    preferred_element_type=jnp.float32,
                )
                total = total.reshape(4, 4, rows, length).astype(jnp.bfloat16)
                buf[x, :, :, :, start : start + length] = total

    def send_to(self, phase, p, by, value, cols, slot, kind):
        order = ORDERS[p]
        axis = order[phase]
        lead = (slice(None),) * phase
        copy = pltpu.make_async_remote_copy(
            src_ref=self.buf.at[region(self.at, order, phase, value, cols)],
            dst_ref=self.rest[phase].at[(slot,) + lead + (slice(None), cols)],
            send_sem=self.send.at[phase, p, kind],
            recv_sem=self.recv.at[phase, p, kind],
            device_id={"seq": seq_of(moved(self.at, axis, by))},
        )
        copy.start()
        self.copies[phase, p, kind] = copy

    def added(self, phase, p, value, cols, slots):
        order, buf, room = ORDERS[p], self.buf, self.rest[phase]

        @pl.loop(0, 4**phase)
        def _(i):
            free = ((), (i,), (i // 4, i % 4))[phase]
            index = list(region(self.at, order, phase, value, cols))
            for n, axis in enumerate(sorted(order[:phase])):
                index[axis] = free[n]
            index = tuple(index)
            total = buf[index].astype(jnp.float32)
            for slot in slots:
                total = total + room[(slot,) + free + (slice(None), cols)].astype(jnp.float32)
            if phase == 0 and len(slots) == 2:
                self.out_ref[:, cols] = total
            else:
                buf[index] = total.astype(jnp.bfloat16)

    def first(self, phase, p):
        c = self.at[ORDERS[p][phase]]
        low, high = self.spans(p)
        self.send_to(phase, p, 1, (c + 2) % 4, low, 2, 0)
        self.send_to(phase, p, 3, (c + 2) % 4, high, 2, 1)
        self.send_to(phase, p, 1, (c + 1) % 4, high, 0, 2)
        self.send_to(phase, p, 3, (c + 3) % 4, low, 1, 3)

    def second(self, phase, p):
        c = self.at[ORDERS[p][phase]]
        low, high = self.spans(p)
        self.copies[phase, p, 0].wait_recv()
        self.added(phase, p, (c + 1) % 4, low, (2,))
        self.send_to(phase, p, 1, (c + 1) % 4, low, 0, 4)
        self.copies[phase, p, 1].wait_recv()
        self.added(phase, p, (c + 3) % 4, high, (2,))
        self.send_to(phase, p, 3, (c + 3) % 4, high, 1, 5)

    def third_step(self, phase, p):
        c = self.at[ORDERS[p][phase]]
        low, high = self.spans(p)
        self.copies[phase, p, 2].wait_recv()
        self.copies[phase, p, 5].wait_recv()
        self.added(phase, p, c, high, (0, 1))
        self.copies[phase, p, 3].wait_recv()
        self.copies[phase, p, 4].wait_recv()
        self.added(phase, p, c, low, (0, 1))

    def finish(self, phase):
        for p in range(3):
            self.third_step(phase, p)
            if phase > 0:
                self.first(phase - 1, p)

    def end(self):
        for copy in self.copies.values():
            copy.wait_send()


def scatter_shapes(rows, columns):
    return [
        pltpu.VMEM((4, 4, 4, rows, columns), jnp.bfloat16),
        [pltpu.VMEM((3,) + (4,) * phase + (rows, columns), jnp.bfloat16) for phase in range(3)],
        pltpu.SemaphoreType.DMA((3, 3, 6)),
        pltpu.SemaphoreType.DMA((3, 3, 6)),
    ]


def scatter_kernel(
    plan, lefts, right, scanned, small, out_ref, scan_out, small_out, buf, rest, send, recv, scan_scratch, small_scratch
):
    me, at = coordinates()
    greet_all(me)
    sums = Scatter(at, plan, lefts, right, out_ref, buf, rest, send, recv)
    others = []
    if scanned is not None:
        got, made, sems = scan_scratch
        others.append(Scan(True, at, me, scanned, scan_out, got, made, sems))
    if small is not None:
        got, sems = small_scratch
        others.append(Small(at, me, small, small_out, got, sems))
    for other in others:
        other.begin()
    for p in range(3):
        sums.product(p)
        sums.first(2, p)
    for other in others:
        other.middle()
    for phase in (2, 1, 0):
        for p in range(3):
            sums.second(phase, p)
        sums.finish(phase)
    for other in others:
        other.end()
    sums.end()


def scatter_rows(lefts, right, plan, collective, scanned=None, small=None):
    model, columns = lefts[0].shape[1], right.shape[1]
    rows = model // 64
    vmem = pl.BlockSpec(memory_space=pltpu.VMEM)
    scan_scratch = small_scratch = None
    out_shape = [jax.ShapeDtypeStruct((rows, columns), jnp.float32), None, None]
    if scanned is not None:
        size, heads, width = scanned.shape
        scan_scratch = scan_shapes(size, heads - 8, width)
        out_shape[1] = jax.ShapeDtypeStruct((size, heads - 8, width), jnp.float32)
    if small is not None:
        small_scratch = [pltpu.VMEM(small.shape, jnp.float32), pltpu.SemaphoreType.DMA((4,))]
        out_shape[2] = jax.ShapeDtypeStruct(small.shape, jnp.float32)
    spec = lambda tree: jax.tree.map(lambda _: vmem, tree)
    return pl.pallas_call(
        functools.partial(scatter_kernel, plan),
        out_shape=out_shape,
        in_specs=spec([lefts, right, scanned, small]),
        out_specs=spec(out_shape),
        scratch_shapes=scatter_shapes(rows, columns) + [scan_scratch, small_scratch],
        compiler_params=params(collective, vmem_limit_bytes=60 * MIB),
        name="scatter_rows",
    )(lefts, right, scanned, small)


def pair_kernel(x_ref, out_ref, theirs, send, recv):
    greet_sibling()
    copy = pltpu.make_async_remote_copy(
        src_ref=x_ref,
        dst_ref=theirs,
        send_sem=send,
        recv_sem=recv,
        device_id={"head": 1 - lax.axis_index("head")},
    )
    copy.start()
    copy.wait()
    rows = x_ref.shape[0]
    step = min(rows, 16)

    @pl.loop(0, rows // step)
    def _(i):
        here = pl.ds(pl.multiple_of(i * step, step), step)
        out_ref[here] = x_ref[here] + theirs[here]


def pair_total(x, collective):
    return pl.pallas_call(
        pair_kernel,
        out_shape=jax.ShapeDtypeStruct(x.shape, x.dtype),
        in_specs=[pl.BlockSpec(memory_space=pltpu.VMEM)],
        out_specs=pl.BlockSpec(memory_space=pltpu.VMEM),
        scratch_shapes=[
            pltpu.VMEM(x.shape, x.dtype),
            pltpu.SemaphoreType.DMA,
            pltpu.SemaphoreType.DMA,
        ],
        compiler_params=params(collective),
        name="pair_total",
    )(x)


def small_message(parts):
    flat = jnp.concatenate([part.reshape(-1) for part in parts])
    size = flat.shape[0]
    each = -(-size // (64 * 1024)) * 1024
    return jnp.pad(flat, (0, 64 * each - size)).reshape(64, each // 128, 128)


def small_parts(parts, out):
    out, result, start = out.reshape(-1), [], 0
    for part in parts:
        result.append(out[start : start + part.size].reshape(part.shape))
        start += part.size
    return result


def routing_kernel(routes_ref, weights_ref, position_ref, weight_ref):
    experts, tokens = position_ref.shape
    expert = lax.broadcasted_iota(jnp.int32, (experts, tokens), 0)
    named = jnp.zeros((experts, tokens), jnp.float32)
    weight = jnp.zeros((experts, tokens), jnp.float32)
    for k in range(routes_ref.shape[0]):
        hit = expert == routes_ref[k : k + 1, :]
        named = named + jnp.where(hit, 1.0, 0.0)
        weight = weight + jnp.where(hit, weights_ref[k : k + 1, :], 0.0)
    earlier = jnp.where(
        lax.broadcasted_iota(jnp.int32, (tokens, tokens), 0)
        < lax.broadcasted_iota(jnp.int32, (tokens, tokens), 1),
        1.0,
        0.0,
    ).astype(jnp.bfloat16)
    count = jnp.dot(named.astype(jnp.bfloat16), earlier, preferred_element_type=jnp.float32)
    position_ref[...] = jnp.where(named > 0.0, count, -1.0)
    weight_ref[...] = weight


def routing(routes, route_weights, experts):
    tokens = routes.shape[0]
    return pl.pallas_call(
        routing_kernel,
        out_shape=[jax.ShapeDtypeStruct((experts, tokens), jnp.float32)] * 2,
        name="routing",
    )(routes.T, route_weights.T)


def chosen_slots(position, first, count, slots):
    tokens = position.shape[1]
    number = lax.broadcasted_iota(jnp.int32, (count, slots, tokens), 1)
    number = (number + slots * lax.axis_index("head")).astype(jnp.float32)
    return jnp.where(position[:, None, :] == number, 1.0, 0.0).reshape(count * slots, tokens)


def send_kernel(slots, weigh, position_ref, weight_ref, rows_ref, out_ref):
    position = position_ref[...]
    chosen = chosen_slots(position, 0, position.shape[0], slots)
    rows = jnp.dot(
        chosen.astype(jnp.bfloat16), rows_ref[...], preferred_element_type=jnp.float32
    )
    if weigh:
        weighted = chosen.reshape(-1, slots, chosen.shape[1]) * weight_ref[...][:, None, :]
        rows = rows * jnp.sum(weighted.reshape(chosen.shape), axis=1, keepdims=True)
    out_ref[...] = rows.astype(jnp.bfloat16).reshape(out_ref.shape)


def send_rows(position, weight, rows, slots, weigh):
    experts, tokens = position.shape
    width = rows.shape[1]
    step = 16
    whole = pl.BlockSpec((tokens, width), lambda i: (0, 0))
    mine = pl.BlockSpec((step, tokens), lambda i: (i, 0))
    out = pl.BlockSpec((step, slots, width), lambda i: (i, 0, 0))
    return pl.pallas_call(
        functools.partial(send_kernel, slots, weigh),
        grid=(experts // step,),
        out_shape=jax.ShapeDtypeStruct((experts, slots, width), jnp.bfloat16),
        in_specs=[mine, mine, whole],
        out_specs=out,
        compiler_params=pltpu.CompilerParams(vmem_limit_bytes=40 * MIB),
        name="send_grads" if weigh else "send_rows",
    )(position, weight, rows)


def combine_kernel(slots, weigh, position_ref, weight_ref, rows_ref, out_ref):
    position = position_ref[...]
    count = position.shape[0]
    chosen = chosen_slots(position, 0, count, slots)
    rows = rows_ref[...].reshape(count * slots, rows_ref.shape[2])

    def over_slots(picked):
        return lax.dot_general(
            picked, rows, (((0,), (0,)), ((), ())), preferred_element_type=jnp.float32
        )

    @pl.when(pl.program_id(0) == 0)
    def _():
        out_ref[...] = jnp.zeros_like(out_ref)

    if weigh:
        weighted = chosen.reshape(count, slots, -1) * weight_ref[...][:, None, :]
        weighted = weighted.reshape(chosen.shape)
        high = weighted.astype(jnp.bfloat16)
        less = (weighted - high.astype(jnp.float32)).astype(jnp.bfloat16)
        out_ref[...] += over_slots(high) + over_slots(less)
    else:
        out_ref[...] += over_slots(chosen.astype(jnp.bfloat16))


def combine(position, weight, home, weigh):
    experts, tokens = position.shape
    _, slots, width = home.shape
    step = 16
    mine = pl.BlockSpec((step, tokens), lambda i: (i, 0))
    rows = pl.BlockSpec((step, slots, width), lambda i: (i, 0, 0))
    out = pl.BlockSpec((tokens, width), lambda i: (0, 0))
    return pl.pallas_call(
        functools.partial(combine_kernel, slots, weigh),
        grid=(experts // step,),
        out_shape=jax.ShapeDtypeStruct((tokens, width), jnp.float32),
        in_specs=[mine, mine, rows],
        out_specs=out,
        compiler_params=pltpu.CompilerParams(vmem_limit_bytes=40 * MIB),
        name="combine_mix" if weigh else "combine_grads",
    )(position, weight, home)


HIGHEST = lax.Precision.HIGHEST
EPSILON = 1e-05


def shifted(value, axis, steps):
    count = lax.axis_size(axis)
    leading, last = (max(0, -steps), min(count, count - steps))
    return lax.ppermute(value, axis, [(source, source + steps) for source in range(leading, last)])


def product(left_side, right_side):
    return jnp.dot(left_side, right_side, preferred_element_type=jnp.float32)


def product_nt(left_side, right_side):
    return lax.dot_general(
        left_side, right_side, (((1,), (1,)), ((), ())), preferred_element_type=jnp.float32
    )


def product_tn(left_side, right_side):
    return lax.dot_general(
        left_side, right_side, (((0,), (0,)), ((), ())), preferred_element_type=jnp.float32
    )


def silu(operand):
    return operand * jax.nn.sigmoid(operand)


def silu_slope(operand):
    sig_part = jax.nn.sigmoid(operand)
    return sig_part * (1.0 + operand * (1.0 - sig_part))


def rms_scale(operand):
    return lax.rsqrt(jnp.mean(operand * operand, axis=-1, keepdims=True) + EPSILON)


def norm_back(operand, row_scale, gain_vec, grad_rows):
    gain_grad = jnp.sum(grad_rows * operand * row_scale, axis=0)
    inner_mean = jnp.mean(operand * gain_vec * grad_rows, axis=-1, keepdims=True)
    return (gain_grad, row_scale * gain_vec * grad_rows - operand * row_scale**3 * inner_mean)


def group_state(heads_x, state_in, step_size, decay_rate):
    cum_decay = jnp.cumsum(-step_size * decay_rate[None, :], axis=0)
    tail_decay = cum_decay[-1]
    tok_weight = jnp.exp(tail_decay[None, :] - cum_decay) * step_size
    state_new = jnp.einsum("th,thp,tn->hpn", tok_weight, heads_x, state_in, precision=HIGHEST)
    return (jnp.exp(tail_decay), state_new)


def group_out(heads_x, state_in, state_read, step_size, decay_rate, state_start, skip_gain):
    length_rows = heads_x.shape[0]
    cum_decay = jnp.cumsum(-step_size * decay_rate[None, :], axis=0)
    causal = (jnp.arange(length_rows)[:, None] >= jnp.arange(length_rows)[None, :])[:, :, None]
    gap_decay = cum_decay[:, None, :] - cum_decay[None, :, :]
    decay_mat = jnp.where(causal, jnp.exp(jnp.where(causal, gap_decay, 0.0)), 0.0)
    scores = jnp.dot(state_read, state_in.T, precision=HIGHEST)
    mixing = decay_mat * scores[:, :, None] * step_size[None, :, :]
    within_part = jnp.einsum("tsh,shp->thp", mixing, heads_x, precision=HIGHEST)
    carried_part = jnp.exp(cum_decay)[:, :, None] * jnp.einsum(
        "tn,hpn->thp", state_read, state_start, precision=HIGHEST
    )
    return within_part + carried_part + skip_gain[None, :, None] * heads_x


def per_device(
    layer_in,
    norm_first,
    mixer_in,
    state_proj,
    step_proj,
    step_bias,
    conv_main,
    conv_state,
    decay_rate,
    skip_gain,
    gate_gain,
    mixer_out,
    norm_second,
    shared_gate_up,
    shared_down,
    expert_gate_up,
    expert_down,
    routes,
    route_weights,
    grad_out,
):
    tokens = layer_in.shape[0]
    model_width = layer_in.shape[1]
    inner_dev = mixer_in.shape[2]
    inner_all = inner_dev * lax.axis_size("head")
    state_size = state_proj.shape[1] // 2
    heads_dev = step_proj.shape[1]
    head_size = inner_dev // heads_dev
    conv_taps = conv_main.shape[0]
    shared_dev = shared_down.shape[1]
    local_experts = expert_gate_up.shape[0]
    seq_devices = lax.axis_size("seq")
    experts_all = local_experts * seq_devices
    choices_per = routes.shape[1]
    capacity = max(2, tokens * choices_per * 4 // (3 * experts_all))
    slot_count = local_experts * seq_devices * capacity
    gathered = gather_rows(
        jnp.concatenate(
            [
                mixer_in.reshape(-1, 2 * inner_dev),
                state_proj,
                jnp.pad(step_proj, ((0, 0), (0, 128 - heads_dev))),
            ],
            axis=1,
        ),
        0,
    ).reshape(model_width, -1)
    full_in = gathered[:, : 2 * inner_dev]
    full_state = gathered[:, 2 * inner_dev : 2 * inner_dev + 2 * state_size]
    full_step = gathered[:, 2 * inner_dev + 2 * state_size :][:, :heads_dev]
    late_rows = jnp.concatenate(
        [mixer_out, shared_gate_up.reshape(-1, 2 * shared_dev), shared_down], axis=1
    )
    full_in, late_rows, grad_out_late = lax.optimization_barrier((full_in, late_rows, grad_out))
    gathered = lax.all_gather(late_rows, "seq", axis=0, tiled=True)
    full_out = gathered[:, :inner_dev]
    shared_flat = gathered[:, inner_dev : inner_dev + 2 * shared_dev]
    full_down = gathered[:, inner_dev + 2 * shared_dev :]
    slots_dev = capacity // lax.axis_size("head")
    position, slot_weight = routing(routes, route_weights, experts_all)
    grads_out = send_rows(position, slot_weight, grad_out_late, slots_dev, True)
    grads_in = lax.all_to_all(grads_out, "seq", split_axis=0, concat_axis=0, tiled=True)
    resid_in = layer_in.astype(jnp.float32)
    scale_first = rms_scale(resid_in)
    normed = (resid_in * scale_first * norm_first).astype(jnp.bfloat16)
    zx_both = product(normed, full_in)
    gate_z = zx_both[:, :inner_dev]
    pre_x = zx_both[:, inner_dev:]
    pre_bc = product(normed, full_state)
    step_raw = product(normed, full_step) + step_bias
    conv_input = jnp.concatenate([pre_x, pre_bc], axis=1)
    edge_rows = shifted(conv_input[tokens - (conv_taps - 1) :], "seq", 1)
    padded = jnp.concatenate([edge_rows, conv_input], axis=0)
    kernel = jnp.concatenate([conv_main, conv_state], axis=1)
    conv_sum = kernel[0] * padded[0:tokens]
    for tap_index in range(1, conv_taps):
        conv_sum = conv_sum + kernel[tap_index] * padded[tap_index : tap_index + tokens]
    active = silu(conv_sum)
    heads_x = active[:, :inner_dev].reshape(tokens, heads_dev, head_size)
    state_in = active[:, inner_dev : inner_dev + state_size]
    state_read = active[:, inner_dev + state_size :]
    step_size = jax.nn.softplus(step_raw)
    decay_total, state_local = group_state(heads_x, state_in, step_size, decay_rate)
    state_start = carried(decay_total, state_local, 2)
    ssd = group_out(
        heads_x, state_in, state_read, step_size, decay_rate, state_start, skip_gain
    ).reshape(tokens, inner_dev)
    gate_act = silu(gate_z)
    gated_ssd = ssd * gate_act
    gate_scale = lax.rsqrt(pair_total(jnp.sum(gated_ssd * gated_ssd, axis=1).reshape(-1, 128), 4).reshape(-1) / inner_all + EPSILON)[
        :, None
    ]
    normed_gate = (gated_ssd * gate_scale * gate_gain).astype(jnp.bfloat16)
    mixer_sum = pair_total(product_nt(normed_gate, full_out), 6)
    residual = resid_in + mixer_sum
    scale_second = rms_scale(residual)
    normed_second = (residual * scale_second * norm_second).astype(jnp.bfloat16)
    shared_both = product(normed_second, shared_flat)
    shared_gate = shared_both[:, :shared_dev]
    shared_up = shared_both[:, shared_dev:]
    shared_hid = (silu(shared_gate) * shared_up).astype(jnp.bfloat16)
    shared_part = product_nt(shared_hid, full_down)
    rows_out = send_rows(position, slot_weight, normed_second, slots_dev, False)
    grad_home, res_sums, expert_gate_up_grad, expert_down_grad = experts(
        rows_out,
        grads_in,
        expert_gate_up.reshape(model_width, -1),
        expert_down.reshape(-1, model_width),
        11,
    )
    grad_float = grad_out.astype(jnp.float32)
    home_rows = lax.all_to_all(res_sums, "seq", split_axis=0, concat_axis=0, tiled=True)
    expert_grad_rows = combine(position, slot_weight, grad_home, False)
    grad_shared_hid = product(grad_out, full_down)
    grad_shared_gate = grad_shared_hid * shared_up * silu_slope(shared_gate)
    grad_shared_up = grad_shared_hid * silu(shared_gate)
    grad_shared_both = jnp.concatenate([grad_shared_gate, grad_shared_up], axis=1).astype(
        jnp.bfloat16
    )
    grad_normed_second = pair_total(product_nt(grad_shared_both, shared_flat) + expert_grad_rows, 8)
    norm_second_grad, grad_resid_norm = norm_back(
        residual, scale_second, norm_second, grad_normed_second
    )
    grad_resid = grad_float + grad_resid_norm
    grad_mix = grad_resid.astype(jnp.bfloat16)
    grad_normed_gate = product(grad_mix, full_out)
    weighted = grad_normed_gate * gate_gain
    inner_dot = pair_total(jnp.sum(weighted * gated_ssd, axis=1).reshape(-1, 128), 5).reshape(-1)[:, None]
    grad_gated = gate_scale * weighted - gated_ssd * gate_scale**3 * inner_dot / inner_all
    gate_gain_grad = jnp.sum(grad_normed_gate * gated_ssd * gate_scale, axis=0)
    grad_ssd = grad_gated * gate_act
    grad_gate_z = grad_gated * ssd * silu_slope(gate_z)
    _, pull_out = jax.vjp(
        group_out, heads_x, state_in, state_read, step_size, decay_rate, state_start, skip_gain
    )
    (
        grad_x_first,
        grad_in_first,
        grad_read,
        grad_step_first,
        grad_rate_first,
        grad_start,
        skip_gain_grad,
    ) = pull_out(grad_ssd.reshape(tokens, heads_dev, head_size))
    late_plan = (
        ((0, 0, 1024),),
        ((0, 1024, 512), (1, 1536, 512)),
        ((1, 2048, 512), (2, 2560, 512)),
    )
    summed_late, grad_next, _ = scatter_rows(
        [grad_mix, normed_second, grad_out],
        jnp.concatenate([normed_gate, grad_shared_both, shared_hid], axis=1),
        late_plan,
        3,
        scanned=scan_message(decay_total, grad_start),
    )
    grad_next = grad_next.transpose(1, 0, 2)
    grad_decay = jnp.sum(grad_next * state_start, axis=(1, 2))
    _, pull_state = jax.vjp(group_state, heads_x, state_in, step_size, decay_rate)
    grad_x_second, grad_in_second, grad_step_second, grad_rate_second = pull_state(
        (grad_decay, grad_next)
    )
    decay_rate_grad = grad_rate_first + grad_rate_second
    grad_bc = pair_total(
        jnp.concatenate([grad_in_first + grad_in_second, grad_read], axis=1), 10
    )
    grad_active = jnp.concatenate(
        [(grad_x_first + grad_x_second).reshape(tokens, inner_dev), grad_bc], axis=1
    )
    grad_conv = grad_active * silu_slope(conv_sum)
    grad_padded = jnp.pad(kernel[0] * grad_conv, ((0, conv_taps - 1), (0, 0)))
    for tap_index in range(1, conv_taps):
        grad_padded = grad_padded + jnp.pad(
            kernel[tap_index] * grad_conv, ((tap_index, conv_taps - 1 - tap_index), (0, 0))
        )
    kernel_grad = jnp.stack(
        [
            jnp.sum(grad_conv * padded[tap_index : tap_index + tokens], axis=0)
            for tap_index in range(conv_taps)
        ]
    )
    spill_rows = shifted(grad_padded[: conv_taps - 1], "seq", -1)
    grad_pre = grad_padded[conv_taps - 1 :]
    grad_pre = jnp.concatenate(
        [grad_pre[: tokens - (conv_taps - 1)], grad_pre[tokens - (conv_taps - 1) :] + spill_rows],
        axis=0,
    )
    grad_step_raw = (grad_step_first + grad_step_second) * jax.nn.sigmoid(step_raw)
    step_bias_grad = jnp.sum(grad_step_raw, axis=0)
    grad_zx = jnp.concatenate([grad_gate_z, grad_pre[:, :inner_dev]], axis=1).astype(jnp.bfloat16)
    grad_bc_low = grad_pre[:, inner_dev:].astype(jnp.bfloat16)
    grad_step_low = grad_step_raw.astype(jnp.bfloat16)
    in_partial = product_nt(grad_zx, full_in) + product_nt(
        grad_step_low, full_step
    )
    grad_normed = pair_total(in_partial, 9) + product_nt(grad_bc_low, full_state)
    norm_first_grad, grad_in_norm = norm_back(resid_in, scale_first, norm_first, grad_normed)
    input_grad = grad_resid + grad_in_norm
    small = (
        norm_first_grad,
        norm_second_grad,
        step_bias_grad,
        kernel_grad[:, :inner_dev],
        kernel_grad[:, inner_dev:],
        decay_rate_grad,
        skip_gain_grad,
        gate_gain_grad,
    )
    summed, _, small_sums = scatter_rows(
        [normed],
        jnp.concatenate(
            [grad_zx, grad_bc_low, jnp.pad(grad_step_low, ((0, 0), (0, 128 - heads_dev)))], axis=1
        ),
        tuple(((0, start, 1152),) for start in (0, 1152, 2304)),
        15,
        small=small_message(small),
    )
    small_sums = small_parts(small, small_sums)
    expert_mix = combine(position, slot_weight, home_rows, True)
    branch_sum = pair_total(shared_part + expert_mix, 7)
    layer_out = (residual + branch_sum).astype(jnp.bfloat16)
    wide = 2 * inner_dev + 2 * state_size
    weight_sums = (
        summed[:, : 2 * inner_dev].reshape(-1, 2, inner_dev),
        summed[:, 2 * inner_dev : wide],
        summed[:, wide : wide + heads_dev],
        summed_late[:, :inner_dev],
        summed_late[:, inner_dev : inner_dev + 2 * shared_dev].reshape(-1, 2, shared_dev),
        summed_late[:, inner_dev + 2 * shared_dev :],
    )
    return (
        layer_out,
        input_grad,
        small_sums[0],
        weight_sums[0],
        weight_sums[1],
        weight_sums[2],
        small_sums[2],
        small_sums[3],
        small_sums[4],
        small_sums[5],
        small_sums[6],
        small_sums[7],
        weight_sums[3],
        small_sums[1],
        weight_sums[4],
        weight_sums[5],
        expert_gate_up_grad,
        expert_down_grad,
    )


def solution(mesh):
    placed = (
        P("seq", None),
        P(),
        P("seq", None, "head"),
        P("seq", None),
        P("seq", "head"),
        P("head"),
        P(None, "head"),
        P(),
        P("head"),
        P("head"),
        P("head"),
        P("seq", "head"),
        P(),
        P("seq", None, "head"),
        P("seq", "head"),
        P("seq", None, None, "head"),
        P("seq", "head", None),
        P("seq", None),
        P("seq", None),
        P("seq", None),
    )
    return jax.shard_map(
        per_device,
        mesh=mesh,
        in_specs=placed,
        out_specs=(
            P("seq", None),
            P("seq", None),
            P(),
            P("seq", None, "head"),
            P("seq", None),
            P("seq", "head"),
            P("head"),
            P(None, "head"),
            P(),
            P("head"),
            P("head"),
            P("head"),
            P("seq", "head"),
            P(),
            P("seq", None, "head"),
            P("seq", "head"),
            P("seq", None, None, "head"),
            P("seq", "head", None),
        ),
        check_vma=False,
    )
```

```python
import functools
import jax
import jax.numpy as jnp
from jax import lax
from jax.experimental import pallas as pl
from jax.experimental.pallas import tpu as pltpu
from jax.sharding import PartitionSpec as P

ORDERS = ((0, 1, 2), (1, 2, 0), (2, 0, 1))
MIB = 1 << 20
EPSILON = 1e-05


def coordinates():
    me = lax.axis_index("seq")
    return me, [me // 16, (me // 4) % 4, me % 4]


def seq_of(at):
    return at[0] * 16 + at[1] * 4 + at[2]


def moved(at, axis, by):
    return [(c + by) % 4 if i == axis else c for i, c in enumerate(at)]


def greet_neighbours(at, count=6):
    barrier = pltpu.get_barrier_semaphore()
    for axis in range(3):
        for by in (1, 3):
            pl.semaphore_signal(barrier, inc=1, device_id={"seq": seq_of(moved(at, axis, by))})
    pl.semaphore_wait(barrier, count)


def greet_all(me):
    barrier = pltpu.get_barrier_semaphore()

    @pl.loop(1, 64)
    def _(k):
        pl.semaphore_signal(barrier, inc=1, device_id={"seq": (me + k) % 64})

    pl.semaphore_wait(barrier, 63)


def parts_of(columns):
    third = columns // 3
    tiles = third // 128
    half = tiles // 2 * 128
    return third, half


def region(at, order, phase, value, cols):
    index = [None] * 3
    for i in range(3):
        if i < phase:
            index[order[i]] = slice(None)
        elif i == phase:
            index[order[i]] = value
        else:
            index[order[i]] = at[order[i]]
    return tuple(index) + (slice(None), cols)


def torus_target(at, k):
    return ((at[0] + k // 16) % 4) * 16 + ((at[1] + k // 4) % 4) * 4 + (at[2] + k) % 4


def params(collective, **more):
    return pltpu.CompilerParams(collective_id=collective, has_side_effects=True, **more)


def greet_all_and_sibling(me):
    barrier = pltpu.get_barrier_semaphore()

    @pl.loop(1, 64)
    def _(k):
        pl.semaphore_signal(barrier, inc=1, device_id={"seq": (me + k) % 64})

    pl.semaphore_signal(barrier, inc=1, device_id={"head": 1 - lax.axis_index("head")})
    pl.semaphore_wait(barrier, 64)


def greet_sibling():
    barrier = pltpu.get_barrier_semaphore()
    pl.semaphore_signal(barrier, inc=1, device_id={"head": 1 - lax.axis_index("head")})
    pl.semaphore_wait(barrier, 1)


def experts_kernel(
    rows_ref,
    grads_ref,
    gate_up_ref,
    down_ref,
    home_ref,
    res_ref,
    gate_up_grad_ref,
    down_grad_ref,
    slot_in,
    grad_slots,
    theirs_x,
    theirs_y,
    sums,
    wide_grad,
    send,
    home_send,
    home_recv,
    sems,
):
    me, at = coordinates()
    head = lax.axis_index("head")
    sibling = {"head": 1 - head}
    mine, place = me // 8, me % 8
    names = ("recv", "fwd_send", "fwd_recv", "kept", "given_send", "given_recv")
    names += ("x_send", "x_recv", "y_send", "y_recv")
    sem = {name: sems.at[n] for n, name in enumerate(names)}
    greet_all_and_sibling(me)

    def group(c):
        return pl.ds(pl.multiple_of(c * 8, 8), 8)

    own = pltpu.make_async_copy(rows_ref.at[me], slot_in.at[me, head], sem["recv"].at[mine])
    own.start()

    @pl.loop(0, 64)
    def _(k):
        j = ((mine - k // 8) % 8) * 8 + (place + k) % 8

        @pl.when(k > 0)
        def _():
            pltpu.make_async_remote_copy(
                src_ref=rows_ref.at[j],
                dst_ref=slot_in.at[me, head],
                send_sem=send,
                recv_sem=sem["recv"].at[mine],
                device_id={"seq": j},
            ).start()

    def given(c):
        return pltpu.make_async_remote_copy(
            src_ref=grads_ref.at[group(c)],
            dst_ref=grad_slots.at[group(c), head],
            send_sem=sem["given_send"].at[c],
            recv_sem=sem["given_recv"].at[c],
            device_id=sibling,
        )

    def kept(c):
        return pltpu.make_async_copy(
            grads_ref.at[group(c)], grad_slots.at[group(c), head], sem["kept"].at[c]
        )

    def forward(c):
        return pltpu.make_async_remote_copy(
            src_ref=slot_in.at[group(c), head],
            dst_ref=slot_in.at[group(c), head],
            send_sem=sem["fwd_send"].at[c],
            recv_sem=sem["fwd_recv"].at[c],
            device_id=sibling,
        )

    def swap(c, source, target, name):
        return pltpu.make_async_remote_copy(
            src_ref=source.at[group(c), 1 - head],
            dst_ref=target.at[group(c)],
            send_sem=sem[name + "_send"].at[c],
            recv_sem=sem[name + "_recv"].at[c],
            device_id=sibling,
        )

    @pl.loop(0, 8)
    def _(i):
        c = (mine + i) % 8
        kept(c).start()
        given(c).start()

    wide_grad[...] = jnp.zeros_like(wide_grad)
    down_grad_ref[...] = jnp.zeros_like(down_grad_ref)
    hidden = down_ref.shape[0]
    width = down_ref.shape[1]

    def nt(left, right):
        return lax.dot_general(
            left, right, (((1,), (1,)), ((), ())), preferred_element_type=jnp.float32
        )

    def tn(left, right):
        return lax.dot_general(
            left, right, (((0,), (0,)), ((), ())), preferred_element_type=jnp.float32
        )

    @pl.loop(0, 10)
    def _(i):
        @pl.when(i < 8)
        def _():
            c = (mine + i) % 8
            pltpu.make_async_copy(
                rows_ref.at[group(c)], slot_in.at[group(c), head], sem["recv"].at[c]
            ).wait()
            forward(c).start()

        @pl.when((i >= 1) & (i < 9))
        def _():
            c = (mine + i + 7) % 8
            forward(c).wait()
            kept(c).wait()
            given(c).wait()
            rows = slot_in[group(c)].reshape(256, width)
            grads = grad_slots[group(c)].reshape(256, width)
            both = jnp.dot(rows, gate_up_ref[...], preferred_element_type=jnp.float32)
            gate, up = both[:, :hidden], both[:, hidden:]
            sig = jax.nn.sigmoid(gate)
            act = gate * sig
            hid = (act * up).astype(jnp.bfloat16)
            grad_hid = nt(grads, down_ref[...])
            grad_gate = grad_hid * up * (sig * (1.0 + gate * (1.0 - sig)))
            grad_both = jnp.concatenate([grad_gate, grad_hid * act], axis=1).astype(jnp.bfloat16)
            wide_grad[...] += tn(rows, grad_both)
            down_grad_ref[...] += tn(hid, grads)
            back = nt(grad_both, gate_up_ref[...]).astype(jnp.bfloat16)
            slot_in[group(c)] = back.reshape(8, 2, 16, width)
            res = jnp.dot(hid, down_ref[...], preferred_element_type=jnp.float32)
            grad_slots[group(c)] = res.astype(jnp.bfloat16).reshape(8, 2, 16, width)
            swap(c, slot_in, theirs_x, "x").start()
            swap(c, grad_slots, theirs_y, "y").start()

        @pl.when(i >= 2)
        def _():
            c = (mine + i + 6) % 8
            swap(c, slot_in, theirs_x, "x").wait()

            @pl.loop(0, 8)
            def _(n):
                j = c * 8 + (place + n) % 8
                total = slot_in[j, head].astype(jnp.float32) + theirs_x[j].astype(jnp.float32)
                sums[j] = total.astype(sums.dtype)

                @pl.when(j != me)
                def _():
                    pltpu.make_async_remote_copy(
                        src_ref=sums.at[j],
                        dst_ref=home_ref.at[me],
                        send_sem=home_send,
                        recv_sem=home_recv,
                        device_id={"seq": j},
                    ).start()

                @pl.when(j == me)
                def _():
                    pltpu.make_async_copy(sums.at[me], home_ref.at[me], home_recv).start()

            swap(c, grad_slots, theirs_y, "y").wait()

            @pl.loop(0, 8)
            def _(n):
                j = c * 8 + n
                total = grad_slots[j, head].astype(jnp.float32) + theirs_y[j].astype(jnp.float32)
                res_ref[j] = total.astype(res_ref.dtype)

    tiles = hidden // 128
    for tile in range(tiles):
        for which in range(2):
            start = which * hidden + tile * 128
            gate_up_grad_ref[pl.ds(tile * 2 + which, width, stride=2 * tiles), :] = wide_grad[
                :, start : start + 128
            ]
    some = pl.ds(0, 63)
    pltpu.make_async_copy(rows_ref.at[some], rows_ref.at[some], send).wait()
    pltpu.make_async_copy(sums.at[some], sums.at[some], home_send).wait()
    pltpu.make_async_copy(sums, home_ref, home_recv).wait()


def experts(rows, grads, gate_up, down, collective):
    hidden, width = down.shape
    half, bf16 = rows.shape, rows.dtype
    whole = (half[0], 2) + half[1:]
    vmem = pl.BlockSpec(memory_space=pltpu.VMEM)
    home, res, wide, down_grad = pl.pallas_call(
        experts_kernel,
        out_shape=[
            jax.ShapeDtypeStruct(half, bf16),
            jax.ShapeDtypeStruct(half, bf16),
            jax.ShapeDtypeStruct((width * 2 * hidden // 128, 128), jnp.float32),
            jax.ShapeDtypeStruct((hidden, width), jnp.float32),
        ],
        in_specs=[vmem] * 4,
        out_specs=[pl.BlockSpec(memory_space=pl.ANY)] + [vmem] * 3,
        scratch_shapes=[
            pltpu.VMEM(whole, bf16),
            pltpu.VMEM(whole, bf16),
            pltpu.VMEM(half, bf16),
            pltpu.VMEM(half, bf16),
            pltpu.VMEM(half, bf16),
            pltpu.VMEM((width, 2 * hidden), jnp.float32),
            pltpu.SemaphoreType.DMA,
            pltpu.SemaphoreType.DMA,
            pltpu.SemaphoreType.DMA,
            pltpu.SemaphoreType.DMA((10, 8)),
        ],
        compiler_params=params(collective, vmem_limit_bytes=58 * MIB),
        name="experts",
    )(rows, grads, gate_up, down)
    wide = wide.reshape(width, hidden // 128, 2, 128).transpose(0, 2, 1, 3)
    return home, res, wide.reshape(1, width, 2, hidden), down_grad[None]


class Scan:
    def __init__(self, reverse, at, me, x_ref, out_ref, got, made, sems):
        self.reverse, self.at, self.me = reverse, at, me
        self.x_ref, self.out_ref, self.got, self.made = x_ref, out_ref, got, made
        self.send, self.recv, self.back_send, self.back_recv = [sems.at[n] for n in range(4)]

    def spread(self, source, target_ref, send, recv):
        @pl.loop(1, 64)
        def _(k):
            target = torus_target(self.at, k)
            pltpu.make_async_remote_copy(
                src_ref=source.at[target],
                dst_ref=target_ref.at[self.me],
                send_sem=send,
                recv_sem=recv,
                device_id={"seq": target},
            ).start()

    def begin(self):
        self.got[self.me] = self.x_ref[self.me]
        self.spread(self.x_ref, self.got, self.send, self.recv)

    def middle(self):
        some = pl.ds(0, 63)
        x_ref, got, made = self.x_ref, self.got, self.made
        pltpu.make_async_copy(x_ref.at[some], x_ref.at[some], self.send).wait()
        pltpu.make_async_copy(got.at[some], got.at[some], self.recv).wait()
        heads, width = made.shape[1:]
        number = lax.broadcasted_iota(jnp.int32, (heads, width), 0) + heads * self.me
        chosen = number // 64 == lax.broadcasted_iota(jnp.int32, (heads, width), 1)

        def step(k, state):
            at_k = 63 - k if self.reverse else k
            made[at_k] = state
            row = got[at_k, heads : heads + 8, :][0:1, :]
            decay = jnp.sum(jnp.where(chosen, row, 0.0), axis=1, keepdims=True)
            return decay * state + got[at_k, 0:heads, :]

        lax.fori_loop(0, 64, step, jnp.zeros((heads, width), jnp.float32))
        self.out_ref[self.me] = made[self.me]
        self.spread(made, self.out_ref, self.back_send, self.back_recv)

    def end(self):
        some = pl.ds(0, 63)
        made = self.made
        pltpu.make_async_copy(made.at[some], made.at[some], self.back_send).wait()
        pltpu.make_async_copy(made.at[some], made.at[some], self.back_recv).wait()


class Small:
    def __init__(self, at, me, x_ref, out_ref, got, sems):
        self.at, self.me = at, me
        self.x_ref, self.out_ref, self.got = x_ref, out_ref, got
        self.send, self.recv, self.back_send, self.back_recv = [sems.at[n] for n in range(4)]

    def begin(self):
        self.got[self.me] = self.x_ref[self.me]

        @pl.loop(1, 64)
        def _(k):
            target = torus_target(self.at, k)
            pltpu.make_async_remote_copy(
                src_ref=self.x_ref.at[target],
                dst_ref=self.got.at[self.me],
                send_sem=self.send,
                recv_sem=self.recv,
                device_id={"seq": target},
            ).start()

    def middle(self):
        some = pl.ds(0, 63)
        x_ref, got, out_ref, me = self.x_ref, self.got, self.out_ref, self.me
        pltpu.make_async_copy(x_ref.at[some], x_ref.at[some], self.send).wait()
        pltpu.make_async_copy(got.at[some], got.at[some], self.recv).wait()
        out_ref[me] = lax.fori_loop(1, 64, lambda k, total: total + got[k], got[0])

        @pl.loop(1, 64)
        def _(k):
            target = torus_target(self.at, k)
            pltpu.make_async_remote_copy(
                src_ref=out_ref.at[me],
                dst_ref=out_ref.at[me],
                send_sem=self.back_send,
                recv_sem=self.back_recv,
                device_id={"seq": target},
            ).start()

    def end(self):
        some = pl.ds(0, 63)
        got = self.got
        pltpu.make_async_copy(got.at[some], got.at[some], self.back_send).wait()
        pltpu.make_async_copy(got.at[some], got.at[some], self.back_recv).wait()


class Scatter:
    def __init__(self, at, plan, lefts, right, out_ref, buf, rest, send, recv):
        self.at, self.plan, self.lefts, self.right = at, plan, lefts, right
        self.out_ref, self.buf, self.rest, self.send, self.recv = out_ref, buf, rest, send, recv
        self.third, self.half = parts_of(buf.shape[4])
        self.copies = {}

    def spans(self, p):
        start, third, half = p * self.third, self.third, self.half
        return pl.ds(start, half), pl.ds(start + half, third - half)

    def product(self, p):
        buf, right = self.buf, self.right
        rows = buf.shape[3]
        for which, start, length in self.plan[p]:
            left = self.lefts[which]

            @pl.loop(0, 4)
            def _(x):
                across = pl.ds(pl.multiple_of(x * 16 * rows, 128), 16 * rows)
                total = lax.dot_general(
                    left[:, across],
                    right[:, start : start + length],
                    (((0,), (0,)), ((), ())),
                    preferred_element_type=jnp.float32,
                )
                total = total.reshape(4, 4, rows, length).astype(jnp.bfloat16)
                buf[x, :, :, :, start : start + length] = total

    def send_to(self, phase, p, by, value, cols, slot, kind):
        order = ORDERS[p]
        axis = order[phase]
        lead = (slice(None),) * phase
        copy = pltpu.make_async_remote_copy(
            src_ref=self.buf.at[region(self.at, order, phase, value, cols)],
            dst_ref=self.rest[phase].at[(slot,) + lead + (slice(None), cols)],
            send_sem=self.send.at[phase, p, kind],
            recv_sem=self.recv.at[phase, p, kind],
            device_id={"seq": seq_of(moved(self.at, axis, by))},
        )
        copy.start()
        self.copies[phase, p, kind] = copy

    def added(self, phase, p, value, cols, slots):
        order, buf, room = ORDERS[p], self.buf, self.rest[phase]

        @pl.loop(0, 4**phase)
        def _(i):
            free = ((), (i,), (i // 4, i % 4))[phase]
            index = list(region(self.at, order, phase, value, cols))
            for n, axis in enumerate(sorted(order[:phase])):
                index[axis] = free[n]
            index = tuple(index)
            total = buf[index].astype(jnp.float32)
            for slot in slots:
                total = total + room[(slot,) + free + (slice(None), cols)].astype(jnp.float32)
            if phase == 0 and len(slots) == 2:
                self.out_ref[:, cols] = total
            else:
                buf[index] = total.astype(jnp.bfloat16)

    def first(self, phase, p):
        c = self.at[ORDERS[p][phase]]
        low, high = self.spans(p)
        self.send_to(phase, p, 1, (c + 2) % 4, low, 2, 0)
        self.send_to(phase, p, 3, (c + 2) % 4, high, 2, 1)
        self.send_to(phase, p, 1, (c + 1) % 4, high, 0, 2)
        self.send_to(phase, p, 3, (c + 3) % 4, low, 1, 3)

    def second(self, phase, p):
        c = self.at[ORDERS[p][phase]]
        low, high = self.spans(p)
        self.copies[phase, p, 0].wait_recv()
        self.added(phase, p, (c + 1) % 4, low, (2,))
        self.send_to(phase, p, 1, (c + 1) % 4, low, 0, 4)
        self.copies[phase, p, 1].wait_recv()
        self.added(phase, p, (c + 3) % 4, high, (2,))
        self.send_to(phase, p, 3, (c + 3) % 4, high, 1, 5)

    def third_step(self, phase, p):
        c = self.at[ORDERS[p][phase]]
        low, high = self.spans(p)
        self.copies[phase, p, 2].wait_recv()
        self.copies[phase, p, 5].wait_recv()
        self.added(phase, p, c, high, (0, 1))
        self.copies[phase, p, 3].wait_recv()
        self.copies[phase, p, 4].wait_recv()
        self.added(phase, p, c, low, (0, 1))

    def finish(self, phase):
        for p in range(3):
            self.third_step(phase, p)
            if phase > 0:
                self.first(phase - 1, p)

    def end(self):
        for copy in self.copies.values():
            copy.wait_send()


def scatter_shapes(rows, columns):
    return [
        pltpu.VMEM((4, 4, 4, rows, columns), jnp.bfloat16),
        [pltpu.VMEM((3,) + (4,) * phase + (rows, columns), jnp.bfloat16) for phase in range(3)],
        pltpu.SemaphoreType.DMA((3, 3, 6)),
        pltpu.SemaphoreType.DMA((3, 3, 6)),
    ]


def dot_nn(left, right):
    return jnp.dot(left, right, preferred_element_type=jnp.float32)


def dot_nt(left, right):
    return lax.dot_general(
        left, right, (((1,), (1,)), ((), ())), preferred_element_type=jnp.float32
    )


def dot_tn(left, right):
    return lax.dot_general(
        left, right, (((0,), (0,)), ((), ())), preferred_element_type=jnp.float32
    )


def low(value):
    return value.astype(jnp.bfloat16)


def split(value, count):
    parts = []
    for _ in range(count):
        parts.append(low(value))
        value = value - parts[-1].astype(jnp.float32)
    return parts


def dot_split(left, right, count, dot=dot_nn):
    return sum(dot(left, part) for part in split(right, count))


def split_dot(left, right, count):
    return sum(dot_nn(part, right) for part in split(left, count))


def dot_three(left, right, dot=dot_nn):
    high, less = split(left, 2)
    other_high, other_less = split(right, 2)
    return dot(high, other_high) + dot(less, other_high) + dot(high, other_less)


def head_spread(lanes, width, size):
    head = lax.broadcasted_iota(jnp.int32, (lanes, width), 0)
    column = lax.broadcasted_iota(jnp.int32, (lanes, width), 1)
    return low(jnp.where(head == column // size, 1.0, 0.0))


def head_gather(lanes, width, size):
    head = lax.broadcasted_iota(jnp.int32, (width, lanes), 1)
    column = lax.broadcasted_iota(jnp.int32, (width, lanes), 0)
    return low(jnp.where(head == column // size, 1.0, 0.0))


def triangle(rows, keep):
    first = lax.broadcasted_iota(jnp.int32, (rows, rows), 0)
    second = lax.broadcasted_iota(jnp.int32, (rows, rows), 1)
    return keep(first, second)


def silu_parts(value):
    sig = jax.nn.sigmoid(value)
    return value * sig, sig * (1.0 + value * (1.0 - sig))


def mixer_back_kernel(
    plan,
    lefts,
    right,
    dy_ref,
    y_ref,
    x_ref,
    bc_ref,
    conv_ref,
    pre_ref,
    gate_ref,
    step_raw_ref,
    numbers_ref,
    taps_ref,
    start_ref,
    out_ref,
    grads_ref,
    taps_grad_ref,
    heads_grad_ref,
    message,
    back,
    got,
    made,
    decayed,
    q,
    spread,
    cum_rows,
    scores,
    acc,
    ext,
    mine,
    theirs,
    buf,
    rest,
    send,
    recv,
    scan_sems,
    sems,
):
    me, at = coordinates()
    head = lax.axis_index("head")
    tokens, width = x_ref.shape
    size = start_ref.shape[1]
    lanes = step_raw_ref.shape[1]
    each = width // 64
    mid = tokens // 2
    cut = 384
    greet_all_and_sibling(me)
    sums = Scatter(at, plan, lefts, right, out_ref, buf, rest, send, recv)
    scan = Scan(True, at, me, message, back, got, made, scan_sems)

    rate = numbers_ref[0:1, :]
    step_raw = step_raw_ref[...]
    step = jax.nn.softplus(step_raw)
    earlier = low(triangle(tokens, lambda t, s: jnp.where(t >= s, 1.0, 0.0)))
    cum = dot_split(earlier, -step * rate, 3)
    cum_rows[...] = cum.T
    tail = cum[tokens - 1 : tokens, :]
    rest_decay = jnp.exp(tail - cum)
    weight = rest_decay * step
    spreader = head_spread(lanes, width, 64)
    gatherer = head_gather(lanes, width, 64)
    spread[...] = split_dot(jnp.exp(cum), spreader, 2)
    held_full, read_full = bc_ref[:, :size], bc_ref[:, size:]
    held, read = low(held_full), low(read_full)

    for c in range(0, width, cut):
        part = dy_ref[:, c : c + cut] * spread[:, c : c + cut]
        decayed[:, c : c + cut] = part
        made_rows = dot_three(part, read_full, dot_tn)
        message[c // each : (c + cut) // each, 0:each, :] = made_rows.reshape(
            cut // each, each, size
        )
    message[:, each : each + 8, :] = jnp.broadcast_to(jnp.exp(tail)[None], (64, 8, lanes))
    scan.begin()
    for p in range(3):
        sums.product(p)
    scan.middle()
    for p in range(3):
        sums.first(2, p)

    spread[...] = split_dot(step, spreader, 2)
    blocks = ((0, 0), (0, 1), (1, 1))
    for n, (s, t) in enumerate(blocks):
        scores[n] = dot_nt(held[s * mid : (s + 1) * mid], read[t * mid : (t + 1) * mid])
    acc[...] = jnp.zeros_like(acc)
    causal = triangle(mid, lambda s, t: s <= t)
    second_head = lax.broadcasted_iota(jnp.int32, (tokens, 128), 1) >= 64

    @pl.loop(0, width // 128)
    def _(i):
        here = pl.ds(pl.multiple_of(i * 128, 128), 128)
        dy, dy_less = split(dy_ref[:, here], 2)
        stepped = x_ref[:, here] * spread[:, here]
        results = []
        for which in range(2):
            row = cum_rows[pl.ds(2 * i + which, 1), :]
            column = jnp.broadcast_to(row, (128, tokens)).T
            mask = second_head if which else jnp.logical_not(second_head)
            values, values_less = split(jnp.where(mask, stepped, 0.0), 2)
            total = [None, None]
            for n, (s, t) in enumerate(blocks):
                gap = row[:, t * mid : (t + 1) * mid] - column[s * mid : (s + 1) * mid]
                decay = jnp.exp(gap)
                if s == t:
                    decay = jnp.where(causal, decay, 0.0)
                later = dy[t * mid : (t + 1) * mid]
                first, later_less = values[s * mid : (s + 1) * mid], dy_less[t * mid : (t + 1) * mid]
                pairs = dot_nt(first, later) + dot_nt(first, later_less)
                pairs = pairs + dot_nt(values_less[s * mid : (s + 1) * mid], later)
                acc[n] += decay * pairs
                part = dot_nn(low(decay * scores[n]), later)
                total[s] = part if total[s] is None else total[s] + part
            results.append(total)
        for s in range(2):
            rows = slice(s * mid, (s + 1) * mid)
            q[rows, here] = jnp.where(second_head[rows], results[1][s], results[0][s])

    scan.end()

    skip = split_dot(jnp.broadcast_to(numbers_ref[1:2, :], (8, lanes)), spreader, 2)[0:1, :]
    grad_weight = grad_step = rows_sum = jnp.zeros((tokens, lanes), jnp.float32)
    skip_grad = jnp.zeros((8, lanes), jnp.float32)
    state_dot = jnp.zeros((lanes, size), jnp.float32)
    held_parts = held_full[:mid], held_full[mid:]
    read_parts = read_full[:mid], read_full[mid:]
    grad_held = dot_three(acc[0], read_parts[0]) + dot_three(acc[1], read_parts[1])
    grad_held = jnp.concatenate([grad_held, dot_three(acc[2], read_parts[1])], axis=0)
    grad_read = dot_three(acc[1], held_parts[0], dot_tn) + dot_three(acc[2], held_parts[1], dot_tn)
    grad_read = jnp.concatenate([dot_three(acc[0], held_parts[0], dot_tn), grad_read], axis=0)
    for c in range(0, width, cut):
        here = slice(c, c + cut)
        x, dy, inner = x_ref[:, here], dy_ref[:, here], q[:, here]
        after = back[c // each : (c + cut) // each].reshape(cut, size)
        start = start_ref[here, :]
        gather = gatherer[here, :]
        weights = split_dot(weight, spreader[:, here], 2)
        through = dot_nt(held, low(after))
        grad_x = inner * spread[:, here] + skip[:, here] * dy + weights * through
        grad_step = grad_step + split_dot(x * inner, gather, 2)
        grad_weight = grad_weight + split_dot(x * through, gather, 2)
        rows_sum = rows_sum + split_dot(dy * (y_ref[:, here] - skip[:, here] * x), gather, 2)
        pairs = jnp.sum(dy * x, axis=0, keepdims=True)
        skip_grad = skip_grad + split_dot(jnp.broadcast_to(pairs, (8, cut)), gather, 2)
        state_dot = state_dot + dot_split(gather, after * start, 2, dot_tn)
        grad_held = grad_held + dot_three(weights * x, after)
        grad_read = grad_read + dot_three(decayed[:, here], start)
        ext[0:tokens, here] = grad_x * silu_parts(conv_ref[:, here])[1]
    mine[:, :size] = grad_held
    mine[:, size:] = grad_read
    swap = pltpu.make_async_remote_copy(
        src_ref=mine,
        dst_ref=theirs,
        send_sem=sems.at[0],
        recv_sem=sems.at[1],
        device_id={"head": 1 - head},
    )
    swap.start()
    for p in range(3):
        sums.second(2, p)

    ones = jnp.ones((8, size), jnp.bfloat16)
    state_grad = dot_split(ones, state_dot, 2, dot_nt)[0:1, :]
    used = grad_weight * weight
    tail_grad = jnp.sum(used, axis=0, keepdims=True) + jnp.exp(tail) * state_grad
    grad_cum = rows_sum - step * grad_step - used
    last = lax.broadcasted_iota(jnp.int32, (tokens, lanes), 0) == tokens - 1
    grad_cum = grad_cum + jnp.where(last, tail_grad, 0.0)
    later = low(triangle(tokens, lambda t, s: jnp.where(t <= s, 1.0, 0.0)))
    grad_log = dot_split(later, grad_cum, 3)
    grad_step = grad_step + grad_weight * rest_decay - rate * grad_log
    grad_raw = grad_step * jax.nn.sigmoid(step_raw)
    heads_grad_ref[...] = jnp.zeros_like(heads_grad_ref)
    heads_grad_ref[0:1, :] = skip_grad[0:1, :]
    heads_grad_ref[1:2, :] = -jnp.sum(step * grad_log, axis=0, keepdims=True)
    heads_grad_ref[2:3, :] = jnp.sum(grad_raw, axis=0, keepdims=True)

    channels = width + 2 * size
    grads_ref[:, 0:width] = gate_ref[...]
    grads_ref[:, width + channels : width + channels + lanes] = low(grad_raw)
    swap.wait()
    ext[0:tokens, width:channels] = (mine[...] + theirs[...]) * silu_parts(
        conv_ref[:, width:channels]
    )[1]
    edge = pltpu.make_async_remote_copy(
        src_ref=ext.at[pl.ds(0, 8)],
        dst_ref=ext.at[pl.ds(tokens, 8)],
        send_sem=sems.at[2],
        recv_sem=sems.at[3],
        device_id={"seq": (me + 63) % 64},
    )
    edge.start()
    sums.finish(2)
    edge.wait()
    there = jnp.where(me == 63, 0.0, 1.0)
    ext[tokens : tokens + 8, :] = ext[tokens : tokens + 8, :] * there
    taps_grad_ref[...] = jnp.zeros_like(taps_grad_ref)

    @pl.loop(0, channels // 256)
    def _(i):
        here = pl.ds(pl.multiple_of(i * 256, 256), 256)
        grad = ext[0:tokens, here]
        total = jnp.zeros_like(grad)
        for j in range(4):
            total = total + taps_ref[j : j + 1, here] * ext[3 - j : 3 - j + tokens, here]
            products = grad * pre_ref[5 + j : 5 + j + tokens, here]
            taps_grad_ref[j : j + 1, here] = jnp.sum(products, axis=0, keepdims=True)
        grads_ref[:, pl.ds(pl.multiple_of(width + i * 256, 256), 256)] = low(total)

    for phase in (1, 0):
        for p in range(3):
            sums.second(phase, p)
        sums.finish(phase)
    sums.end()


def mixer_back(lefts, right, plan, dy, y, x, bc, conv, pre, gate, step_raw, numbers, taps, start, collective):
    model, columns = lefts[0].shape[1], right.shape[1]
    rows = model // 64
    tokens, width = x.shape
    size, lanes = start.shape[1], step_raw.shape[1]
    each, channels, mid = width // 64, width + 2 * size, tokens // 2
    f32, bf16 = jnp.float32, jnp.bfloat16
    vmem = pl.BlockSpec(memory_space=pltpu.VMEM)
    args = (lefts, right, dy, y, x, bc, conv, pre, gate, step_raw, numbers, taps, start)
    return pl.pallas_call(
        functools.partial(mixer_back_kernel, plan),
        out_shape=[
            jax.ShapeDtypeStruct((rows, columns), f32),
            jax.ShapeDtypeStruct((tokens, width + channels + lanes), bf16),
            jax.ShapeDtypeStruct((8, channels), f32),
            jax.ShapeDtypeStruct((8, lanes), f32),
        ],
        in_specs=jax.tree.map(lambda _: vmem, list(args)),
        out_specs=[vmem] * 4,
        scratch_shapes=[
            pltpu.VMEM((64, each + 8, size), f32),
            pltpu.VMEM((64, each, size), f32),
            pltpu.VMEM((64, each + 8, size), f32),
            pltpu.VMEM((64, each, size), f32),
            pltpu.VMEM((tokens, width), f32),
            pltpu.VMEM((tokens, width), f32),
            pltpu.VMEM((tokens, width), f32),
            pltpu.VMEM((lanes, tokens), f32),
            pltpu.VMEM((3, mid, mid), f32),
            pltpu.VMEM((3, mid, mid), f32),
            pltpu.VMEM((tokens + 8, channels), f32),
            pltpu.VMEM((tokens, 2 * size), f32),
            pltpu.VMEM((tokens, 2 * size), f32),
        ]
        + scatter_shapes(rows, columns)
        + [pltpu.SemaphoreType.DMA((4,)), pltpu.SemaphoreType.DMA((4,))],
        compiler_params=params(collective, vmem_limit_bytes=60 * MIB),
        name="mixer_back",
    )(*args)


def input_back_kernel(
    plan,
    left,
    right,
    weights_ref,
    resid_ref,
    gain_ref,
    grad_ref,
    small_ref,
    out_ref,
    input_ref,
    small_out,
    weights,
    mine,
    theirs,
    small,
    small_got,
    buf,
    rest,
    send,
    recv,
    small_sems,
    sems,
):
    me, at = coordinates()
    head = lax.axis_index("head")
    tokens, model = resid_ref.shape
    columns = right.shape[1]
    load = pltpu.make_async_copy(weights_ref, weights, sems.at[0])
    load.start()
    greet_all_and_sibling(me)
    sums = Scatter(at, plan, [left], right, out_ref, buf, rest, send, recv)
    totals = Small(at, me, small, small_out, small_got, small_sems)
    for p in range(3):
        sums.product(p)
        sums.first(2, p)
    load.wait()

    start = columns - 384
    other = pl.multiple_of(start + 128 * (1 - head), 128)
    cut = 256
    swaps = []
    for c in range(0, model, cut):
        rows = slice(c, c + cut)
        total = dot_nt(right[...], weights[rows, :])
        total = total - dot_nt(right[:, pl.ds(other, 128)], weights[rows, pl.ds(other, 128)])
        mine[:, rows] = total
        swap = pltpu.make_async_remote_copy(
            src_ref=mine.at[:, pl.ds(c, cut)],
            dst_ref=theirs.at[:, pl.ds(c, cut)],
            send_sem=sems.at[1 + c // cut],
            recv_sem=sems.at[1 + (model + c) // cut],
            device_id={"head": 1 - head},
        )
        swap.start()
        swaps.append(swap)
    for p in range(3):
        sums.second(2, p)
    square = jnp.zeros((tokens, 1), jnp.float32)
    inner = jnp.zeros((tokens, 1), jnp.float32)
    for n, c in enumerate(range(0, model, cut)):
        rows = slice(c, c + cut)
        swaps[n].wait()
        grad = mine[:, rows] + theirs[:, rows]
        mine[:, rows] = grad
        resid = resid_ref[:, rows].astype(jnp.float32)
        square = square + jnp.sum(resid * resid, axis=1, keepdims=True)
        inner = inner + jnp.sum(resid * gain_ref[:, rows] * grad, axis=1, keepdims=True)
    scale = lax.rsqrt(square / model + EPSILON)
    pull = scale * scale * scale * (inner / model)
    small[...] = small_ref[...]
    for c in range(0, model, cut):
        rows = slice(c, c + cut)
        grad = mine[:, rows]
        resid = resid_ref[:, rows].astype(jnp.float32)
        input_ref[:, rows] = grad_ref[:, rows] + scale * gain_ref[:, rows] * grad - resid * pull
        gain_grad = jnp.sum(grad * resid * scale, axis=0, keepdims=True)
        for tile in range(c // 128, (c + cut) // 128):
            at_tile = tile * 128 - c
            small[tile // 8, tile % 8 : tile % 8 + 1, :] = gain_grad[:, at_tile : at_tile + 128]
    totals.begin()
    sums.finish(2)
    totals.middle()
    for phase in (1, 0):
        for p in range(3):
            sums.second(phase, p)
        sums.finish(phase)
    totals.end()
    sums.end()


def input_back(left, right, plan, weights, resid, gain, grad, small, collective):
    tokens, model = resid.shape
    columns = right.shape[1]
    rows = model // 64
    f32 = jnp.float32
    vmem = pl.BlockSpec(memory_space=pltpu.VMEM)
    return pl.pallas_call(
        functools.partial(input_back_kernel, plan),
        out_shape=[
            jax.ShapeDtypeStruct((rows, columns), f32),
            jax.ShapeDtypeStruct((tokens, model), f32),
            jax.ShapeDtypeStruct(small.shape, f32),
        ],
        in_specs=[vmem, vmem, pl.BlockSpec(memory_space=pl.ANY)] + [vmem] * 4,
        out_specs=[vmem] * 3,
        scratch_shapes=[
            pltpu.VMEM(weights.shape, weights.dtype),
            pltpu.VMEM((tokens, model), f32),
            pltpu.VMEM((tokens, model), f32),
            pltpu.VMEM(small.shape, f32),
            pltpu.VMEM(small.shape, f32),
        ]
        + scatter_shapes(rows, columns)
        + [pltpu.SemaphoreType.DMA((4,)), pltpu.SemaphoreType.DMA((1 + 2 * model // 256,))],
        compiler_params=params(collective, vmem_limit_bytes=62 * MIB),
        name="input_back",
    )(left, right, weights, resid, gain, grad, small)


class Gather:
    def __init__(self, at, x_ref, out_ref, send, recv, local_sem):
        self.at, self.x_ref, self.out_ref, self.send, self.recv = at, x_ref, out_ref, send, recv
        self.third, self.half = parts_of(x_ref.shape[1])
        self.own = pltpu.make_async_copy(x_ref, out_ref.at[at[0], at[1], at[2]], local_sem)
        self.copies = {}

    def put(self, source, here, phase, p, kind, by):
        copy = pltpu.make_async_remote_copy(
            src_ref=source,
            dst_ref=self.out_ref.at[here],
            send_sem=self.send.at[phase, p, kind],
            recv_sem=self.recv.at[phase, p, kind],
            device_id={"seq": seq_of(moved(self.at, ORDERS[p][phase], by))},
        )
        copy.start()
        self.copies[phase, p, kind] = copy

    def first(self, phase):
        if phase == 1:
            self.own.wait()
        if phase > 0:
            self.arrived(phase - 1)
        else:
            self.own.start()
        for p, order in enumerate(ORDERS):
            cols = pl.ds(p * self.third, self.third)
            here = region(self.at, order, phase, self.at[order[phase]], cols)
            source = self.x_ref.at[:, cols] if phase == 0 else self.out_ref.at[here]
            for kind, by in enumerate((1, 3)):
                self.put(source, here, phase, p, kind, by)

    def second(self, phase):
        for p, order in enumerate(ORDERS):
            for kind, by in enumerate((1, 3)):
                start, length = p * self.third, self.half
                if kind:
                    start, length = start + self.half, self.third - self.half
                there = region(
                    self.at, order, phase, (self.at[order[phase]] - by) % 4, pl.ds(start, length)
                )
                self.copies[phase, p, kind].wait_recv()
                self.put(self.out_ref.at[there], there, phase, p, 2 + kind, by)

    def arrived(self, phase):
        for p in range(3):
            for kind in (2, 3):
                self.copies[phase, p, kind].wait_recv()

    def end(self):
        for copy in self.copies.values():
            copy.wait_send()


def gather_shapes():
    return [
        pltpu.SemaphoreType.DMA((3, 3, 4)),
        pltpu.SemaphoreType.DMA((3, 3, 4)),
        pltpu.SemaphoreType.DMA,
    ]


def gather_kernel(x_ref, edge_ref, out_ref, before_ref, send, recv, local_sem, edge_sems):
    me, at = coordinates()
    barrier = pltpu.get_barrier_semaphore()
    pl.semaphore_signal(barrier, inc=1, device_id={"seq": (me + 63) % 64})
    greet_neighbours(at, 7)
    gather = Gather(at, x_ref, out_ref, send, recv, local_sem)
    edge = pltpu.make_async_remote_copy(
        src_ref=edge_ref,
        dst_ref=before_ref,
        send_sem=edge_sems.at[0],
        recv_sem=edge_sems.at[1],
        device_id={"seq": (me + 1) % 64},
    )
    edge.start()
    for phase in range(3):
        gather.first(phase)
        gather.second(phase)
    gather.arrived(2)
    edge.wait()
    gather.end()


def gather_rows(x, edge, collective):
    rows, columns = x.shape
    hbm = pl.BlockSpec(memory_space=pl.ANY)
    return pl.pallas_call(
        gather_kernel,
        out_shape=[
            jax.ShapeDtypeStruct((4, 4, 4, rows, columns), x.dtype),
            jax.ShapeDtypeStruct(edge.shape, edge.dtype),
        ],
        in_specs=[hbm, hbm],
        out_specs=[hbm, hbm],
        scratch_shapes=gather_shapes() + [pltpu.SemaphoreType.DMA((2,))],
        compiler_params=params(collective),
        name="gather_rows",
    )(x, edge)


def mixer_kernel(
    layer_ref,
    edge_ref,
    norm_ref,
    weights_ref,
    numbers_ref,
    taps_ref,
    gain_ref,
    late_ref,
    normed_ref,
    z_ref,
    x_ref,
    bc_ref,
    conv_ref,
    pre_ref,
    step_raw_ref,
    start_ref,
    y_ref,
    gated_ref,
    scale_ref,
    gathered_ref,
    weights,
    normed,
    message,
    got,
    made,
    spread,
    cum_rows,
    scores,
    mine,
    theirs,
    load_sems,
    scan_sems,
    pair_sems,
    send,
    recv,
    local_sem,
):
    me, at = coordinates()
    head = lax.axis_index("head")
    tokens, model = layer_ref.shape
    width = x_ref.shape[1]
    size = bc_ref.shape[1] // 2
    lanes = step_raw_ref.shape[1]
    each = width // 64
    mid = tokens // 2
    cut = 384

    def load(n):
        cols = pl.ds(pl.multiple_of(n * cut, 128), cut)
        return pltpu.make_async_copy(weights_ref.at[:, cols], weights.at[:, cols], load_sems.at[n])

    for n in (8, 4, 5, 6, 7, 0, 1, 2, 3):
        load(n).start()
    greet_all_and_sibling(me)
    gather = Gather(at, late_ref, gathered_ref, send, recv, local_sem)
    gather.first(0)

    def norm(rows):
        rows = rows.astype(jnp.float32)
        scale = lax.rsqrt(jnp.mean(rows * rows, axis=1, keepdims=True) + EPSILON)
        return low(rows * scale * norm_ref[...])

    before = norm(edge_ref[...]).astype(jnp.float32) * jnp.where(me == 0, 0.0, 1.0)
    normed[0:16, :] = low(before)
    normed[16 : 16 + tokens, :] = norm(layer_ref[...])
    normed_ref[...] = normed[16 : 16 + tokens, :]
    gather.second(0)

    def conv(cols):
        total = jnp.zeros((tokens, cols.size), jnp.float32)
        for j in range(4):
            total = total + taps_ref[j : j + 1, cols] * pre_ref[5 + j : 5 + j + tokens, cols]
        conv_ref[:, cols] = total
        return total * jax.nn.sigmoid(total)

    load(8).wait()
    last = dot_nn(normed[...], weights[:, 8 * cut : 9 * cut])
    cols = pl.ds(width, 2 * size)
    pre_ref[:, cols] = last[8:, : 2 * size]
    bc_ref[...] = conv(cols)
    step_raw = last[16:, 2 * size :] + numbers_ref[2:3, :]
    step_raw_ref[...] = step_raw
    step = jax.nn.softplus(step_raw)
    earlier = low(triangle(tokens, lambda t, s: jnp.where(t >= s, 1.0, 0.0)))
    cum = dot_split(earlier, -step * numbers_ref[0:1, :], 3)
    cum_rows[...] = cum.T
    tail = cum[tokens - 1 : tokens, :]
    spreader = head_spread(lanes, width, 64)
    spread[...] = split_dot(jnp.exp(tail - cum) * step, spreader, 2)
    held, read = bc_ref[:, :size], bc_ref[:, size:]
    gather.first(1)

    @pl.loop(0, 4)
    def _(i):
        load(4 + i).wait()
        from_cols = pl.ds(pl.multiple_of((4 + i) * cut, 128), cut)
        here = pl.ds(pl.multiple_of(i * cut, 128), cut)
        pre_ref[:, here] = dot_nn(normed[...], weights[:, from_cols])[8:]
        x = conv(here)
        x_ref[:, here] = x
        made_rows = dot_three(x * spread[:, here], held, dot_tn)
        message[pl.ds(i * (cut // each), cut // each), 0:each, :] = made_rows.reshape(
            cut // each, each, size
        )

    message[:, each : each + 8, :] = jnp.broadcast_to(jnp.exp(tail)[None], (64, 8, lanes))
    scan = Scan(False, at, me, message, start_ref, got, made, scan_sems)
    scan.begin()
    gather.second(1)

    @pl.loop(0, 4)
    def _(i):
        load(i).wait()
        here = pl.ds(pl.multiple_of(i * cut, 128), cut)
        z_ref[:, here] = dot_nn(normed[16 : 16 + tokens, :], weights[:, here])

    scan.middle()
    gather.first(2)

    spread[...] = split_dot(step, spreader, 2)
    blocks = ((0, 0), (1, 0), (1, 1))
    for n, (t, s) in enumerate(blocks):
        rows, columns = slice(t * mid, (t + 1) * mid), slice(s * mid, (s + 1) * mid)
        scores[n] = dot_three(read[rows], held[columns], dot_nt)
    causal = triangle(mid, lambda t, s: t >= s)
    second_head = lax.broadcasted_iota(jnp.int32, (tokens, 128), 1) >= 64

    @pl.loop(0, width // 128)
    def _(i):
        here = pl.ds(pl.multiple_of(i * 128, 128), 128)
        values, values_less = split(x_ref[:, here] * spread[:, here], 2)
        results = []
        for which in range(2):
            row = cum_rows[pl.ds(2 * i + which, 1), :]
            column = jnp.broadcast_to(row, (128, tokens)).T
            total = [None, None]
            for n, (t, s) in enumerate(blocks):
                columns = slice(s * mid, (s + 1) * mid)
                decay = jnp.exp(column[t * mid : (t + 1) * mid] - row[:, columns])
                if s == t:
                    decay = jnp.where(causal, decay, 0.0)
                mixing, mixing_less = split(decay * scores[n], 2)
                part = dot_nn(mixing, values[columns]) + dot_nn(mixing_less, values[columns])
                part = part + dot_nn(mixing, values_less[columns])
                total[t] = part if total[t] is None else total[t] + part
            results.append(total)
        for t in range(2):
            rows = slice(t * mid, (t + 1) * mid)
            y_ref[rows, here] = jnp.where(second_head[rows], results[1][t], results[0][t])

    scan.end()
    skip = split_dot(jnp.broadcast_to(numbers_ref[1:2, :], (8, lanes)), spreader, 2)[0:1, :]
    carry = split_dot(jnp.exp(cum), spreader, 2)
    square = jnp.zeros((tokens, 1), jnp.float32)
    for c in range(0, width, cut):
        here = slice(c, c + cut)
        start = start_ref[c // each : (c + cut) // each].reshape(cut, size)
        through = dot_three(read, start, dot_nt)
        y = y_ref[:, here] + carry[:, here] * through + skip[:, here] * x_ref[:, here]
        y_ref[:, here] = y
        z = z_ref[:, here]
        gated = y * (z * jax.nn.sigmoid(z))
        spread[:, here] = gated
        square = square + jnp.sum(gated * gated, axis=1, keepdims=True)
    mine[...] = jnp.broadcast_to(square, mine.shape)
    swap = pltpu.make_async_remote_copy(
        src_ref=mine,
        dst_ref=theirs,
        send_sem=pair_sems.at[0],
        recv_sem=pair_sems.at[1],
        device_id={"head": 1 - head},
    )
    swap.start()
    gather.second(2)
    swap.wait()
    scale = lax.rsqrt((mine[...] + theirs[...]) / (2 * width) + EPSILON)
    scale_ref[...] = scale
    for c in range(0, width, cut):
        here = slice(c, c + cut)
        gated_ref[:, here] = low(spread[:, here] * scale[:, 0:1] * gain_ref[:, here])
    gather.arrived(2)
    gather.end()


def mixer(layer_in, edge, norm, weights, numbers, taps, gain, late, collective):
    tokens, model = layer_in.shape
    width, channels = gain.shape[1], taps.shape[1]
    lanes = numbers.shape[1]
    size = (channels - width) // 2
    each, mid = width // 64, tokens // 2
    f32, bf16 = jnp.float32, jnp.bfloat16
    vmem, hbm = pl.BlockSpec(memory_space=pltpu.VMEM), pl.BlockSpec(memory_space=pl.ANY)
    out = [
        ((tokens, model), bf16),
        ((tokens, width), f32),
        ((tokens, width), f32),
        ((tokens, 2 * size), f32),
        ((tokens, channels), f32),
        ((tokens + 8, channels), f32),
        ((tokens, lanes), f32),
        ((64, each, size), f32),
        ((tokens, width), f32),
        ((tokens, width), bf16),
        ((tokens, lanes), f32),
        ((4, 4, 4) + late.shape, bf16),
    ]
    return pl.pallas_call(
        mixer_kernel,
        out_shape=[jax.ShapeDtypeStruct(*shape) for shape in out],
        in_specs=[vmem, vmem, vmem, hbm, vmem, vmem, vmem, hbm],
        out_specs=[vmem] * (len(out) - 1) + [hbm],
        scratch_shapes=[
            pltpu.VMEM(weights.shape, bf16),
            pltpu.VMEM((tokens + 16, model), bf16),
            pltpu.VMEM((64, each + 8, size), f32),
            pltpu.VMEM((64, each + 8, size), f32),
            pltpu.VMEM((64, each, size), f32),
            pltpu.VMEM((tokens, width), f32),
            pltpu.VMEM((lanes, tokens), f32),
            pltpu.VMEM((3, mid, mid), f32),
            pltpu.VMEM((tokens, lanes), f32),
            pltpu.VMEM((tokens, lanes), f32),
            pltpu.SemaphoreType.DMA((9,)),
            pltpu.SemaphoreType.DMA((4,)),
            pltpu.SemaphoreType.DMA((2,)),
        ]
        + gather_shapes(),
        compiler_params=params(collective, vmem_limit_bytes=56 * MIB),
        name="mixer",
    )(layer_in, edge, norm, weights, numbers, taps, gain, late)


class PairSum:
    def __init__(self, mine, theirs, sems, cut):
        self.mine, self.theirs, self.sems, self.cut = mine, theirs, sems, cut
        self.count = mine.shape[1] // cut

    def copy(self, n):
        cols = pl.ds(n * self.cut, self.cut)
        return pltpu.make_async_remote_copy(
            src_ref=self.mine.at[:, cols],
            dst_ref=self.theirs.at[:, cols],
            send_sem=self.sems.at[0, n],
            recv_sem=self.sems.at[1, n],
            device_id={"head": 1 - lax.axis_index("head")},
        )


def residual_kernel(
    gated_ref,
    weights_ref,
    layer_ref,
    norm_ref,
    grad_out_ref,
    position_ref,
    resid_ref,
    normed_ref,
    scale_ref,
    rows_ref,
    shared_ref,
    back_ref,
    right_ref,
    weights,
    mine,
    theirs,
    load_sems,
    sems,
):
    tokens, model = layer_ref.shape
    inner = gated_ref.shape[1]
    hidden = right_ref.shape[1] // 3
    cut = 256
    loads = []
    for n, (start, length) in enumerate(
        ((0, inner), (inner + 2 * hidden, hidden), (inner, 2 * hidden))
    ):
        cols = pl.ds(start, length)
        loads.append(
            pltpu.make_async_copy(weights_ref.at[:, cols], weights.at[:, cols], load_sems.at[n])
        )
        loads[-1].start()
    greet_sibling()
    pair = PairSum(mine, theirs, sems, cut)
    loads[0].wait()
    gated = gated_ref[...]
    for n in range(pair.count):
        rows = slice(n * cut, (n + 1) * cut)
        mine[:, rows] = dot_nt(gated, weights[rows, 0:inner])
        pair.copy(n).start()
    loads[1].wait()
    down = slice(inner + 2 * hidden, inner + 3 * hidden)
    both = slice(inner, inner + 2 * hidden)
    grad_hid = dot_nn(grad_out_ref[...], weights[:, down])
    square = jnp.zeros((tokens, 1), jnp.float32)
    for n in range(pair.count):
        rows = slice(n * cut, (n + 1) * cut)
        pair.copy(n).wait()
        resid = layer_ref[:, rows].astype(jnp.float32) + (mine[:, rows] + theirs[:, rows])
        resid_ref[:, rows] = resid
        square = square + jnp.sum(resid * resid, axis=1, keepdims=True)
    scale = lax.rsqrt(square / model + EPSILON)
    scale_ref[...] = jnp.broadcast_to(scale, scale_ref.shape)
    for n in range(pair.count):
        rows = slice(n * cut, (n + 1) * cut)
        normed_ref[:, rows] = low(resid_ref[:, rows] * scale * norm_ref[:, rows])
    normed = normed_ref[...]
    slots = rows_ref.shape[1]
    step = 16

    @pl.loop(0, rows_ref.shape[0] // step)
    def _(i):
        here = pl.ds(pl.multiple_of(i * step, step), step)
        chosen = chosen_slots(position_ref[here, :], 0, step, slots)
        rows_ref[here] = low(dot_nn(low(chosen), normed)).reshape(step, slots, model)

    loads[2].wait()
    gate_up = dot_nn(normed, weights[:, both])
    gate, up = gate_up[:, :hidden], gate_up[:, hidden:]
    act, slope = silu_parts(gate)
    hid = low(act * up)
    right_ref[:, 2 * hidden :] = hid
    right_ref[:, 0:hidden] = low(grad_hid * up * slope)
    right_ref[:, hidden : 2 * hidden] = low(grad_hid * act)
    grads = right_ref[:, 0 : 2 * hidden]
    for n in range(pair.count):
        rows = slice(n * cut, (n + 1) * cut)
        shared_ref[:, rows] = dot_nt(hid, weights[rows, down])
        back_ref[:, rows] = dot_nt(grads, weights[rows, both])


def residual_block(gated, weights, layer_in, norm, grad_out, position, slots, collective):
    tokens, model = layer_in.shape
    hidden = (weights.shape[1] - gated.shape[1]) // 3
    f32, bf16 = jnp.float32, jnp.bfloat16
    vmem, hbm = pl.BlockSpec(memory_space=pltpu.VMEM), pl.BlockSpec(memory_space=pl.ANY)
    out = [
        ((tokens, model), f32),
        ((tokens, model), bf16),
        ((tokens, 128), f32),
        ((position.shape[0], slots, model), bf16),
        ((tokens, model), f32),
        ((tokens, model), f32),
        ((tokens, 3 * hidden), bf16),
    ]
    return pl.pallas_call(
        residual_kernel,
        out_shape=[jax.ShapeDtypeStruct(*shape) for shape in out],
        in_specs=[vmem, hbm] + [vmem] * 4,
        out_specs=[vmem] * len(out),
        scratch_shapes=[
            pltpu.VMEM(weights.shape, bf16),
            pltpu.VMEM((tokens, model), f32),
            pltpu.VMEM((tokens, model), f32),
            pltpu.SemaphoreType.DMA((3,)),
            pltpu.SemaphoreType.DMA((2, model // 256)),
        ],
        compiler_params=params(collective, vmem_limit_bytes=48 * MIB),
        name="residual_block",
    )(gated, weights, layer_in, norm, grad_out, position)


def gate_back_kernel(
    home_ref,
    position_ref,
    back_ref,
    resid_ref,
    scale_ref,
    norm_ref,
    grad_out_ref,
    weights_ref,
    z_ref,
    y_ref,
    gate_scale_ref,
    gain_ref,
    grad_resid_ref,
    grad_mix_ref,
    grad_y_ref,
    grad_z_ref,
    norm_grad_ref,
    gain_grad_ref,
    weights,
    mine,
    theirs,
    stat,
    stat_theirs,
    load_sem,
    sems,
    stat_sems,
):
    tokens, model = resid_ref.shape
    inner = z_ref.shape[1]
    experts, slots = home_ref.shape[:2]
    cut = 256
    load = pltpu.make_async_copy(weights_ref.at[:, pl.ds(0, inner)], weights, load_sem)
    load.start()
    greet_sibling()
    pair = PairSum(mine, theirs, sems, cut)
    mine[...] = back_ref[...]
    step = 16

    @pl.loop(0, experts // step)
    def _(i):
        here = pl.ds(pl.multiple_of(i * step, step), step)
        chosen = low(chosen_slots(position_ref[here, :], 0, step, slots))
        rows = home_ref[here].reshape(step * slots, model)
        mine[...] += dot_tn(chosen, rows)

    for n in range(pair.count):
        pair.copy(n).start()
    scale = scale_ref[:, 0:1]
    inner_sum = jnp.zeros((tokens, 1), jnp.float32)
    for n in range(pair.count):
        cols = slice(n * cut, (n + 1) * cut)
        pair.copy(n).wait()
        grad = mine[:, cols] + theirs[:, cols]
        mine[:, cols] = grad
        resid = resid_ref[:, cols]
        norm_grad_ref[:, cols] = jnp.sum(grad * resid * scale, axis=0, keepdims=True)
        inner_sum = inner_sum + jnp.sum(resid * norm_ref[:, cols] * grad, axis=1, keepdims=True)
    pull = scale * scale * scale * (inner_sum / model)
    for n in range(pair.count):
        cols = slice(n * cut, (n + 1) * cut)
        grad = scale * norm_ref[:, cols] * mine[:, cols] - resid_ref[:, cols] * pull
        grad = grad_out_ref[:, cols].astype(jnp.float32) + grad
        grad_resid_ref[:, cols] = grad
        grad_mix_ref[:, cols] = low(grad)
    load.wait()
    grad_mix = grad_mix_ref[...]
    gate_scale = gate_scale_ref[:, 0:1]
    wide = 384
    dots = jnp.zeros((tokens, 1), jnp.float32)
    for c in range(0, inner, wide):
        cols = slice(c, c + wide)
        grad = dot_nn(grad_mix, weights[:, cols])
        z = z_ref[:, cols]
        gated = y_ref[:, cols] * (z * jax.nn.sigmoid(z))
        gain_grad_ref[:, cols] = jnp.sum(grad * gated * gate_scale, axis=0, keepdims=True)
        weighted = grad * gain_ref[:, cols]
        grad_y_ref[:, cols] = weighted
        dots = dots + jnp.sum(weighted * gated, axis=1, keepdims=True)
    stat[...] = jnp.broadcast_to(dots, stat.shape)
    swap = pltpu.make_async_remote_copy(
        src_ref=stat,
        dst_ref=stat_theirs,
        send_sem=stat_sems.at[0],
        recv_sem=stat_sems.at[1],
        device_id={"head": 1 - lax.axis_index("head")},
    )
    swap.start()
    swap.wait()
    dots = (stat[...] + stat_theirs[...])[:, 0:1]
    pull = gate_scale * gate_scale * gate_scale * (dots / (2 * inner))
    for c in range(0, inner, wide):
        cols = slice(c, c + wide)
        z, y = z_ref[:, cols], y_ref[:, cols]
        act, slope = silu_parts(z)
        grad = gate_scale * grad_y_ref[:, cols] - y * act * pull
        grad_y_ref[:, cols] = grad * act
        grad_z_ref[:, cols] = low(grad * y * slope)


def gate_back(home, position, back, resid, scale, norm, grad_out, weights, z, y, gate_scale, gain, collective):
    tokens, model = resid.shape
    inner = z.shape[1]
    f32, bf16 = jnp.float32, jnp.bfloat16
    vmem, hbm = pl.BlockSpec(memory_space=pltpu.VMEM), pl.BlockSpec(memory_space=pl.ANY)
    out = [
        ((tokens, model), f32),
        ((tokens, model), bf16),
        ((tokens, inner), f32),
        ((tokens, inner), bf16),
        ((1, model), f32),
        ((1, inner), f32),
    ]
    return pl.pallas_call(
        gate_back_kernel,
        out_shape=[jax.ShapeDtypeStruct(*shape) for shape in out],
        in_specs=[vmem] * 7 + [hbm] + [vmem] * 4,
        out_specs=[vmem] * len(out),
        scratch_shapes=[
            pltpu.VMEM((model, inner), bf16),
            pltpu.VMEM((tokens, model), f32),
            pltpu.VMEM((tokens, model), f32),
            pltpu.VMEM((tokens, 128), f32),
            pltpu.VMEM((tokens, 128), f32),
            pltpu.SemaphoreType.DMA,
            pltpu.SemaphoreType.DMA((2, model // 256)),
            pltpu.SemaphoreType.DMA((2,)),
        ],
        compiler_params=params(collective, vmem_limit_bytes=48 * MIB),
        name="gate_back",
    )(home, position, back, resid, scale, norm, grad_out, weights, z, y, gate_scale, gain)


def pair_kernel(x_ref, out_ref, theirs, send, recv):
    greet_sibling()
    copy = pltpu.make_async_remote_copy(
        src_ref=x_ref,
        dst_ref=theirs,
        send_sem=send,
        recv_sem=recv,
        device_id={"head": 1 - lax.axis_index("head")},
    )
    copy.start()
    copy.wait()
    rows = x_ref.shape[0]
    step = min(rows, 16)

    @pl.loop(0, rows // step)
    def _(i):
        here = pl.ds(pl.multiple_of(i * step, step), step)
        out_ref[here] = x_ref[here] + theirs[here]


def pair_total(x, collective):
    return pl.pallas_call(
        pair_kernel,
        out_shape=jax.ShapeDtypeStruct(x.shape, x.dtype),
        in_specs=[pl.BlockSpec(memory_space=pltpu.VMEM)],
        out_specs=pl.BlockSpec(memory_space=pltpu.VMEM),
        scratch_shapes=[
            pltpu.VMEM(x.shape, x.dtype),
            pltpu.SemaphoreType.DMA,
            pltpu.SemaphoreType.DMA,
        ],
        compiler_params=params(collective),
        name="pair_total",
    )(x)


def small_message(parts):
    flat = jnp.concatenate([part.reshape(-1) for part in parts])
    size = flat.shape[0]
    each = -(-size // (64 * 1024)) * 1024
    return jnp.pad(flat, (0, 64 * each - size)).reshape(64, each // 128, 128)


def small_parts(parts, out):
    out, result, start = out.reshape(-1), [], 0
    for part in parts:
        result.append(out[start : start + part.size].reshape(part.shape))
        start += part.size
    return result


def routing_kernel(routes_ref, weights_ref, position_ref, weight_ref):
    experts, tokens = position_ref.shape
    expert = lax.broadcasted_iota(jnp.int32, (experts, tokens), 0)
    named = jnp.zeros((experts, tokens), jnp.float32)
    weight = jnp.zeros((experts, tokens), jnp.float32)
    for k in range(routes_ref.shape[0]):
        hit = expert == routes_ref[k : k + 1, :]
        named = named + jnp.where(hit, 1.0, 0.0)
        weight = weight + jnp.where(hit, weights_ref[k : k + 1, :], 0.0)
    earlier = jnp.where(
        lax.broadcasted_iota(jnp.int32, (tokens, tokens), 0)
        < lax.broadcasted_iota(jnp.int32, (tokens, tokens), 1),
        1.0,
        0.0,
    ).astype(jnp.bfloat16)
    count = jnp.dot(named.astype(jnp.bfloat16), earlier, preferred_element_type=jnp.float32)
    position_ref[...] = jnp.where(named > 0.0, count, -1.0)
    weight_ref[...] = weight


def routing(routes, route_weights, experts):
    tokens = routes.shape[0]
    return pl.pallas_call(
        routing_kernel,
        out_shape=[jax.ShapeDtypeStruct((experts, tokens), jnp.float32)] * 2,
        name="routing",
    )(routes.T, route_weights.T)


def chosen_slots(position, first, count, slots):
    tokens = position.shape[1]
    number = lax.broadcasted_iota(jnp.int32, (count, slots, tokens), 1)
    number = (number + slots * lax.axis_index("head")).astype(jnp.float32)
    return jnp.where(position[:, None, :] == number, 1.0, 0.0).reshape(count * slots, tokens)


def send_kernel(slots, weigh, position_ref, weight_ref, rows_ref, out_ref):
    position = position_ref[...]
    chosen = chosen_slots(position, 0, position.shape[0], slots)
    rows = jnp.dot(
        chosen.astype(jnp.bfloat16), rows_ref[...], preferred_element_type=jnp.float32
    )
    if weigh:
        weighted = chosen.reshape(-1, slots, chosen.shape[1]) * weight_ref[...][:, None, :]
        rows = rows * jnp.sum(weighted.reshape(chosen.shape), axis=1, keepdims=True)
    out_ref[...] = rows.astype(jnp.bfloat16).reshape(out_ref.shape)


def send_rows(position, weight, rows, slots, weigh):
    experts, tokens = position.shape
    width = rows.shape[1]
    step = 16
    whole = pl.BlockSpec((tokens, width), lambda i: (0, 0))
    mine = pl.BlockSpec((step, tokens), lambda i: (i, 0))
    out = pl.BlockSpec((step, slots, width), lambda i: (i, 0, 0))
    return pl.pallas_call(
        functools.partial(send_kernel, slots, weigh),
        grid=(experts // step,),
        out_shape=jax.ShapeDtypeStruct((experts, slots, width), jnp.bfloat16),
        in_specs=[mine, mine, whole],
        out_specs=out,
        compiler_params=pltpu.CompilerParams(vmem_limit_bytes=40 * MIB),
        name="send_grads" if weigh else "send_rows",
    )(position, weight, rows)


def combine_kernel(slots, weigh, position_ref, weight_ref, rows_ref, out_ref):
    position = position_ref[...]
    count = position.shape[0]
    chosen = chosen_slots(position, 0, count, slots)
    rows = rows_ref[...].reshape(count * slots, rows_ref.shape[2])

    def over_slots(picked):
        return lax.dot_general(
            picked, rows, (((0,), (0,)), ((), ())), preferred_element_type=jnp.float32
        )

    @pl.when(pl.program_id(0) == 0)
    def _():
        out_ref[...] = jnp.zeros_like(out_ref)

    if weigh:
        weighted = chosen.reshape(count, slots, -1) * weight_ref[...][:, None, :]
        weighted = weighted.reshape(chosen.shape)
        high = weighted.astype(jnp.bfloat16)
        less = (weighted - high.astype(jnp.float32)).astype(jnp.bfloat16)
        out_ref[...] += over_slots(high) + over_slots(less)
    else:
        out_ref[...] += over_slots(chosen.astype(jnp.bfloat16))


def combine(position, weight, home, weigh):
    experts, tokens = position.shape
    _, slots, width = home.shape
    step = 16
    mine = pl.BlockSpec((step, tokens), lambda i: (i, 0))
    rows = pl.BlockSpec((step, slots, width), lambda i: (i, 0, 0))
    out = pl.BlockSpec((tokens, width), lambda i: (0, 0))
    return pl.pallas_call(
        functools.partial(combine_kernel, slots, weigh),
        grid=(experts // step,),
        out_shape=jax.ShapeDtypeStruct((tokens, width), jnp.float32),
        in_specs=[mine, mine, rows],
        out_specs=out,
        compiler_params=pltpu.CompilerParams(vmem_limit_bytes=40 * MIB),
        name="combine_mix" if weigh else "combine_grads",
    )(position, weight, home)


def per_device(
    layer_in,
    norm_first,
    mixer_in,
    state_proj,
    step_proj,
    step_bias,
    conv_main,
    conv_state,
    decay_rate,
    skip_gain,
    gate_gain,
    mixer_out,
    norm_second,
    shared_gate_up,
    shared_down,
    expert_gate_up,
    expert_down,
    routes,
    route_weights,
    grad_out,
):
    tokens, model_width = layer_in.shape
    inner_dev = mixer_in.shape[2]
    state_size = state_proj.shape[1] // 2
    heads_dev = step_proj.shape[1]
    conv_taps = conv_main.shape[0]
    shared_dev = shared_down.shape[1]
    local_experts = expert_gate_up.shape[0]
    experts_all = local_experts * lax.axis_size("seq")
    choices_per = routes.shape[1]
    capacity = max(2, tokens * choices_per * 4 // (3 * experts_all))
    slots_dev = capacity // lax.axis_size("head")
    lanes = 128
    pad_heads = lambda v: jnp.pad(v, ((0, 0), (0, lanes - heads_dev)))
    gathered, edge = gather_rows(
        jnp.concatenate(
            [mixer_in.reshape(-1, 2 * inner_dev), state_proj, pad_heads(step_proj)], axis=1
        ),
        layer_in[tokens - 16 :],
        0,
    )
    late_rows = jnp.concatenate(
        [mixer_out, shared_gate_up.reshape(-1, 2 * shared_dev), shared_down], axis=1
    )
    weights_in, late_rows, grad_out_late = lax.optimization_barrier(
        (gathered.reshape(model_width, -1), late_rows, grad_out)
    )
    position, slot_weight = routing(routes, route_weights, experts_all)
    grads_out = send_rows(position, slot_weight, grad_out_late, slots_dev, True)
    grads_in = lax.all_to_all(grads_out, "seq", split_axis=0, concat_axis=0, tiled=True)
    numbers = jnp.pad(
        jnp.stack([decay_rate, skip_gain, step_bias]), ((0, 5), (0, lanes - heads_dev))
    )
    taps = jnp.pad(jnp.concatenate([conv_main, conv_state], axis=1), ((0, 8 - conv_taps), (0, 0)))
    (
        normed,
        gate_z,
        heads_x,
        state_both,
        conv_sum,
        pre,
        step_raw,
        state_start,
        ssd,
        normed_gate,
        gate_scale,
        gathered,
    ) = mixer(
        layer_in, edge, norm_first[None], weights_in, numbers, taps, gate_gain[None], late_rows, 1
    )
    weights_late = gathered.reshape(model_width, -1)
    residual, normed_second, scale_second, rows_out, shared_part, shared_back, shared_right = (
        residual_block(
            normed_gate,
            weights_late,
            layer_in,
            norm_second[None],
            grad_out,
            position,
            slots_dev,
            2,
        )
    )
    grad_home, res_sums, expert_gate_up_grad, expert_down_grad = experts(
        rows_out,
        grads_in,
        expert_gate_up.reshape(model_width, -1),
        expert_down.reshape(-1, model_width),
        3,
    )
    home_rows = lax.all_to_all(res_sums, "seq", split_axis=0, concat_axis=0, tiled=True)
    grad_resid, grad_mix, grad_ssd, grad_gate_z, norm_second_grad, gate_gain_grad = gate_back(
        grad_home,
        position,
        shared_back,
        residual,
        scale_second,
        norm_second[None],
        grad_out,
        weights_late,
        gate_z,
        ssd,
        gate_scale,
        gate_gain[None],
        4,
    )
    late_plan = (
        ((0, 0, 1024),),
        ((0, 1024, 512), (1, 1536, 512)),
        ((1, 2048, 512), (2, 2560, 512)),
    )
    summed_late, right_grads, taps_grad, heads_grad = mixer_back(
        [grad_mix, normed_second, grad_out],
        jnp.concatenate([normed_gate, shared_right], axis=1),
        late_plan,
        grad_ssd,
        ssd,
        heads_x,
        state_both,
        conv_sum,
        pre,
        grad_gate_z,
        step_raw,
        numbers,
        taps,
        state_start.reshape(inner_dev, state_size),
        5,
    )
    home_rows, right_grads = lax.optimization_barrier((home_rows, right_grads))
    small = (
        jnp.zeros_like(norm_first),
        norm_second_grad,
        heads_grad[2, :heads_dev],
        taps_grad[:conv_taps, :inner_dev],
        taps_grad[:conv_taps, inner_dev:],
        heads_grad[1, :heads_dev],
        heads_grad[0, :heads_dev],
        gate_gain_grad,
    )
    summed, input_grad, small_sums = input_back(
        normed,
        right_grads,
        tuple(((0, start, 1152),) for start in (0, 1152, 2304)),
        weights_in,
        layer_in,
        norm_first[None],
        grad_resid,
        small_message(small),
        6,
    )
    small_sums = small_parts(small, small_sums)
    expert_mix = combine(position, slot_weight, home_rows, True)
    branch_sum = pair_total(shared_part + expert_mix, 7)
    layer_out = (residual + branch_sum).astype(jnp.bfloat16)
    wide = 2 * inner_dev + 2 * state_size
    weight_sums = (
        summed[:, : 2 * inner_dev].reshape(-1, 2, inner_dev),
        summed[:, 2 * inner_dev : wide],
        summed[:, wide : wide + heads_dev],
        summed_late[:, :inner_dev],
        summed_late[:, inner_dev : inner_dev + 2 * shared_dev].reshape(-1, 2, shared_dev),
        summed_late[:, inner_dev + 2 * shared_dev :],
    )
    return (
        layer_out,
        input_grad,
        small_sums[0],
        weight_sums[0],
        weight_sums[1],
        weight_sums[2],
        small_sums[2],
        small_sums[3],
        small_sums[4],
        small_sums[5],
        small_sums[6],
        small_sums[7].reshape(-1),
        weight_sums[3],
        small_sums[1].reshape(-1),
        weight_sums[4],
        weight_sums[5],
        expert_gate_up_grad,
        expert_down_grad,
    )


def solution(mesh):
    placed = (
        P("seq", None),
        P(),
        P("seq", None, "head"),
        P("seq", None),
        P("seq", "head"),
        P("head"),
        P(None, "head"),
        P(),
        P("head"),
        P("head"),
        P("head"),
        P("seq", "head"),
        P(),
        P("seq", None, "head"),
        P("seq", "head"),
        P("seq", None, None, "head"),
        P("seq", "head", None),
        P("seq", None),
        P("seq", None),
        P("seq", None),
    )
    return jax.shard_map(
        per_device,
        mesh=mesh,
        in_specs=placed,
        out_specs=(
            P("seq", None),
            P("seq", None),
            P(),
            P("seq", None, "head"),
            P("seq", None),
            P("seq", "head"),
            P("head"),
            P(None, "head"),
            P(),
            P("head"),
            P("head"),
            P("head"),
            P("seq", "head"),
            P(),
            P("seq", None, "head"),
            P("seq", "head"),
            P("seq", None, None, "head"),
            P("seq", "head", None),
        ),
        check_vma=False,
    )
```

```python
import functools
import jax
import jax.numpy as jnp
from jax import lax
from jax.experimental import pallas as pl
from jax.experimental.pallas import tpu as pltpu
from jax.sharding import PartitionSpec as P

ORDERS = ((0, 1, 2), (1, 2, 0), (2, 0, 1))
MIB = 1 << 20
EPSILON = 1e-05


def coordinates():
    me = lax.axis_index("seq")
    return me, [me // 16, (me // 4) % 4, me % 4]


def seq_of(at):
    return at[0] * 16 + at[1] * 4 + at[2]


def moved(at, axis, by):
    return [(c + by) % 4 if i == axis else c for i, c in enumerate(at)]


def announce(me, with_sibling):
    barrier = pltpu.get_barrier_semaphore()

    @pl.loop(1, 64)
    def _(k):
        pl.semaphore_signal(barrier, inc=1, device_id={"seq": lax.rem(me + k, 64)})

    if with_sibling:
        pl.semaphore_signal(barrier, inc=1, device_id={"head": 1 - lax.axis_index("head")})


def await_all(with_sibling):
    pl.semaphore_wait(pltpu.get_barrier_semaphore(), 64 if with_sibling else 63)


def parts_of(columns):
    third = columns // 3
    tiles = third // 128
    half = tiles // 2 * 128
    return third, half


def region(at, order, phase, value, cols):
    index = [None] * 3
    for i in range(3):
        if i < phase:
            index[order[i]] = slice(None)
        elif i == phase:
            index[order[i]] = value
        else:
            index[order[i]] = at[order[i]]
    return tuple(index) + (slice(None), cols)


class Ways:
    def __init__(self, at):
        self.at = at

    def group(self, g, back=False):
        x, z, y = self.at
        sign, lead = (-1, 8) if back else (1, 0)
        near, far = lax.rem(g, 4), g // 4
        xs = [lax.rem(x + lead + sign * a, 4) * 16 for a in range(4)]
        zs = [lax.rem(z + lead + sign * (near + a), 4) * 4 for a in range(4)]
        ys = [lax.rem(y + lead + sign * (far + a), 4) for a in range(4)]
        return [(g * 8 + n, xs[n % 4] + zs[n % 4] + ys[(n % 4 + n // 4 * 2) % 4]) for n in range(8)]

    def each(self, first, last, body, back=False):
        @pl.loop(first, last)
        def _(g):
            for n, (k, device) in enumerate(self.group(g, back)):
                if n == 0:
                    pl.when(k > 0)(functools.partial(body, k, device))
                else:
                    body(k, device)


def params(collective, **more):
    return pltpu.CompilerParams(collective_id=collective, has_side_effects=True, **more)


def greet_sibling():
    barrier = pltpu.get_barrier_semaphore()
    pl.semaphore_signal(barrier, inc=1, device_id={"head": 1 - lax.axis_index("head")})
    pl.semaphore_wait(barrier, 1)


def experts_kernel(
    rows_ref,
    grads_ref,
    gate_up_ref,
    down_ref,
    home_ref,
    res_ref,
    gate_up_grad_ref,
    down_grad_ref,
    slot_in,
    grad_slots,
    theirs_x,
    theirs_y,
    sums,
    wide_grad,
    send,
    home_send,
    home_recv,
    sems,
):
    me, at = coordinates()
    head = lax.axis_index("head")
    sibling = {"head": 1 - head}
    names = ("recv", "fwd_send", "fwd_recv", "kept", "given_send", "given_recv")
    names += ("x_send", "x_recv", "y_send", "y_recv")
    sem = {name: sems.at[n] for n, name in enumerate(names)}
    announce(me, True)
    wide_grad[...] = jnp.zeros_like(wide_grad)
    down_grad_ref[...] = jnp.zeros_like(down_grad_ref)
    ways = Ways(at)
    await_all(True)

    def group(c):
        return pl.ds(pl.multiple_of(c * 8, 8), 8)

    own = pltpu.make_async_copy(rows_ref.at[me], slot_in.at[0, head], sem["recv"].at[0])
    own.start()

    def put(k, target):
        pltpu.make_async_remote_copy(
            src_ref=rows_ref.at[target],
            dst_ref=slot_in.at[k, head],
            send_sem=send,
            recv_sem=sem["recv"].at[k // 8],
            device_id={"seq": target},
        ).start()

    ways.each(0, 8, put)

    def given(c):
        return pltpu.make_async_remote_copy(
            src_ref=grads_ref.at[group(c)],
            dst_ref=grad_slots.at[group(c), head],
            send_sem=sem["given_send"].at[c],
            recv_sem=sem["given_recv"].at[c],
            device_id=sibling,
        )

    def kept(c):
        return pltpu.make_async_copy(
            grads_ref.at[group(c)], grad_slots.at[group(c), head], sem["kept"].at[c]
        )

    def forward(c):
        return pltpu.make_async_remote_copy(
            src_ref=slot_in.at[group(c), head],
            dst_ref=slot_in.at[group(c), head],
            send_sem=sem["fwd_send"].at[c],
            recv_sem=sem["fwd_recv"].at[c],
            device_id=sibling,
        )

    def swap(c, source, target, name):
        return pltpu.make_async_remote_copy(
            src_ref=source.at[group(c), 1 - head],
            dst_ref=target.at[group(c)],
            send_sem=sem[name + "_send"].at[c],
            recv_sem=sem[name + "_recv"].at[c],
            device_id=sibling,
        )

    @pl.loop(0, 8)
    def _(c):
        kept(c).start()
        given(c).start()

    hidden = down_ref.shape[0]
    width = down_ref.shape[1]

    def nt(left, right):
        return lax.dot_general(
            left, right, (((1,), (1,)), ((), ())), preferred_element_type=jnp.float32
        )

    def tn(left, right):
        return lax.dot_general(
            left, right, (((0,), (0,)), ((), ())), preferred_element_type=jnp.float32
        )

    @pl.loop(0, 10)
    def _(i):
        @pl.when(i < 8)
        def _():
            c = i
            pltpu.make_async_copy(
                rows_ref.at[group(c)], slot_in.at[group(c), head], sem["recv"].at[c]
            ).wait()
            forward(c).start()

        @pl.when((i >= 1) & (i < 9))
        def _():
            c = i - 1
            forward(c).wait()
            kept(c).wait()
            given(c).wait()
            rows = slot_in[group(c)].reshape(256, width)
            grads = grad_slots[group(c)].reshape(256, width)
            both = jnp.dot(rows, gate_up_ref[...], preferred_element_type=jnp.float32)
            gate, up = both[:, :hidden], both[:, hidden:]
            sig = jax.nn.sigmoid(gate)
            act = gate * sig
            hid = (act * up).astype(jnp.bfloat16)
            grad_hid = nt(grads, down_ref[...])
            grad_gate = grad_hid * up * (sig * (1.0 + gate * (1.0 - sig)))
            grad_both = jnp.concatenate([grad_gate, grad_hid * act], axis=1).astype(jnp.bfloat16)
            wide_grad[...] += tn(rows, grad_both)
            down_grad_ref[...] += tn(hid, grads)
            back = nt(grad_both, gate_up_ref[...]).astype(jnp.bfloat16)
            slot_in[group(c)] = back.reshape(8, 2, 16, width)
            res = jnp.dot(hid, down_ref[...], preferred_element_type=jnp.float32)
            grad_slots[group(c)] = res.astype(jnp.bfloat16).reshape(8, 2, 16, width)
            swap(c, slot_in, theirs_x, "x").start()
            swap(c, grad_slots, theirs_y, "y").start()

        @pl.when(i >= 2)
        def _():
            c = i - 2
            swap(c, slot_in, theirs_x, "x").wait()

            def add(k):
                total = slot_in[k, head].astype(jnp.float32) + theirs_x[k].astype(jnp.float32)
                sums[k] = total.astype(sums.dtype)

            def put_home(k, source):
                add(k)
                pltpu.make_async_remote_copy(
                    src_ref=sums.at[k],
                    dst_ref=home_ref.at[me],
                    send_sem=home_send,
                    recv_sem=home_recv,
                    device_id={"seq": source},
                ).start()

            @pl.when(c == 0)
            def _():
                add(0)
                pltpu.make_async_copy(sums.at[0], home_ref.at[me], home_recv).start()

            ways.each(c, c + 1, put_home, back=True)
            swap(c, grad_slots, theirs_y, "y").wait()

            @pl.loop(0, 8)
            def _(n):
                j = c * 8 + n
                total = grad_slots[j, head].astype(jnp.float32) + theirs_y[j].astype(jnp.float32)
                res_ref[j] = total.astype(res_ref.dtype)

    tiles = hidden // 128
    for tile in range(tiles):
        for which in range(2):
            start = which * hidden + tile * 128
            gate_up_grad_ref[pl.ds(tile * 2 + which, width, stride=2 * tiles), :] = wide_grad[
                :, start : start + 128
            ]
    some = pl.ds(0, 63)
    pltpu.make_async_copy(rows_ref.at[some], rows_ref.at[some], send).wait()
    pltpu.make_async_copy(sums.at[some], sums.at[some], home_send).wait()
    pltpu.make_async_copy(sums, home_ref, home_recv).wait()


def experts(rows, grads, gate_up, down, collective):
    hidden, width = down.shape
    half, bf16 = rows.shape, rows.dtype
    whole = (half[0], 2) + half[1:]
    vmem = pl.BlockSpec(memory_space=pltpu.VMEM)
    home, res, wide, down_grad = pl.pallas_call(
        experts_kernel,
        out_shape=[
            jax.ShapeDtypeStruct(half, bf16),
            jax.ShapeDtypeStruct(half, bf16),
            jax.ShapeDtypeStruct((width * 2 * hidden // 128, 128), jnp.float32),
            jax.ShapeDtypeStruct((hidden, width), jnp.float32),
        ],
        in_specs=[vmem] * 4,
        out_specs=[pl.BlockSpec(memory_space=pl.ANY)] + [vmem] * 3,
        scratch_shapes=[
            pltpu.VMEM(whole, bf16),
            pltpu.VMEM(whole, bf16),
            pltpu.VMEM(half, bf16),
            pltpu.VMEM(half, bf16),
            pltpu.VMEM(half, bf16),
            pltpu.VMEM((width, 2 * hidden), jnp.float32),
            pltpu.SemaphoreType.DMA,
            pltpu.SemaphoreType.DMA,
            pltpu.SemaphoreType.DMA,
            pltpu.SemaphoreType.DMA((10, 8)),
        ],
        compiler_params=params(collective, vmem_limit_bytes=58 * MIB),
        name="experts",
    )(rows, grads, gate_up, down)
    wide = wide.reshape(width, hidden // 128, 2, 128).transpose(0, 2, 1, 3)
    return home, res, wide.reshape(1, width, 2, hidden), down_grad[None]


class Scan:
    def __init__(self, reverse, at, me, x_ref, out_ref, got, made, sems):
        self.reverse, self.at, self.me = reverse, at, me
        self.x_ref, self.out_ref, self.got, self.made = x_ref, out_ref, got, made
        self.send, self.recv, self.back_send, self.back_recv = [sems.at[n] for n in range(4)]

    def spread(self, source, target_ref, send, recv):
        def put(_, target):
            pltpu.make_async_remote_copy(
                src_ref=source.at[target],
                dst_ref=target_ref.at[self.me],
                send_sem=send,
                recv_sem=recv,
                device_id={"seq": target},
            ).start()

        Ways(self.at).each(0, 8, put)

    def begin(self):
        self.got[self.me] = self.x_ref[self.me]
        self.spread(self.x_ref, self.got, self.send, self.recv)

    def middle(self):
        some = pl.ds(0, 63)
        x_ref, got, made = self.x_ref, self.got, self.made
        pltpu.make_async_copy(x_ref.at[some], x_ref.at[some], self.send).wait()
        pltpu.make_async_copy(got.at[some], got.at[some], self.recv).wait()
        heads, width = made.shape[1:]
        number = lax.broadcasted_iota(jnp.int32, (heads, width), 0) + heads * self.me
        chosen = number // 64 == lax.broadcasted_iota(jnp.int32, (heads, width), 1)

        def step(k, state):
            at_k = 63 - k if self.reverse else k
            made[at_k] = state
            row = got[at_k, heads : heads + 8, :][0:1, :]
            decay = jnp.sum(jnp.where(chosen, row, 0.0), axis=1, keepdims=True)
            return decay * state + got[at_k, 0:heads, :]

        lax.fori_loop(0, 64, step, jnp.zeros((heads, width), jnp.float32), unroll=8)
        self.out_ref[self.me] = made[self.me]
        self.spread(made, self.out_ref, self.back_send, self.back_recv)

    def end(self):
        some = pl.ds(0, 63)
        made = self.made
        pltpu.make_async_copy(made.at[some], made.at[some], self.back_send).wait()
        pltpu.make_async_copy(made.at[some], made.at[some], self.back_recv).wait()


class Small:
    def __init__(self, at, me, x_ref, out_ref, got, sems):
        self.at, self.me = at, me
        self.x_ref, self.out_ref, self.got = x_ref, out_ref, got
        self.send, self.recv, self.back_send, self.back_recv = [sems.at[n] for n in range(4)]

    def begin(self):
        self.got[self.me] = self.x_ref[self.me]

        def put(_, target):
            pltpu.make_async_remote_copy(
                src_ref=self.x_ref.at[target],
                dst_ref=self.got.at[self.me],
                send_sem=self.send,
                recv_sem=self.recv,
                device_id={"seq": target},
            ).start()

        Ways(self.at).each(0, 8, put)

    def middle(self):
        some = pl.ds(0, 63)
        x_ref, got, out_ref, me = self.x_ref, self.got, self.out_ref, self.me
        pltpu.make_async_copy(x_ref.at[some], x_ref.at[some], self.send).wait()
        pltpu.make_async_copy(got.at[some], got.at[some], self.recv).wait()
        out_ref[me] = lax.fori_loop(1, 64, lambda k, total: total + got[k], got[0], unroll=9)

        def put(_, target):
            pltpu.make_async_remote_copy(
                src_ref=out_ref.at[me],
                dst_ref=out_ref.at[me],
                send_sem=self.back_send,
                recv_sem=self.back_recv,
                device_id={"seq": target},
            ).start()

        Ways(self.at).each(0, 8, put)

    def end(self):
        some = pl.ds(0, 63)
        got = self.got
        pltpu.make_async_copy(got.at[some], got.at[some], self.back_send).wait()
        pltpu.make_async_copy(got.at[some], got.at[some], self.back_recv).wait()


class Scatter:
    def __init__(self, at, plan, lefts, right, out_ref, buf, rest, send, recv):
        self.at, self.plan, self.lefts, self.right = at, plan, lefts, right
        self.out_ref, self.buf, self.rest, self.send, self.recv = out_ref, buf, rest, send, recv
        self.third, self.half = parts_of(buf.shape[4])
        self.copies = {}

    def spans(self, p):
        start, third, half = p * self.third, self.third, self.half
        return pl.ds(start, half), pl.ds(start + half, third - half)

    def product(self, p):
        buf, right = self.buf, self.right
        rows = buf.shape[3]
        for which, start, length in self.plan[p]:
            left = self.lefts[which]

            @pl.loop(0, 4)
            def _(x):
                across = pl.ds(pl.multiple_of(x * 16 * rows, 128), 16 * rows)
                total = lax.dot_general(
                    left[:, across],
                    right[:, start : start + length],
                    (((0,), (0,)), ((), ())),
                    preferred_element_type=jnp.float32,
                )
                total = total.reshape(4, 4, rows, length).astype(jnp.bfloat16)
                buf[x, :, :, :, start : start + length] = total

    def send_to(self, phase, p, by, value, cols, slot, kind):
        order = ORDERS[p]
        axis = order[phase]
        lead = (slice(None),) * phase
        copy = pltpu.make_async_remote_copy(
            src_ref=self.buf.at[region(self.at, order, phase, value, cols)],
            dst_ref=self.rest[phase].at[(slot,) + lead + (slice(None), cols)],
            send_sem=self.send.at[phase, p, kind],
            recv_sem=self.recv.at[phase, p, kind],
            device_id={"seq": seq_of(moved(self.at, axis, by))},
        )
        copy.start()
        self.copies[phase, p, kind] = copy

    def added(self, phase, p, value, cols, slots):
        order, buf, room = ORDERS[p], self.buf, self.rest[phase]

        @pl.loop(0, 4**phase)
        def _(i):
            free = ((), (i,), (i // 4, i % 4))[phase]
            index = list(region(self.at, order, phase, value, cols))
            for n, axis in enumerate(sorted(order[:phase])):
                index[axis] = free[n]
            index = tuple(index)
            total = buf[index].astype(jnp.float32)
            for slot in slots:
                total = total + room[(slot,) + free + (slice(None), cols)].astype(jnp.float32)
            if phase == 0 and len(slots) == 2:
                self.out_ref[:, cols] = total
            else:
                buf[index] = total.astype(jnp.bfloat16)

    def first(self, phase, p):
        self.first_far(phase, p)
        self.first_near(phase, p)

    def first_far(self, phase, p):
        c = self.at[ORDERS[p][phase]]
        low, high = self.spans(p)
        self.send_to(phase, p, 1, (c + 2) % 4, low, 2, 0)
        self.send_to(phase, p, 3, (c + 2) % 4, high, 2, 1)

    def first_near(self, phase, p):
        c = self.at[ORDERS[p][phase]]
        low, high = self.spans(p)
        self.send_to(phase, p, 1, (c + 1) % 4, high, 0, 2)
        self.send_to(phase, p, 3, (c + 3) % 4, low, 1, 3)

    def second(self, phase, p):
        c = self.at[ORDERS[p][phase]]
        low, high = self.spans(p)
        self.copies[phase, p, 0].wait_recv()
        self.added(phase, p, (c + 1) % 4, low, (2,))
        self.send_to(phase, p, 1, (c + 1) % 4, low, 0, 4)
        self.copies[phase, p, 1].wait_recv()
        self.added(phase, p, (c + 3) % 4, high, (2,))
        self.send_to(phase, p, 3, (c + 3) % 4, high, 1, 5)

    def third_step(self, phase, p):
        c = self.at[ORDERS[p][phase]]
        low, high = self.spans(p)
        self.copies[phase, p, 2].wait_recv()
        self.copies[phase, p, 5].wait_recv()
        self.added(phase, p, c, high, (0, 1))
        self.copies[phase, p, 3].wait_recv()
        self.copies[phase, p, 4].wait_recv()
        self.added(phase, p, c, low, (0, 1))

    def finish(self, phase):
        for p in range(3):
            self.third_step(phase, p)
            if phase > 0:
                self.first(phase - 1, p)

    def end(self):
        for copy in self.copies.values():
            copy.wait_send()


def scatter_shapes(rows, columns):
    return [
        pltpu.VMEM((4, 4, 4, rows, columns), jnp.bfloat16),
        [pltpu.VMEM((3,) + (4,) * phase + (rows, columns), jnp.bfloat16) for phase in range(3)],
        pltpu.SemaphoreType.DMA((3, 3, 6)),
        pltpu.SemaphoreType.DMA((3, 3, 6)),
    ]


def dot_nn(left, right):
    return jnp.dot(left, right, preferred_element_type=jnp.float32)


def dot_nt(left, right):
    return lax.dot_general(
        left, right, (((1,), (1,)), ((), ())), preferred_element_type=jnp.float32
    )


def dot_tn(left, right):
    return lax.dot_general(
        left, right, (((0,), (0,)), ((), ())), preferred_element_type=jnp.float32
    )


def low(value):
    return value.astype(jnp.bfloat16)


def split(value, count):
    parts = []
    for _ in range(count):
        parts.append(low(value))
        value = value - parts[-1].astype(jnp.float32)
    return parts


def dot_split(left, right, count, dot=dot_nn):
    return sum(dot(left, part) for part in split(right, count))


def split_dot(left, right, count):
    return sum(dot_nn(part, right) for part in split(left, count))


def dot_three(left, right, dot=dot_nn):
    high, less = split(left, 2)
    other_high, other_less = split(right, 2)
    return dot(high, other_high) + dot(less, other_high) + dot(high, other_less)


def head_spread(lanes, width, size):
    head = lax.broadcasted_iota(jnp.int32, (lanes, width), 0)
    column = lax.broadcasted_iota(jnp.int32, (lanes, width), 1)
    return low(jnp.where(head == column // size, 1.0, 0.0))


def head_gather(lanes, width, size):
    head = lax.broadcasted_iota(jnp.int32, (width, lanes), 1)
    column = lax.broadcasted_iota(jnp.int32, (width, lanes), 0)
    return low(jnp.where(head == column // size, 1.0, 0.0))


def triangle(rows, keep):
    first = lax.broadcasted_iota(jnp.int32, (rows, rows), 0)
    second = lax.broadcasted_iota(jnp.int32, (rows, rows), 1)
    return keep(first, second)


def silu_parts(value):
    sig = jax.nn.sigmoid(value)
    return value * sig, sig * (1.0 + value * (1.0 - sig))


def mixer_back_kernel(
    plan,
    lefts,
    right,
    dy_ref,
    y_ref,
    x_ref,
    bc_ref,
    conv_ref,
    pre_ref,
    gate_ref,
    step_raw_ref,
    numbers_ref,
    taps_ref,
    start_ref,
    out_ref,
    grads_ref,
    taps_grad_ref,
    heads_grad_ref,
    message,
    back,
    got,
    made,
    decayed,
    q,
    spread,
    cum_rows,
    scores,
    acc,
    ext,
    mine,
    theirs,
    buf,
    rest,
    send,
    recv,
    scan_sems,
    sems,
):
    me, at = coordinates()
    head = lax.axis_index("head")
    tokens, width = x_ref.shape
    size = start_ref.shape[1]
    lanes = step_raw_ref.shape[1]
    each = width // 64
    mid = tokens // 2
    cut = 384
    announce(me, True)
    sums = Scatter(at, plan, lefts, right, out_ref, buf, rest, send, recv)
    scan = Scan(True, at, me, message, back, got, made, scan_sems)

    rate = numbers_ref[0:1, :]
    step_raw = step_raw_ref[...]
    step = jax.nn.softplus(step_raw)
    earlier = low(triangle(tokens, lambda t, s: jnp.where(t >= s, 1.0, 0.0)))
    cum = dot_split(earlier, -step * rate, 3)
    cum_rows[...] = cum.T
    tail = cum[tokens - 1 : tokens, :]
    rest_decay = jnp.exp(tail - cum)
    weight = rest_decay * step
    spreader = head_spread(lanes, width, 64)
    gatherer = head_gather(lanes, width, 64)
    spread[...] = split_dot(jnp.exp(cum), spreader, 2)
    held_full, read_full = bc_ref[:, :size], bc_ref[:, size:]
    held, read = low(held_full), low(read_full)

    for c in range(0, width, cut):
        part = dy_ref[:, c : c + cut] * spread[:, c : c + cut]
        decayed[:, c : c + cut] = part
        made_rows = dot_three(part, read_full, dot_tn)
        message[c // each : (c + cut) // each, 0:each, :] = made_rows.reshape(
            cut // each, each, size
        )
    message[:, each : each + 8, :] = jnp.broadcast_to(jnp.exp(tail)[None], (64, 8, lanes))
    await_all(True)
    scan.begin()
    for p in range(3):
        sums.product(p)
        sums.first_far(2, p)
    scan.middle()
    for p in range(3):
        sums.first_near(2, p)

    spread[...] = split_dot(step, spreader, 2)
    blocks = ((0, 0), (0, 1), (1, 1))
    for n, (s, t) in enumerate(blocks):
        scores[n] = dot_nt(held[s * mid : (s + 1) * mid], read[t * mid : (t + 1) * mid])
    acc[...] = jnp.zeros_like(acc)
    causal = triangle(mid, lambda s, t: s <= t)
    second_head = lax.broadcasted_iota(jnp.int32, (tokens, 128), 1) >= 64

    @pl.loop(0, width // 128)
    def _(i):
        here = pl.ds(pl.multiple_of(i * 128, 128), 128)
        dy, dy_less = split(dy_ref[:, here], 2)
        stepped = x_ref[:, here] * spread[:, here]
        results = []
        for which in range(2):
            row = cum_rows[pl.ds(2 * i + which, 1), :]
            column = jnp.broadcast_to(row, (128, tokens)).T
            mask = second_head if which else jnp.logical_not(second_head)
            values, values_less = split(jnp.where(mask, stepped, 0.0), 2)
            total = [None, None]
            for n, (s, t) in enumerate(blocks):
                gap = row[:, t * mid : (t + 1) * mid] - column[s * mid : (s + 1) * mid]
                decay = jnp.exp(gap)
                if s == t:
                    decay = jnp.where(causal, decay, 0.0)
                later = dy[t * mid : (t + 1) * mid]
                first, later_less = values[s * mid : (s + 1) * mid], dy_less[t * mid : (t + 1) * mid]
                pairs = dot_nt(first, later) + dot_nt(first, later_less)
                pairs = pairs + dot_nt(values_less[s * mid : (s + 1) * mid], later)
                acc[n] += decay * pairs
                part = dot_nn(low(decay * scores[n]), later)
                total[s] = part if total[s] is None else total[s] + part
            results.append(total)
        for s in range(2):
            rows = slice(s * mid, (s + 1) * mid)
            q[rows, here] = jnp.where(second_head[rows], results[1][s], results[0][s])

    for p in range(3):
        sums.second(2, p)
    scan.end()

    skip = split_dot(jnp.broadcast_to(numbers_ref[1:2, :], (8, lanes)), spreader, 2)[0:1, :]
    grad_weight = grad_step = rows_sum = jnp.zeros((tokens, lanes), jnp.float32)
    skip_grad = jnp.zeros((8, lanes), jnp.float32)
    state_dot = jnp.zeros((lanes, size), jnp.float32)
    held_parts = held_full[:mid], held_full[mid:]
    read_parts = read_full[:mid], read_full[mid:]
    grad_held = dot_three(acc[0], read_parts[0]) + dot_three(acc[1], read_parts[1])
    grad_held = jnp.concatenate([grad_held, dot_three(acc[2], read_parts[1])], axis=0)
    grad_read = dot_three(acc[1], held_parts[0], dot_tn) + dot_three(acc[2], held_parts[1], dot_tn)
    grad_read = jnp.concatenate([dot_three(acc[0], held_parts[0], dot_tn), grad_read], axis=0)
    for c in range(0, width, cut):
        here = slice(c, c + cut)
        x, dy, inner = x_ref[:, here], dy_ref[:, here], q[:, here]
        after = back[c // each : (c + cut) // each].reshape(cut, size)
        start = start_ref[here, :]
        gather = gatherer[here, :]
        weights = split_dot(weight, spreader[:, here], 2)
        through = dot_nt(held, low(after))
        grad_x = inner * spread[:, here] + skip[:, here] * dy + weights * through
        grad_step = grad_step + split_dot(x * inner, gather, 2)
        grad_weight = grad_weight + split_dot(x * through, gather, 2)
        rows_sum = rows_sum + split_dot(dy * (y_ref[:, here] - skip[:, here] * x), gather, 2)
        pairs = jnp.sum(dy * x, axis=0, keepdims=True)
        skip_grad = skip_grad + split_dot(jnp.broadcast_to(pairs, (8, cut)), gather, 2)
        state_dot = state_dot + dot_split(gather, after * start, 2, dot_tn)
        grad_held = grad_held + dot_three(weights * x, after)
        grad_read = grad_read + dot_three(decayed[:, here], start)
        ext[0:tokens, here] = grad_x * silu_parts(conv_ref[:, here])[1]
    mine[:, :size] = grad_held
    mine[:, size:] = grad_read
    swap = pltpu.make_async_remote_copy(
        src_ref=mine,
        dst_ref=theirs,
        send_sem=sems.at[0],
        recv_sem=sems.at[1],
        device_id={"head": 1 - head},
    )
    swap.start()

    ones = jnp.ones((8, size), jnp.bfloat16)
    state_grad = dot_split(ones, state_dot, 2, dot_nt)[0:1, :]
    used = grad_weight * weight
    tail_grad = jnp.sum(used, axis=0, keepdims=True) + jnp.exp(tail) * state_grad
    grad_cum = rows_sum - step * grad_step - used
    last = lax.broadcasted_iota(jnp.int32, (tokens, lanes), 0) == tokens - 1
    grad_cum = grad_cum + jnp.where(last, tail_grad, 0.0)
    later = low(triangle(tokens, lambda t, s: jnp.where(t <= s, 1.0, 0.0)))
    grad_log = dot_split(later, grad_cum, 3)
    grad_step = grad_step + grad_weight * rest_decay - rate * grad_log
    grad_raw = grad_step * jax.nn.sigmoid(step_raw)
    heads_grad_ref[...] = jnp.zeros_like(heads_grad_ref)
    heads_grad_ref[0:1, :] = skip_grad[0:1, :]
    heads_grad_ref[1:2, :] = -jnp.sum(step * grad_log, axis=0, keepdims=True)
    heads_grad_ref[2:3, :] = jnp.sum(grad_raw, axis=0, keepdims=True)

    channels = width + 2 * size
    grads_ref[:, 0:width] = gate_ref[...]
    grads_ref[:, width + channels : width + channels + lanes] = low(grad_raw)
    swap.wait()
    ext[0:tokens, width:channels] = (mine[...] + theirs[...]) * silu_parts(
        conv_ref[:, width:channels]
    )[1]
    edge = pltpu.make_async_remote_copy(
        src_ref=ext.at[pl.ds(0, 8)],
        dst_ref=ext.at[pl.ds(tokens, 8)],
        send_sem=sems.at[2],
        recv_sem=sems.at[3],
        device_id={"seq": (me + 63) % 64},
    )
    edge.start()
    sums.finish(2)
    edge.wait()
    there = jnp.where(me == 63, 0.0, 1.0)
    ext[tokens : tokens + 8, :] = ext[tokens : tokens + 8, :] * there
    taps_grad_ref[...] = jnp.zeros_like(taps_grad_ref)

    @pl.loop(0, channels // 256)
    def _(i):
        here = pl.ds(pl.multiple_of(i * 256, 256), 256)
        grad = ext[0:tokens, here]
        total = jnp.zeros_like(grad)
        for j in range(4):
            total = total + taps_ref[j : j + 1, here] * ext[3 - j : 3 - j + tokens, here]
            products = grad * pre_ref[5 + j : 5 + j + tokens, here]
            taps_grad_ref[j : j + 1, here] = jnp.sum(products, axis=0, keepdims=True)
        grads_ref[:, pl.ds(pl.multiple_of(width + i * 256, 256), 256)] = low(total)

    for phase in (1, 0):
        for p in range(3):
            sums.second(phase, p)
        sums.finish(phase)
    sums.end()


def mixer_back(lefts, right, plan, dy, y, x, bc, conv, pre, gate, step_raw, numbers, taps, start, collective):
    model, columns = lefts[0].shape[1], right.shape[1]
    rows = model // 64
    tokens, width = x.shape
    size, lanes = start.shape[1], step_raw.shape[1]
    each, channels, mid = width // 64, width + 2 * size, tokens // 2
    f32, bf16 = jnp.float32, jnp.bfloat16
    vmem = pl.BlockSpec(memory_space=pltpu.VMEM)
    args = (lefts, right, dy, y, x, bc, conv, pre, gate, step_raw, numbers, taps, start)
    return pl.pallas_call(
        functools.partial(mixer_back_kernel, plan),
        out_shape=[
            jax.ShapeDtypeStruct((rows, columns), f32),
            jax.ShapeDtypeStruct((tokens, width + channels + lanes), bf16),
            jax.ShapeDtypeStruct((8, channels), f32),
            jax.ShapeDtypeStruct((8, lanes), f32),
        ],
        in_specs=jax.tree.map(lambda _: vmem, list(args)),
        out_specs=[vmem] * 4,
        scratch_shapes=[
            pltpu.VMEM((64, each + 8, size), f32),
            pltpu.VMEM((64, each, size), f32),
            pltpu.VMEM((64, each + 8, size), f32),
            pltpu.VMEM((64, each, size), f32),
            pltpu.VMEM((tokens, width), f32),
            pltpu.VMEM((tokens, width), f32),
            pltpu.VMEM((tokens, width), f32),
            pltpu.VMEM((lanes, tokens), f32),
            pltpu.VMEM((3, mid, mid), f32),
            pltpu.VMEM((3, mid, mid), f32),
            pltpu.VMEM((tokens + 8, channels), f32),
            pltpu.VMEM((tokens, 2 * size), f32),
            pltpu.VMEM((tokens, 2 * size), f32),
        ]
        + scatter_shapes(rows, columns)
        + [pltpu.SemaphoreType.DMA((4,)), pltpu.SemaphoreType.DMA((4,))],
        compiler_params=params(collective, vmem_limit_bytes=60 * MIB),
        name="mixer_back",
    )(*args)


def input_back_kernel(
    plan,
    left,
    right,
    weights_ref,
    resid_ref,
    gain_ref,
    grad_ref,
    small_ref,
    res_ref,
    position_ref,
    weight_ref,
    shared_ref,
    block_ref,
    out_ref,
    input_ref,
    small_out,
    layer_ref,
    weights,
    mine,
    theirs,
    theirs_mix,
    home,
    small,
    small_got,
    buf,
    rest,
    send,
    recv,
    small_sems,
    sems,
    home_sems,
    mix_sems,
):
    me, at = coordinates()
    head = lax.axis_index("head")
    tokens, model = resid_ref.shape
    columns = right.shape[1]
    load = pltpu.make_async_copy(weights_ref, weights, sems.at[0])
    load.start()
    announce(me, True)
    sums = Scatter(at, plan, [left], right, out_ref, buf, rest, send, recv)
    totals = Small(at, me, small, small_out, small_got, small_sems)
    own = pltpu.make_async_copy(res_ref.at[0], home.at[me], home_sems.at[2])
    own.start()

    def put(k, source):
        pltpu.make_async_remote_copy(
            src_ref=res_ref.at[k],
            dst_ref=home.at[me],
            send_sem=home_sems.at[0],
            recv_sem=home_sems.at[1],
            device_id={"seq": source},
        ).start()

    ways = Ways(at)
    for p in range(3):
        sums.product(p)
        if p == 0:
            await_all(True)
        sums.first(2, p)
    load.wait()

    start = columns - 384
    other = pl.multiple_of(start + 128 * (1 - head), 128)
    cut = 256
    swaps = []
    for c in range(0, model, cut):
        rows = slice(c, c + cut)
        total = dot_nt(right[...], weights[rows, :])
        total = total - dot_nt(right[:, pl.ds(other, 128)], weights[rows, pl.ds(other, 128)])
        mine[:, rows] = total
        swap = pltpu.make_async_remote_copy(
            src_ref=mine.at[:, pl.ds(c, cut)],
            dst_ref=theirs.at[:, pl.ds(c, cut)],
            send_sem=sems.at[1 + c // cut],
            recv_sem=sems.at[1 + (model + c) // cut],
            device_id={"head": 1 - head},
        )
        swap.start()
        swaps.append(swap)
    for p in range(3):
        sums.second(2, p)
    ways.each(0, 8, put, back=True)
    square = jnp.zeros((tokens, 1), jnp.float32)
    inner = jnp.zeros((tokens, 1), jnp.float32)
    for n, c in enumerate(range(0, model, cut)):
        rows = slice(c, c + cut)
        swaps[n].wait()
        grad = mine[:, rows] + theirs[:, rows]
        mine[:, rows] = grad
        resid = resid_ref[:, rows].astype(jnp.float32)
        square = square + jnp.sum(resid * resid, axis=1, keepdims=True)
        inner = inner + jnp.sum(resid * gain_ref[:, rows] * grad, axis=1, keepdims=True)
    scale = lax.rsqrt(square / model + EPSILON)
    pull = scale * scale * scale * (inner / model)
    small[...] = small_ref[...]
    for c in range(0, model, cut):
        rows = slice(c, c + cut)
        grad = mine[:, rows]
        resid = resid_ref[:, rows].astype(jnp.float32)
        input_ref[:, rows] = grad_ref[:, rows] + scale * gain_ref[:, rows] * grad - resid * pull
        gain_grad = jnp.sum(grad * resid * scale, axis=0, keepdims=True)
        for tile in range(c // 128, (c + cut) // 128):
            at_tile = tile * 128 - c
            small[tile // 8, tile % 8 : tile % 8 + 1, :] = gain_grad[:, at_tile : at_tile + 128]
    totals.begin()
    sums.finish(2)
    totals.middle()
    for p in range(3):
        sums.second(1, p)

    own.wait()
    some = pl.ds(0, 63)
    pltpu.make_async_copy(home.at[some], home.at[some], home_sems.at[1]).wait()
    slots, step = home.shape[1], 16
    mine[...] = shared_ref[...]

    @pl.loop(0, home.shape[0] // step)
    def _(i):
        here = pl.ds(pl.multiple_of(i * step, step), step)
        chosen = chosen_slots(position_ref[here, :], slots)
        weighted = chosen.reshape(step, slots, -1) * weight_ref[here, :][:, None, :]
        high, less = split(weighted.reshape(chosen.shape), 2)
        rows = home[here].reshape(step * slots, model)
        mine[...] += dot_tn(high, rows) + dot_tn(less, rows)

    pair = PairSum(mine, theirs_mix, mix_sems, cut)
    for n in range(pair.count):
        pair.copy(n).start()
    sums.finish(1)
    for p in range(3):
        sums.second(0, p)
    for n in range(pair.count):
        cols = slice(n * cut, (n + 1) * cut)
        pair.copy(n).wait()
        layer_ref[:, cols] = low(block_ref[:, cols] + (mine[:, cols] + theirs_mix[:, cols]))
    sums.finish(0)
    totals.end()
    sums.end()
    pltpu.make_async_copy(home.at[some], home.at[some], home_sems.at[0]).wait()


def input_back(
    left, right, plan, weights, resid, gain, grad, small, res, position, weight, shared, block, collective
):
    tokens, model = resid.shape
    columns = right.shape[1]
    rows = model // 64
    f32 = jnp.float32
    vmem, hbm = pl.BlockSpec(memory_space=pltpu.VMEM), pl.BlockSpec(memory_space=pl.ANY)
    return pl.pallas_call(
        functools.partial(input_back_kernel, plan),
        out_shape=[
            jax.ShapeDtypeStruct((rows, columns), f32),
            jax.ShapeDtypeStruct((tokens, model), f32),
            jax.ShapeDtypeStruct(small.shape, f32),
            jax.ShapeDtypeStruct((tokens, model), jnp.bfloat16),
        ],
        in_specs=[vmem, vmem, hbm] + [vmem] * 4 + [hbm] + [vmem] * 4,
        out_specs=[vmem] * 4,
        scratch_shapes=[
            pltpu.VMEM(weights.shape, weights.dtype),
            pltpu.VMEM((tokens, model), f32),
            pltpu.VMEM((tokens, model), f32),
            pltpu.VMEM((tokens, model), f32),
            pltpu.VMEM(res.shape, res.dtype),
            pltpu.VMEM(small.shape, f32),
            pltpu.VMEM(small.shape, f32),
        ]
        + scatter_shapes(rows, columns)
        + [pltpu.SemaphoreType.DMA((4,)), pltpu.SemaphoreType.DMA((1 + 2 * model // 256,))]
        + [pltpu.SemaphoreType.DMA((3,)), pltpu.SemaphoreType.DMA((2, model // 256))],
        compiler_params=params(collective, vmem_limit_bytes=62 * MIB),
        name="input_back",
    )(left, right, weights, resid, gain, grad, small, res, position, weight, shared, block)


class Gather:
    def __init__(self, at, x_ref, out_ref, send, recv, local_sem):
        self.at, self.x_ref, self.out_ref, self.send, self.recv = at, x_ref, out_ref, send, recv
        self.third, self.half = parts_of(out_ref.shape[4])
        if x_ref is not None:
            self.own = pltpu.make_async_copy(x_ref, out_ref.at[at[0], at[1], at[2]], local_sem)
        self.copies = {}

    def put(self, source, here, phase, p, kind, by):
        copy = pltpu.make_async_remote_copy(
            src_ref=source,
            dst_ref=self.out_ref.at[here],
            send_sem=self.send.at[phase, p, kind],
            recv_sem=self.recv.at[phase, p, kind],
            device_id={"seq": seq_of(moved(self.at, ORDERS[p][phase], by))},
        )
        copy.start()
        self.copies[phase, p, kind] = copy

    def first(self, phase):
        if phase == 1:
            self.own.wait()
        if phase == 0:
            self.own.start()
        elif (phase - 1, 0, 2) in self.copies:
            self.arrived(phase - 1)
        for p, order in enumerate(ORDERS):
            cols = pl.ds(p * self.third, self.third)
            here = region(self.at, order, phase, self.at[order[phase]], cols)
            source = self.x_ref.at[:, cols] if phase == 0 else self.out_ref.at[here]
            for kind, by in enumerate((1, 3)):
                self.put(source, here, phase, p, kind, by)

    def second(self, phase):
        for p, order in enumerate(ORDERS):
            for kind, by in enumerate((1, 3)):
                start, length = p * self.third, self.half
                if kind:
                    start, length = start + self.half, self.third - self.half
                there = region(
                    self.at, order, phase, (self.at[order[phase]] - by) % 4, pl.ds(start, length)
                )
                self.copies[phase, p, kind].wait_recv()
                self.put(self.out_ref.at[there], there, phase, p, 2 + kind, by)

    def arrived(self, phase):
        for p in range(3):
            for kind in (2, 3):
                self.copies[phase, p, kind].wait_recv()

    def end(self):
        for copy in self.copies.values():
            copy.wait_send()


def gather_shapes():
    return [
        pltpu.SemaphoreType.DMA((3, 3, 4)),
        pltpu.SemaphoreType.DMA((3, 3, 4)),
        pltpu.SemaphoreType.DMA,
    ]


def slot_tables(routes_ref, weights_ref, position_ref, weight_ref):
    experts, tokens = position_ref.shape
    expert = lax.broadcasted_iota(jnp.int32, (experts, tokens), 0)
    named = jnp.zeros((experts, tokens), jnp.float32)
    weight = jnp.zeros((experts, tokens), jnp.float32)
    for k in range(routes_ref.shape[0]):
        hit = expert == routes_ref[k : k + 1, :]
        named = named + jnp.where(hit, 1.0, 0.0)
        weight = weight + jnp.where(hit, weights_ref[k : k + 1, :], 0.0)
    earlier = low(triangle(tokens, lambda t, s: jnp.where(t < s, 1.0, 0.0)))
    position_ref[...] = jnp.where(named > 0.0, dot_nn(low(named), earlier), -1.0)
    weight_ref[...] = weight


def chosen_slots(position, slots):
    count, tokens = position.shape
    number = lax.broadcasted_iota(jnp.int32, (count, slots, tokens), 1)
    number = (number + slots * lax.axis_index("head")).astype(jnp.float32)
    return jnp.where(position[:, None, :] == number, 1.0, 0.0).reshape(count * slots, tokens)


def gather_kernel(
    x_ref,
    late_ref,
    layer_ref,
    routes_ref,
    weights_ref,
    grads_ref,
    out_ref,
    late_out,
    before_ref,
    position_ref,
    weight_ref,
    slots_ref,
    rows,
    send,
    recv,
    local_sem,
    late_send,
    late_recv,
    late_sem,
    sems,
):
    me, at = coordinates()
    announce(me, False)
    gather = Gather(at, x_ref, out_ref, send, recv, local_sem)
    late = Gather(at, late_ref, late_out, late_send, late_recv, late_sem)
    await_all(False)
    gather.first(0)
    late.first(0)
    edge = pltpu.make_async_remote_copy(
        src_ref=layer_ref.at[pl.ds(layer_ref.shape[0] - 16, 16)],
        dst_ref=before_ref,
        send_sem=sems.at[0],
        recv_sem=sems.at[1],
        device_id={"seq": (me + 1) % 64},
    )
    edge.start()
    slot_tables(routes_ref, weights_ref, position_ref, weight_ref)
    grads = grads_ref[...]
    slots, step = rows.shape[1], 16

    @pl.loop(0, rows.shape[0] // step)
    def _(i):
        here = pl.ds(pl.multiple_of(i * step, step), step)
        chosen = chosen_slots(position_ref[here, :], slots)
        weighted = chosen.reshape(step, slots, -1) * weight_ref[here, :][:, None, :]
        scale = jnp.sum(weighted.reshape(chosen.shape), axis=1, keepdims=True)
        rows[here] = low(dot_nn(low(chosen), grads) * scale).reshape(step, slots, -1)

    own = pltpu.make_async_copy(rows.at[me], slots_ref.at[0], sems.at[2])
    own.start()

    def put(k, target):
        pltpu.make_async_remote_copy(
            src_ref=rows.at[target],
            dst_ref=slots_ref.at[k],
            send_sem=sems.at[3],
            recv_sem=sems.at[4],
            device_id={"seq": target},
        ).start()

    ways = Ways(at)
    gather.second(0)
    late.second(0)
    ways.each(0, 1, put)
    gather.first(1)
    late.first(1)
    ways.each(1, 2, put)
    gather.second(1)
    late.second(1)
    ways.each(2, 3, put)
    gather.first(2)
    ways.each(3, 4, put)
    gather.second(2)
    ways.each(4, 8, put)
    late.arrived(1)
    late.end()
    gather.arrived(2)
    edge.wait()
    gather.end()
    own.wait()
    some = pl.ds(0, 63)
    pltpu.make_async_copy(rows.at[some], rows.at[some], sems.at[3]).wait()
    pltpu.make_async_copy(rows.at[some], rows.at[some], sems.at[4]).wait()


def gather_rows(x, late, layer_in, routes, route_weights, grads, experts, slots, collective):
    rows, columns = x.shape
    tokens, model = grads.shape
    hbm, vmem = pl.BlockSpec(memory_space=pl.ANY), pl.BlockSpec(memory_space=pltpu.VMEM)
    return pl.pallas_call(
        gather_kernel,
        out_shape=[
            jax.ShapeDtypeStruct((4, 4, 4, rows, columns), x.dtype),
            jax.ShapeDtypeStruct((4, 4, 4) + late.shape, late.dtype),
            jax.ShapeDtypeStruct((16, model), layer_in.dtype),
            jax.ShapeDtypeStruct((experts, tokens), jnp.float32),
            jax.ShapeDtypeStruct((experts, tokens), jnp.float32),
            jax.ShapeDtypeStruct((experts, slots, model), grads.dtype),
        ],
        in_specs=[hbm, hbm, hbm, vmem, vmem, vmem],
        out_specs=[hbm, hbm, hbm, vmem, vmem, hbm],
        scratch_shapes=[pltpu.VMEM((experts, slots, model), grads.dtype)]
        + gather_shapes()
        + gather_shapes()
        + [pltpu.SemaphoreType.DMA((5,))],
        compiler_params=params(collective, vmem_limit_bytes=60 * MIB),
        name="gather_rows",
    )(x, late, layer_in, routes.T, route_weights.T, grads)


def mixer_kernel(
    layer_ref,
    edge_ref,
    norm_ref,
    weights_ref,
    numbers_ref,
    taps_ref,
    gain_ref,
    _,
    normed_ref,
    z_ref,
    x_ref,
    bc_ref,
    conv_ref,
    pre_ref,
    step_raw_ref,
    start_ref,
    y_ref,
    gated_ref,
    scale_ref,
    gathered_ref,
    weights,
    normed,
    message,
    got,
    made,
    spread,
    cum_rows,
    scores,
    mine,
    theirs,
    load_sems,
    scan_sems,
    pair_sems,
    send,
    recv,
):
    me, at = coordinates()
    head = lax.axis_index("head")
    tokens, model = layer_ref.shape
    width = x_ref.shape[1]
    size = bc_ref.shape[1] // 2
    lanes = step_raw_ref.shape[1]
    each = width // 64
    mid = tokens // 2
    cut = 384

    def load(n):
        cols = pl.ds(pl.multiple_of(n * cut, 128), cut)
        return pltpu.make_async_copy(weights_ref.at[:, cols], weights.at[:, cols], load_sems.at[n])

    for n in (8, 4, 5, 6, 7, 0, 1, 2, 3):
        load(n).start()
    announce(me, True)
    gather = Gather(at, None, gathered_ref, send, recv, None)

    def norm(rows):
        rows = rows.astype(jnp.float32)
        scale = lax.rsqrt(jnp.mean(rows * rows, axis=1, keepdims=True) + EPSILON)
        return low(rows * scale * norm_ref[...])

    before = norm(edge_ref[...]).astype(jnp.float32) * jnp.where(me == 0, 0.0, 1.0)
    normed[0:16, :] = low(before)
    normed[16 : 16 + tokens, :] = norm(layer_ref[...])
    normed_ref[...] = normed[16 : 16 + tokens, :]
    await_all(True)
    gather.first(2)

    def conv(cols):
        total = jnp.zeros((tokens, cols.size), jnp.float32)
        for j in range(4):
            total = total + taps_ref[j : j + 1, cols] * pre_ref[5 + j : 5 + j + tokens, cols]
        conv_ref[:, cols] = total
        return total * jax.nn.sigmoid(total)

    load(8).wait()
    last = dot_nn(normed[...], weights[:, 8 * cut : 9 * cut])
    cols = pl.ds(width, 2 * size)
    pre_ref[:, cols] = last[8:, : 2 * size]
    bc_ref[...] = conv(cols)
    step_raw = last[16:, 2 * size :] + numbers_ref[2:3, :]
    step_raw_ref[...] = step_raw
    step = jax.nn.softplus(step_raw)
    earlier = low(triangle(tokens, lambda t, s: jnp.where(t >= s, 1.0, 0.0)))
    cum = dot_split(earlier, -step * numbers_ref[0:1, :], 3)
    cum_rows[...] = cum.T
    tail = cum[tokens - 1 : tokens, :]
    spreader = head_spread(lanes, width, 64)
    spread[...] = split_dot(jnp.exp(tail - cum) * step, spreader, 2)
    held, read = bc_ref[:, :size], bc_ref[:, size:]

    @pl.loop(0, 4)
    def _(i):
        load(4 + i).wait()
        from_cols = pl.ds(pl.multiple_of((4 + i) * cut, 128), cut)
        here = pl.ds(pl.multiple_of(i * cut, 128), cut)
        pre_ref[:, here] = dot_nn(normed[...], weights[:, from_cols])[8:]
        x = conv(here)
        x_ref[:, here] = x
        made_rows = dot_three(x * spread[:, here], held, dot_tn)
        message[pl.ds(i * (cut // each), cut // each), 0:each, :] = made_rows.reshape(
            cut // each, each, size
        )

    message[:, each : each + 8, :] = jnp.broadcast_to(jnp.exp(tail)[None], (64, 8, lanes))
    scan = Scan(False, at, me, message, start_ref, got, made, scan_sems)
    scan.begin()
    gather.second(2)

    @pl.loop(0, 4)
    def _(i):
        load(i).wait()
        here = pl.ds(pl.multiple_of(i * cut, 128), cut)
        z_ref[:, here] = dot_nn(normed[16 : 16 + tokens, :], weights[:, here])

    scan.middle()

    spread[...] = split_dot(step, spreader, 2)
    blocks = ((0, 0), (1, 0), (1, 1))
    for n, (t, s) in enumerate(blocks):
        rows, columns = slice(t * mid, (t + 1) * mid), slice(s * mid, (s + 1) * mid)
        scores[n] = dot_three(read[rows], held[columns], dot_nt)
    causal = triangle(mid, lambda t, s: t >= s)
    second_head = lax.broadcasted_iota(jnp.int32, (tokens, 128), 1) >= 64

    @pl.loop(0, width // 128)
    def _(i):
        here = pl.ds(pl.multiple_of(i * 128, 128), 128)
        values, values_less = split(x_ref[:, here] * spread[:, here], 2)
        results = []
        for which in range(2):
            row = cum_rows[pl.ds(2 * i + which, 1), :]
            column = jnp.broadcast_to(row, (128, tokens)).T
            total = [None, None]
            for n, (t, s) in enumerate(blocks):
                columns = slice(s * mid, (s + 1) * mid)
                decay = jnp.exp(column[t * mid : (t + 1) * mid] - row[:, columns])
                if s == t:
                    decay = jnp.where(causal, decay, 0.0)
                mixing, mixing_less = split(decay * scores[n], 2)
                part = dot_nn(mixing, values[columns]) + dot_nn(mixing_less, values[columns])
                part = part + dot_nn(mixing, values_less[columns])
                total[t] = part if total[t] is None else total[t] + part
            results.append(total)
        for t in range(2):
            rows = slice(t * mid, (t + 1) * mid)
            y_ref[rows, here] = jnp.where(second_head[rows], results[1][t], results[0][t])

    scan.end()
    skip = split_dot(jnp.broadcast_to(numbers_ref[1:2, :], (8, lanes)), spreader, 2)[0:1, :]
    carry = split_dot(jnp.exp(cum), spreader, 2)
    square = jnp.zeros((tokens, 1), jnp.float32)
    for c in range(0, width, cut):
        here = slice(c, c + cut)
        start = start_ref[c // each : (c + cut) // each].reshape(cut, size)
        through = dot_three(read, start, dot_nt)
        y = y_ref[:, here] + carry[:, here] * through + skip[:, here] * x_ref[:, here]
        y_ref[:, here] = y
        z = z_ref[:, here]
        gated = y * (z * jax.nn.sigmoid(z))
        spread[:, here] = gated
        square = square + jnp.sum(gated * gated, axis=1, keepdims=True)
    mine[...] = jnp.broadcast_to(square, mine.shape)
    swap = pltpu.make_async_remote_copy(
        src_ref=mine,
        dst_ref=theirs,
        send_sem=pair_sems.at[0],
        recv_sem=pair_sems.at[1],
        device_id={"head": 1 - head},
    )
    swap.start()
    swap.wait()
    scale = lax.rsqrt((mine[...] + theirs[...]) / (2 * width) + EPSILON)
    scale_ref[...] = scale
    for c in range(0, width, cut):
        here = slice(c, c + cut)
        gated_ref[:, here] = low(spread[:, here] * scale[:, 0:1] * gain_ref[:, here])
    gather.arrived(2)
    gather.end()


def mixer(layer_in, edge, norm, weights, numbers, taps, gain, late, collective):
    tokens, model = layer_in.shape
    width, channels = gain.shape[1], taps.shape[1]
    lanes = numbers.shape[1]
    size = (channels - width) // 2
    each, mid = width // 64, tokens // 2
    f32, bf16 = jnp.float32, jnp.bfloat16
    vmem, hbm = pl.BlockSpec(memory_space=pltpu.VMEM), pl.BlockSpec(memory_space=pl.ANY)
    out = [
        ((tokens, model), bf16),
        ((tokens, width), f32),
        ((tokens, width), f32),
        ((tokens, 2 * size), f32),
        ((tokens, channels), f32),
        ((tokens + 8, channels), f32),
        ((tokens, lanes), f32),
        ((64, each, size), f32),
        ((tokens, width), f32),
        ((tokens, width), bf16),
        ((tokens, lanes), f32),
        (late.shape, bf16),
    ]
    return pl.pallas_call(
        mixer_kernel,
        out_shape=[jax.ShapeDtypeStruct(*shape) for shape in out],
        in_specs=[vmem, vmem, vmem, hbm, vmem, vmem, vmem, hbm],
        out_specs=[vmem] * (len(out) - 1) + [hbm],
        scratch_shapes=[
            pltpu.VMEM(weights.shape, bf16),
            pltpu.VMEM((tokens + 16, model), bf16),
            pltpu.VMEM((64, each + 8, size), f32),
            pltpu.VMEM((64, each + 8, size), f32),
            pltpu.VMEM((64, each, size), f32),
            pltpu.VMEM((tokens, width), f32),
            pltpu.VMEM((lanes, tokens), f32),
            pltpu.VMEM((3, mid, mid), f32),
            pltpu.VMEM((tokens, lanes), f32),
            pltpu.VMEM((tokens, lanes), f32),
            pltpu.SemaphoreType.DMA((9,)),
            pltpu.SemaphoreType.DMA((4,)),
            pltpu.SemaphoreType.DMA((2,)),
        ]
        + gather_shapes()[:2],
        input_output_aliases={7: len(out) - 1},
        compiler_params=params(collective, vmem_limit_bytes=56 * MIB),
        name="mixer",
    )(layer_in, edge, norm, weights, numbers, taps, gain, late)


class PairSum:
    def __init__(self, mine, theirs, sems, cut):
        self.mine, self.theirs, self.sems, self.cut = mine, theirs, sems, cut
        self.count = mine.shape[1] // cut

    def copy(self, n):
        cols = pl.ds(n * self.cut, self.cut)
        return pltpu.make_async_remote_copy(
            src_ref=self.mine.at[:, cols],
            dst_ref=self.theirs.at[:, cols],
            send_sem=self.sems.at[0, n],
            recv_sem=self.sems.at[1, n],
            device_id={"head": 1 - lax.axis_index("head")},
        )


def residual_kernel(
    gated_ref,
    weights_ref,
    layer_ref,
    norm_ref,
    grad_out_ref,
    position_ref,
    resid_ref,
    normed_ref,
    scale_ref,
    rows_ref,
    shared_ref,
    back_ref,
    right_ref,
    weights,
    mine,
    theirs,
    load_sems,
    sems,
):
    tokens, model = layer_ref.shape
    inner = gated_ref.shape[1]
    hidden = right_ref.shape[1] // 3
    cut = 256
    loads = []
    for n, (start, length) in enumerate(
        ((0, inner), (inner + 2 * hidden, hidden), (inner, 2 * hidden))
    ):
        cols = pl.ds(start, length)
        loads.append(
            pltpu.make_async_copy(weights_ref.at[:, cols], weights.at[:, cols], load_sems.at[n])
        )
        loads[-1].start()
    greet_sibling()
    pair = PairSum(mine, theirs, sems, cut)
    loads[0].wait()
    gated = gated_ref[...]
    for n in range(pair.count):
        rows = slice(n * cut, (n + 1) * cut)
        mine[:, rows] = dot_nt(gated, weights[rows, 0:inner])
        pair.copy(n).start()
    loads[1].wait()
    down = slice(inner + 2 * hidden, inner + 3 * hidden)
    both = slice(inner, inner + 2 * hidden)
    grad_hid = dot_nn(grad_out_ref[...], weights[:, down])
    square = jnp.zeros((tokens, 1), jnp.float32)
    for n in range(pair.count):
        rows = slice(n * cut, (n + 1) * cut)
        pair.copy(n).wait()
        resid = layer_ref[:, rows].astype(jnp.float32) + (mine[:, rows] + theirs[:, rows])
        resid_ref[:, rows] = resid
        square = square + jnp.sum(resid * resid, axis=1, keepdims=True)
    scale = lax.rsqrt(square / model + EPSILON)
    scale_ref[...] = jnp.broadcast_to(scale, scale_ref.shape)
    for n in range(pair.count):
        rows = slice(n * cut, (n + 1) * cut)
        normed_ref[:, rows] = low(resid_ref[:, rows] * scale * norm_ref[:, rows])
    normed = normed_ref[...]
    slots = rows_ref.shape[1]
    step = 16

    @pl.loop(0, rows_ref.shape[0] // step)
    def _(i):
        here = pl.ds(pl.multiple_of(i * step, step), step)
        chosen = chosen_slots(position_ref[here, :], slots)
        rows_ref[here] = low(dot_nn(low(chosen), normed)).reshape(step, slots, model)

    loads[2].wait()
    gate_up = dot_nn(normed, weights[:, both])
    gate, up = gate_up[:, :hidden], gate_up[:, hidden:]
    act, slope = silu_parts(gate)
    hid = low(act * up)
    right_ref[:, 2 * hidden :] = hid
    right_ref[:, 0:hidden] = low(grad_hid * up * slope)
    right_ref[:, hidden : 2 * hidden] = low(grad_hid * act)
    grads = right_ref[:, 0 : 2 * hidden]
    for n in range(pair.count):
        rows = slice(n * cut, (n + 1) * cut)
        shared_ref[:, rows] = dot_nt(hid, weights[rows, down])
        back_ref[:, rows] = dot_nt(grads, weights[rows, both])


def residual_block(gated, weights, layer_in, norm, grad_out, position, slots, collective):
    tokens, model = layer_in.shape
    hidden = (weights.shape[1] - gated.shape[1]) // 3
    f32, bf16 = jnp.float32, jnp.bfloat16
    vmem, hbm = pl.BlockSpec(memory_space=pltpu.VMEM), pl.BlockSpec(memory_space=pl.ANY)
    out = [
        ((tokens, model), f32),
        ((tokens, model), bf16),
        ((tokens, 128), f32),
        ((position.shape[0], slots, model), bf16),
        ((tokens, model), f32),
        ((tokens, model), f32),
        ((tokens, 3 * hidden), bf16),
    ]
    return pl.pallas_call(
        residual_kernel,
        out_shape=[jax.ShapeDtypeStruct(*shape) for shape in out],
        in_specs=[vmem, hbm] + [vmem] * 4,
        out_specs=[vmem] * len(out),
        scratch_shapes=[
            pltpu.VMEM(weights.shape, bf16),
            pltpu.VMEM((tokens, model), f32),
            pltpu.VMEM((tokens, model), f32),
            pltpu.SemaphoreType.DMA((3,)),
            pltpu.SemaphoreType.DMA((2, model // 256)),
        ],
        compiler_params=params(collective, vmem_limit_bytes=48 * MIB),
        name="residual_block",
    )(gated, weights, layer_in, norm, grad_out, position)


def gate_back_kernel(
    home_ref,
    position_ref,
    back_ref,
    resid_ref,
    scale_ref,
    norm_ref,
    grad_out_ref,
    weights_ref,
    z_ref,
    y_ref,
    gate_scale_ref,
    gain_ref,
    grad_resid_ref,
    grad_mix_ref,
    grad_y_ref,
    grad_z_ref,
    norm_grad_ref,
    gain_grad_ref,
    weights,
    mine,
    theirs,
    stat,
    stat_theirs,
    load_sem,
    sems,
    stat_sems,
):
    tokens, model = resid_ref.shape
    inner = z_ref.shape[1]
    experts, slots = home_ref.shape[:2]
    cut = 256
    load = pltpu.make_async_copy(weights_ref.at[:, pl.ds(0, inner)], weights, load_sem)
    load.start()
    greet_sibling()
    pair = PairSum(mine, theirs, sems, cut)
    mine[...] = back_ref[...]
    step = 16

    @pl.loop(0, experts // step)
    def _(i):
        here = pl.ds(pl.multiple_of(i * step, step), step)
        chosen = low(chosen_slots(position_ref[here, :], slots))
        rows = home_ref[here].reshape(step * slots, model)
        mine[...] += dot_tn(chosen, rows)

    for n in range(pair.count):
        pair.copy(n).start()
    scale = scale_ref[:, 0:1]
    inner_sum = jnp.zeros((tokens, 1), jnp.float32)
    for n in range(pair.count):
        cols = slice(n * cut, (n + 1) * cut)
        pair.copy(n).wait()
        grad = mine[:, cols] + theirs[:, cols]
        mine[:, cols] = grad
        resid = resid_ref[:, cols]
        norm_grad_ref[:, cols] = jnp.sum(grad * resid * scale, axis=0, keepdims=True)
        inner_sum = inner_sum + jnp.sum(resid * norm_ref[:, cols] * grad, axis=1, keepdims=True)
    pull = scale * scale * scale * (inner_sum / model)
    for n in range(pair.count):
        cols = slice(n * cut, (n + 1) * cut)
        grad = scale * norm_ref[:, cols] * mine[:, cols] - resid_ref[:, cols] * pull
        grad = grad_out_ref[:, cols].astype(jnp.float32) + grad
        grad_resid_ref[:, cols] = grad
        grad_mix_ref[:, cols] = low(grad)
    load.wait()
    grad_mix = grad_mix_ref[...]
    gate_scale = gate_scale_ref[:, 0:1]
    wide = 384
    dots = jnp.zeros((tokens, 1), jnp.float32)
    for c in range(0, inner, wide):
        cols = slice(c, c + wide)
        grad = dot_nn(grad_mix, weights[:, cols])
        z = z_ref[:, cols]
        gated = y_ref[:, cols] * (z * jax.nn.sigmoid(z))
        gain_grad_ref[:, cols] = jnp.sum(grad * gated * gate_scale, axis=0, keepdims=True)
        weighted = grad * gain_ref[:, cols]
        grad_y_ref[:, cols] = weighted
        dots = dots + jnp.sum(weighted * gated, axis=1, keepdims=True)
    stat[...] = jnp.broadcast_to(dots, stat.shape)
    swap = pltpu.make_async_remote_copy(
        src_ref=stat,
        dst_ref=stat_theirs,
        send_sem=stat_sems.at[0],
        recv_sem=stat_sems.at[1],
        device_id={"head": 1 - lax.axis_index("head")},
    )
    swap.start()
    swap.wait()
    dots = (stat[...] + stat_theirs[...])[:, 0:1]
    pull = gate_scale * gate_scale * gate_scale * (dots / (2 * inner))
    for c in range(0, inner, wide):
        cols = slice(c, c + wide)
        z, y = z_ref[:, cols], y_ref[:, cols]
        act, slope = silu_parts(z)
        grad = gate_scale * grad_y_ref[:, cols] - y * act * pull
        grad_y_ref[:, cols] = grad * act
        grad_z_ref[:, cols] = low(grad * y * slope)


def gate_back(home, position, back, resid, scale, norm, grad_out, weights, z, y, gate_scale, gain, collective):
    tokens, model = resid.shape
    inner = z.shape[1]
    f32, bf16 = jnp.float32, jnp.bfloat16
    vmem, hbm = pl.BlockSpec(memory_space=pltpu.VMEM), pl.BlockSpec(memory_space=pl.ANY)
    out = [
        ((tokens, model), f32),
        ((tokens, model), bf16),
        ((tokens, inner), f32),
        ((tokens, inner), bf16),
        ((1, model), f32),
        ((1, inner), f32),
    ]
    return pl.pallas_call(
        gate_back_kernel,
        out_shape=[jax.ShapeDtypeStruct(*shape) for shape in out],
        in_specs=[vmem] * 7 + [hbm] + [vmem] * 4,
        out_specs=[vmem] * len(out),
        scratch_shapes=[
            pltpu.VMEM((model, inner), bf16),
            pltpu.VMEM((tokens, model), f32),
            pltpu.VMEM((tokens, model), f32),
            pltpu.VMEM((tokens, 128), f32),
            pltpu.VMEM((tokens, 128), f32),
            pltpu.SemaphoreType.DMA,
            pltpu.SemaphoreType.DMA((2, model // 256)),
            pltpu.SemaphoreType.DMA((2,)),
        ],
        compiler_params=params(collective, vmem_limit_bytes=48 * MIB),
        name="gate_back",
    )(home, position, back, resid, scale, norm, grad_out, weights, z, y, gate_scale, gain)


def small_message(parts):
    flat = jnp.concatenate([part.reshape(-1) for part in parts])
    size = flat.shape[0]
    each = -(-size // (64 * 1024)) * 1024
    return jnp.pad(flat, (0, 64 * each - size)).reshape(64, each // 128, 128)


def small_parts(parts, out):
    out, result, start = out.reshape(-1), [], 0
    for part in parts:
        result.append(out[start : start + part.size].reshape(part.shape))
        start += part.size
    return result


def per_device(
    layer_in,
    norm_first,
    mixer_in,
    state_proj,
    step_proj,
    step_bias,
    conv_main,
    conv_state,
    decay_rate,
    skip_gain,
    gate_gain,
    mixer_out,
    norm_second,
    shared_gate_up,
    shared_down,
    expert_gate_up,
    expert_down,
    routes,
    route_weights,
    grad_out,
):
    tokens, model_width = layer_in.shape
    inner_dev = mixer_in.shape[2]
    state_size = state_proj.shape[1] // 2
    heads_dev = step_proj.shape[1]
    conv_taps = conv_main.shape[0]
    shared_dev = shared_down.shape[1]
    local_experts = expert_gate_up.shape[0]
    experts_all = local_experts * lax.axis_size("seq")
    choices_per = routes.shape[1]
    capacity = max(2, tokens * choices_per * 4 // (3 * experts_all))
    slots_dev = capacity // lax.axis_size("head")
    lanes = 128
    pad_heads = lambda v: jnp.pad(v, ((0, 0), (0, lanes - heads_dev)))
    late_rows = jnp.concatenate(
        [mixer_out, shared_gate_up.reshape(-1, 2 * shared_dev), shared_down], axis=1
    )
    gathered, late_rows, edge, position, slot_weight, grads_in = gather_rows(
        jnp.concatenate(
            [mixer_in.reshape(-1, 2 * inner_dev), state_proj, pad_heads(step_proj)], axis=1
        ),
        late_rows,
        layer_in,
        routes,
        route_weights,
        grad_out,
        experts_all,
        slots_dev,
        0,
    )
    weights_in = gathered.reshape(model_width, -1)
    numbers = jnp.pad(
        jnp.stack([decay_rate, skip_gain, step_bias]), ((0, 5), (0, lanes - heads_dev))
    )
    taps = jnp.pad(jnp.concatenate([conv_main, conv_state], axis=1), ((0, 8 - conv_taps), (0, 0)))
    (
        normed,
        gate_z,
        heads_x,
        state_both,
        conv_sum,
        pre,
        step_raw,
        state_start,
        ssd,
        normed_gate,
        gate_scale,
        gathered,
    ) = mixer(
        layer_in, edge, norm_first[None], weights_in, numbers, taps, gate_gain[None], late_rows, 1
    )
    weights_late = gathered.reshape(model_width, -1)
    residual, normed_second, scale_second, rows_out, shared_part, shared_back, shared_right = (
        residual_block(
            normed_gate,
            weights_late,
            layer_in,
            norm_second[None],
            grad_out,
            position,
            slots_dev,
            2,
        )
    )
    grad_home, res_sums, expert_gate_up_grad, expert_down_grad = experts(
        rows_out,
        grads_in,
        expert_gate_up.reshape(model_width, -1),
        expert_down.reshape(-1, model_width),
        3,
    )
    grad_resid, grad_mix, grad_ssd, grad_gate_z, norm_second_grad, gate_gain_grad = gate_back(
        grad_home,
        position,
        shared_back,
        residual,
        scale_second,
        norm_second[None],
        grad_out,
        weights_late,
        gate_z,
        ssd,
        gate_scale,
        gate_gain[None],
        4,
    )
    late_plan = (
        ((0, 0, 1024),),
        ((0, 1024, 512), (1, 1536, 512)),
        ((1, 2048, 512), (2, 2560, 512)),
    )
    summed_late, right_grads, taps_grad, heads_grad = mixer_back(
        [grad_mix, normed_second, grad_out],
        jnp.concatenate([normed_gate, shared_right], axis=1),
        late_plan,
        grad_ssd,
        ssd,
        heads_x,
        state_both,
        conv_sum,
        pre,
        grad_gate_z,
        step_raw,
        numbers,
        taps,
        state_start.reshape(inner_dev, state_size),
        5,
    )
    small = (
        jnp.zeros_like(norm_first),
        norm_second_grad,
        heads_grad[2, :heads_dev],
        taps_grad[:conv_taps, :inner_dev],
        taps_grad[:conv_taps, inner_dev:],
        heads_grad[1, :heads_dev],
        heads_grad[0, :heads_dev],
        gate_gain_grad,
    )
    summed, input_grad, small_sums, layer_out = input_back(
        normed,
        right_grads,
        tuple(((0, start, 1152),) for start in (0, 1152, 2304)),
        weights_in,
        layer_in,
        norm_first[None],
        grad_resid,
        small_message(small),
        res_sums,
        position,
        slot_weight,
        shared_part,
        residual,
        6,
    )
    small_sums = small_parts(small, small_sums)
    wide = 2 * inner_dev + 2 * state_size
    weight_sums = (
        summed[:, : 2 * inner_dev].reshape(-1, 2, inner_dev),
        summed[:, 2 * inner_dev : wide],
        summed[:, wide : wide + heads_dev],
        summed_late[:, :inner_dev],
        summed_late[:, inner_dev : inner_dev + 2 * shared_dev].reshape(-1, 2, shared_dev),
        summed_late[:, inner_dev + 2 * shared_dev :],
    )
    return (
        layer_out,
        input_grad,
        small_sums[0],
        weight_sums[0],
        weight_sums[1],
        weight_sums[2],
        small_sums[2],
        small_sums[3],
        small_sums[4],
        small_sums[5],
        small_sums[6],
        small_sums[7].reshape(-1),
        weight_sums[3],
        small_sums[1].reshape(-1),
        weight_sums[4],
        weight_sums[5],
        expert_gate_up_grad,
        expert_down_grad,
    )


def solution(mesh):
    placed = (
        P("seq", None),
        P(),
        P("seq", None, "head"),
        P("seq", None),
        P("seq", "head"),
        P("head"),
        P(None, "head"),
        P(),
        P("head"),
        P("head"),
        P("head"),
        P("seq", "head"),
        P(),
        P("seq", None, "head"),
        P("seq", "head"),
        P("seq", None, None, "head"),
        P("seq", "head", None),
        P("seq", None),
        P("seq", None),
        P("seq", None),
    )
    return jax.shard_map(
        per_device,
        mesh=mesh,
        in_specs=placed,
        out_specs=(
            P("seq", None),
            P("seq", None),
            P(),
            P("seq", None, "head"),
            P("seq", None),
            P("seq", "head"),
            P("head"),
            P(None, "head"),
            P(),
            P("head"),
            P("head"),
            P("head"),
            P("seq", "head"),
            P(),
            P("seq", None, "head"),
            P("seq", "head"),
            P("seq", None, None, "head"),
            P("seq", "head", None),
        ),
        check_vma=False,
    )
```

```python
import functools
import jax
import jax.numpy as jnp
from jax import lax
from jax.experimental import pallas as pl
from jax.experimental.pallas import tpu as pltpu
from jax.sharding import PartitionSpec as P

ORDERS = ((0, 1, 2), (1, 2, 0), (2, 0, 1))
VMEM = 62 << 20
EPSILON = 1e-05


def coordinates():
    me = lax.axis_index("seq")
    return me, [me // 16, (me // 4) % 4, me % 4]


def seq_of(at):
    return at[0] * 16 + at[1] * 4 + at[2]


def moved(at, axis, by):
    return [(c + by) % 4 if i == axis else c for i, c in enumerate(at)]


def announce(me, with_sibling):
    barrier = pltpu.get_barrier_semaphore()

    @pl.loop(1, 64)
    def _(k):
        pl.semaphore_signal(barrier, inc=1, device_id={"seq": lax.rem(me + k, 64)})

    if with_sibling:
        pl.semaphore_signal(barrier, inc=1, device_id={"head": 1 - lax.axis_index("head")})


def await_all(with_sibling):
    pl.semaphore_wait(pltpu.get_barrier_semaphore(), 64 if with_sibling else 63)


def parts_of(columns):
    third = columns // 3
    tiles = third // 128
    half = tiles // 2 * 128
    return third, half


def region(at, order, phase, value, cols):
    index = [None] * 3
    for i in range(3):
        if i < phase:
            index[order[i]] = slice(None)
        elif i == phase:
            index[order[i]] = value
        else:
            index[order[i]] = at[order[i]]
    return tuple(index) + (slice(None), cols)


class Ways:
    def __init__(self, at):
        self.at = at

    def group(self, g, back=False):
        x, z, y = self.at
        sign, lead = (-1, 8) if back else (1, 0)
        near, far = lax.rem(g, 4), g // 4
        xs = [lax.rem(x + lead + sign * a, 4) * 16 for a in range(4)]
        zs = [lax.rem(z + lead + sign * (near + a), 4) * 4 for a in range(4)]
        ys = [lax.rem(y + lead + sign * (far + a), 4) for a in range(4)]
        return [(g * 8 + n, xs[n % 4] + zs[n % 4] + ys[(n % 4 + n // 4 * 2) % 4]) for n in range(8)]

    def each(self, first, last, body, back=False):
        @pl.loop(first, last)
        def _(g):
            for n, (k, device) in enumerate(self.group(g, back)):
                if n == 0:
                    pl.when(k > 0)(functools.partial(body, k, device))
                else:
                    body(k, device)


class Lazy:
    def __init__(self, source, ref, sem):
        self.ref, self.copy = ref, pltpu.make_async_copy(source, ref, sem)
        self.shape, self.dtype = ref.shape, ref.dtype
        self.copy.start()

    def ready(self):
        if self.copy is not None:
            self.copy.wait()
            self.copy = None
        return self.ref

    @property
    def at(self):
        return self.ready().at

    def __getitem__(self, index):
        return self.ready()[index]


class Eager:
    def __init__(self, target, ref, sem):
        self.ref, self.copy, self.going = ref, pltpu.make_async_copy(ref, target, sem), False
        self.shape, self.dtype, self.at = ref.shape, ref.dtype, ref.at

    def __getitem__(self, index):
        return self.ref[index]

    def __setitem__(self, index, value):
        self.ref[index] = value

    def flush(self):
        if not self.going:
            self.going = True
            self.copy.start()


def ready(*refs):
    for ref in refs:
        if isinstance(ref, Lazy):
            ref.ready()


def call(kernel, out_shape, in_specs, out_specs, scratch_shapes, **options):
    def run(*args):
        leaves, tree = jax.tree.flatten(list(args))
        specs = tree.flatten_up_to(list(in_specs))
        shapes, out_tree = jax.tree.flatten(list(out_shape))
        out_kinds = out_tree.flatten_up_to(list(out_specs))
        lazy = [n for n, spec in enumerate(specs) if spec is Lazy]
        eager = [n for n, spec in enumerate(out_kinds) if spec is Eager]
        hbm = pl.BlockSpec(memory_space=pl.ANY)
        buffers = [pltpu.VMEM(leaves[n].shape, leaves[n].dtype) for n in lazy]
        buffers += [pltpu.VMEM(shapes[n].shape, shapes[n].dtype) for n in eager]
        buffers += [pltpu.SemaphoreType.DMA((max(1, len(lazy)),))]
        buffers += [pltpu.SemaphoreType.DMA((max(1, len(eager)),))]
        own = len(scratch_shapes)

        def body(*refs):
            ins, outs = list(refs[: len(leaves)]), list(refs[len(leaves) :][: len(shapes)])
            rest = refs[len(leaves) + len(shapes) :]
            more = rest[own:]
            for n, index in enumerate(lazy):
                ins[index] = Lazy(ins[index], more[n], more[-2].at[n])
            for n, index in enumerate(eager):
                outs[index] = Eager(outs[index], more[len(lazy) + n], more[-1].at[n])
            kernel(*tree.unflatten(ins), *out_tree.unflatten(outs), *rest[:own])
            for index in lazy:
                ins[index].ready()
            for index in eager:
                outs[index].flush()
            for index in eager:
                outs[index].copy.wait()

        out = pl.pallas_call(
            body,
            out_shape=shapes,
            in_specs=[hbm if spec is Lazy else spec for spec in specs],
            out_specs=[hbm if kind is Eager else kind for kind in out_kinds],
            scratch_shapes=list(scratch_shapes) + buffers,
            **options,
        )(*leaves)
        return out_tree.unflatten(out)

    return run


def emit_kernel(*refs):
    count = len(refs) // 2
    for n in range(count):
        refs[count + n][...] = refs[n][...]


def emit(arrays):
    return pl.pallas_call(
        emit_kernel,
        out_shape=[jax.ShapeDtypeStruct(array.shape, array.dtype) for array in arrays],
        name="emit",
    )(*arrays)


class Spread:
    def __init__(self, at, me, source, target, sems, first, last, back):
        self.at, self.me, self.source, self.target = at, me, source, target
        self.sems = sems
        self.first, self.last, self.back = first, last, back

    def start(self, first=None, last=None):
        first = self.first if first is None else first
        last = self.last if last is None else last
        if first == 0:
            own = self.source.at[0 if self.back else self.me]
            pltpu.make_async_copy(own, self.target.at[0], self.sems.at[1]).start()

        def put(k, device):
            pltpu.make_async_remote_copy(
                src_ref=self.source.at[k if self.back else device],
                dst_ref=self.target.at[k - 8 * self.first],
                send_sem=self.sems.at[0],
                recv_sem=self.sems.at[1 + k // 8],
                device_id={"seq": device},
            ).start()

        Ways(self.at).each(first, last, put, self.back)

    def arrived(self, first, last):
        for g in range(first, last):
            here = self.target.at[pl.ds(8 * (g - self.first), 8)]
            pltpu.make_async_copy(here, here, self.sems.at[1 + g]).wait()

    def sent(self):
        count = 8 * (self.last - self.first)
        here = self.target.at[pl.ds(0, count - 1 if self.first == 0 else count)]
        pltpu.make_async_copy(here, here, self.sems.at[0]).wait()

    def wait(self):
        self.arrived(self.first, self.last)
        self.sent()


OUT = ((0, 6), (6, 8))
HOME = ((0, 3), (3, 8))


def part_shape(span, rows):
    return jax.ShapeDtypeStruct((8 * (span[1] - span[0]),) + rows.shape[1:], rows.dtype)


def params(collective, **more):
    return pltpu.CompilerParams(collective_id=collective, has_side_effects=True, **more)


class PairSum:
    def __init__(self, mine, theirs, sems, cut):
        self.mine, self.theirs, self.sems, self.cut = mine, theirs, sems, cut
        self.count = mine.shape[1] // cut

    def copy(self, n):
        cols = pl.ds(n * self.cut, self.cut)
        return pltpu.make_async_remote_copy(
            src_ref=self.mine.at[:, cols],
            dst_ref=self.theirs.at[:, cols],
            send_sem=self.sems.at[0, n],
            recv_sem=self.sems.at[1, n],
            device_id={"head": 1 - lax.axis_index("head")},
        )


def experts_kernel(
    gated_ref,
    weights_ref,
    layer_ref,
    table_ref,
    position_ref,
    grads_refs,
    gate_up_ref,
    down_ref,
    grad_out_ref,
    home_ref,
    res_ref,
    gate_up_grad_ref,
    down_grad_ref,
    shared_ref,
    back_ref,
    right_ref,
    resid_ref,
    normed_ref,
    scale_ref,
    rows_ref,
    mine,
    theirs,
    slot_in,
    grad_slots,
    theirs_x,
    theirs_y,
    sums,
    wide_grad,
    weights,
    load_sems,
    pair_sems,
    send,
    home_send,
    home_recv,
    sems,
):
    me, at = coordinates()
    head = lax.axis_index("head")
    sibling = {"head": 1 - head}
    names = ("recv", "fwd_send", "fwd_recv", "kept", "given_send", "given_recv")
    names += ("x_send", "x_recv", "y_send", "y_recv")
    sem = {name: sems.at[n] for n, name in enumerate(names)}
    announce(me, True)
    shared_hidden = right_ref.shape[1] // 3
    tokens, model = layer_ref.shape
    inner = gated_ref.shape[1]
    loads = []
    for n, cols in enumerate((pl.ds(0, inner), pl.ds(inner, 3 * shared_hidden))):
        loads.append(
            pltpu.make_async_copy(weights_ref.at[:, cols], weights.at[:, cols], load_sems.at[n])
        )
        loads[n].start()
    norm_ref = table_ref.at[5:6, 0:model]
    wide_grad[...] = jnp.zeros_like(wide_grad)
    down_grad_ref[...] = jnp.zeros_like(down_grad_ref)
    ways = Ways(at)
    await_all(True)

    def group(c):
        return pl.ds(pl.multiple_of(c * 8, 8), 8)

    def given(c, source=None):
        there = grad_slots.at[group(c), head]
        return pltpu.make_async_remote_copy(
            src_ref=there if source is None else source,
            dst_ref=there,
            send_sem=sem["given_send"].at[c],
            recv_sem=sem["given_recv"].at[c],
            device_id=sibling,
        )

    def kept(c, source=None):
        there = grad_slots.at[group(c), head]
        return pltpu.make_async_copy(there if source is None else source, there, sem["kept"].at[c])

    def forward(c):
        return pltpu.make_async_remote_copy(
            src_ref=slot_in.at[group(c), head],
            dst_ref=slot_in.at[group(c), head],
            send_sem=sem["fwd_send"].at[c],
            recv_sem=sem["fwd_recv"].at[c],
            device_id=sibling,
        )

    def swap(c, source, target, name):
        return pltpu.make_async_remote_copy(
            src_ref=source.at[group(c), 1 - head],
            dst_ref=target.at[group(c)],
            send_sem=sem[name + "_send"].at[c],
            recv_sem=sem[name + "_recv"].at[c],
            device_id=sibling,
        )

    for (first, last), grads_ref in zip(OUT, grads_refs):
        for c in range(first, last):
            source = grads_ref.at[pl.ds(8 * (c - first), 8)]
            kept(c, source).start()
            given(c, source).start()

    cut = 256
    pair = PairSum(mine, theirs, pair_sems, cut)
    loads[0].wait()
    gated = gated_ref[...]
    for n in range(pair.count):
        rows = slice(n * cut, (n + 1) * cut)
        mine[:, rows] = dot_nt(gated, weights[rows, 0:inner])
        pair.copy(n).start()
    loads[1].wait()
    both = slice(inner, inner + 2 * shared_hidden)
    less = slice(inner + 2 * shared_hidden, inner + 3 * shared_hidden)
    shared_grad_hid = dot_nn(grad_out_ref[...], weights[:, less])
    square = jnp.zeros((tokens, 1), jnp.float32)
    for n in range(pair.count):
        rows = slice(n * cut, (n + 1) * cut)
        pair.copy(n).wait()
        resid = layer_ref[:, rows].astype(jnp.float32) + (mine[:, rows] + theirs[:, rows])
        resid_ref[:, rows] = resid
        square = square + jnp.sum(resid * resid, axis=1, keepdims=True)
    scale = lax.rsqrt(square / model + EPSILON)
    scale_ref[...] = jnp.broadcast_to(scale, scale_ref.shape)
    for n in range(pair.count):
        rows = slice(n * cut, (n + 1) * cut)
        normed_ref[:, rows] = low(resid_ref[:, rows] * scale * norm_ref[:, rows])
    resid_ref.flush()
    normed_ref.flush()
    ready(position_ref)
    normed = normed_ref[...]
    slots, step = rows_ref.shape[1], 16

    @pl.loop(0, rows_ref.shape[0] // step)
    def _(i):
        here = pl.ds(pl.multiple_of(i * step, step), step)
        chosen = chosen_slots(position_ref[here, :], slots)
        rows_ref[here] = low(dot_nn(low(chosen), normed)).reshape(step, slots, model)

    own = pltpu.make_async_copy(rows_ref.at[me], slot_in.at[0, head], sem["recv"].at[0])
    own.start()

    def put(k, target):
        pltpu.make_async_remote_copy(
            src_ref=rows_ref.at[target],
            dst_ref=slot_in.at[k, head],
            send_sem=send,
            recv_sem=sem["recv"].at[k // 8],
            device_id={"seq": target},
        ).start()

    ways.each(0, 8, put)

    hidden = down_ref.shape[0]
    width = down_ref.shape[1]

    def nt(left, right):
        return lax.dot_general(
            left, right, (((1,), (1,)), ((), ())), preferred_element_type=jnp.float32
        )

    def tn(left, right):
        return lax.dot_general(
            left, right, (((0,), (0,)), ((), ())), preferred_element_type=jnp.float32
        )

    gate_up = dot_nn(normed, weights[:, both])
    gate, up = gate_up[:, :shared_hidden], gate_up[:, shared_hidden:]
    act, slope = silu_parts(gate)
    hid = low(act * up)
    right_ref[:, 2 * shared_hidden :] = hid
    right_ref[:, 0:shared_hidden] = low(shared_grad_hid * up * slope)
    right_ref[:, shared_hidden : 2 * shared_hidden] = low(shared_grad_hid * act)
    grads = right_ref[:, 0 : 2 * shared_hidden]
    for c in range(0, width, 256):
        rows = slice(c, c + 256)
        shared_ref[:, rows] = dot_nt(hid, weights[rows, less])
        back_ref[:, rows] = dot_nt(grads, weights[rows, both])
    for ref in (shared_ref, back_ref, right_ref):
        ref.flush()
    ready(gate_up_ref, down_ref)

    @pl.loop(0, 10)
    def _(i):
        @pl.when(i < 8)
        def _():
            c = i
            pltpu.make_async_copy(
                rows_ref.at[group(c)], slot_in.at[group(c), head], sem["recv"].at[c]
            ).wait()
            forward(c).start()

        @pl.when((i >= 1) & (i < 9))
        def _():
            c = i - 1
            forward(c).wait()
            kept(c).wait()
            given(c).wait()
            rows = slot_in[group(c)].reshape(256, width)
            grads = grad_slots[group(c)].reshape(256, width)
            both = jnp.dot(rows, gate_up_ref[...], preferred_element_type=jnp.float32)
            gate, up = both[:, :hidden], both[:, hidden:]
            sig = jax.nn.sigmoid(gate)
            act = gate * sig
            hid = (act * up).astype(jnp.bfloat16)
            grad_hid = nt(grads, down_ref[...])
            grad_gate = grad_hid * up * (sig * (1.0 + gate * (1.0 - sig)))
            grad_both = jnp.concatenate([grad_gate, grad_hid * act], axis=1).astype(jnp.bfloat16)
            wide_grad[...] += tn(rows, grad_both)
            down_grad_ref[...] += tn(hid, grads)
            back = nt(grad_both, gate_up_ref[...]).astype(jnp.bfloat16)
            slot_in[group(c)] = back.reshape(8, 2, 16, width)
            res = jnp.dot(hid, down_ref[...], preferred_element_type=jnp.float32)
            grad_slots[group(c)] = res.astype(jnp.bfloat16).reshape(8, 2, 16, width)
            swap(c, slot_in, theirs_x, "x").start()
            swap(c, grad_slots, theirs_y, "y").start()

        @pl.when(i >= 2)
        def _():
            c = i - 2
            swap(c, slot_in, theirs_x, "x").wait()

            def add(k):
                total = slot_in[k, head].astype(jnp.float32) + theirs_x[k].astype(jnp.float32)
                sums[k] = total.astype(sums.dtype)

            def put_home(k, source):
                add(k)
                pltpu.make_async_remote_copy(
                    src_ref=sums.at[k],
                    dst_ref=home_ref.at[me],
                    send_sem=home_send,
                    recv_sem=home_recv,
                    device_id={"seq": source},
                ).start()

            @pl.when(c == 0)
            def _():
                add(0)
                pltpu.make_async_copy(sums.at[0], home_ref.at[me], home_recv).start()

            ways.each(c, c + 1, put_home, back=True)
            swap(c, grad_slots, theirs_y, "y").wait()

            @pl.loop(0, 8)
            def _(n):
                j = c * 8 + n
                total = grad_slots[j, head].astype(jnp.float32) + theirs_y[j].astype(jnp.float32)
                res_ref[j] = total.astype(res_ref.dtype)

    tiles = hidden // 128
    for tile in range(tiles):
        for which in range(2):
            start = which * hidden + tile * 128
            gate_up_grad_ref[pl.ds(tile * 2 + which, width, stride=2 * tiles), :] = wide_grad[
                :, start : start + 128
            ]
    some = pl.ds(0, 63)
    pltpu.make_async_copy(rows_ref.at[some], rows_ref.at[some], send).wait()
    pltpu.make_async_copy(sums.at[some], sums.at[some], home_send).wait()
    pltpu.make_async_copy(sums, home_ref, home_recv).wait()


def experts(
    gated, weights, layer_in, table, position, grads, gate_up, down, grad_out, slots, collective
):
    tokens, model = layer_in.shape
    shared_hidden = (weights.shape[1] - gated.shape[1]) // 3
    hidden, width = down.shape
    half, bf16 = (position.shape[0], slots, model), jnp.bfloat16
    whole = (half[0], 2) + half[1:]
    vmem, hbm = pl.BlockSpec(memory_space=pltpu.VMEM), pl.BlockSpec(memory_space=pl.ANY)
    home, res, wide, down_grad, *shared = call(
        experts_kernel,
        out_shape=[
            jax.ShapeDtypeStruct(half, bf16),
            jax.ShapeDtypeStruct(half, bf16),
            jax.ShapeDtypeStruct((width * 2 * hidden // 128, 128), jnp.float32),
            jax.ShapeDtypeStruct((hidden, width), jnp.float32),
            jax.ShapeDtypeStruct((tokens, width), jnp.float32),
            jax.ShapeDtypeStruct((tokens, width), jnp.float32),
            jax.ShapeDtypeStruct((tokens, 3 * shared_hidden), bf16),
            jax.ShapeDtypeStruct((tokens, model), jnp.float32),
            jax.ShapeDtypeStruct((tokens, model), bf16),
            jax.ShapeDtypeStruct((tokens, 128), jnp.float32),
        ],
        in_specs=[Lazy, hbm, Lazy, vmem, Lazy, [hbm] * len(grads), Lazy, Lazy, Lazy],
        out_specs=[hbm] + [vmem] * 3 + [Eager] * 5 + [vmem],
        scratch_shapes=[
            pltpu.VMEM(half, bf16),
            pltpu.VMEM((tokens, model), jnp.float32),
            pltpu.VMEM((tokens, model), jnp.float32),
            pltpu.VMEM(whole, bf16),
            pltpu.VMEM(whole, bf16),
            pltpu.VMEM(half, bf16),
            pltpu.VMEM(half, bf16),
            pltpu.VMEM(half, bf16),
            pltpu.VMEM((width, 2 * hidden), jnp.float32),
            pltpu.VMEM(weights.shape, bf16),
            pltpu.SemaphoreType.DMA((2,)),
            pltpu.SemaphoreType.DMA((2, model // 256)),
            pltpu.SemaphoreType.DMA,
            pltpu.SemaphoreType.DMA,
            pltpu.SemaphoreType.DMA,
            pltpu.SemaphoreType.DMA((10, 8)),
        ],
        compiler_params=params(collective, vmem_limit_bytes=VMEM),
        name="experts",
    )(gated, weights, layer_in, table, position, grads, gate_up, down, grad_out)
    wide = wide.reshape(width, hidden // 128, 2, 128).transpose(0, 2, 1, 3)
    return home, res, wide.reshape(1, width, 2, hidden), down_grad[None], *shared


class Scan:
    def __init__(self, reverse, at, me, x_ref, out_ref, got, made, sems):
        self.reverse, self.at, self.me = reverse, at, me
        self.x_ref, self.out_ref, self.got, self.made = x_ref, out_ref, got, made
        self.send, self.recv, self.back_send, self.back_recv = [sems.at[n] for n in range(4)]

    def spread(self, source, target_ref, send, recv):
        def put(_, target):
            pltpu.make_async_remote_copy(
                src_ref=source.at[target],
                dst_ref=target_ref.at[self.me],
                send_sem=send,
                recv_sem=recv,
                device_id={"seq": target},
            ).start()

        Ways(self.at).each(0, 8, put)

    def begin(self):
        self.got[self.me] = self.x_ref[self.me]
        self.spread(self.x_ref, self.got, self.send, self.recv)

    def middle(self):
        some = pl.ds(0, 63)
        x_ref, got, made = self.x_ref, self.got, self.made
        pltpu.make_async_copy(x_ref.at[some], x_ref.at[some], self.send).wait()
        pltpu.make_async_copy(got.at[some], got.at[some], self.recv).wait()
        heads, width = made.shape[1:]
        number = lax.broadcasted_iota(jnp.int32, (heads, width), 0) + heads * self.me
        chosen = number // 64 == lax.broadcasted_iota(jnp.int32, (heads, width), 1)

        def step(k, state):
            at_k = 63 - k if self.reverse else k
            made[at_k] = state
            rows = got[at_k].astype(jnp.float32)
            row = jnp.sum(rows[heads:], axis=0, keepdims=True)
            decay = jnp.sum(jnp.where(chosen, row, 0.0), axis=1, keepdims=True)
            return decay * state + rows[:heads]

        lax.fori_loop(0, 64, step, jnp.zeros((heads, width), jnp.float32), unroll=8)
        self.out_ref[self.me] = made[self.me]
        self.spread(made, self.out_ref, self.back_send, self.back_recv)

    def end(self):
        some = pl.ds(0, 63)
        made = self.made
        pltpu.make_async_copy(made.at[some], made.at[some], self.back_send).wait()
        pltpu.make_async_copy(made.at[some], made.at[some], self.back_recv).wait()


def scan_rows(states, decay):
    decays = [part.astype(jnp.float32) for part in split(decay, 3)]
    decays = jnp.concatenate(decays + [jnp.zeros((5, decay.shape[1]), jnp.float32)], axis=0)
    decays = jnp.broadcast_to(decays[None], (states.shape[0],) + decays.shape)
    return low(jnp.concatenate([states, decays], axis=1))


class Small:
    def __init__(self, at, me, x_ref, out_ref, got, sems):
        self.at, self.me = at, me
        self.x_ref, self.out_ref, self.got = x_ref, out_ref, got
        self.send, self.recv, self.back_send, self.back_recv = [sems.at[n] for n in range(4)]

    def begin(self):
        self.got[self.me] = self.x_ref[self.me]

        def put(_, target):
            pltpu.make_async_remote_copy(
                src_ref=self.x_ref.at[target],
                dst_ref=self.got.at[self.me],
                send_sem=self.send,
                recv_sem=self.recv,
                device_id={"seq": target},
            ).start()

        Ways(self.at).each(0, 8, put)

    def middle(self):
        some = pl.ds(0, 63)
        x_ref, got, out_ref, me = self.x_ref, self.got, self.out_ref, self.me
        pltpu.make_async_copy(x_ref.at[some], x_ref.at[some], self.send).wait()
        pltpu.make_async_copy(got.at[some], got.at[some], self.recv).wait()
        out_ref[me] = lax.fori_loop(1, 64, lambda k, total: total + got[k], got[0], unroll=9)

        def put(_, target):
            pltpu.make_async_remote_copy(
                src_ref=out_ref.at[me],
                dst_ref=out_ref.at[me],
                send_sem=self.back_send,
                recv_sem=self.back_recv,
                device_id={"seq": target},
            ).start()

        Ways(self.at).each(0, 8, put)

    def end(self):
        some = pl.ds(0, 63)
        got = self.got
        pltpu.make_async_copy(got.at[some], got.at[some], self.back_send).wait()
        pltpu.make_async_copy(got.at[some], got.at[some], self.back_recv).wait()


class Scatter:
    def __init__(self, at, plan, lefts, rights, out_ref, buf, rest, send, recv):
        self.at, self.plan, self.lefts, self.rights = at, plan, lefts, rights
        self.out_ref, self.buf, self.rest, self.send, self.recv = out_ref, buf, rest, send, recv
        self.third, self.half = parts_of(buf.shape[4])
        self.copies = {}

    def spans(self, p):
        start, third, half = p * self.third, self.third, self.half
        return pl.ds(start, half), pl.ds(start + half, third - half)

    def product(self, p):
        buf = self.buf
        rows = buf.shape[3]
        for which, other, first, start, length in self.plan[p]:
            left, right = self.lefts[which], self.rights[other]
            ready(left, right)

            @pl.loop(0, 4)
            def _(x):
                across = pl.ds(pl.multiple_of(x * 16 * rows, 128), 16 * rows)
                total = lax.dot_general(
                    left[:, across],
                    right[:, first : first + length],
                    (((0,), (0,)), ((), ())),
                    preferred_element_type=jnp.float32,
                )
                total = total.reshape(4, 4, rows, length).astype(jnp.bfloat16)
                buf[x, :, :, :, start : start + length] = total

    def send_to(self, phase, p, by, value, cols, slot, kind):
        order = ORDERS[p]
        axis = order[phase]
        lead = (slice(None),) * phase
        copy = pltpu.make_async_remote_copy(
            src_ref=self.buf.at[region(self.at, order, phase, value, cols)],
            dst_ref=self.rest[phase].at[(slot,) + lead + (slice(None), cols)],
            send_sem=self.send.at[phase, p, kind],
            recv_sem=self.recv.at[phase, p, kind],
            device_id={"seq": seq_of(moved(self.at, axis, by))},
        )
        copy.start()
        self.copies[phase, p, kind] = copy

    def added(self, phase, p, value, cols, slots):
        order, buf, room = ORDERS[p], self.buf, self.rest[phase]

        @pl.loop(0, 4**phase)
        def _(i):
            free = ((), (i,), (i // 4, i % 4))[phase]
            index = list(region(self.at, order, phase, value, cols))
            for n, axis in enumerate(sorted(order[:phase])):
                index[axis] = free[n]
            index = tuple(index)
            total = buf[index].astype(jnp.float32)
            for slot in slots:
                total = total + room[(slot,) + free + (slice(None), cols)].astype(jnp.float32)
            if phase == 0 and len(slots) == 2:
                self.out_ref[:, cols] = total
            else:
                buf[index] = total.astype(jnp.bfloat16)

    def first(self, phase, p):
        self.first_far(phase, p)
        self.first_near(phase, p)

    def first_far(self, phase, p):
        c = self.at[ORDERS[p][phase]]
        low, high = self.spans(p)
        self.send_to(phase, p, 1, (c + 2) % 4, low, 2, 0)
        self.send_to(phase, p, 3, (c + 2) % 4, high, 2, 1)

    def first_near(self, phase, p):
        c = self.at[ORDERS[p][phase]]
        low, high = self.spans(p)
        self.send_to(phase, p, 1, (c + 1) % 4, high, 0, 2)
        self.send_to(phase, p, 3, (c + 3) % 4, low, 1, 3)

    def second(self, phase, p):
        c = self.at[ORDERS[p][phase]]
        low, high = self.spans(p)
        self.copies[phase, p, 0].wait_recv()
        self.added(phase, p, (c + 1) % 4, low, (2,))
        self.send_to(phase, p, 1, (c + 1) % 4, low, 0, 4)
        self.copies[phase, p, 1].wait_recv()
        self.added(phase, p, (c + 3) % 4, high, (2,))
        self.send_to(phase, p, 3, (c + 3) % 4, high, 1, 5)

    def third_step(self, phase, p):
        c = self.at[ORDERS[p][phase]]
        low, high = self.spans(p)
        self.copies[phase, p, 2].wait_recv()
        self.copies[phase, p, 5].wait_recv()
        self.added(phase, p, c, high, (0, 1))
        self.copies[phase, p, 3].wait_recv()
        self.copies[phase, p, 4].wait_recv()
        self.added(phase, p, c, low, (0, 1))

    def finish(self, phase):
        for p in range(3):
            self.third_step(phase, p)
            if phase > 0:
                self.first(phase - 1, p)

    def end(self):
        for copy in self.copies.values():
            copy.wait_send()


def scatter_shapes(rows, columns):
    return [
        pltpu.VMEM((4, 4, 4, rows, columns), jnp.bfloat16),
        [pltpu.VMEM((3,) + (4,) * phase + (rows, columns), jnp.bfloat16) for phase in range(3)],
        pltpu.SemaphoreType.DMA((3, 3, 6)),
        pltpu.SemaphoreType.DMA((3, 3, 6)),
    ]


def dot_nn(left, right):
    return jnp.dot(left, right, preferred_element_type=jnp.float32)


def dot_nt(left, right):
    return lax.dot_general(
        left, right, (((1,), (1,)), ((), ())), preferred_element_type=jnp.float32
    )


def dot_tn(left, right):
    return lax.dot_general(
        left, right, (((0,), (0,)), ((), ())), preferred_element_type=jnp.float32
    )


def low(value):
    return value.astype(jnp.bfloat16)


def split(value, count):
    parts = []
    for _ in range(count):
        parts.append(low(value))
        value = value - parts[-1].astype(jnp.float32)
    return parts


def dot_split(left, right, count, dot=dot_nn):
    return sum(dot(left, part) for part in split(right, count))


def split_dot(left, right, count):
    return sum(dot_nn(part, right) for part in split(left, count))


def dot_three(left, right, dot=dot_nn):
    high, less = split(left, 2)
    other_high, other_less = split(right, 2)
    return dot(high, other_high) + dot(less, other_high) + dot(high, other_less)


def head_spread(lanes, width, size):
    head = lax.broadcasted_iota(jnp.int32, (lanes, width), 0)
    column = lax.broadcasted_iota(jnp.int32, (lanes, width), 1)
    return low(jnp.where(head == column // size, 1.0, 0.0))


def head_gather(lanes, width, size):
    head = lax.broadcasted_iota(jnp.int32, (width, lanes), 1)
    column = lax.broadcasted_iota(jnp.int32, (width, lanes), 0)
    return low(jnp.where(head == column // size, 1.0, 0.0))


def triangle(rows, keep):
    first = lax.broadcasted_iota(jnp.int32, (rows, rows), 0)
    second = lax.broadcasted_iota(jnp.int32, (rows, rows), 1)
    return keep(first, second)


def silu_parts(value):
    sig = jax.nn.sigmoid(value)
    return value * sig, sig * (1.0 + value * (1.0 - sig))


def mixer_back_kernel(
    lefts,
    rights,
    home_ref,
    position_ref,
    add_ref,
    resid_ref,
    scale_ref,
    weights_ref,
    z_ref,
    gate_scale_ref,
    y_ref,
    x_ref,
    bc_ref,
    conv_ref,
    pre_ref,
    step_raw_ref,
    table_ref,
    start_ref,
    res_ref,
    mixer_out_ref,
    gate_up_ref,
    down_ref,
    grads_ref,
    taps_grad_ref,
    heads_grad_ref,
    results_ref,
    grad_resid_ref,
    norm_grad_ref,
    gain_grad_ref,
    weights,
    grad_mix,
    dy_ref,
    stat,
    stat_theirs,
    message,
    back,
    got,
    made,
    decayed,
    q,
    spread,
    cum_rows,
    scores,
    acc,
    ext,
    mine,
    theirs,
    shared_out,
    shared_scratch,
    mix_scratch,
    scan_sems,
    sems,
    home_sems,
    load_sem,
    pair_sems,
    stat_sems,
):
    me, at = coordinates()
    head = lax.axis_index("head")
    tokens, width = x_ref.shape
    model = resid_ref.shape[1]
    size = start_ref.shape[1]
    lanes = step_raw_ref.shape[1]
    each = width // 64
    mid = tokens // 2
    cut = 384
    numbers_ref, taps_ref = table_ref.at[8:16, 0:lanes], table_ref
    norm_ref, gain_ref = table_ref.at[5:6, 0:model], table_ref.at[6:7, 0:width]
    announce(me, True)
    added = pltpu.make_async_copy(add_ref, q, load_sem.at[1])
    added.start()
    load = pltpu.make_async_copy(weights_ref.at[:, pl.ds(0, width)], weights, load_sem.at[0])
    load.start()
    normed_second, grad_out = lefts
    normed_gate, shared_right = rights
    third = width // 3
    plan = [((n // 2, 0, n * third, n * third, third),) for n in range(3)]
    shared = Scatter(at, plan, lefts, [shared_right], shared_out, *shared_scratch)
    plan = [((0, 0, n * third, n * third, third),) for n in range(3)]
    mix = Scatter(at, plan, [grad_mix], [normed_gate], mixer_out_ref, *mix_scratch)
    scan = Scan(True, at, me, message, back, got, made, scan_sems)
    results = Spread(at, me, res_ref, results_ref, home_sems, *HOME[0], True)

    gate_cut = 256
    pair = PairSum(q, decayed, pair_sems, gate_cut)
    added.wait()
    ready(home_ref, position_ref)
    slots, step = home_ref.shape[1], 16

    @pl.loop(0, home_ref.shape[0] // step)
    def _(i):
        here = pl.ds(pl.multiple_of(i * step, step), step)
        chosen = low(chosen_slots(position_ref[here, :], slots))
        q[...] += dot_tn(chosen, home_ref[here].reshape(step * slots, model))

    await_all(True)
    for n in range(pair.count):
        pair.copy(n).start()
    for p in range(3):
        shared.product(p)
        shared.first(2, p)
    scale = scale_ref[:, 0:1]
    inner_sum = jnp.zeros((tokens, 1), jnp.float32)
    for n in range(pair.count):
        cols = slice(n * gate_cut, (n + 1) * gate_cut)
        pair.copy(n).wait()
        grad = q[:, cols] + decayed[:, cols]
        q[:, cols] = grad
        resid = resid_ref[:, cols]
        norm_grad_ref[:, cols] = jnp.sum(grad * resid * scale, axis=0, keepdims=True)
        inner_sum = inner_sum + jnp.sum(resid * norm_ref[:, cols] * grad, axis=1, keepdims=True)
    pull = scale * scale * scale * (inner_sum / model)
    for n in range(pair.count):
        cols = slice(n * gate_cut, (n + 1) * gate_cut)
        grad = scale * norm_ref[:, cols] * q[:, cols] - resid_ref[:, cols] * pull
        grad = grad_out[:, cols].astype(jnp.float32) + grad
        grad_resid_ref[:, cols] = grad
        grad_mix[:, cols] = low(grad)
    grad_resid_ref.flush()

    load.wait()
    gate_scale = gate_scale_ref[:, 0:1]
    dots = jnp.zeros((tokens, 1), jnp.float32)
    for c in range(0, width, cut):
        cols = slice(c, c + cut)
        grad = dot_nn(grad_mix[...], weights[:, cols])
        z = z_ref[:, cols]
        gated = y_ref[:, cols] * (z * jax.nn.sigmoid(z))
        gain_grad_ref[:, cols] = jnp.sum(grad * gated * gate_scale, axis=0, keepdims=True)
        weighted = grad * gain_ref[:, cols]
        dy_ref[:, cols] = weighted
        dots = dots + jnp.sum(weighted * gated, axis=1, keepdims=True)
    stat[...] = jnp.broadcast_to(dots, stat.shape)
    stat_swap = pltpu.make_async_remote_copy(
        src_ref=stat,
        dst_ref=stat_theirs,
        send_sem=stat_sems.at[0],
        recv_sem=stat_sems.at[1],
        device_id={"head": 1 - head},
    )
    stat_swap.start()
    for p in range(3):
        mix.product(p)
        mix.first(2, p)
    for p in range(3):
        shared.second(2, p)
    stat_swap.wait()
    dots = (stat[...] + stat_theirs[...])[:, 0:1]
    pull = gate_scale * gate_scale * gate_scale * (dots / (2 * width))
    for c in range(0, width, cut):
        cols = slice(c, c + cut)
        z, y = z_ref[:, cols], y_ref[:, cols]
        act, slope = silu_parts(z)
        grad = gate_scale * dy_ref[:, cols] - y * act * pull
        dy_ref[:, cols] = grad * act
        grads_ref[:, cols] = low(grad * y * slope)

    rate = numbers_ref[0:1, :]
    step_raw = step_raw_ref[...]
    step = jax.nn.softplus(step_raw)
    earlier = low(triangle(tokens, lambda t, s: jnp.where(t >= s, 1.0, 0.0)))
    cum = dot_split(earlier, -step * rate, 3)
    cum_rows[...] = cum.T
    tail = cum[tokens - 1 : tokens, :]
    rest_decay = jnp.exp(tail - cum)
    weight = rest_decay * step
    spreader = head_spread(lanes, width, 64)
    gatherer = head_gather(lanes, width, 64)
    spread[...] = split_dot(jnp.exp(cum), spreader, 2)
    held_full, read_full = bc_ref[:, :size], bc_ref[:, size:]
    held, read = low(held_full), low(read_full)

    for c in range(0, width, cut):
        part = dy_ref[:, c : c + cut] * spread[:, c : c + cut]
        decayed[:, c : c + cut] = part
        made_rows = dot_three(part, read_full, dot_tn)
        made_rows = made_rows.reshape(cut // each, each, size)
        message[c // each : (c + cut) // each] = scan_rows(made_rows, jnp.exp(tail))
    scan.begin()
    for p in range(3):
        mix.second(2, p)
    shared.finish(2)
    scan.middle()

    spread[...] = split_dot(step, spreader, 2)
    blocks = ((0, 0), (0, 1), (1, 1))
    for n, (s, t) in enumerate(blocks):
        scores[n] = dot_nt(held[s * mid : (s + 1) * mid], read[t * mid : (t + 1) * mid])
    acc[...] = jnp.zeros_like(acc)
    causal = triangle(mid, lambda s, t: s <= t)
    ready(x_ref)
    second_head = lax.broadcasted_iota(jnp.int32, (tokens, 128), 1) >= 64

    @pl.loop(0, width // 128)
    def _(i):
        here = pl.ds(pl.multiple_of(i * 128, 128), 128)
        dy, dy_less = split(dy_ref[:, here], 2)
        stepped = x_ref[:, here] * spread[:, here]
        results = []
        for which in range(2):
            row = cum_rows[pl.ds(2 * i + which, 1), :]
            column = jnp.broadcast_to(row, (128, tokens)).T
            mask = second_head if which else jnp.logical_not(second_head)
            values, values_less = split(jnp.where(mask, stepped, 0.0), 2)
            total = [None, None]
            for n, (s, t) in enumerate(blocks):
                gap = row[:, t * mid : (t + 1) * mid] - column[s * mid : (s + 1) * mid]
                decay = jnp.exp(gap)
                if s == t:
                    decay = jnp.where(causal, decay, 0.0)
                later = dy[t * mid : (t + 1) * mid]
                first, later_less = values[s * mid : (s + 1) * mid], dy_less[t * mid : (t + 1) * mid]
                pairs = dot_nt(first, later) + dot_nt(first, later_less)
                pairs = pairs + dot_nt(values_less[s * mid : (s + 1) * mid], later)
                acc[n] += decay * pairs
                part = dot_nn(low(decay * scores[n]), later)
                total[s] = part if total[s] is None else total[s] + part
            results.append(total)
        for s in range(2):
            rows = slice(s * mid, (s + 1) * mid)
            q[rows, here] = jnp.where(second_head[rows], results[1][s], results[0][s])

    for p in range(3):
        shared.second(1, p)
    shared.finish(1)
    mix.finish(2)
    results.start(HOME[0][0], HOME[0][0] + 1)
    scan.end()

    skip = split_dot(jnp.broadcast_to(numbers_ref[1:2, :], (8, lanes)), spreader, 2)[0:1, :]
    grad_weight = grad_step = rows_sum = jnp.zeros((tokens, lanes), jnp.float32)
    skip_grad = jnp.zeros((8, lanes), jnp.float32)
    state_dot = jnp.zeros((lanes, size), jnp.float32)
    held_parts = held_full[:mid], held_full[mid:]
    read_parts = read_full[:mid], read_full[mid:]
    grad_held = dot_three(acc[0], read_parts[0]) + dot_three(acc[1], read_parts[1])
    grad_held = jnp.concatenate([grad_held, dot_three(acc[2], read_parts[1])], axis=0)
    grad_read = dot_three(acc[1], held_parts[0], dot_tn) + dot_three(acc[2], held_parts[1], dot_tn)
    grad_read = jnp.concatenate([dot_three(acc[0], held_parts[0], dot_tn), grad_read], axis=0)
    for c in range(0, width, cut):
        here = slice(c, c + cut)
        x, dy, inner = x_ref[:, here], dy_ref[:, here], q[:, here]
        after = back[c // each : (c + cut) // each].reshape(cut, size)
        start = start_ref[here, :]
        gather = gatherer[here, :]
        weights = split_dot(weight, spreader[:, here], 2)
        through = dot_nt(held, low(after))
        grad_x = inner * spread[:, here] + skip[:, here] * dy + weights * through
        grad_step = grad_step + split_dot(x * inner, gather, 2)
        grad_weight = grad_weight + split_dot(x * through, gather, 2)
        rows_sum = rows_sum + split_dot(dy * (y_ref[:, here] - skip[:, here] * x), gather, 2)
        pairs = jnp.sum(dy * x, axis=0, keepdims=True)
        skip_grad = skip_grad + split_dot(jnp.broadcast_to(pairs, (8, cut)), gather, 2)
        state_dot = state_dot + dot_split(gather, after * start, 2, dot_tn)
        grad_held = grad_held + dot_three(weights * x, after)
        grad_read = grad_read + dot_three(decayed[:, here], start)
        ext[0:tokens, here] = grad_x * silu_parts(conv_ref[:, here])[1]
    mine[:, :size] = grad_held
    mine[:, size:] = grad_read
    swap = pltpu.make_async_remote_copy(
        src_ref=mine,
        dst_ref=theirs,
        send_sem=sems.at[0],
        recv_sem=sems.at[1],
        device_id={"head": 1 - head},
    )
    swap.start()
    for p in range(3):
        shared.second(0, p)
    for p in range(3):
        mix.second(1, p)
    results.start(HOME[0][0] + 1, HOME[0][0] + 2)

    ones = jnp.ones((8, size), jnp.bfloat16)
    state_grad = dot_split(ones, state_dot, 2, dot_nt)[0:1, :]
    used = grad_weight * weight
    tail_grad = jnp.sum(used, axis=0, keepdims=True) + jnp.exp(tail) * state_grad
    grad_cum = rows_sum - step * grad_step - used
    last = lax.broadcasted_iota(jnp.int32, (tokens, lanes), 0) == tokens - 1
    grad_cum = grad_cum + jnp.where(last, tail_grad, 0.0)
    later = low(triangle(tokens, lambda t, s: jnp.where(t <= s, 1.0, 0.0)))
    grad_log = dot_split(later, grad_cum, 3)
    grad_step = grad_step + grad_weight * rest_decay - rate * grad_log
    grad_raw = grad_step * jax.nn.sigmoid(step_raw)
    heads_grad_ref[...] = jnp.zeros_like(heads_grad_ref)
    heads_grad_ref[0:1, :] = skip_grad[0:1, :]
    heads_grad_ref[1:2, :] = -jnp.sum(step * grad_log, axis=0, keepdims=True)
    heads_grad_ref[2:3, :] = jnp.sum(grad_raw, axis=0, keepdims=True)

    channels = width + 2 * size
    grads_ref[:, width + channels : width + channels + lanes] = low(grad_raw)
    swap.wait()
    ext[0:tokens, width:channels] = (mine[...] + theirs[...]) * silu_parts(
        conv_ref[:, width:channels]
    )[1]
    edge = pltpu.make_async_remote_copy(
        src_ref=ext.at[pl.ds(0, 8)],
        dst_ref=ext.at[pl.ds(tokens, 8)],
        send_sem=sems.at[2],
        recv_sem=sems.at[3],
        device_id={"seq": (me + 63) % 64},
    )
    edge.start()
    shared.finish(0)
    mix.finish(1)
    results.start(HOME[0][0] + 2, HOME[0][1])
    edge.wait()
    there = jnp.where(me == 63, 0.0, 1.0)
    ext[tokens : tokens + 8, :] = ext[tokens : tokens + 8, :] * there
    taps_grad_ref[...] = jnp.zeros_like(taps_grad_ref)
    ready(pre_ref)

    @pl.loop(0, channels // 256)
    def _(i):
        here = pl.ds(pl.multiple_of(i * 256, 256), 256)
        grad = ext[0:tokens, here]
        total = jnp.zeros_like(grad)
        for j in range(4):
            total = total + taps_ref[j : j + 1, here] * ext[3 - j : 3 - j + tokens, here]
            products = grad * pre_ref[5 + j : 5 + j + tokens, here]
            taps_grad_ref[j : j + 1, here] = jnp.sum(products, axis=0, keepdims=True)
        grads_ref[:, pl.ds(pl.multiple_of(width + i * 256, 256), 256)] = low(total)

    for p in range(3):
        mix.second(0, p)
    mix.finish(0)
    hidden = down_ref.shape[1]
    for n in range(2):
        gate_up_ref[:, n, :] = shared_out[:, n * hidden : (n + 1) * hidden]
    down_ref[...] = shared_out[:, 2 * hidden :]
    shared.end()
    mix.end()
    results.wait()


def mixer_back(
    lefts,
    rights,
    home,
    position,
    add,
    resid,
    scale,
    weights,
    z,
    gate_scale,
    y,
    x,
    bc,
    conv,
    pre,
    step_raw,
    table,
    start,
    res,
    collective,
):
    tokens, model = resid.shape
    rows = model // 64
    width = x.shape[1]
    hidden = rights[1].shape[1] // 3
    size, lanes = start.shape[1], step_raw.shape[1]
    each, channels, mid = width // 64, width + 2 * size, tokens // 2
    f32, bf16 = jnp.float32, jnp.bfloat16
    vmem, hbm = pl.BlockSpec(memory_space=pltpu.VMEM), pl.BlockSpec(memory_space=pl.ANY)
    return call(
        mixer_back_kernel,
        out_shape=[
            jax.ShapeDtypeStruct((rows, width), f32),
            jax.ShapeDtypeStruct((rows, 2, hidden), f32),
            jax.ShapeDtypeStruct((rows, hidden), f32),
            jax.ShapeDtypeStruct((tokens, width + channels + lanes), bf16),
            jax.ShapeDtypeStruct((8, channels), f32),
            jax.ShapeDtypeStruct((8, lanes), f32),
            part_shape(HOME[0], res),
            jax.ShapeDtypeStruct((tokens, model), f32),
            jax.ShapeDtypeStruct((1, model), f32),
            jax.ShapeDtypeStruct((1, width), f32),
        ],
        in_specs=[[Lazy] * len(lefts), [Lazy] * len(rights)]
        + [Lazy, Lazy, hbm, Lazy, Lazy, hbm]
        + [Lazy] * 4
        + [vmem, Lazy, Lazy, vmem, vmem, Lazy, hbm],
        out_specs=[vmem] * 6 + [hbm, Eager, vmem, vmem],
        scratch_shapes=[
            pltpu.VMEM((model, width), bf16),
            pltpu.VMEM((tokens, model), bf16),
            pltpu.VMEM((tokens, width), f32),
            pltpu.VMEM((tokens, 128), f32),
            pltpu.VMEM((tokens, 128), f32),
            pltpu.VMEM((64, each + 8, size), bf16),
            pltpu.VMEM((64, each, size), f32),
            pltpu.VMEM((64, each + 8, size), bf16),
            pltpu.VMEM((64, each, size), f32),
            pltpu.VMEM((tokens, width), f32),
            pltpu.VMEM((tokens, width), f32),
            pltpu.VMEM((tokens, width), f32),
            pltpu.VMEM((lanes, tokens), f32),
            pltpu.VMEM((3, mid, mid), f32),
            pltpu.VMEM((3, mid, mid), f32),
            pltpu.VMEM((tokens + 8, channels), f32),
            pltpu.VMEM((tokens, 2 * size), f32),
            pltpu.VMEM((tokens, 2 * size), f32),
            pltpu.VMEM((rows, 3 * hidden), f32),
            scatter_shapes(rows, 3 * hidden),
            scatter_shapes(rows, width),
            pltpu.SemaphoreType.DMA((4,)),
            pltpu.SemaphoreType.DMA((4,)),
            pltpu.SemaphoreType.DMA((9,)),
            pltpu.SemaphoreType.DMA((2,)),
            pltpu.SemaphoreType.DMA((2, model // 256)),
            pltpu.SemaphoreType.DMA((2,)),
        ],
        compiler_params=params(collective, vmem_limit_bytes=VMEM),
        name="mixer_back",
    )(
        lefts, rights, home, position, add, resid, scale, weights, z, gate_scale, y, x, bc, conv,
        pre, step_raw, table, start, res,
    )


def input_back_kernel(
    plan,
    left,
    right,
    weights_ref,
    resid_ref,
    table_ref,
    grad_ref,
    res_ref,
    near_refs,
    position_ref,
    weight_ref,
    shared_ref,
    block_ref,
    taps_ref,
    heads_ref,
    norm_ref,
    gate_gain_ref,
    mixer_in_ref,
    state_ref,
    step_ref,
    input_ref,
    layer_ref,
    norm_first_out,
    norm_second_out,
    gate_gain_out,
    conv_main_out,
    conv_state_out,
    heads_outs,
    weights,
    mine,
    theirs,
    theirs_mix,
    home,
    named,
    weighed,
    small,
    small_got,
    small_out,
    out_ref,
    buf,
    rest,
    send,
    recv,
    small_sems,
    sems,
    home_sems,
    mix_sems,
):
    me, at = coordinates()
    head = lax.axis_index("head")
    tokens, model = resid_ref.shape
    columns = right.shape[1]
    gain_ref = table_ref.at[4:5, 0:model]
    load = pltpu.make_async_copy(weights_ref, weights, sems.at[0])
    load.start()
    announce(me, True)
    sums = Scatter(at, plan, [left], [right], out_ref, buf, rest, send, recv)
    totals = Small(at, me, small, small_out, small_got, small_sems)
    results = Spread(at, me, res_ref, home, home_sems, *HOME[1], True)
    for p in range(3):
        sums.product(p)
        if p == 0:
            await_all(True)
            results.start(HOME[1][0], HOME[1][0] + 1)
        sums.first(2, p)
    load.wait()

    start = columns - 384
    other = pl.multiple_of(start + 128 * (1 - head), 128)
    cut = 256
    swaps = []
    for c in range(0, model, cut):
        rows = slice(c, c + cut)
        total = dot_nt(right[...], weights[rows, :])
        total = total - dot_nt(right[:, pl.ds(other, 128)], weights[rows, pl.ds(other, 128)])
        mine[:, rows] = total
        swap = pltpu.make_async_remote_copy(
            src_ref=mine.at[:, pl.ds(c, cut)],
            dst_ref=theirs.at[:, pl.ds(c, cut)],
            send_sem=sems.at[1 + c // cut],
            recv_sem=sems.at[1 + (model + c) // cut],
            device_id={"head": 1 - head},
        )
        swap.start()
        swaps.append(swap)
    for p in range(3):
        sums.second(2, p)
    square = jnp.zeros((tokens, 1), jnp.float32)
    inner = jnp.zeros((tokens, 1), jnp.float32)
    for n, c in enumerate(range(0, model, cut)):
        rows = slice(c, c + cut)
        swaps[n].wait()
        grad = mine[:, rows] + theirs[:, rows]
        mine[:, rows] = grad
        resid = resid_ref[:, rows].astype(jnp.float32)
        square = square + jnp.sum(resid * resid, axis=1, keepdims=True)
        inner = inner + jnp.sum(resid * gain_ref[:, rows] * grad, axis=1, keepdims=True)
    scale = lax.rsqrt(square / model + EPSILON)
    pull = scale * scale * scale * (inner / model)
    tiles, inner_tiles = model // 128, gate_gain_ref.shape[1] // 128
    channel_tiles = taps_ref.shape[1] // 128
    small[...] = jnp.zeros_like(small)

    def put_small(row, value):
        small[row // 8, row % 8 : row % 8 + 1, :] = value

    for tile in range(tiles):
        put_small(tiles + tile, norm_ref[:, tile * 128 : (tile + 1) * 128])
    for tile in range(inner_tiles):
        put_small(2 * tiles + tile, gate_gain_ref[:, tile * 128 : (tile + 1) * 128])
    taps_row = 2 * tiles + inner_tiles
    for tap in range(4):
        for tile in range(channel_tiles):
            row = taps_row + tap * channel_tiles + tile
            put_small(row, taps_ref[tap : tap + 1, tile * 128 : (tile + 1) * 128])
    heads_row = taps_row + 4 * channel_tiles
    for n in range(3):
        put_small(heads_row + n, heads_ref[n : n + 1, :])
    for c in range(0, model, cut):
        rows = slice(c, c + cut)
        grad = mine[:, rows]
        resid = resid_ref[:, rows].astype(jnp.float32)
        input_ref[:, rows] = grad_ref[:, rows] + scale * gain_ref[:, rows] * grad - resid * pull
        gain_grad = jnp.sum(grad * resid * scale, axis=0, keepdims=True)
        for tile in range(c // 128, (c + cut) // 128):
            at_tile = tile * 128 - c
            put_small(tile, gain_grad[:, at_tile : at_tile + 128])
    totals.begin()
    results.start(HOME[1][0] + 1, HOME[1][0] + 2)
    input_ref.flush()
    sums.finish(2)
    totals.middle()
    results.start(HOME[1][0] + 2, HOME[1][0] + 3)
    mine[...] = shared_ref[...]
    slots = home.shape[1]

    def mix(span, rows_ref):
        @pl.loop(*span)
        def _(g):
            for n, (_, expert) in enumerate(Ways(at).group(g)):
                named[n : n + 1, :] = position_ref[pl.ds(expert, 1), :]
                weighed[n : n + 1, :] = weight_ref[pl.ds(expert, 1), :]
            chosen = chosen_slots(named[...], slots)
            weighted = chosen.reshape(8, slots, -1) * weighed[...][:, None, :]
            high, less = split(weighted.reshape(chosen.shape), 2)
            here = pl.ds(pl.multiple_of((g - span[0]) * 8, 8), 8)
            rows = rows_ref[here].reshape(8 * slots, model)
            mine[...] += dot_tn(high, rows) + dot_tn(less, rows)

    ready(position_ref, weight_ref, *near_refs)
    for span, near_ref in zip(HOME, near_refs):
        mix(span, near_ref)
    for p in range(3):
        sums.second(1, p)
    results.start(HOME[1][0] + 3, HOME[1][0] + 4)
    results.arrived(HOME[1][0], HOME[1][0] + 2)
    mix((HOME[1][0], HOME[1][0] + 2), home)
    sums.finish(1)
    results.start(HOME[1][0] + 4, HOME[1][1])
    for p in range(3):
        sums.second(0, p)
    results.arrived(HOME[1][0] + 2, HOME[1][1])
    mix((HOME[1][0] + 2, HOME[1][1]), home.at[pl.ds(16, home.shape[0] - 16)])
    pair = PairSum(mine, theirs_mix, mix_sems, cut)
    for n in range(pair.count):
        pair.copy(n).start()
    sums.finish(0)
    for n in range(pair.count):
        cols = slice(n * cut, (n + 1) * cut)
        pair.copy(n).wait()
        layer_ref[:, cols] = low(block_ref[:, cols] + (mine[:, cols] + theirs_mix[:, cols]))
    totals.end()

    def get_small(row):
        return small_out[row // 8, row % 8 : row % 8 + 1, :]

    for tile in range(tiles):
        norm_first_out[tile : tile + 1, :] = get_small(tile)
        norm_second_out[tile : tile + 1, :] = get_small(tiles + tile)
    for tile in range(inner_tiles):
        gate_gain_out[tile : tile + 1, :] = get_small(2 * tiles + tile)
    for tap in range(4):
        for tile in range(channel_tiles):
            value = get_small(taps_row + tap * channel_tiles + tile)
            if tile < inner_tiles:
                conv_main_out[tap : tap + 1, tile * 128 : (tile + 1) * 128] = value
            else:
                start = (tile - inner_tiles) * 128
                conv_state_out[tap : tap + 1, start : start + 128] = value
    for n, heads_out in enumerate(heads_outs):
        heads_out[...] = get_small(heads_row + n)[:, : heads_out.shape[1]]
    results.sent()
    inner = mixer_in_ref.shape[2]
    for n in range(2):
        mixer_in_ref[:, n, :] = out_ref[:, n * inner : (n + 1) * inner]
    wide = 2 * inner + state_ref.shape[1]
    state_ref[...] = out_ref[:, 2 * inner : wide]
    step_ref[...] = out_ref[:, wide : wide + 128][:, : step_ref.shape[1]]
    sums.end()


def input_back(
    left,
    right,
    plan,
    weights,
    resid,
    table,
    grad,
    res,
    near,
    position,
    weight,
    shared,
    block,
    taps,
    heads,
    norm,
    gate_gain,
    heads_dev,
    collective,
):
    tokens, model = resid.shape
    columns = right.shape[1]
    rows = model // 64
    inner, channels = gate_gain.shape[1], taps.shape[1]
    f32 = jnp.float32
    vmem, hbm = pl.BlockSpec(memory_space=pltpu.VMEM), pl.BlockSpec(memory_space=pl.ANY)
    return call(
        functools.partial(input_back_kernel, plan),
        out_shape=[
            jax.ShapeDtypeStruct((rows, 2, inner), f32),
            jax.ShapeDtypeStruct((rows, channels - inner), f32),
            jax.ShapeDtypeStruct((rows, heads_dev), f32),
            jax.ShapeDtypeStruct((tokens, model), f32),
            jax.ShapeDtypeStruct((tokens, model), jnp.bfloat16),
            jax.ShapeDtypeStruct((model // 128, 128), f32),
            jax.ShapeDtypeStruct((model // 128, 128), f32),
            jax.ShapeDtypeStruct((inner // 128, 128), f32),
            jax.ShapeDtypeStruct((4, inner), f32),
            jax.ShapeDtypeStruct((4, channels - inner), f32),
            [jax.ShapeDtypeStruct((1, heads_dev), f32)] * 3,
        ],
        in_specs=[vmem, vmem, hbm, Lazy, vmem, Lazy] + [hbm, [Lazy] * len(near)] + [Lazy] * 8,
        out_specs=[vmem] * 3 + [Eager] * 2 + [vmem] * 5 + [[vmem] * 3],
        scratch_shapes=[
            pltpu.VMEM(weights.shape, weights.dtype),
            pltpu.VMEM((tokens, model), f32),
            pltpu.VMEM((tokens, model), f32),
            pltpu.VMEM((tokens, model), f32),
            pltpu.VMEM(part_shape(HOME[1], res).shape, res.dtype),
            pltpu.VMEM((8, tokens), f32),
            pltpu.VMEM((8, tokens), f32),
            pltpu.VMEM((64, 8, 128), f32),
            pltpu.VMEM((64, 8, 128), f32),
            pltpu.VMEM((64, 8, 128), f32),
            pltpu.VMEM((rows, columns), f32),
        ]
        + scatter_shapes(rows, columns)
        + [pltpu.SemaphoreType.DMA((4,)), pltpu.SemaphoreType.DMA((1 + 2 * model // 256,))]
        + [pltpu.SemaphoreType.DMA((9,)), pltpu.SemaphoreType.DMA((2, model // 256))],
        compiler_params=params(collective, vmem_limit_bytes=VMEM),
        name="input_back",
    )(
        left, right, weights, resid, table, grad, res, near, position, weight, shared, block,
        taps, heads, norm, gate_gain,
    )


class Gather:
    def __init__(self, at, x_ref, out_ref, send, recv, local_sem):
        self.at, self.x_ref, self.out_ref, self.send, self.recv = at, x_ref, out_ref, send, recv
        self.third, self.half = parts_of(out_ref.shape[4])
        if x_ref is not None:
            self.own = pltpu.make_async_copy(x_ref, out_ref.at[at[0], at[1], at[2]], local_sem)
        self.copies = {}

    def put(self, source, here, phase, p, kind, by):
        copy = pltpu.make_async_remote_copy(
            src_ref=source,
            dst_ref=self.out_ref.at[here],
            send_sem=self.send.at[phase, p, kind],
            recv_sem=self.recv.at[phase, p, kind],
            device_id={"seq": seq_of(moved(self.at, ORDERS[p][phase], by))},
        )
        copy.start()
        self.copies[phase, p, kind] = copy

    def first(self, phase):
        if phase == 1:
            self.own.wait()
        if phase == 0:
            self.own.start()
        elif (phase - 1, 0, 2) in self.copies:
            self.arrived(phase - 1)
        for p, order in enumerate(ORDERS):
            cols = pl.ds(p * self.third, self.third)
            here = region(self.at, order, phase, self.at[order[phase]], cols)
            source = self.x_ref.at[:, cols] if phase == 0 else self.out_ref.at[here]
            for kind, by in enumerate((1, 3)):
                self.put(source, here, phase, p, kind, by)

    def second(self, phase):
        for p, order in enumerate(ORDERS):
            for kind, by in enumerate((1, 3)):
                start, length = p * self.third, self.half
                if kind:
                    start, length = start + self.half, self.third - self.half
                there = region(
                    self.at, order, phase, (self.at[order[phase]] - by) % 4, pl.ds(start, length)
                )
                self.copies[phase, p, kind].wait_recv()
                self.put(self.out_ref.at[there], there, phase, p, 2 + kind, by)

    def arrived(self, phase):
        for p in range(3):
            for kind in (2, 3):
                self.copies[phase, p, kind].wait_recv()

    def end(self):
        for copy in self.copies.values():
            copy.wait_send()


def gather_shapes():
    return [
        pltpu.SemaphoreType.DMA((3, 3, 4)),
        pltpu.SemaphoreType.DMA((3, 3, 4)),
        pltpu.SemaphoreType.DMA,
    ]


def slot_tables(routes_ref, weights_ref, position_ref, weight_ref):
    experts, tokens = position_ref.shape
    expert = lax.broadcasted_iota(jnp.int32, (experts, tokens), 0)
    named = jnp.zeros((experts, tokens), jnp.float32)
    weight = jnp.zeros((experts, tokens), jnp.float32)
    for k in range(routes_ref.shape[0]):
        hit = expert == routes_ref[k : k + 1, :]
        named = named + jnp.where(hit, 1.0, 0.0)
        weight = weight + jnp.where(hit, weights_ref[k : k + 1, :], 0.0)
    earlier = low(triangle(tokens, lambda t, s: jnp.where(t < s, 1.0, 0.0)))
    position_ref[...] = jnp.where(named > 0.0, dot_nn(low(named), earlier), -1.0)
    weight_ref[...] = weight


def chosen_slots(position, slots):
    count, tokens = position.shape
    number = lax.broadcasted_iota(jnp.int32, (count, slots, tokens), 1)
    number = (number + slots * lax.axis_index("head")).astype(jnp.float32)
    return jnp.where(position[:, None, :] == number, 1.0, 0.0).reshape(count * slots, tokens)


def gather_kernel(
    x_ref,
    late_ref,
    layer_ref,
    routes_ref,
    weights_ref,
    grads_ref,
    vectors,
    out_ref,
    late_out,
    before_ref,
    position_ref,
    weight_ref,
    rows,
    slots_ref,
    table_ref,
    send,
    recv,
    local_sem,
    late_send,
    late_recv,
    late_sem,
    sems,
    out_sems,
):
    me, at = coordinates()
    announce(me, False)
    gather = Gather(at, x_ref, out_ref, send, recv, local_sem)
    late = Gather(at, late_ref, late_out, late_send, late_recv, late_sem)
    conv_main, conv_state, gains, numbers = vectors
    width, heads = conv_main.shape[1], numbers[0].shape[1]
    table_ref[...] = jnp.zeros_like(table_ref)
    table_ref[0:4, 0:width] = conv_main[...]
    table_ref[0:4, width:] = conv_state[...]
    for n, gain in enumerate(gains):
        for tile in range(gain.shape[0]):
            table_ref[4 + n : 5 + n, tile * 128 : (tile + 1) * 128] = gain[tile : tile + 1, :]
    for n, number in enumerate(numbers):
        table_ref[8 + n : 9 + n, 0:heads] = number[...]
    slot_tables(routes_ref, weights_ref, position_ref, weight_ref)
    grads = grads_ref[...]
    slots, step = rows.shape[1], 16

    @pl.loop(0, rows.shape[0] // step)
    def _(i):
        here = pl.ds(pl.multiple_of(i * step, step), step)
        chosen = chosen_slots(position_ref[here, :], slots)
        weighted = chosen.reshape(step, slots, -1) * weight_ref[here, :][:, None, :]
        scale = jnp.sum(weighted.reshape(chosen.shape), axis=1, keepdims=True)
        rows[here] = low(dot_nn(low(chosen), grads) * scale).reshape(step, slots, -1)

    await_all(False)
    gather.first(0)
    late.first(0)
    edge = pltpu.make_async_remote_copy(
        src_ref=layer_ref.at[pl.ds(layer_ref.shape[0] - 16, 16)],
        dst_ref=before_ref,
        send_sem=sems.at[0],
        recv_sem=sems.at[1],
        device_id={"seq": (me + 1) % 64},
    )
    edge.start()
    out = Spread(at, me, rows, slots_ref, out_sems, *OUT[0], False)
    gather.second(0)
    late.second(0)
    out.start(0, 1)
    gather.first(1)
    late.first(1)
    out.start(1, 2)
    gather.second(1)
    late.second(1)
    out.start(2, 3)
    gather.first(2)
    gather.second(2)
    out.start(3, OUT[0][1])
    late.arrived(1)
    late.end()
    gather.arrived(2)
    edge.wait()
    gather.end()
    out.wait()


def gather_rows(x, late, layer_in, routes, route_weights, grads, vectors, experts, slots, collective):
    rows, columns = x.shape
    channels = vectors[0].shape[1] + vectors[1].shape[1]
    tokens, model = grads.shape
    grad_rows = jax.ShapeDtypeStruct((experts, slots, model), grads.dtype)
    hbm, vmem = pl.BlockSpec(memory_space=pl.ANY), pl.BlockSpec(memory_space=pltpu.VMEM)
    return call(
        gather_kernel,
        out_shape=[
            jax.ShapeDtypeStruct((4, 4, 4, rows, columns), x.dtype),
            jax.ShapeDtypeStruct((4, 4, 4) + late.shape, late.dtype),
            jax.ShapeDtypeStruct((16, model), layer_in.dtype),
            jax.ShapeDtypeStruct((experts, tokens), jnp.float32),
            jax.ShapeDtypeStruct((experts, tokens), jnp.float32),
            grad_rows,
            part_shape(OUT[0], grad_rows),
            jax.ShapeDtypeStruct((16, channels), jnp.float32),
        ],
        in_specs=[hbm, hbm, hbm, vmem, vmem, Lazy, [vmem, vmem, [vmem] * 3, [vmem] * 3]],
        out_specs=[hbm, hbm, hbm, vmem, vmem, vmem, hbm, vmem],
        scratch_shapes=gather_shapes() + gather_shapes() + [pltpu.SemaphoreType.DMA((2,))]
        + [pltpu.SemaphoreType.DMA((9,))],
        compiler_params=params(collective, vmem_limit_bytes=VMEM),
        name="gather_rows",
    )(x, late, layer_in, routes.T, route_weights.T, grads, vectors)


def mixer_kernel(
    layer_ref,
    edge_ref,
    table_ref,
    weights_ref,
    _,
    rows_ref,
    normed_ref,
    z_ref,
    x_ref,
    bc_ref,
    conv_ref,
    pre_ref,
    step_raw_ref,
    start_ref,
    y_ref,
    gated_ref,
    scale_ref,
    gathered_ref,
    slots_ref,
    weights,
    normed,
    message,
    got,
    made,
    spread,
    cum_rows,
    scores,
    mine,
    theirs,
    load_sems,
    scan_sems,
    pair_sems,
    send,
    recv,
    slot_sems,
):
    me, at = coordinates()
    head = lax.axis_index("head")
    tokens, model = layer_ref.shape
    width = x_ref.shape[1]
    size = bc_ref.shape[1] // 2
    lanes = step_raw_ref.shape[1]
    each = width // 64
    mid = tokens // 2
    cut = 384
    norm_ref, gain_ref = table_ref.at[4:5, 0:model], table_ref.at[6:7, 0:width]
    numbers_ref, taps_ref = table_ref.at[8:16, 0:lanes], table_ref

    def load(n):
        cols = pl.ds(pl.multiple_of(n * cut, 128), cut)
        return pltpu.make_async_copy(weights_ref.at[:, cols], weights.at[:, cols], load_sems.at[n])

    for n in (8, 4, 5, 6, 7, 0, 1, 2, 3):
        load(n).start()
    announce(me, True)
    gather = Gather(at, None, gathered_ref, send, recv, None)

    def norm(rows):
        rows = rows.astype(jnp.float32)
        scale = lax.rsqrt(jnp.mean(rows * rows, axis=1, keepdims=True) + EPSILON)
        return low(rows * scale * norm_ref[...])

    before = norm(edge_ref[...]).astype(jnp.float32) * jnp.where(me == 0, 0.0, 1.0)
    normed[0:16, :] = low(before)
    normed[16 : 16 + tokens, :] = norm(layer_ref[...])
    normed_ref[...] = normed[16 : 16 + tokens, :]
    normed_ref.flush()
    await_all(True)
    gather.first(2)

    def conv(cols):
        total = jnp.zeros((tokens, cols.size), jnp.float32)
        for j in range(4):
            total = total + taps_ref[j : j + 1, cols] * pre_ref[5 + j : 5 + j + tokens, cols]
        conv_ref[:, cols] = total
        return total * jax.nn.sigmoid(total)

    load(8).wait()
    last = dot_nn(normed[...], weights[:, 8 * cut : 9 * cut])
    cols = pl.ds(width, 2 * size)
    pre_ref[:, cols] = last[8:, : 2 * size]
    bc_ref[...] = conv(cols)
    bc_ref.flush()
    step_raw = last[16:, 2 * size :] + numbers_ref[2:3, :]
    step_raw_ref[...] = step_raw
    step = jax.nn.softplus(step_raw)
    earlier = low(triangle(tokens, lambda t, s: jnp.where(t >= s, 1.0, 0.0)))
    cum = dot_split(earlier, -step * numbers_ref[0:1, :], 3)
    cum_rows[...] = cum.T
    tail = cum[tokens - 1 : tokens, :]
    spreader = head_spread(lanes, width, 64)
    spread[...] = split_dot(jnp.exp(tail - cum) * step, spreader, 2)
    held, read = bc_ref[:, :size], bc_ref[:, size:]

    @pl.loop(0, 4)
    def _(i):
        load(4 + i).wait()
        from_cols = pl.ds(pl.multiple_of((4 + i) * cut, 128), cut)
        here = pl.ds(pl.multiple_of(i * cut, 128), cut)
        pre_ref[:, here] = dot_nn(normed[...], weights[:, from_cols])[8:]
        x = conv(here)
        x_ref[:, here] = x
        made_rows = dot_three(x * spread[:, here], held, dot_tn)
        made_rows = made_rows.reshape(cut // each, each, size)
        message[pl.ds(i * (cut // each), cut // each)] = scan_rows(made_rows, jnp.exp(tail))

    for ref in (x_ref, pre_ref, conv_ref):
        ref.flush()
    scan = Scan(False, at, me, message, start_ref, got, made, scan_sems)
    scan.begin()

    @pl.loop(0, 4)
    def _(i):
        load(i).wait()
        here = pl.ds(pl.multiple_of(i * cut, 128), cut)
        z_ref[:, here] = dot_nn(normed[16 : 16 + tokens, :], weights[:, here])

    z_ref.flush()
    scan.middle()
    out = Spread(at, me, rows_ref, slots_ref, slot_sems, *OUT[1], False)
    gather.second(2)
    out.start()

    spread[...] = split_dot(step, spreader, 2)
    blocks = ((0, 0), (1, 0), (1, 1))
    for n, (t, s) in enumerate(blocks):
        rows, columns = slice(t * mid, (t + 1) * mid), slice(s * mid, (s + 1) * mid)
        scores[n] = dot_three(read[rows], held[columns], dot_nt)
    causal = triangle(mid, lambda t, s: t >= s)
    second_head = lax.broadcasted_iota(jnp.int32, (tokens, 128), 1) >= 64

    @pl.loop(0, width // 128)
    def _(i):
        here = pl.ds(pl.multiple_of(i * 128, 128), 128)
        values, values_less = split(x_ref[:, here] * spread[:, here], 2)
        results = []
        for which in range(2):
            row = cum_rows[pl.ds(2 * i + which, 1), :]
            column = jnp.broadcast_to(row, (128, tokens)).T
            total = [None, None]
            for n, (t, s) in enumerate(blocks):
                columns = slice(s * mid, (s + 1) * mid)
                decay = jnp.exp(column[t * mid : (t + 1) * mid] - row[:, columns])
                if s == t:
                    decay = jnp.where(causal, decay, 0.0)
                mixing, mixing_less = split(decay * scores[n], 2)
                part = dot_nn(mixing, values[columns]) + dot_nn(mixing_less, values[columns])
                part = part + dot_nn(mixing, values_less[columns])
                total[t] = part if total[t] is None else total[t] + part
            results.append(total)
        for t in range(2):
            rows = slice(t * mid, (t + 1) * mid)
            y_ref[rows, here] = jnp.where(second_head[rows], results[1][t], results[0][t])

    scan.end()
    skip = split_dot(jnp.broadcast_to(numbers_ref[1:2, :], (8, lanes)), spreader, 2)[0:1, :]
    carry = split_dot(jnp.exp(cum), spreader, 2)
    square = jnp.zeros((tokens, 1), jnp.float32)
    for c in range(0, width, cut):
        here = slice(c, c + cut)
        start = start_ref[c // each : (c + cut) // each].reshape(cut, size)
        through = dot_three(read, start, dot_nt)
        y = y_ref[:, here] + carry[:, here] * through + skip[:, here] * x_ref[:, here]
        y_ref[:, here] = y
        z = z_ref[:, here]
        gated = y * (z * jax.nn.sigmoid(z))
        spread[:, here] = gated
        square = square + jnp.sum(gated * gated, axis=1, keepdims=True)
    y_ref.flush()
    mine[...] = jnp.broadcast_to(square, mine.shape)
    swap = pltpu.make_async_remote_copy(
        src_ref=mine,
        dst_ref=theirs,
        send_sem=pair_sems.at[0],
        recv_sem=pair_sems.at[1],
        device_id={"head": 1 - head},
    )
    swap.start()
    swap.wait()
    scale = lax.rsqrt((mine[...] + theirs[...]) / (2 * width) + EPSILON)
    scale_ref[...] = scale
    for c in range(0, width, cut):
        here = slice(c, c + cut)
        gated_ref[:, here] = low(spread[:, here] * scale[:, 0:1] * gain_ref[:, here])
    gather.arrived(2)
    gather.end()
    out.wait()


def mixer(layer_in, edge, table, weights, width, late, grad_rows, collective):
    tokens, model = layer_in.shape
    channels, lanes = table.shape[1], 128
    size = (channels - width) // 2
    each, mid = width // 64, tokens // 2
    f32, bf16 = jnp.float32, jnp.bfloat16
    vmem, hbm = pl.BlockSpec(memory_space=pltpu.VMEM), pl.BlockSpec(memory_space=pl.ANY)
    out = [
        ((tokens, model), bf16),
        ((tokens, width), f32),
        ((tokens, width), f32),
        ((tokens, 2 * size), f32),
        ((tokens, channels), f32),
        ((tokens + 8, channels), f32),
        ((tokens, lanes), f32),
        ((64, each, size), f32),
        ((tokens, width), f32),
        ((tokens, width), bf16),
        ((tokens, lanes), f32),
        (late.shape, bf16),
        (part_shape(OUT[1], grad_rows).shape, bf16),
    ]
    return call(
        mixer_kernel,
        out_shape=[jax.ShapeDtypeStruct(*shape) for shape in out],
        in_specs=[vmem, vmem, vmem, hbm, hbm, hbm],
        out_specs=[Eager] * 6 + [vmem] * 2 + [Eager] * 2 + [vmem] + [hbm] * 2,
        scratch_shapes=[
            pltpu.VMEM(weights.shape, bf16),
            pltpu.VMEM((tokens + 16, model), bf16),
            pltpu.VMEM((64, each + 8, size), bf16),
            pltpu.VMEM((64, each + 8, size), bf16),
            pltpu.VMEM((64, each, size), f32),
            pltpu.VMEM((tokens, width), f32),
            pltpu.VMEM((lanes, tokens), f32),
            pltpu.VMEM((3, mid, mid), f32),
            pltpu.VMEM((tokens, lanes), f32),
            pltpu.VMEM((tokens, lanes), f32),
            pltpu.SemaphoreType.DMA((9,)),
            pltpu.SemaphoreType.DMA((4,)),
            pltpu.SemaphoreType.DMA((2,)),
        ]
        + gather_shapes()[:2]
        + [pltpu.SemaphoreType.DMA((9,))],
        input_output_aliases={4: len(out) - 2},
        compiler_params=params(collective, vmem_limit_bytes=VMEM),
        name="mixer",
    )(layer_in, edge, table, weights, late, grad_rows)


def per_device(
    layer_in,
    norm_first,
    mixer_in,
    state_proj,
    step_proj,
    step_bias,
    conv_main,
    conv_state,
    decay_rate,
    skip_gain,
    gate_gain,
    mixer_out,
    norm_second,
    shared_gate_up,
    shared_down,
    expert_gate_up,
    expert_down,
    routes,
    route_weights,
    grad_out,
):
    tokens, model_width = layer_in.shape
    inner_dev = mixer_in.shape[2]
    state_size = state_proj.shape[1] // 2
    heads_dev = step_proj.shape[1]
    conv_taps = conv_main.shape[0]
    shared_dev = shared_down.shape[1]
    local_experts = expert_gate_up.shape[0]
    experts_all = local_experts * lax.axis_size("seq")
    choices_per = routes.shape[1]
    capacity = max(2, tokens * choices_per * 4 // (3 * experts_all))
    slots_dev = capacity // lax.axis_size("head")
    lanes = 128
    pad_heads = lambda v: jnp.pad(v, ((0, 0), (0, lanes - heads_dev)))
    late_rows = jnp.concatenate(
        [mixer_out, shared_gate_up.reshape(-1, 2 * shared_dev), shared_down], axis=1
    )
    vectors = [
        conv_main,
        conv_state,
        [gain.reshape(-1, 128) for gain in (norm_first, norm_second, gate_gain)],
        [number[None] for number in (decay_rate, skip_gain, step_bias)],
    ]
    gathered, late_rows, edge, position, slot_weight, grads_out, grads_first, table = gather_rows(
        jnp.concatenate(
            [mixer_in.reshape(-1, 2 * inner_dev), state_proj, pad_heads(step_proj)], axis=1
        ),
        late_rows,
        layer_in,
        routes,
        route_weights,
        grad_out,
        vectors,
        experts_all,
        slots_dev,
        0,
    )
    weights_in = gathered.reshape(model_width, -1)
    (
        normed,
        gate_z,
        heads_x,
        state_both,
        conv_sum,
        pre,
        step_raw,
        state_start,
        ssd,
        normed_gate,
        gate_scale,
        gathered,
        grads_second,
    ) = mixer(
        layer_in,
        edge,
        table,
        weights_in,
        inner_dev,
        late_rows,
        grads_out,
        1,
    )
    weights_late = gathered.reshape(model_width, -1)
    (
        grad_home,
        res_sums,
        expert_gate_up_grad,
        expert_down_grad,
        shared_part,
        shared_back,
        shared_right,
        residual,
        normed_second,
        scale_second,
    ) = experts(
        normed_gate,
        weights_late,
        layer_in,
        table,
        position,
        [grads_first, grads_second],
        expert_gate_up.reshape(model_width, -1),
        expert_down.reshape(-1, model_width),
        grad_out,
        slots_dev,
        2,
    )
    (
        mixer_out_grad,
        shared_gate_up_grad,
        shared_down_grad,
        right_grads,
        taps_grad,
        heads_grad,
        home_near,
        grad_resid,
        norm_second_grad,
        gate_gain_grad,
    ) = mixer_back(
        [normed_second, grad_out],
        [normed_gate, shared_right],
        grad_home,
        position,
        shared_back,
        residual,
        scale_second,
        weights_late,
        gate_z,
        gate_scale,
        ssd,
        heads_x,
        state_both,
        conv_sum,
        pre,
        step_raw,
        table,
        state_start.reshape(inner_dev, state_size),
        res_sums,
        3,
    )
    (
        mixer_in_grad,
        state_proj_grad,
        step_proj_grad,
        input_grad,
        layer_out,
        norm_first_sum,
        norm_second_sum,
        gate_gain_sum,
        conv_main_grad,
        conv_state_grad,
        (skip_gain_grad, decay_rate_grad, step_bias_grad),
    ) = input_back(
        normed,
        right_grads,
        tuple(((0, 0, start, start, 1152),) for start in (0, 1152, 2304)),
        weights_in,
        layer_in,
        table,
        grad_resid,
        res_sums,
        [home_near],
        position,
        slot_weight,
        shared_part,
        residual,
        taps_grad,
        heads_grad,
        norm_second_grad,
        gate_gain_grad,
        heads_dev,
        4,
    )
    (
        mixer_in_grad,
        state_proj_grad,
        step_proj_grad,
        norm_first_sum,
        norm_second_sum,
        gate_gain_sum,
        conv_main_grad,
        conv_state_grad,
        skip_gain_grad,
        decay_rate_grad,
        step_bias_grad,
        mixer_out_grad,
        shared_gate_up_grad,
        shared_down_grad,
    ) = emit(
        [
            mixer_in_grad,
            state_proj_grad,
            step_proj_grad,
            norm_first_sum,
            norm_second_sum,
            gate_gain_sum,
            conv_main_grad,
            conv_state_grad,
            skip_gain_grad,
            decay_rate_grad,
            step_bias_grad,
            mixer_out_grad,
            shared_gate_up_grad,
            shared_down_grad,
        ]
    )
    return (
        layer_out,
        input_grad,
        norm_first_sum.reshape(-1),
        mixer_in_grad,
        state_proj_grad,
        step_proj_grad,
        step_bias_grad.reshape(-1),
        conv_main_grad,
        conv_state_grad,
        decay_rate_grad.reshape(-1),
        skip_gain_grad.reshape(-1),
        gate_gain_sum.reshape(-1),
        mixer_out_grad,
        norm_second_sum.reshape(-1),
        shared_gate_up_grad,
        shared_down_grad,
        expert_gate_up_grad,
        expert_down_grad,
    )


def solution(mesh):
    placed = (
        P("seq", None),
        P(),
        P("seq", None, "head"),
        P("seq", None),
        P("seq", "head"),
        P("head"),
        P(None, "head"),
        P(),
        P("head"),
        P("head"),
        P("head"),
        P("seq", "head"),
        P(),
        P("seq", None, "head"),
        P("seq", "head"),
        P("seq", None, None, "head"),
        P("seq", "head", None),
        P("seq", None),
        P("seq", None),
        P("seq", None),
    )
    return jax.shard_map(
        per_device,
        mesh=mesh,
        in_specs=placed,
        out_specs=(
            P("seq", None),
            P("seq", None),
            P(),
            P("seq", None, "head"),
            P("seq", None),
            P("seq", "head"),
            P("head"),
            P(None, "head"),
            P(),
            P("head"),
            P("head"),
            P("head"),
            P("seq", "head"),
            P(),
            P("seq", None, "head"),
            P("seq", "head"),
            P("seq", None, None, "head"),
            P("seq", "head", None),
        ),
        check_vma=False,
    )
```

```python
import functools
import jax
import jax.numpy as jnp
from jax import lax
from jax.experimental import pallas as pl
from jax.experimental.pallas import tpu as pltpu
from jax.sharding import PartitionSpec as P

ORDERS = ((0, 1, 2), (1, 2, 0), (2, 0, 1))
VMEM = 62 << 20
EPSILON = 1e-05


def coordinates():
    me = lax.axis_index("seq")
    return me, [me // 16, (me // 4) % 4, me % 4]


def seq_of(at):
    return at[0] * 16 + at[1] * 4 + at[2]


def moved(at, axis, by):
    return [(c + by) % 4 if i == axis else c for i, c in enumerate(at)]


def announce(me, with_sibling):
    barrier = pltpu.get_barrier_semaphore()

    @pl.loop(1, 64)
    def _(k):
        pl.semaphore_signal(barrier, inc=1, device_id={"seq": lax.rem(me + k, 64)})

    if with_sibling:
        pl.semaphore_signal(barrier, inc=1, device_id={"head": 1 - lax.axis_index("head")})


def await_all(with_sibling):
    pl.semaphore_wait(pltpu.get_barrier_semaphore(), 64 if with_sibling else 63)


def parts_of(columns):
    third = columns // 3
    tiles = third // 128
    half = tiles // 2 * 128
    return third, half


def region(at, order, phase, value, cols):
    index = [None] * 3
    for i in range(3):
        if i < phase:
            index[order[i]] = slice(None)
        elif i == phase:
            index[order[i]] = value
        else:
            index[order[i]] = at[order[i]]
    return tuple(index) + (slice(None), cols)


class Ways:
    def __init__(self, at):
        self.at = at

    def group(self, g, back=False):
        x, z, y = self.at
        sign, lead = (-1, 8) if back else (1, 0)
        near, far = lax.rem(g, 4), g // 4
        xs = [lax.rem(x + lead + sign * a, 4) * 16 for a in range(4)]
        zs = [lax.rem(z + lead + sign * (near + a), 4) * 4 for a in range(4)]
        ys = [lax.rem(y + lead + sign * (far + a), 4) for a in range(4)]
        return [(g * 8 + n, xs[n % 4] + zs[n % 4] + ys[(n % 4 + n // 4 * 2) % 4]) for n in range(8)]

    def each(self, first, last, body, back=False):
        @pl.loop(first, last)
        def _(g):
            for n, (k, device) in enumerate(self.group(g, back)):
                if n == 0:
                    pl.when(k > 0)(functools.partial(body, k, device))
                else:
                    body(k, device)


class Lazy:
    def __init__(self, source, ref, sem):
        self.ref, self.copy = ref, pltpu.make_async_copy(source, ref, sem)
        self.shape, self.dtype = ref.shape, ref.dtype
        self.copy.start()

    def ready(self):
        if self.copy is not None:
            self.copy.wait()
            self.copy = None
        return self.ref

    @property
    def at(self):
        return self.ready().at

    def __getitem__(self, index):
        return self.ready()[index]


class Eager:
    def __init__(self, target, ref, sem):
        self.ref, self.copy, self.going = ref, pltpu.make_async_copy(ref, target, sem), False
        self.shape, self.dtype, self.at = ref.shape, ref.dtype, ref.at

    def __getitem__(self, index):
        return self.ref[index]

    def __setitem__(self, index, value):
        self.ref[index] = value

    def flush(self):
        if not self.going:
            self.going = True
            self.copy.start()


def ready(*refs):
    for ref in refs:
        if isinstance(ref, Lazy):
            ref.ready()


def call(kernel, out_shape, in_specs, out_specs, scratch_shapes, **options):
    def run(*args):
        leaves, tree = jax.tree.flatten(list(args))
        specs = tree.flatten_up_to(list(in_specs))
        shapes, out_tree = jax.tree.flatten(list(out_shape))
        out_kinds = out_tree.flatten_up_to(list(out_specs))
        lazy = [n for n, spec in enumerate(specs) if spec is Lazy]
        eager = [n for n, spec in enumerate(out_kinds) if spec is Eager]
        hbm = pl.BlockSpec(memory_space=pl.ANY)
        buffers = [pltpu.VMEM(leaves[n].shape, leaves[n].dtype) for n in lazy]
        buffers += [pltpu.VMEM(shapes[n].shape, shapes[n].dtype) for n in eager]
        buffers += [pltpu.SemaphoreType.DMA((max(1, len(lazy)),))]
        buffers += [pltpu.SemaphoreType.DMA((max(1, len(eager)),))]
        own = len(scratch_shapes)

        def body(*refs):
            ins, outs = list(refs[: len(leaves)]), list(refs[len(leaves) :][: len(shapes)])
            rest = refs[len(leaves) + len(shapes) :]
            more = rest[own:]
            for n, index in enumerate(lazy):
                ins[index] = Lazy(ins[index], more[n], more[-2].at[n])
            for n, index in enumerate(eager):
                outs[index] = Eager(outs[index], more[len(lazy) + n], more[-1].at[n])
            kernel(*tree.unflatten(ins), *out_tree.unflatten(outs), *rest[:own])
            for index in lazy:
                ins[index].ready()
            for index in eager:
                outs[index].flush()
            for index in eager:
                outs[index].copy.wait()

        out = pl.pallas_call(
            body,
            out_shape=shapes,
            in_specs=[hbm if spec is Lazy else spec for spec in specs],
            out_specs=[hbm if kind is Eager else kind for kind in out_kinds],
            scratch_shapes=list(scratch_shapes) + buffers,
            **options,
        )(*leaves)
        return out_tree.unflatten(out)

    return run


def emit_kernel(large, *refs):
    count = (len(refs) - large - 1) // 2
    sources, targets = refs[:count], refs[count : 2 * count]
    buffers, sems = refs[2 * count : -1], refs[-1]
    pieces = []
    for n in range(large):
        rows = sources[n].shape[0] // 4
        for part in range(4):
            here = pl.ds(part * rows, rows)
            place = buffers[n].at[here]
            come = pltpu.make_async_copy(sources[n].at[here], place, sems.at[0, n, part])
            go = pltpu.make_async_copy(place, targets[n].at[here], sems.at[1, n, part])
            come.start()
            pieces.append((come, go))
    for n in range(large, count):
        targets[n][...] = sources[n][...]
    for come, go in pieces:
        come.wait()
        go.start()
    for _, go in pieces:
        go.wait()


def emit(large, small):
    arrays = list(large) + list(small)
    specs = [pl.BlockSpec(memory_space=pl.ANY)] * len(large)
    specs += [pl.BlockSpec(memory_space=pltpu.VMEM)] * len(small)
    return pl.pallas_call(
        functools.partial(emit_kernel, len(large)),
        out_shape=[jax.ShapeDtypeStruct(array.shape, array.dtype) for array in arrays],
        in_specs=specs,
        out_specs=specs,
        scratch_shapes=[pltpu.VMEM(array.shape, array.dtype) for array in large]
        + [pltpu.SemaphoreType.DMA((2, len(large), 4))],
        compiler_params=pltpu.CompilerParams(vmem_limit_bytes=VMEM),
        name="emit",
    )(*arrays)


class Spread:
    def __init__(self, at, me, source, target, sems, first, last, back):
        self.at, self.me, self.source, self.target = at, me, source, target
        self.sems = sems
        self.first, self.last, self.back = first, last, back

    def start(self, first=None, last=None):
        first = self.first if first is None else first
        last = self.last if last is None else last
        if first == 0:
            own = self.source.at[0 if self.back else self.me]
            pltpu.make_async_copy(own, self.target.at[0], self.sems.at[1]).start()

        def put(k, device):
            pltpu.make_async_remote_copy(
                src_ref=self.source.at[k if self.back else device],
                dst_ref=self.target.at[k - 8 * self.first],
                send_sem=self.sems.at[0],
                recv_sem=self.sems.at[1 + k // 8],
                device_id={"seq": device},
            ).start()

        Ways(self.at).each(first, last, put, self.back)

    def arrived(self, first, last):
        for g in range(first, last):
            here = self.target.at[pl.ds(8 * (g - self.first), 8)]
            pltpu.make_async_copy(here, here, self.sems.at[1 + g]).wait()

    def sent(self):
        count = 8 * (self.last - self.first)
        here = self.target.at[pl.ds(0, count - 1 if self.first == 0 else count)]
        pltpu.make_async_copy(here, here, self.sems.at[0]).wait()

    def wait(self):
        self.arrived(self.first, self.last)
        self.sent()


OUT = ((0, 4), (4, 5), (5, 8))
HOME = ((0, 4), (4, 8))


def part_shape(span, rows):
    return jax.ShapeDtypeStruct((8 * (span[1] - span[0]),) + rows.shape[1:], rows.dtype)


def params(collective, **more):
    return pltpu.CompilerParams(collective_id=collective, has_side_effects=True, **more)


class PairSum:
    def __init__(self, mine, theirs, sems, cut):
        self.mine, self.theirs, self.sems, self.cut = mine, theirs, sems, cut
        self.count = mine.shape[1] // cut

    def copy(self, n):
        cols = pl.ds(n * self.cut, self.cut)
        return pltpu.make_async_remote_copy(
            src_ref=self.mine.at[:, cols],
            dst_ref=self.theirs.at[:, cols],
            send_sem=self.sems.at[0, n],
            recv_sem=self.sems.at[1, n],
            device_id={"head": 1 - lax.axis_index("head")},
        )


def experts_kernel(
    gated_ref,
    weights_ref,
    layer_ref,
    table_ref,
    position_ref,
    grads_refs,
    grad_rows_ref,
    gate_up_ref,
    down_ref,
    grad_out_ref,
    home_ref,
    res_ref,
    gate_up_grad_ref,
    down_grad_ref,
    shared_ref,
    back_ref,
    right_ref,
    resid_ref,
    normed_ref,
    scale_ref,
    rows_ref,
    grads_here,
    mine,
    theirs,
    slot_in,
    grad_slots,
    theirs_x,
    theirs_y,
    sums,
    wide_grad,
    weights,
    load_sems,
    pair_sems,
    out_sems,
    send,
    home_send,
    home_recv,
    sems,
):
    me, at = coordinates()
    head = lax.axis_index("head")
    sibling = {"head": 1 - head}
    names = ("recv", "fwd_send", "fwd_recv", "kept", "given_send", "given_recv")
    names += ("x_send", "x_recv", "y_send", "y_recv")
    sem = {name: sems.at[n] for n, name in enumerate(names)}
    announce(me, True)
    shared_hidden = right_ref.shape[1] // 3
    tokens, model = layer_ref.shape
    inner = gated_ref.shape[1]
    loads = []
    for n, cols in enumerate((pl.ds(0, inner), pl.ds(inner, 3 * shared_hidden))):
        loads.append(
            pltpu.make_async_copy(weights_ref.at[:, cols], weights.at[:, cols], load_sems.at[n])
        )
        loads[n].start()
    norm_ref = table_ref.at[5:6, 0:model]
    wide_grad[...] = jnp.zeros_like(wide_grad)
    down_grad_ref[...] = jnp.zeros_like(down_grad_ref)
    ways = Ways(at)
    await_all(True)
    out = Spread(at, me, grad_rows_ref, grads_here, out_sems, *OUT[2], False)

    def group(c):
        return pl.ds(pl.multiple_of(c * 8, 8), 8)

    def given(c, source=None):
        there = grad_slots.at[group(c), head]
        return pltpu.make_async_remote_copy(
            src_ref=there if source is None else source,
            dst_ref=there,
            send_sem=sem["given_send"].at[c],
            recv_sem=sem["given_recv"].at[c],
            device_id=sibling,
        )

    def kept(c, source=None):
        there = grad_slots.at[group(c), head]
        return pltpu.make_async_copy(there if source is None else source, there, sem["kept"].at[c])

    def forward(c):
        return pltpu.make_async_remote_copy(
            src_ref=slot_in.at[group(c), head],
            dst_ref=slot_in.at[group(c), head],
            send_sem=sem["fwd_send"].at[c],
            recv_sem=sem["fwd_recv"].at[c],
            device_id=sibling,
        )

    def swap(c, source, target, name):
        return pltpu.make_async_remote_copy(
            src_ref=source.at[group(c), 1 - head],
            dst_ref=target.at[group(c)],
            send_sem=sem[name + "_send"].at[c],
            recv_sem=sem[name + "_recv"].at[c],
            device_id=sibling,
        )

    for (first, last), grads_ref in zip(OUT, grads_refs):
        for c in range(first, last):
            source = grads_ref.at[pl.ds(8 * (c - first), 8)]
            kept(c, source).start()
            given(c, source).start()

    out.start()

    cut = 256
    pair = PairSum(mine, theirs, pair_sems, cut)
    loads[0].wait()
    gated = gated_ref[...]
    for n in range(pair.count):
        rows = slice(n * cut, (n + 1) * cut)
        mine[:, rows] = dot_nt(gated, weights[rows, 0:inner])
        pair.copy(n).start()
    loads[1].wait()
    both = slice(inner, inner + 2 * shared_hidden)
    less = slice(inner + 2 * shared_hidden, inner + 3 * shared_hidden)
    shared_grad_hid = dot_nn(grad_out_ref[...], weights[:, less])
    square = jnp.zeros((tokens, 1), jnp.float32)
    for n in range(pair.count):
        rows = slice(n * cut, (n + 1) * cut)
        pair.copy(n).wait()
        resid = layer_ref[:, rows].astype(jnp.float32) + (mine[:, rows] + theirs[:, rows])
        resid_ref[:, rows] = resid
        square = square + jnp.sum(resid * resid, axis=1, keepdims=True)
    scale = lax.rsqrt(square / model + EPSILON)
    scale_ref[...] = jnp.broadcast_to(scale, scale_ref.shape)
    for n in range(pair.count):
        rows = slice(n * cut, (n + 1) * cut)
        normed_ref[:, rows] = low(resid_ref[:, rows] * scale * norm_ref[:, rows])
    resid_ref.flush()
    normed_ref.flush()
    ready(position_ref)
    normed = normed_ref[...]
    slots, step = rows_ref.shape[1], 16

    @pl.loop(0, rows_ref.shape[0] // step)
    def _(i):
        here = pl.ds(pl.multiple_of(i * step, step), step)
        chosen = chosen_slots(position_ref[here, :], slots)
        rows_ref[here] = low(dot_nn(low(chosen), normed)).reshape(step, slots, model)

    own = pltpu.make_async_copy(rows_ref.at[me], slot_in.at[0, head], sem["recv"].at[0])
    own.start()

    def put(k, target):
        pltpu.make_async_remote_copy(
            src_ref=rows_ref.at[target],
            dst_ref=slot_in.at[k, head],
            send_sem=send,
            recv_sem=sem["recv"].at[k // 8],
            device_id={"seq": target},
        ).start()

    ways.each(0, 8, put)

    hidden = down_ref.shape[0]
    width = down_ref.shape[1]

    def nt(left, right):
        return lax.dot_general(
            left, right, (((1,), (1,)), ((), ())), preferred_element_type=jnp.float32
        )

    def tn(left, right):
        return lax.dot_general(
            left, right, (((0,), (0,)), ((), ())), preferred_element_type=jnp.float32
        )

    gate_up = dot_nn(normed, weights[:, both])
    gate, up = gate_up[:, :shared_hidden], gate_up[:, shared_hidden:]
    act, slope = silu_parts(gate)
    hid = low(act * up)
    right_ref[:, 2 * shared_hidden :] = hid
    right_ref[:, 0:shared_hidden] = low(shared_grad_hid * up * slope)
    right_ref[:, shared_hidden : 2 * shared_hidden] = low(shared_grad_hid * act)
    grads = right_ref[:, 0 : 2 * shared_hidden]
    for c in range(0, width, 256):
        rows = slice(c, c + 256)
        shared_ref[:, rows] = dot_nt(hid, weights[rows, less])
        back_ref[:, rows] = dot_nt(grads, weights[rows, both])
    for ref in (shared_ref, back_ref, right_ref):
        ref.flush()
    ready(gate_up_ref, down_ref)

    @pl.loop(0, 10)
    def _(i):
        @pl.when(i < 8)
        def _():
            c = i
            pltpu.make_async_copy(
                rows_ref.at[group(c)], slot_in.at[group(c), head], sem["recv"].at[c]
            ).wait()
            forward(c).start()

        for late in range(*OUT[2]):

            @pl.when(i == late - 2)
            def _():
                out.arrived(late, late + 1)
                source = grads_here.at[pl.ds(8 * (late - OUT[2][0]), 8)]
                kept(late, source).start()
                given(late, source).start()

        @pl.when((i >= 1) & (i < 9))
        def _():
            c = i - 1
            forward(c).wait()
            kept(c).wait()
            given(c).wait()
            rows = slot_in[group(c)].reshape(256, width)
            grads = grad_slots[group(c)].reshape(256, width)
            both = jnp.dot(rows, gate_up_ref[...], preferred_element_type=jnp.float32)
            gate, up = both[:, :hidden], both[:, hidden:]
            sig = jax.nn.sigmoid(gate)
            act = gate * sig
            hid = (act * up).astype(jnp.bfloat16)
            grad_hid = nt(grads, down_ref[...])
            grad_gate = grad_hid * up * (sig * (1.0 + gate * (1.0 - sig)))
            grad_both = jnp.concatenate([grad_gate, grad_hid * act], axis=1).astype(jnp.bfloat16)
            wide_grad[...] += tn(rows, grad_both)
            down_grad_ref[...] += tn(hid, grads)
            back = nt(grad_both, gate_up_ref[...]).astype(jnp.bfloat16)
            slot_in[group(c)] = back.reshape(8, 2, 16, width)
            res = jnp.dot(hid, down_ref[...], preferred_element_type=jnp.float32)
            grad_slots[group(c)] = res.astype(jnp.bfloat16).reshape(8, 2, 16, width)
            swap(c, slot_in, theirs_x, "x").start()
            swap(c, grad_slots, theirs_y, "y").start()

        @pl.when(i >= 2)
        def _():
            c = i - 2
            swap(c, slot_in, theirs_x, "x").wait()

            def add(k):
                total = slot_in[k, head].astype(jnp.float32) + theirs_x[k].astype(jnp.float32)
                sums[k] = total.astype(sums.dtype)

            def put_home(k, source):
                add(k)
                pltpu.make_async_remote_copy(
                    src_ref=sums.at[k],
                    dst_ref=home_ref.at[me],
                    send_sem=home_send,
                    recv_sem=home_recv,
                    device_id={"seq": source},
                ).start()

            @pl.when(c == 0)
            def _():
                add(0)
                pltpu.make_async_copy(sums.at[0], home_ref.at[me], home_recv).start()

            ways.each(c, c + 1, put_home, back=True)
            swap(c, grad_slots, theirs_y, "y").wait()

            @pl.loop(0, 8)
            def _(n):
                j = c * 8 + n
                total = grad_slots[j, head].astype(jnp.float32) + theirs_y[j].astype(jnp.float32)
                res_ref[j] = total.astype(res_ref.dtype)

    out.sent()
    tiles = hidden // 128
    for tile in range(tiles):
        for which in range(2):
            start = which * hidden + tile * 128
            gate_up_grad_ref[pl.ds(tile * 2 + which, width, stride=2 * tiles), :] = wide_grad[
                :, start : start + 128
            ]
    some = pl.ds(0, 63)
    pltpu.make_async_copy(rows_ref.at[some], rows_ref.at[some], send).wait()
    pltpu.make_async_copy(sums.at[some], sums.at[some], home_send).wait()
    pltpu.make_async_copy(sums, home_ref, home_recv).wait()


def experts(
    gated, weights, layer_in, table, position, grads, grad_rows, gate_up, down, grad_out, slots, collective
):
    tokens, model = layer_in.shape
    shared_hidden = (weights.shape[1] - gated.shape[1]) // 3
    hidden, width = down.shape
    half, bf16 = (position.shape[0], slots, model), jnp.bfloat16
    whole = (half[0], 2) + half[1:]
    vmem, hbm = pl.BlockSpec(memory_space=pltpu.VMEM), pl.BlockSpec(memory_space=pl.ANY)
    home, res, wide, down_grad, *shared = call(
        experts_kernel,
        out_shape=[
            jax.ShapeDtypeStruct(half, bf16),
            jax.ShapeDtypeStruct(half, bf16),
            jax.ShapeDtypeStruct((width * 2 * hidden // 128, 128), jnp.float32),
            jax.ShapeDtypeStruct((hidden, width), jnp.float32),
            jax.ShapeDtypeStruct((tokens, width), jnp.float32),
            jax.ShapeDtypeStruct((tokens, width), jnp.float32),
            jax.ShapeDtypeStruct((tokens, 3 * shared_hidden), bf16),
            jax.ShapeDtypeStruct((tokens, model), jnp.float32),
            jax.ShapeDtypeStruct((tokens, model), bf16),
            jax.ShapeDtypeStruct((tokens, 128), jnp.float32),
        ],
        in_specs=[Lazy, hbm, Lazy, vmem, Lazy, [hbm] * len(grads), hbm, Lazy, Lazy, Lazy],
        out_specs=[hbm] + [vmem] * 3 + [Eager] * 5 + [vmem],
        scratch_shapes=[
            pltpu.VMEM(half, bf16),
            pltpu.VMEM(part_shape(OUT[2], grad_rows).shape, bf16),
            pltpu.VMEM((tokens, model), jnp.float32),
            pltpu.VMEM((tokens, model), jnp.float32),
            pltpu.VMEM(whole, bf16),
            pltpu.VMEM(whole, bf16),
            pltpu.VMEM(half, bf16),
            pltpu.VMEM(half, bf16),
            pltpu.VMEM(half, bf16),
            pltpu.VMEM((width, 2 * hidden), jnp.float32),
            pltpu.VMEM(weights.shape, bf16),
            pltpu.SemaphoreType.DMA((2,)),
            pltpu.SemaphoreType.DMA((2, model // 256)),
            pltpu.SemaphoreType.DMA((9,)),
            pltpu.SemaphoreType.DMA,
            pltpu.SemaphoreType.DMA,
            pltpu.SemaphoreType.DMA,
            pltpu.SemaphoreType.DMA((10, 8)),
        ],
        compiler_params=params(collective, vmem_limit_bytes=VMEM),
        name="experts",
    )(gated, weights, layer_in, table, position, grads, grad_rows, gate_up, down, grad_out)
    return home, res, wide, down_grad, *shared


class Scan:
    def __init__(self, reverse, at, me, x_ref, out_ref, got, made, sems):
        self.reverse, self.at, self.me = reverse, at, me
        self.x_ref, self.out_ref, self.got, self.made = x_ref, out_ref, got, made
        self.send, self.recv, self.back_send, self.back_recv = [sems.at[n] for n in range(4)]

    def spread(self, source, target_ref, send, recv):
        def put(_, target):
            pltpu.make_async_remote_copy(
                src_ref=source.at[target],
                dst_ref=target_ref.at[self.me],
                send_sem=send,
                recv_sem=recv,
                device_id={"seq": target},
            ).start()

        Ways(self.at).each(0, 8, put)

    def begin(self):
        self.got[self.me] = self.x_ref[self.me]
        self.spread(self.x_ref, self.got, self.send, self.recv)

    def middle(self):
        some = pl.ds(0, 63)
        x_ref, got, made = self.x_ref, self.got, self.made
        pltpu.make_async_copy(x_ref.at[some], x_ref.at[some], self.send).wait()
        pltpu.make_async_copy(got.at[some], got.at[some], self.recv).wait()
        heads, width = made.shape[1:]
        number = lax.broadcasted_iota(jnp.int32, (heads, width), 0) + heads * self.me
        chosen = number // 64 == lax.broadcasted_iota(jnp.int32, (heads, width), 1)

        def step(k, state):
            at_k = 63 - k if self.reverse else k
            made[at_k] = state
            rows = got[at_k].astype(jnp.float32)
            row = jnp.sum(rows[heads:], axis=0, keepdims=True)
            decay = jnp.sum(jnp.where(chosen, row, 0.0), axis=1, keepdims=True)
            return decay * state + rows[:heads]

        lax.fori_loop(0, 64, step, jnp.zeros((heads, width), jnp.float32), unroll=8)
        self.out_ref[self.me] = made[self.me]
        self.spread(made, self.out_ref, self.back_send, self.back_recv)

    def end(self):
        some = pl.ds(0, 63)
        made = self.made
        pltpu.make_async_copy(made.at[some], made.at[some], self.back_send).wait()
        pltpu.make_async_copy(made.at[some], made.at[some], self.back_recv).wait()


def scan_rows(states, decay):
    decays = [part.astype(jnp.float32) for part in split(decay, 3)]
    decays = jnp.concatenate(decays + [jnp.zeros((5, decay.shape[1]), jnp.float32)], axis=0)
    decays = jnp.broadcast_to(decays[None], (states.shape[0],) + decays.shape)
    return low(jnp.concatenate([states, decays], axis=1))


class Small:
    def __init__(self, at, me, x_ref, out_ref, got, sems):
        self.at, self.me = at, me
        self.x_ref, self.out_ref, self.got = x_ref, out_ref, got
        self.send, self.recv, self.back_send, self.back_recv = [sems.at[n] for n in range(4)]

    def begin(self):
        self.got[self.me] = self.x_ref[self.me]

        def put(_, target):
            pltpu.make_async_remote_copy(
                src_ref=self.x_ref.at[target],
                dst_ref=self.got.at[self.me],
                send_sem=self.send,
                recv_sem=self.recv,
                device_id={"seq": target},
            ).start()

        Ways(self.at).each(0, 8, put)

    def middle(self):
        some = pl.ds(0, 63)
        x_ref, got, out_ref, me = self.x_ref, self.got, self.out_ref, self.me
        pltpu.make_async_copy(x_ref.at[some], x_ref.at[some], self.send).wait()
        pltpu.make_async_copy(got.at[some], got.at[some], self.recv).wait()
        out_ref[me] = lax.fori_loop(1, 64, lambda k, total: total + got[k], got[0], unroll=9)

        def put(_, target):
            pltpu.make_async_remote_copy(
                src_ref=out_ref.at[me],
                dst_ref=out_ref.at[me],
                send_sem=self.back_send,
                recv_sem=self.back_recv,
                device_id={"seq": target},
            ).start()

        Ways(self.at).each(0, 8, put)

    def end(self):
        some = pl.ds(0, 63)
        got = self.got
        pltpu.make_async_copy(got.at[some], got.at[some], self.back_send).wait()
        pltpu.make_async_copy(got.at[some], got.at[some], self.back_recv).wait()


class Scatter:
    def __init__(self, at, plan, lefts, rights, out_ref, buf, rest, send, recv):
        self.at, self.plan, self.lefts, self.rights = at, plan, lefts, rights
        self.out_ref, self.buf, self.rest, self.send, self.recv = out_ref, buf, rest, send, recv
        self.third, self.half = parts_of(buf.shape[4])
        self.copies = {}

    def spans(self, p):
        start, third, half = p * self.third, self.third, self.half
        return pl.ds(start, half), pl.ds(start + half, third - half)

    def product(self, p):
        buf = self.buf
        rows = buf.shape[3]
        for which, other, first, start, length in self.plan[p]:
            left, right = self.lefts[which], self.rights[other]
            ready(left, right)

            @pl.loop(0, 4)
            def _(x):
                across = pl.ds(pl.multiple_of(x * 16 * rows, 128), 16 * rows)
                total = lax.dot_general(
                    left[:, across],
                    right[:, first : first + length],
                    (((0,), (0,)), ((), ())),
                    preferred_element_type=jnp.float32,
                )
                total = total.reshape(4, 4, rows, length).astype(jnp.bfloat16)
                buf[x, :, :, :, start : start + length] = total

    def send_to(self, phase, p, by, value, cols, slot, kind):
        order = ORDERS[p]
        axis = order[phase]
        lead = (slice(None),) * phase
        copy = pltpu.make_async_remote_copy(
            src_ref=self.buf.at[region(self.at, order, phase, value, cols)],
            dst_ref=self.rest[phase].at[(slot,) + lead + (slice(None), cols)],
            send_sem=self.send.at[phase, p, kind],
            recv_sem=self.recv.at[phase, p, kind],
            device_id={"seq": seq_of(moved(self.at, axis, by))},
        )
        copy.start()
        self.copies[phase, p, kind] = copy

    def added(self, phase, p, value, cols, slots):
        order, buf, room = ORDERS[p], self.buf, self.rest[phase]

        @pl.loop(0, 4**phase)
        def _(i):
            free = ((), (i,), (i // 4, i % 4))[phase]
            index = list(region(self.at, order, phase, value, cols))
            for n, axis in enumerate(sorted(order[:phase])):
                index[axis] = free[n]
            index = tuple(index)
            total = buf[index].astype(jnp.float32)
            for slot in slots:
                total = total + room[(slot,) + free + (slice(None), cols)].astype(jnp.float32)
            if phase == 0 and len(slots) == 2:
                self.out_ref[:, cols] = total
            else:
                buf[index] = total.astype(jnp.bfloat16)

    def first(self, phase, p):
        self.first_far(phase, p)
        self.first_near(phase, p)

    def first_far(self, phase, p):
        c = self.at[ORDERS[p][phase]]
        low, high = self.spans(p)
        self.send_to(phase, p, 1, (c + 2) % 4, low, 2, 0)
        self.send_to(phase, p, 3, (c + 2) % 4, high, 2, 1)

    def first_near(self, phase, p):
        c = self.at[ORDERS[p][phase]]
        low, high = self.spans(p)
        self.send_to(phase, p, 1, (c + 1) % 4, high, 0, 2)
        self.send_to(phase, p, 3, (c + 3) % 4, low, 1, 3)

    def second(self, phase, p):
        c = self.at[ORDERS[p][phase]]
        low, high = self.spans(p)
        self.copies[phase, p, 0].wait_recv()
        self.added(phase, p, (c + 1) % 4, low, (2,))
        self.send_to(phase, p, 1, (c + 1) % 4, low, 0, 4)
        self.copies[phase, p, 1].wait_recv()
        self.added(phase, p, (c + 3) % 4, high, (2,))
        self.send_to(phase, p, 3, (c + 3) % 4, high, 1, 5)

    def third_step(self, phase, p):
        c = self.at[ORDERS[p][phase]]
        low, high = self.spans(p)
        self.copies[phase, p, 2].wait_recv()
        self.copies[phase, p, 5].wait_recv()
        self.added(phase, p, c, high, (0, 1))
        self.copies[phase, p, 3].wait_recv()
        self.copies[phase, p, 4].wait_recv()
        self.added(phase, p, c, low, (0, 1))

    def finish(self, phase):
        for p in range(3):
            self.third_step(phase, p)
            if phase > 0:
                self.first(phase - 1, p)

    def end(self):
        for copy in self.copies.values():
            copy.wait_send()


def scatter_shapes(rows, columns):
    return [
        pltpu.VMEM((4, 4, 4, rows, columns), jnp.bfloat16),
        [pltpu.VMEM((3,) + (4,) * phase + (rows, columns), jnp.bfloat16) for phase in range(3)],
        pltpu.SemaphoreType.DMA((3, 3, 6)),
        pltpu.SemaphoreType.DMA((3, 3, 6)),
    ]


def dot_nn(left, right):
    return jnp.dot(left, right, preferred_element_type=jnp.float32)


def dot_nt(left, right):
    return lax.dot_general(
        left, right, (((1,), (1,)), ((), ())), preferred_element_type=jnp.float32
    )


def dot_tn(left, right):
    return lax.dot_general(
        left, right, (((0,), (0,)), ((), ())), preferred_element_type=jnp.float32
    )


def low(value):
    return value.astype(jnp.bfloat16)


def split(value, count):
    parts = []
    for _ in range(count):
        parts.append(low(value))
        value = value - parts[-1].astype(jnp.float32)
    return parts


def dot_split(left, right, count, dot=dot_nn):
    return sum(dot(left, part) for part in split(right, count))


def split_dot(left, right, count):
    return sum(dot_nn(part, right) for part in split(left, count))


def dot_three(left, right, dot=dot_nn):
    high, less = split(left, 2)
    other_high, other_less = split(right, 2)
    return dot(high, other_high) + dot(less, other_high) + dot(high, other_less)


def head_spread(lanes, width, size):
    head = lax.broadcasted_iota(jnp.int32, (lanes, width), 0)
    column = lax.broadcasted_iota(jnp.int32, (lanes, width), 1)
    return low(jnp.where(head == column // size, 1.0, 0.0))


def head_gather(lanes, width, size):
    head = lax.broadcasted_iota(jnp.int32, (width, lanes), 1)
    column = lax.broadcasted_iota(jnp.int32, (width, lanes), 0)
    return low(jnp.where(head == column // size, 1.0, 0.0))


def triangle(rows, keep):
    first = lax.broadcasted_iota(jnp.int32, (rows, rows), 0)
    second = lax.broadcasted_iota(jnp.int32, (rows, rows), 1)
    return keep(first, second)


def silu_parts(value):
    sig = jax.nn.sigmoid(value)
    return value * sig, sig * (1.0 + value * (1.0 - sig))


def mixer_back_kernel(
    lefts,
    rights,
    home_ref,
    position_ref,
    add_ref,
    resid_ref,
    scale_ref,
    weights_ref,
    z_ref,
    gate_scale_ref,
    y_ref,
    x_ref,
    bc_ref,
    conv_ref,
    pre_ref,
    step_raw_ref,
    table_ref,
    start_ref,
    res_ref,
    mixer_out_ref,
    gate_up_ref,
    down_ref,
    grads_ref,
    taps_grad_ref,
    heads_grad_ref,
    results_ref,
    grad_resid_ref,
    norm_grad_ref,
    gain_grad_ref,
    weights,
    grad_mix,
    dy_ref,
    stat,
    stat_theirs,
    message,
    back,
    got,
    made,
    decayed,
    q,
    spread,
    cum_rows,
    scores,
    acc,
    ext,
    mine,
    theirs,
    shared_out,
    shared_scratch,
    mix_scratch,
    scan_sems,
    sems,
    home_sems,
    load_sem,
    pair_sems,
    stat_sems,
):
    me, at = coordinates()
    head = lax.axis_index("head")
    tokens, width = x_ref.shape
    model = resid_ref.shape[1]
    size = start_ref.shape[1]
    lanes = step_raw_ref.shape[1]
    each = width // 64
    mid = tokens // 2
    cut = 384
    numbers_ref, taps_ref = table_ref.at[8:16, 0:lanes], table_ref
    norm_ref, gain_ref = table_ref.at[5:6, 0:model], table_ref.at[6:7, 0:width]
    announce(me, True)
    added = pltpu.make_async_copy(add_ref, q, load_sem.at[1])
    added.start()
    load = pltpu.make_async_copy(weights_ref.at[:, pl.ds(0, width)], weights, load_sem.at[0])
    load.start()
    normed_second, grad_out = lefts
    normed_gate, shared_right = rights
    third = width // 3
    plan = [((n // 2, 0, n * third, n * third, third),) for n in range(3)]
    shared = Scatter(at, plan, lefts, [shared_right], shared_out, *shared_scratch)
    plan = [((0, 0, n * third, n * third, third),) for n in range(3)]
    mix = Scatter(at, plan, [grad_mix], [normed_gate], mixer_out_ref, *mix_scratch)
    scan = Scan(True, at, me, message, back, got, made, scan_sems)
    results = Spread(at, me, res_ref, results_ref, home_sems, *HOME[0], True)

    gate_cut = 256
    pair = PairSum(q, decayed, pair_sems, gate_cut)
    added.wait()
    ready(home_ref, position_ref)
    slots, step = home_ref.shape[1], 16

    @pl.loop(0, home_ref.shape[0] // step)
    def _(i):
        here = pl.ds(pl.multiple_of(i * step, step), step)
        chosen = low(chosen_slots(position_ref[here, :], slots))
        q[...] += dot_tn(chosen, home_ref[here].reshape(step * slots, model))

    await_all(True)
    for n in range(pair.count):
        pair.copy(n).start()
    results.start(HOME[0][0], HOME[0][0] + 1)
    for p in range(3):
        shared.product(p)
        shared.first(2, p)
    scale = scale_ref[:, 0:1]
    inner_sum = jnp.zeros((tokens, 1), jnp.float32)
    for n in range(pair.count):
        cols = slice(n * gate_cut, (n + 1) * gate_cut)
        pair.copy(n).wait()
        grad = q[:, cols] + decayed[:, cols]
        q[:, cols] = grad
        resid = resid_ref[:, cols]
        norm_grad_ref[:, cols] = jnp.sum(grad * resid * scale, axis=0, keepdims=True)
        inner_sum = inner_sum + jnp.sum(resid * norm_ref[:, cols] * grad, axis=1, keepdims=True)
    pull = scale * scale * scale * (inner_sum / model)
    for n in range(pair.count):
        cols = slice(n * gate_cut, (n + 1) * gate_cut)
        grad = scale * norm_ref[:, cols] * q[:, cols] - resid_ref[:, cols] * pull
        grad = grad_out[:, cols].astype(jnp.float32) + grad
        grad_resid_ref[:, cols] = grad
        grad_mix[:, cols] = low(grad)
    grad_resid_ref.flush()

    load.wait()
    gate_scale = gate_scale_ref[:, 0:1]
    dots = jnp.zeros((tokens, 1), jnp.float32)
    for c in range(0, width, cut):
        cols = slice(c, c + cut)
        grad = dot_nn(grad_mix[...], weights[:, cols])
        z = z_ref[:, cols]
        gated = y_ref[:, cols] * (z * jax.nn.sigmoid(z))
        gain_grad_ref[:, cols] = jnp.sum(grad * gated * gate_scale, axis=0, keepdims=True)
        weighted = grad * gain_ref[:, cols]
        dy_ref[:, cols] = weighted
        dots = dots + jnp.sum(weighted * gated, axis=1, keepdims=True)
    stat[...] = jnp.broadcast_to(dots, stat.shape)
    stat_swap = pltpu.make_async_remote_copy(
        src_ref=stat,
        dst_ref=stat_theirs,
        send_sem=stat_sems.at[0],
        recv_sem=stat_sems.at[1],
        device_id={"head": 1 - head},
    )
    stat_swap.start()
    for p in range(3):
        mix.product(p)
        mix.first(2, p)
    for p in range(3):
        shared.second(2, p)
    stat_swap.wait()
    dots = (stat[...] + stat_theirs[...])[:, 0:1]
    pull = gate_scale * gate_scale * gate_scale * (dots / (2 * width))
    for c in range(0, width, cut):
        cols = slice(c, c + cut)
        z, y = z_ref[:, cols], y_ref[:, cols]
        act, slope = silu_parts(z)
        grad = gate_scale * dy_ref[:, cols] - y * act * pull
        dy_ref[:, cols] = grad * act
        grads_ref[:, cols] = low(grad * y * slope)

    rate = numbers_ref[0:1, :]
    step_raw = step_raw_ref[...]
    step = jax.nn.softplus(step_raw)
    earlier = low(triangle(tokens, lambda t, s: jnp.where(t >= s, 1.0, 0.0)))
    cum = dot_split(earlier, -step * rate, 3)
    cum_rows[...] = cum.T
    tail = cum[tokens - 1 : tokens, :]
    rest_decay = jnp.exp(tail - cum)
    weight = rest_decay * step
    spreader = head_spread(lanes, width, 64)
    gatherer = head_gather(lanes, width, 64)
    spread[...] = split_dot(jnp.exp(cum), spreader, 2)
    held_full, read_full = bc_ref[:, :size], bc_ref[:, size:]
    held, read = low(held_full), low(read_full)

    for c in range(0, width, cut):
        part = dy_ref[:, c : c + cut] * spread[:, c : c + cut]
        decayed[:, c : c + cut] = part
        made_rows = dot_three(part, read_full, dot_tn)
        made_rows = made_rows.reshape(cut // each, each, size)
        message[c // each : (c + cut) // each] = scan_rows(made_rows, jnp.exp(tail))
    scan.begin()
    for p in range(3):
        mix.second(2, p)
    shared.finish(2)
    scan.middle()

    spread[...] = split_dot(step, spreader, 2)
    blocks = ((0, 0), (0, 1), (1, 1))
    for n, (s, t) in enumerate(blocks):
        scores[n] = dot_nt(held[s * mid : (s + 1) * mid], read[t * mid : (t + 1) * mid])
    acc[...] = jnp.zeros_like(acc)
    causal = triangle(mid, lambda s, t: s <= t)
    ready(x_ref)
    second_head = lax.broadcasted_iota(jnp.int32, (tokens, 128), 1) >= 64

    @pl.loop(0, width // 128)
    def _(i):
        here = pl.ds(pl.multiple_of(i * 128, 128), 128)
        dy, dy_less = split(dy_ref[:, here], 2)
        stepped = x_ref[:, here] * spread[:, here]
        results = []
        for which in range(2):
            row = cum_rows[pl.ds(2 * i + which, 1), :]
            column = jnp.broadcast_to(row, (128, tokens)).T
            mask = second_head if which else jnp.logical_not(second_head)
            values, values_less = split(jnp.where(mask, stepped, 0.0), 2)
            total = [None, None]
            for n, (s, t) in enumerate(blocks):
                gap = row[:, t * mid : (t + 1) * mid] - column[s * mid : (s + 1) * mid]
                decay = jnp.exp(gap)
                if s == t:
                    decay = jnp.where(causal, decay, 0.0)
                later = dy[t * mid : (t + 1) * mid]
                first, later_less = values[s * mid : (s + 1) * mid], dy_less[t * mid : (t + 1) * mid]
                pairs = dot_nt(first, later) + dot_nt(first, later_less)
                pairs = pairs + dot_nt(values_less[s * mid : (s + 1) * mid], later)
                acc[n] += decay * pairs
                part = dot_nn(low(decay * scores[n]), later)
                total[s] = part if total[s] is None else total[s] + part
            results.append(total)
        for s in range(2):
            rows = slice(s * mid, (s + 1) * mid)
            q[rows, here] = jnp.where(second_head[rows], results[1][s], results[0][s])

    for p in range(3):
        shared.second(1, p)
    shared.finish(1)
    mix.finish(2)
    results.start(HOME[0][0] + 1, HOME[0][0] + 2)
    scan.end()

    skip = split_dot(jnp.broadcast_to(numbers_ref[1:2, :], (8, lanes)), spreader, 2)[0:1, :]
    grad_weight = grad_step = rows_sum = jnp.zeros((tokens, lanes), jnp.float32)
    skip_grad = jnp.zeros((8, lanes), jnp.float32)
    state_dot = jnp.zeros((lanes, size), jnp.float32)
    held_parts = held_full[:mid], held_full[mid:]
    read_parts = read_full[:mid], read_full[mid:]
    grad_held = dot_three(acc[0], read_parts[0]) + dot_three(acc[1], read_parts[1])
    grad_held = jnp.concatenate([grad_held, dot_three(acc[2], read_parts[1])], axis=0)
    grad_read = dot_three(acc[1], held_parts[0], dot_tn) + dot_three(acc[2], held_parts[1], dot_tn)
    grad_read = jnp.concatenate([dot_three(acc[0], held_parts[0], dot_tn), grad_read], axis=0)
    for c in range(0, width, cut):
        here = slice(c, c + cut)
        x, dy, inner = x_ref[:, here], dy_ref[:, here], q[:, here]
        after = back[c // each : (c + cut) // each].reshape(cut, size)
        start = start_ref[here, :]
        gather = gatherer[here, :]
        weights = split_dot(weight, spreader[:, here], 2)
        through = dot_nt(held, low(after))
        grad_x = inner * spread[:, here] + skip[:, here] * dy + weights * through
        grad_step = grad_step + split_dot(x * inner, gather, 2)
        grad_weight = grad_weight + split_dot(x * through, gather, 2)
        rows_sum = rows_sum + split_dot(dy * (y_ref[:, here] - skip[:, here] * x), gather, 2)
        pairs = jnp.sum(dy * x, axis=0, keepdims=True)
        skip_grad = skip_grad + split_dot(jnp.broadcast_to(pairs, (8, cut)), gather, 2)
        state_dot = state_dot + dot_split(gather, after * start, 2, dot_tn)
        grad_held = grad_held + dot_three(weights * x, after)
        grad_read = grad_read + dot_three(decayed[:, here], start)
        ext[0:tokens, here] = grad_x * silu_parts(conv_ref[:, here])[1]
    mine[:, :size] = grad_held
    mine[:, size:] = grad_read
    swap = pltpu.make_async_remote_copy(
        src_ref=mine,
        dst_ref=theirs,
        send_sem=sems.at[0],
        recv_sem=sems.at[1],
        device_id={"head": 1 - head},
    )
    swap.start()
    for p in range(3):
        shared.second(0, p)
    for p in range(3):
        mix.second(1, p)
    results.start(HOME[0][0] + 2, HOME[0][0] + 3)

    ones = jnp.ones((8, size), jnp.bfloat16)
    state_grad = dot_split(ones, state_dot, 2, dot_nt)[0:1, :]
    used = grad_weight * weight
    tail_grad = jnp.sum(used, axis=0, keepdims=True) + jnp.exp(tail) * state_grad
    grad_cum = rows_sum - step * grad_step - used
    last = lax.broadcasted_iota(jnp.int32, (tokens, lanes), 0) == tokens - 1
    grad_cum = grad_cum + jnp.where(last, tail_grad, 0.0)
    later = low(triangle(tokens, lambda t, s: jnp.where(t <= s, 1.0, 0.0)))
    grad_log = dot_split(later, grad_cum, 3)
    grad_step = grad_step + grad_weight * rest_decay - rate * grad_log
    grad_raw = grad_step * jax.nn.sigmoid(step_raw)
    heads_grad_ref[...] = jnp.zeros_like(heads_grad_ref)
    heads_grad_ref[0:1, :] = skip_grad[0:1, :]
    heads_grad_ref[1:2, :] = -jnp.sum(step * grad_log, axis=0, keepdims=True)
    heads_grad_ref[2:3, :] = jnp.sum(grad_raw, axis=0, keepdims=True)

    channels = width + 2 * size
    grads_ref[:, width + channels : width + channels + lanes] = low(grad_raw)
    swap.wait()
    ext[0:tokens, width:channels] = (mine[...] + theirs[...]) * silu_parts(
        conv_ref[:, width:channels]
    )[1]
    edge = pltpu.make_async_remote_copy(
        src_ref=ext.at[pl.ds(0, 8)],
        dst_ref=ext.at[pl.ds(tokens, 8)],
        send_sem=sems.at[2],
        recv_sem=sems.at[3],
        device_id={"seq": (me + 63) % 64},
    )
    edge.start()
    shared.finish(0)
    mix.finish(1)
    results.start(HOME[0][0] + 3, HOME[0][1])
    edge.wait()
    there = jnp.where(me == 63, 0.0, 1.0)
    ext[tokens : tokens + 8, :] = ext[tokens : tokens + 8, :] * there
    taps_grad_ref[...] = jnp.zeros_like(taps_grad_ref)
    ready(pre_ref)

    @pl.loop(0, channels // 256)
    def _(i):
        here = pl.ds(pl.multiple_of(i * 256, 256), 256)
        grad = ext[0:tokens, here]
        total = jnp.zeros_like(grad)
        for j in range(4):
            total = total + taps_ref[j : j + 1, here] * ext[3 - j : 3 - j + tokens, here]
            products = grad * pre_ref[5 + j : 5 + j + tokens, here]
            taps_grad_ref[j : j + 1, here] = jnp.sum(products, axis=0, keepdims=True)
        grads_ref[:, pl.ds(pl.multiple_of(width + i * 256, 256), 256)] = low(total)

    for p in range(3):
        mix.second(0, p)
    mix.finish(0)
    hidden = down_ref.shape[1]
    for n in range(2):
        gate_up_ref[:, n, :] = shared_out[:, n * hidden : (n + 1) * hidden]
    down_ref[...] = shared_out[:, 2 * hidden :]
    shared.end()
    mix.end()
    results.wait()


def mixer_back(
    lefts,
    rights,
    home,
    position,
    add,
    resid,
    scale,
    weights,
    z,
    gate_scale,
    y,
    x,
    bc,
    conv,
    pre,
    step_raw,
    table,
    start,
    res,
    collective,
):
    tokens, model = resid.shape
    rows = model // 64
    width = x.shape[1]
    hidden = rights[1].shape[1] // 3
    size, lanes = start.shape[1], step_raw.shape[1]
    each, channels, mid = width // 64, width + 2 * size, tokens // 2
    f32, bf16 = jnp.float32, jnp.bfloat16
    vmem, hbm = pl.BlockSpec(memory_space=pltpu.VMEM), pl.BlockSpec(memory_space=pl.ANY)
    return call(
        mixer_back_kernel,
        out_shape=[
            jax.ShapeDtypeStruct((rows, width), f32),
            jax.ShapeDtypeStruct((rows, 2, hidden), f32),
            jax.ShapeDtypeStruct((rows, hidden), f32),
            jax.ShapeDtypeStruct((tokens, width + channels + lanes), bf16),
            jax.ShapeDtypeStruct((8, channels), f32),
            jax.ShapeDtypeStruct((8, lanes), f32),
            part_shape(HOME[0], res),
            jax.ShapeDtypeStruct((tokens, model), f32),
            jax.ShapeDtypeStruct((1, model), f32),
            jax.ShapeDtypeStruct((1, width), f32),
        ],
        in_specs=[[Lazy] * len(lefts), [Lazy] * len(rights)]
        + [Lazy, Lazy, hbm, Lazy, Lazy, hbm]
        + [Lazy] * 4
        + [vmem, Lazy, Lazy, vmem, vmem, Lazy, hbm],
        out_specs=[vmem] * 6 + [hbm, Eager, vmem, vmem],
        scratch_shapes=[
            pltpu.VMEM((model, width), bf16),
            pltpu.VMEM((tokens, model), bf16),
            pltpu.VMEM((tokens, width), f32),
            pltpu.VMEM((tokens, 128), f32),
            pltpu.VMEM((tokens, 128), f32),
            pltpu.VMEM((64, each + 8, size), bf16),
            pltpu.VMEM((64, each, size), f32),
            pltpu.VMEM((64, each + 8, size), bf16),
            pltpu.VMEM((64, each, size), f32),
            pltpu.VMEM((tokens, width), f32),
            pltpu.VMEM((tokens, width), f32),
            pltpu.VMEM((tokens, width), f32),
            pltpu.VMEM((lanes, tokens), f32),
            pltpu.VMEM((3, mid, mid), f32),
            pltpu.VMEM((3, mid, mid), f32),
            pltpu.VMEM((tokens + 8, channels), f32),
            pltpu.VMEM((tokens, 2 * size), f32),
            pltpu.VMEM((tokens, 2 * size), f32),
            pltpu.VMEM((rows, 3 * hidden), f32),
            scatter_shapes(rows, 3 * hidden),
            scatter_shapes(rows, width),
            pltpu.SemaphoreType.DMA((4,)),
            pltpu.SemaphoreType.DMA((4,)),
            pltpu.SemaphoreType.DMA((9,)),
            pltpu.SemaphoreType.DMA((2,)),
            pltpu.SemaphoreType.DMA((2, model // 256)),
            pltpu.SemaphoreType.DMA((2,)),
        ],
        compiler_params=params(collective, vmem_limit_bytes=VMEM),
        name="mixer_back",
    )(
        lefts, rights, home, position, add, resid, scale, weights, z, gate_scale, y, x, bc, conv,
        pre, step_raw, table, start, res,
    )


def input_back_kernel(
    plan,
    left,
    right,
    weights_ref,
    resid_ref,
    table_ref,
    grad_ref,
    res_ref,
    near_refs,
    position_ref,
    weight_ref,
    shared_ref,
    block_ref,
    taps_ref,
    heads_ref,
    norm_ref,
    gate_gain_ref,
    mixer_in_ref,
    state_ref,
    step_ref,
    input_ref,
    layer_ref,
    norm_first_out,
    norm_second_out,
    gate_gain_out,
    conv_main_out,
    conv_state_out,
    heads_outs,
    weights,
    mine,
    theirs,
    theirs_mix,
    home,
    named,
    weighed,
    small,
    small_got,
    small_out,
    out_ref,
    buf,
    rest,
    send,
    recv,
    small_sems,
    sems,
    home_sems,
    mix_sems,
):
    me, at = coordinates()
    head = lax.axis_index("head")
    tokens, model = resid_ref.shape
    columns = right.shape[1]
    gain_ref = table_ref.at[4:5, 0:model]
    load = pltpu.make_async_copy(weights_ref, weights, sems.at[0])
    load.start()
    announce(me, True)
    sums = Scatter(at, plan, [left], [right], out_ref, buf, rest, send, recv)
    totals = Small(at, me, small, small_out, small_got, small_sems)
    results = Spread(at, me, res_ref, home, home_sems, *HOME[1], True)
    for p in range(3):
        sums.product(p)
        if p == 0:
            await_all(True)
            results.start(HOME[1][0], HOME[1][0] + 1)
        sums.first(2, p)
    load.wait()

    start = columns - 384
    other = pl.multiple_of(start + 128 * (1 - head), 128)
    cut = 256
    swaps = []
    for c in range(0, model, cut):
        rows = slice(c, c + cut)
        total = dot_nt(right[...], weights[rows, :])
        total = total - dot_nt(right[:, pl.ds(other, 128)], weights[rows, pl.ds(other, 128)])
        mine[:, rows] = total
        swap = pltpu.make_async_remote_copy(
            src_ref=mine.at[:, pl.ds(c, cut)],
            dst_ref=theirs.at[:, pl.ds(c, cut)],
            send_sem=sems.at[1 + c // cut],
            recv_sem=sems.at[1 + (model + c) // cut],
            device_id={"head": 1 - head},
        )
        swap.start()
        swaps.append(swap)
    for p in range(3):
        sums.second(2, p)
    square = jnp.zeros((tokens, 1), jnp.float32)
    inner = jnp.zeros((tokens, 1), jnp.float32)
    for n, c in enumerate(range(0, model, cut)):
        rows = slice(c, c + cut)
        swaps[n].wait()
        grad = mine[:, rows] + theirs[:, rows]
        mine[:, rows] = grad
        resid = resid_ref[:, rows].astype(jnp.float32)
        square = square + jnp.sum(resid * resid, axis=1, keepdims=True)
        inner = inner + jnp.sum(resid * gain_ref[:, rows] * grad, axis=1, keepdims=True)
    scale = lax.rsqrt(square / model + EPSILON)
    pull = scale * scale * scale * (inner / model)
    tiles, inner_tiles = model // 128, gate_gain_ref.shape[1] // 128
    channel_tiles = taps_ref.shape[1] // 128
    small[...] = jnp.zeros_like(small)

    def put_small(row, value):
        small[row // 8, row % 8 : row % 8 + 1, :] = value

    for tile in range(tiles):
        put_small(tiles + tile, norm_ref[:, tile * 128 : (tile + 1) * 128])
    for tile in range(inner_tiles):
        put_small(2 * tiles + tile, gate_gain_ref[:, tile * 128 : (tile + 1) * 128])
    taps_row = 2 * tiles + inner_tiles
    for tap in range(4):
        for tile in range(channel_tiles):
            row = taps_row + tap * channel_tiles + tile
            put_small(row, taps_ref[tap : tap + 1, tile * 128 : (tile + 1) * 128])
    heads_row = taps_row + 4 * channel_tiles
    for n in range(3):
        put_small(heads_row + n, heads_ref[n : n + 1, :])
    for c in range(0, model, cut):
        rows = slice(c, c + cut)
        grad = mine[:, rows]
        resid = resid_ref[:, rows].astype(jnp.float32)
        input_ref[:, rows] = grad_ref[:, rows] + scale * gain_ref[:, rows] * grad - resid * pull
        gain_grad = jnp.sum(grad * resid * scale, axis=0, keepdims=True)
        for tile in range(c // 128, (c + cut) // 128):
            at_tile = tile * 128 - c
            put_small(tile, gain_grad[:, at_tile : at_tile + 128])
    totals.begin()
    results.start(HOME[1][0] + 1, HOME[1][0] + 2)
    input_ref.flush()
    sums.finish(2)
    totals.middle()
    results.start(HOME[1][0] + 2, HOME[1][0] + 3)
    mine[...] = shared_ref[...]
    slots = home.shape[1]

    def mix(span, rows_ref):
        @pl.loop(*span)
        def _(g):
            for n, (_, expert) in enumerate(Ways(at).group(g)):
                named[n : n + 1, :] = position_ref[pl.ds(expert, 1), :]
                weighed[n : n + 1, :] = weight_ref[pl.ds(expert, 1), :]
            chosen = chosen_slots(named[...], slots)
            weighted = chosen.reshape(8, slots, -1) * weighed[...][:, None, :]
            high, less = split(weighted.reshape(chosen.shape), 2)
            here = pl.ds(pl.multiple_of((g - span[0]) * 8, 8), 8)
            rows = rows_ref[here].reshape(8 * slots, model)
            mine[...] += dot_tn(high, rows) + dot_tn(less, rows)

    ready(position_ref, weight_ref, *near_refs)
    for span, near_ref in zip(HOME, near_refs):
        mix(span, near_ref)
    for p in range(3):
        sums.second(1, p)
    results.start(HOME[1][0] + 3, HOME[1][1])
    results.arrived(HOME[1][0], HOME[1][0] + 2)
    mix((HOME[1][0], HOME[1][0] + 2), home)
    sums.finish(1)
    for p in range(3):
        sums.second(0, p)
    results.arrived(HOME[1][0] + 2, HOME[1][1])
    mix((HOME[1][0] + 2, HOME[1][1]), home.at[pl.ds(16, home.shape[0] - 16)])
    pair = PairSum(mine, theirs_mix, mix_sems, cut)
    for n in range(pair.count):
        pair.copy(n).start()
    sums.finish(0)
    for n in range(pair.count):
        cols = slice(n * cut, (n + 1) * cut)
        pair.copy(n).wait()
        layer_ref[:, cols] = low(block_ref[:, cols] + (mine[:, cols] + theirs_mix[:, cols]))
    totals.end()

    def get_small(row):
        return small_out[row // 8, row % 8 : row % 8 + 1, :]

    for tile in range(tiles):
        norm_first_out[tile : tile + 1, :] = get_small(tile)
        norm_second_out[tile : tile + 1, :] = get_small(tiles + tile)
    for tile in range(inner_tiles):
        gate_gain_out[tile : tile + 1, :] = get_small(2 * tiles + tile)
    for tap in range(4):
        for tile in range(channel_tiles):
            value = get_small(taps_row + tap * channel_tiles + tile)
            if tile < inner_tiles:
                conv_main_out[tap : tap + 1, tile * 128 : (tile + 1) * 128] = value
            else:
                start = (tile - inner_tiles) * 128
                conv_state_out[tap : tap + 1, start : start + 128] = value
    for n, heads_out in enumerate(heads_outs):
        heads_out[...] = get_small(heads_row + n)[:, : heads_out.shape[1]]
    results.sent()
    inner = mixer_in_ref.shape[2]
    for n in range(2):
        mixer_in_ref[:, n, :] = out_ref[:, n * inner : (n + 1) * inner]
    wide = 2 * inner + state_ref.shape[1]
    state_ref[...] = out_ref[:, 2 * inner : wide]
    step_ref[...] = out_ref[:, wide : wide + 128][:, : step_ref.shape[1]]
    sums.end()


def input_back(
    left,
    right,
    plan,
    weights,
    resid,
    table,
    grad,
    res,
    near,
    position,
    weight,
    shared,
    block,
    taps,
    heads,
    norm,
    gate_gain,
    heads_dev,
    collective,
):
    tokens, model = resid.shape
    columns = right.shape[1]
    rows = model // 64
    inner, channels = gate_gain.shape[1], taps.shape[1]
    f32 = jnp.float32
    vmem, hbm = pl.BlockSpec(memory_space=pltpu.VMEM), pl.BlockSpec(memory_space=pl.ANY)
    return call(
        functools.partial(input_back_kernel, plan),
        out_shape=[
            jax.ShapeDtypeStruct((rows, 2, inner), f32),
            jax.ShapeDtypeStruct((rows, channels - inner), f32),
            jax.ShapeDtypeStruct((rows, heads_dev), f32),
            jax.ShapeDtypeStruct((tokens, model), f32),
            jax.ShapeDtypeStruct((tokens, model), jnp.bfloat16),
            jax.ShapeDtypeStruct((model // 128, 128), f32),
            jax.ShapeDtypeStruct((model // 128, 128), f32),
            jax.ShapeDtypeStruct((inner // 128, 128), f32),
            jax.ShapeDtypeStruct((4, inner), f32),
            jax.ShapeDtypeStruct((4, channels - inner), f32),
            [jax.ShapeDtypeStruct((1, heads_dev), f32)] * 3,
        ],
        in_specs=[vmem, vmem, hbm, Lazy, vmem, Lazy] + [hbm, [Lazy] * len(near)] + [Lazy] * 8,
        out_specs=[vmem] * 3 + [Eager] * 2 + [vmem] * 5 + [[vmem] * 3],
        scratch_shapes=[
            pltpu.VMEM(weights.shape, weights.dtype),
            pltpu.VMEM((tokens, model), f32),
            pltpu.VMEM((tokens, model), f32),
            pltpu.VMEM((tokens, model), f32),
            pltpu.VMEM(part_shape(HOME[1], res).shape, res.dtype),
            pltpu.VMEM((8, tokens), f32),
            pltpu.VMEM((8, tokens), f32),
            pltpu.VMEM((64, 8, 128), f32),
            pltpu.VMEM((64, 8, 128), f32),
            pltpu.VMEM((64, 8, 128), f32),
            pltpu.VMEM((rows, columns), f32),
        ]
        + scatter_shapes(rows, columns)
        + [pltpu.SemaphoreType.DMA((4,)), pltpu.SemaphoreType.DMA((1 + 2 * model // 256,))]
        + [pltpu.SemaphoreType.DMA((9,)), pltpu.SemaphoreType.DMA((2, model // 256))],
        compiler_params=params(collective, vmem_limit_bytes=VMEM),
        name="input_back",
    )(
        left, right, weights, resid, table, grad, res, near, position, weight, shared, block,
        taps, heads, norm, gate_gain,
    )


class Gather:
    def __init__(self, at, x_ref, out_ref, send, recv, local_sem):
        self.at, self.x_ref, self.out_ref, self.send, self.recv = at, x_ref, out_ref, send, recv
        self.third, self.half = parts_of(out_ref.shape[4])
        if x_ref is not None:
            self.own = pltpu.make_async_copy(x_ref, out_ref.at[at[0], at[1], at[2]], local_sem)
        self.copies = {}

    def put(self, source, here, phase, p, kind, by):
        copy = pltpu.make_async_remote_copy(
            src_ref=source,
            dst_ref=self.out_ref.at[here],
            send_sem=self.send.at[phase, p, kind],
            recv_sem=self.recv.at[phase, p, kind],
            device_id={"seq": seq_of(moved(self.at, ORDERS[p][phase], by))},
        )
        copy.start()
        self.copies[phase, p, kind] = copy

    def first(self, phase):
        if phase == 1:
            self.own.wait()
        if phase == 0:
            self.own.start()
        elif (phase - 1, 0, 2) in self.copies:
            self.arrived(phase - 1)
        for p, order in enumerate(ORDERS):
            cols = pl.ds(p * self.third, self.third)
            here = region(self.at, order, phase, self.at[order[phase]], cols)
            source = self.x_ref.at[:, cols] if phase == 0 else self.out_ref.at[here]
            for kind, by in enumerate((1, 3)):
                self.put(source, here, phase, p, kind, by)

    def second(self, phase):
        for p, order in enumerate(ORDERS):
            for kind, by in enumerate((1, 3)):
                start, length = p * self.third, self.half
                if kind:
                    start, length = start + self.half, self.third - self.half
                there = region(
                    self.at, order, phase, (self.at[order[phase]] - by) % 4, pl.ds(start, length)
                )
                self.copies[phase, p, kind].wait_recv()
                self.put(self.out_ref.at[there], there, phase, p, 2 + kind, by)

    def arrived(self, phase):
        for p in range(3):
            for kind in (2, 3):
                self.copies[phase, p, kind].wait_recv()

    def end(self):
        for copy in self.copies.values():
            copy.wait_send()


def gather_shapes():
    return [
        pltpu.SemaphoreType.DMA((3, 3, 4)),
        pltpu.SemaphoreType.DMA((3, 3, 4)),
        pltpu.SemaphoreType.DMA,
    ]


def slot_tables(routes_ref, weights_ref, position_ref, weight_ref):
    experts, tokens = position_ref.shape
    expert = lax.broadcasted_iota(jnp.int32, (experts, tokens), 0)
    named = jnp.zeros((experts, tokens), jnp.float32)
    weight = jnp.zeros((experts, tokens), jnp.float32)
    for k in range(routes_ref.shape[0]):
        hit = expert == routes_ref[k : k + 1, :]
        named = named + jnp.where(hit, 1.0, 0.0)
        weight = weight + jnp.where(hit, weights_ref[k : k + 1, :], 0.0)
    earlier = low(triangle(tokens, lambda t, s: jnp.where(t < s, 1.0, 0.0)))
    position_ref[...] = jnp.where(named > 0.0, dot_nn(low(named), earlier), -1.0)
    weight_ref[...] = weight


def chosen_slots(position, slots):
    count, tokens = position.shape
    number = lax.broadcasted_iota(jnp.int32, (count, slots, tokens), 1)
    number = (number + slots * lax.axis_index("head")).astype(jnp.float32)
    return jnp.where(position[:, None, :] == number, 1.0, 0.0).reshape(count * slots, tokens)


def gather_kernel(
    early_refs,
    late_refs,
    wide_in,
    layer_ref,
    routes_ref,
    weights_ref,
    grads_ref,
    vectors,
    out_ref,
    late_out,
    before_ref,
    position_ref,
    weight_ref,
    rows,
    slots_ref,
    table_ref,
    wide_ref,
    x_ref,
    late_ref,
    send,
    recv,
    local_sem,
    late_send,
    late_recv,
    late_sem,
    sems,
    out_sems,
):
    me, at = coordinates()
    announce(me, False)
    def beside(target, sources):
        column = 0
        for source in sources:
            value = source[...]
            if value.ndim == 3:
                value = value.astype(jnp.float32)
                halves = [low(value[:, n, :]) for n in range(2)]
            else:
                halves = [value]
            for half in halves:
                target[:, column : column + half.shape[1]] = half
                column = column + half.shape[1]

    rows_step = x_ref.shape[1] - 128
    x_ref[:, rows_step:] = jnp.zeros((x_ref.shape[0], 128), x_ref.dtype)
    beside(x_ref, early_refs)
    beside(late_ref, late_refs)
    gather = Gather(at, x_ref, out_ref, send, recv, local_sem)
    late = Gather(at, late_ref, late_out, late_send, late_recv, late_sem)
    conv_main, conv_state, gains, numbers = vectors
    width, heads = conv_main.shape[1], numbers[0].shape[1]
    table_ref[...] = jnp.zeros_like(table_ref)
    table_ref[0:4, 0:width] = conv_main[...]
    table_ref[0:4, width:] = conv_state[...]
    for n, gain in enumerate(gains):
        for tile in range(gain.shape[0]):
            table_ref[4 + n : 5 + n, tile * 128 : (tile + 1) * 128] = gain[tile : tile + 1, :]
    for n, number in enumerate(numbers):
        table_ref[8 + n : 9 + n, 0:heads] = number[...]
    slot_tables(routes_ref, weights_ref, position_ref, weight_ref)
    grads = grads_ref[...]
    slots, step = rows.shape[1], 16

    @pl.loop(0, rows.shape[0] // step)
    def _(i):
        here = pl.ds(pl.multiple_of(i * step, step), step)
        chosen = chosen_slots(position_ref[here, :], slots)
        weighted = chosen.reshape(step, slots, -1) * weight_ref[here, :][:, None, :]
        scale = jnp.sum(weighted.reshape(chosen.shape), axis=1, keepdims=True)
        rows[here] = low(dot_nn(low(chosen), grads) * scale).reshape(step, slots, -1)

    await_all(False)
    gather.first(0)
    late.first(0)
    edge = pltpu.make_async_remote_copy(
        src_ref=layer_ref.at[pl.ds(layer_ref.shape[0] - 16, 16)],
        dst_ref=before_ref,
        send_sem=sems.at[0],
        recv_sem=sems.at[1],
        device_id={"seq": (me + 1) % 64},
    )
    edge.start()
    out = Spread(at, me, rows, slots_ref, out_sems, *OUT[0], False)
    gather.second(0)
    late.second(0)
    out.start(0, 1)
    gather.first(1)
    late.first(1)
    out.start(1, 2)
    gather.second(1)
    late.second(1)
    out.start(2, 3)
    gather.first(2)
    gather.second(2)
    out.start(3, OUT[0][1])
    ready(wide_in)
    hidden = wide_in.shape[2]

    @pl.loop(0, wide_in.shape[0] // 64)
    def _(i):
        here = pl.ds(pl.multiple_of(i * 64, 64), 64)
        value = wide_in[here].astype(jnp.float32)
        for n in range(2):
            wide_ref[here, n * hidden : (n + 1) * hidden] = low(value[:, n, :])

    late.arrived(1)
    late.end()
    gather.arrived(2)
    edge.wait()
    gather.end()
    out.wait()


def gather_rows(
    early, late, wide, layer_in, routes, route_weights, grads, vectors, experts, slots, collective
):
    rows = early[0].shape[0]
    bf16 = early[0].dtype
    count = lambda arrays: sum(array.size // rows for array in arrays)
    columns = -(-count(early) // 128) * 128
    channels = vectors[0].shape[1] + vectors[1].shape[1]
    tokens, model = grads.shape
    grad_rows = jax.ShapeDtypeStruct((experts, slots, model), grads.dtype)
    hbm, vmem = pl.BlockSpec(memory_space=pl.ANY), pl.BlockSpec(memory_space=pltpu.VMEM)
    return call(
        gather_kernel,
        out_shape=[
            jax.ShapeDtypeStruct((4, 4, 4, rows, columns), bf16),
            jax.ShapeDtypeStruct((4, 4, 4, rows, count(late)), bf16),
            jax.ShapeDtypeStruct((16, model), layer_in.dtype),
            jax.ShapeDtypeStruct((experts, tokens), jnp.float32),
            jax.ShapeDtypeStruct((experts, tokens), jnp.float32),
            grad_rows,
            part_shape(OUT[0], grad_rows),
            jax.ShapeDtypeStruct((16, channels), jnp.float32),
            jax.ShapeDtypeStruct((wide.shape[0], 2 * wide.shape[2]), bf16),
        ],
        in_specs=[[vmem] * len(early), [vmem] * len(late), Lazy, hbm, vmem, vmem, Lazy, [vmem, vmem, [vmem] * 3, [vmem] * 3]],
        out_specs=[hbm, hbm, hbm, vmem, vmem, vmem, hbm, vmem, vmem],
        scratch_shapes=[pltpu.VMEM((rows, columns), bf16), pltpu.VMEM((rows, count(late)), bf16)]
        + gather_shapes()
        + gather_shapes() + [pltpu.SemaphoreType.DMA((2,))]
        + [pltpu.SemaphoreType.DMA((9,))],
        compiler_params=params(collective, vmem_limit_bytes=VMEM),
        name="gather_rows",
    )(early, late, wide, layer_in, routes.T, route_weights.T, grads, vectors)


def mixer_kernel(
    layer_ref,
    edge_ref,
    table_ref,
    weights_ref,
    _,
    rows_ref,
    normed_ref,
    z_ref,
    x_ref,
    bc_ref,
    conv_ref,
    pre_ref,
    step_raw_ref,
    start_ref,
    y_ref,
    gated_ref,
    scale_ref,
    gathered_ref,
    slots_ref,
    weights,
    normed,
    message,
    got,
    made,
    spread,
    cum_rows,
    scores,
    mine,
    theirs,
    load_sems,
    scan_sems,
    pair_sems,
    send,
    recv,
    slot_sems,
):
    me, at = coordinates()
    head = lax.axis_index("head")
    tokens, model = layer_ref.shape
    width = x_ref.shape[1]
    size = bc_ref.shape[1] // 2
    lanes = step_raw_ref.shape[1]
    each = width // 64
    mid = tokens // 2
    cut = 384
    norm_ref, gain_ref = table_ref.at[4:5, 0:model], table_ref.at[6:7, 0:width]
    numbers_ref, taps_ref = table_ref.at[8:16, 0:lanes], table_ref

    def load(n):
        cols = pl.ds(pl.multiple_of(n * cut, 128), cut)
        return pltpu.make_async_copy(weights_ref.at[:, cols], weights.at[:, cols], load_sems.at[n])

    for n in (8, 4, 5, 6, 7, 0, 1, 2, 3):
        load(n).start()
    announce(me, True)
    gather = Gather(at, None, gathered_ref, send, recv, None)

    def norm(rows):
        rows = rows.astype(jnp.float32)
        scale = lax.rsqrt(jnp.mean(rows * rows, axis=1, keepdims=True) + EPSILON)
        return low(rows * scale * norm_ref[...])

    before = norm(edge_ref[...]).astype(jnp.float32) * jnp.where(me == 0, 0.0, 1.0)
    normed[0:16, :] = low(before)
    normed[16 : 16 + tokens, :] = norm(layer_ref[...])
    normed_ref[...] = normed[16 : 16 + tokens, :]
    normed_ref.flush()
    await_all(True)
    gather.first(2)

    def conv(cols):
        total = jnp.zeros((tokens, cols.size), jnp.float32)
        for j in range(4):
            total = total + taps_ref[j : j + 1, cols] * pre_ref[5 + j : 5 + j + tokens, cols]
        conv_ref[:, cols] = total
        return total * jax.nn.sigmoid(total)

    load(8).wait()
    last = dot_nn(normed[...], weights[:, 8 * cut : 9 * cut])
    cols = pl.ds(width, 2 * size)
    pre_ref[:, cols] = last[8:, : 2 * size]
    bc_ref[...] = conv(cols)
    bc_ref.flush()
    step_raw = last[16:, 2 * size :] + numbers_ref[2:3, :]
    step_raw_ref[...] = step_raw
    step = jax.nn.softplus(step_raw)
    earlier = low(triangle(tokens, lambda t, s: jnp.where(t >= s, 1.0, 0.0)))
    cum = dot_split(earlier, -step * numbers_ref[0:1, :], 3)
    cum_rows[...] = cum.T
    tail = cum[tokens - 1 : tokens, :]
    spreader = head_spread(lanes, width, 64)
    spread[...] = split_dot(jnp.exp(tail - cum) * step, spreader, 2)
    held, read = bc_ref[:, :size], bc_ref[:, size:]

    @pl.loop(0, 4)
    def _(i):
        load(4 + i).wait()
        from_cols = pl.ds(pl.multiple_of((4 + i) * cut, 128), cut)
        here = pl.ds(pl.multiple_of(i * cut, 128), cut)
        pre_ref[:, here] = dot_nn(normed[...], weights[:, from_cols])[8:]
        x = conv(here)
        x_ref[:, here] = x
        made_rows = dot_three(x * spread[:, here], held, dot_tn)
        made_rows = made_rows.reshape(cut // each, each, size)
        message[pl.ds(i * (cut // each), cut // each)] = scan_rows(made_rows, jnp.exp(tail))

    for ref in (x_ref, pre_ref, conv_ref):
        ref.flush()
    scan = Scan(False, at, me, message, start_ref, got, made, scan_sems)
    scan.begin()

    @pl.loop(0, 4)
    def _(i):
        load(i).wait()
        here = pl.ds(pl.multiple_of(i * cut, 128), cut)
        z_ref[:, here] = dot_nn(normed[16 : 16 + tokens, :], weights[:, here])

    z_ref.flush()
    scan.middle()
    out = Spread(at, me, rows_ref, slots_ref, slot_sems, *OUT[1], False)
    gather.second(2)
    out.start()

    spread[...] = split_dot(step, spreader, 2)
    blocks = ((0, 0), (1, 0), (1, 1))
    for n, (t, s) in enumerate(blocks):
        rows, columns = slice(t * mid, (t + 1) * mid), slice(s * mid, (s + 1) * mid)
        scores[n] = dot_three(read[rows], held[columns], dot_nt)
    causal = triangle(mid, lambda t, s: t >= s)
    second_head = lax.broadcasted_iota(jnp.int32, (tokens, 128), 1) >= 64

    @pl.loop(0, width // 128)
    def _(i):
        here = pl.ds(pl.multiple_of(i * 128, 128), 128)
        values, values_less = split(x_ref[:, here] * spread[:, here], 2)
        results = []
        for which in range(2):
            row = cum_rows[pl.ds(2 * i + which, 1), :]
            column = jnp.broadcast_to(row, (128, tokens)).T
            total = [None, None]
            for n, (t, s) in enumerate(blocks):
                columns = slice(s * mid, (s + 1) * mid)
                decay = jnp.exp(column[t * mid : (t + 1) * mid] - row[:, columns])
                if s == t:
                    decay = jnp.where(causal, decay, 0.0)
                mixing, mixing_less = split(decay * scores[n], 2)
                part = dot_nn(mixing, values[columns]) + dot_nn(mixing_less, values[columns])
                part = part + dot_nn(mixing, values_less[columns])
                total[t] = part if total[t] is None else total[t] + part
            results.append(total)
        for t in range(2):
            rows = slice(t * mid, (t + 1) * mid)
            y_ref[rows, here] = jnp.where(second_head[rows], results[1][t], results[0][t])

    scan.end()
    skip = split_dot(jnp.broadcast_to(numbers_ref[1:2, :], (8, lanes)), spreader, 2)[0:1, :]
    carry = split_dot(jnp.exp(cum), spreader, 2)
    square = jnp.zeros((tokens, 1), jnp.float32)
    for c in range(0, width, cut):
        here = slice(c, c + cut)
        start = start_ref[c // each : (c + cut) // each].reshape(cut, size)
        through = dot_three(read, start, dot_nt)
        y = y_ref[:, here] + carry[:, here] * through + skip[:, here] * x_ref[:, here]
        y_ref[:, here] = y
        z = z_ref[:, here]
        gated = y * (z * jax.nn.sigmoid(z))
        spread[:, here] = gated
        square = square + jnp.sum(gated * gated, axis=1, keepdims=True)
    y_ref.flush()
    mine[...] = jnp.broadcast_to(square, mine.shape)
    swap = pltpu.make_async_remote_copy(
        src_ref=mine,
        dst_ref=theirs,
        send_sem=pair_sems.at[0],
        recv_sem=pair_sems.at[1],
        device_id={"head": 1 - head},
    )
    swap.start()
    swap.wait()
    scale = lax.rsqrt((mine[...] + theirs[...]) / (2 * width) + EPSILON)
    scale_ref[...] = scale
    for c in range(0, width, cut):
        here = slice(c, c + cut)
        gated_ref[:, here] = low(spread[:, here] * scale[:, 0:1] * gain_ref[:, here])
    gather.arrived(2)
    gather.end()
    out.wait()


def mixer(layer_in, edge, table, weights, width, late, grad_rows, collective):
    tokens, model = layer_in.shape
    channels, lanes = table.shape[1], 128
    size = (channels - width) // 2
    each, mid = width // 64, tokens // 2
    f32, bf16 = jnp.float32, jnp.bfloat16
    vmem, hbm = pl.BlockSpec(memory_space=pltpu.VMEM), pl.BlockSpec(memory_space=pl.ANY)
    out = [
        ((tokens, model), bf16),
        ((tokens, width), f32),
        ((tokens, width), f32),
        ((tokens, 2 * size), f32),
        ((tokens, channels), f32),
        ((tokens + 8, channels), f32),
        ((tokens, lanes), f32),
        ((64, each, size), f32),
        ((tokens, width), f32),
        ((tokens, width), bf16),
        ((tokens, lanes), f32),
        (late.shape, bf16),
        (part_shape(OUT[1], grad_rows).shape, bf16),
    ]
    return call(
        mixer_kernel,
        out_shape=[jax.ShapeDtypeStruct(*shape) for shape in out],
        in_specs=[vmem, vmem, vmem, hbm, hbm, hbm],
        out_specs=[Eager] * 6 + [vmem] * 2 + [Eager] * 2 + [vmem] + [hbm] * 2,
        scratch_shapes=[
            pltpu.VMEM(weights.shape, bf16),
            pltpu.VMEM((tokens + 16, model), bf16),
            pltpu.VMEM((64, each + 8, size), bf16),
            pltpu.VMEM((64, each + 8, size), bf16),
            pltpu.VMEM((64, each, size), f32),
            pltpu.VMEM((tokens, width), f32),
            pltpu.VMEM((lanes, tokens), f32),
            pltpu.VMEM((3, mid, mid), f32),
            pltpu.VMEM((tokens, lanes), f32),
            pltpu.VMEM((tokens, lanes), f32),
            pltpu.SemaphoreType.DMA((9,)),
            pltpu.SemaphoreType.DMA((4,)),
            pltpu.SemaphoreType.DMA((2,)),
        ]
        + gather_shapes()[:2]
        + [pltpu.SemaphoreType.DMA((9,))],
        input_output_aliases={4: len(out) - 2},
        compiler_params=params(collective, vmem_limit_bytes=VMEM),
        name="mixer",
    )(layer_in, edge, table, weights, late, grad_rows)


def per_device(
    layer_in,
    norm_first,
    mixer_in,
    state_proj,
    step_proj,
    step_bias,
    conv_main,
    conv_state,
    decay_rate,
    skip_gain,
    gate_gain,
    mixer_out,
    norm_second,
    shared_gate_up,
    shared_down,
    expert_gate_up,
    expert_down,
    routes,
    route_weights,
    grad_out,
):
    tokens, model_width = layer_in.shape
    inner_dev = mixer_in.shape[2]
    state_size = state_proj.shape[1] // 2
    heads_dev = step_proj.shape[1]
    conv_taps = conv_main.shape[0]
    shared_dev = shared_down.shape[1]
    local_experts = expert_gate_up.shape[0]
    experts_all = local_experts * lax.axis_size("seq")
    choices_per = routes.shape[1]
    capacity = max(2, tokens * choices_per * 4 // (3 * experts_all))
    slots_dev = capacity // lax.axis_size("head")
    lanes = 128
    vectors = [
        conv_main,
        conv_state,
        [gain.reshape(-1, 128) for gain in (norm_first, norm_second, gate_gain)],
        [number[None] for number in (decay_rate, skip_gain, step_bias)],
    ]
    gathered, late_rows, edge, position, slot_weight, grads_out, grads_first, table, gate_up = gather_rows(
        [mixer_in, state_proj, step_proj],
        [mixer_out, shared_gate_up, shared_down],
        expert_gate_up.reshape(expert_gate_up.shape[1:]),
        layer_in,
        routes,
        route_weights,
        grad_out,
        vectors,
        experts_all,
        slots_dev,
        0,
    )
    weights_in = gathered.reshape(model_width, -1)
    (
        normed,
        gate_z,
        heads_x,
        state_both,
        conv_sum,
        pre,
        step_raw,
        state_start,
        ssd,
        normed_gate,
        gate_scale,
        gathered,
        grads_second,
    ) = mixer(
        layer_in,
        edge,
        table,
        weights_in,
        inner_dev,
        late_rows,
        grads_out,
        1,
    )
    weights_late = gathered.reshape(model_width, -1)
    (
        grad_home,
        res_sums,
        expert_gate_up_grad,
        expert_down_grad,
        shared_part,
        shared_back,
        shared_right,
        residual,
        normed_second,
        scale_second,
    ) = experts(
        normed_gate,
        weights_late,
        layer_in,
        table,
        position,
        [grads_first, grads_second],
        grads_out,
        gate_up,
        expert_down.reshape(-1, model_width),
        grad_out,
        slots_dev,
        2,
    )
    (
        mixer_out_grad,
        shared_gate_up_grad,
        shared_down_grad,
        right_grads,
        taps_grad,
        heads_grad,
        home_near,
        grad_resid,
        norm_second_grad,
        gate_gain_grad,
    ) = mixer_back(
        [normed_second, grad_out],
        [normed_gate, shared_right],
        grad_home,
        position,
        shared_back,
        residual,
        scale_second,
        weights_late,
        gate_z,
        gate_scale,
        ssd,
        heads_x,
        state_both,
        conv_sum,
        pre,
        step_raw,
        table,
        state_start.reshape(inner_dev, state_size),
        res_sums,
        3,
    )
    (
        mixer_in_grad,
        state_proj_grad,
        step_proj_grad,
        input_grad,
        layer_out,
        norm_first_sum,
        norm_second_sum,
        gate_gain_sum,
        conv_main_grad,
        conv_state_grad,
        (skip_gain_grad, decay_rate_grad, step_bias_grad),
    ) = input_back(
        normed,
        right_grads,
        tuple(((0, 0, start, start, 1152),) for start in (0, 1152, 2304)),
        weights_in,
        layer_in,
        table,
        grad_resid,
        res_sums,
        [home_near],
        position,
        slot_weight,
        shared_part,
        residual,
        taps_grad,
        heads_grad,
        norm_second_grad,
        gate_gain_grad,
        heads_dev,
        4,
    )
    (
        layer_out,
        input_grad,
        expert_gate_up_grad,
        expert_down_grad,
        mixer_in_grad,
        state_proj_grad,
        step_proj_grad,
        norm_first_sum,
        norm_second_sum,
        gate_gain_sum,
        conv_main_grad,
        conv_state_grad,
        skip_gain_grad,
        decay_rate_grad,
        step_bias_grad,
        mixer_out_grad,
        shared_gate_up_grad,
        shared_down_grad,
    ) = emit(
        [layer_out, input_grad, expert_gate_up_grad, expert_down_grad],
        [
            mixer_in_grad,
            state_proj_grad,
            step_proj_grad,
            norm_first_sum,
            norm_second_sum,
            gate_gain_sum,
            conv_main_grad,
            conv_state_grad,
            skip_gain_grad,
            decay_rate_grad,
            step_bias_grad,
            mixer_out_grad,
            shared_gate_up_grad,
            shared_down_grad,
        ],
    )
    expert_gate_up_grad = expert_gate_up_grad.reshape(model_width, -1, 2, lanes)
    expert_gate_up_grad = expert_gate_up_grad.transpose(0, 2, 1, 3).reshape(expert_gate_up.shape)
    return (
        layer_out,
        input_grad,
        norm_first_sum.reshape(-1),
        mixer_in_grad,
        state_proj_grad,
        step_proj_grad,
        step_bias_grad.reshape(-1),
        conv_main_grad,
        conv_state_grad,
        decay_rate_grad.reshape(-1),
        skip_gain_grad.reshape(-1),
        gate_gain_sum.reshape(-1),
        mixer_out_grad,
        norm_second_sum.reshape(-1),
        shared_gate_up_grad,
        shared_down_grad,
        expert_gate_up_grad,
        expert_down_grad[None],
    )


def solution(mesh):
    placed = (
        P("seq", None),
        P(),
        P("seq", None, "head"),
        P("seq", None),
        P("seq", "head"),
        P("head"),
        P(None, "head"),
        P(),
        P("head"),
        P("head"),
        P("head"),
        P("seq", "head"),
        P(),
        P("seq", None, "head"),
        P("seq", "head"),
        P("seq", None, None, "head"),
        P("seq", "head", None),
        P("seq", None),
        P("seq", None),
        P("seq", None),
    )
    return jax.shard_map(
        per_device,
        mesh=mesh,
        in_specs=placed,
        out_specs=(
            P("seq", None),
            P("seq", None),
            P(),
            P("seq", None, "head"),
            P("seq", None),
            P("seq", "head"),
            P("head"),
            P(None, "head"),
            P(),
            P("head"),
            P("head"),
            P("head"),
            P("seq", "head"),
            P(),
            P("seq", None, "head"),
            P("seq", "head"),
            P("seq", None, None, "head"),
            P("seq", "head", None),
        ),
        check_vma=False,
    )
```

```python
import functools
import jax
import jax.numpy as jnp
from jax import lax
from jax.experimental import pallas as pl
from jax.experimental.pallas import tpu as pltpu
from jax.sharding import PartitionSpec as P

ORDERS = ((0, 1, 2), (1, 2, 0), (2, 0, 1))
VMEM = 62 << 20
EPSILON = 1e-05


def coordinates():
    me = lax.axis_index("seq")
    return me, [me // 16, (me // 4) % 4, me % 4]


def seq_of(at):
    return at[0] * 16 + at[1] * 4 + at[2]


def moved(at, axis, by):
    return [(c + by) % 4 if i == axis else c for i, c in enumerate(at)]


def announce(me, with_sibling):
    barrier = pltpu.get_barrier_semaphore()

    @pl.loop(1, 64)
    def _(k):
        pl.semaphore_signal(barrier, inc=1, device_id={"seq": lax.rem(me + k, 64)})

    if with_sibling:
        pl.semaphore_signal(barrier, inc=1, device_id={"head": 1 - lax.axis_index("head")})


def await_all(with_sibling):
    pl.semaphore_wait(pltpu.get_barrier_semaphore(), 64 if with_sibling else 63)


def parts_of(columns):
    third = columns // 3
    tiles = third // 128
    half = tiles // 2 * 128
    return third, half


def region(at, order, phase, value, cols):
    index = [None] * 3
    for i in range(3):
        if i < phase:
            index[order[i]] = slice(None)
        elif i == phase:
            index[order[i]] = value
        else:
            index[order[i]] = at[order[i]]
    return tuple(index) + (slice(None), cols)


class Ways:
    def __init__(self, at):
        self.at = at

    def group(self, g, back=False):
        x, z, y = self.at
        sign, lead = (-1, 8) if back else (1, 0)
        near, far = lax.rem(g, 4), g // 4
        xs = [lax.rem(x + lead + sign * a, 4) * 16 for a in range(4)]
        zs = [lax.rem(z + lead + sign * (near + a), 4) * 4 for a in range(4)]
        ys = [lax.rem(y + lead + sign * (far + a), 4) for a in range(4)]
        return [(g * 8 + n, xs[n % 4] + zs[n % 4] + ys[(n % 4 + n // 4 * 2) % 4]) for n in range(8)]

    def each(self, first, last, body, back=False):
        @pl.loop(first, last)
        def _(g):
            for n, (k, device) in enumerate(self.group(g, back)):
                if n == 0:
                    pl.when(k > 0)(functools.partial(body, k, device))
                else:
                    body(k, device)


class Lazy:
    def __init__(self, source, ref, sem):
        self.ref, self.copy = ref, pltpu.make_async_copy(source, ref, sem)
        self.shape, self.dtype = ref.shape, ref.dtype
        self.copy.start()

    def ready(self):
        if self.copy is not None:
            self.copy.wait()
            self.copy = None
        return self.ref

    @property
    def at(self):
        return self.ready().at

    def __getitem__(self, index):
        return self.ready()[index]


class Eager:
    def __init__(self, target, ref, sem):
        self.ref, self.copy, self.going = ref, pltpu.make_async_copy(ref, target, sem), False
        self.shape, self.dtype, self.at = ref.shape, ref.dtype, ref.at

    def __getitem__(self, index):
        return self.ref[index]

    def __setitem__(self, index, value):
        self.ref[index] = value

    def flush(self):
        if not self.going:
            self.going = True
            self.copy.start()


def ready(*refs):
    for ref in refs:
        if isinstance(ref, Lazy):
            ref.ready()


def call(kernel, out_shape, in_specs, out_specs, scratch_shapes, **options):
    def run(*args):
        leaves, tree = jax.tree.flatten(list(args))
        specs = tree.flatten_up_to(list(in_specs))
        shapes, out_tree = jax.tree.flatten(list(out_shape))
        out_kinds = out_tree.flatten_up_to(list(out_specs))
        lazy = [n for n, spec in enumerate(specs) if spec is Lazy]
        eager = [n for n, spec in enumerate(out_kinds) if spec is Eager]
        hbm = pl.BlockSpec(memory_space=pl.ANY)
        buffers = [pltpu.VMEM(leaves[n].shape, leaves[n].dtype) for n in lazy]
        buffers += [pltpu.VMEM(shapes[n].shape, shapes[n].dtype) for n in eager]
        buffers += [pltpu.SemaphoreType.DMA((max(1, len(lazy)),))]
        buffers += [pltpu.SemaphoreType.DMA((max(1, len(eager)),))]
        own = len(scratch_shapes)

        def body(*refs):
            ins, outs = list(refs[: len(leaves)]), list(refs[len(leaves) :][: len(shapes)])
            rest = refs[len(leaves) + len(shapes) :]
            more = rest[own:]
            for n, index in enumerate(lazy):
                ins[index] = Lazy(ins[index], more[n], more[-2].at[n])
            for n, index in enumerate(eager):
                outs[index] = Eager(outs[index], more[len(lazy) + n], more[-1].at[n])
            kernel(*tree.unflatten(ins), *out_tree.unflatten(outs), *rest[:own])
            for index in lazy:
                ins[index].ready()
            for index in eager:
                outs[index].flush()
            for index in eager:
                outs[index].copy.wait()

        out = pl.pallas_call(
            body,
            out_shape=shapes,
            in_specs=[hbm if spec is Lazy else spec for spec in specs],
            out_specs=[hbm if kind is Eager else kind for kind in out_kinds],
            scratch_shapes=list(scratch_shapes) + buffers,
            **options,
        )(*leaves)
        return out_tree.unflatten(out)

    return run


def emit_kernel(*refs):
    count = (len(refs) - 1) // 3
    sources, targets, buffers, sems = refs[:count], refs[count : 2 * count], refs[2 * count : -1], refs[-1]
    pieces = []
    for n in range(count):
        rows = sources[n].shape[0]
        parts = 4 if rows >= 256 else 1
        for part in range(parts):
            here = pl.ds(part * (rows // parts), rows // parts)
            place = buffers[n].at[here]
            come = pltpu.make_async_copy(sources[n].at[here], place, sems.at[0, n, part])
            go = pltpu.make_async_copy(place, targets[n].at[here], sems.at[1, n, part])
            come.start()
            pieces.append((come, go))
    for come, go in pieces:
        come.wait()
        go.start()
    for _, go in pieces:
        go.wait()


def emit(arrays):
    hbm = [pl.BlockSpec(memory_space=pl.ANY)] * len(arrays)
    return pl.pallas_call(
        emit_kernel,
        out_shape=[jax.ShapeDtypeStruct(array.shape, array.dtype) for array in arrays],
        in_specs=hbm,
        out_specs=hbm,
        scratch_shapes=[pltpu.VMEM(array.shape, array.dtype) for array in arrays]
        + [pltpu.SemaphoreType.DMA((2, len(arrays), 4))],
        compiler_params=pltpu.CompilerParams(vmem_limit_bytes=VMEM),
        name="emit",
    )(*arrays)


class Spread:
    def __init__(self, at, me, source, target, sems, first, last, back):
        self.at, self.me, self.source, self.target = at, me, source, target
        self.sems = sems
        self.first, self.last, self.back = first, last, back

    def start(self, first=None, last=None):
        first = self.first if first is None else first
        last = self.last if last is None else last
        if first == 0:
            own = self.source.at[0 if self.back else self.me]
            pltpu.make_async_copy(own, self.target.at[0], self.sems.at[1]).start()

        def put(k, device):
            pltpu.make_async_remote_copy(
                src_ref=self.source.at[k if self.back else device],
                dst_ref=self.target.at[k - 8 * self.first],
                send_sem=self.sems.at[0],
                recv_sem=self.sems.at[1 + k // 8],
                device_id={"seq": device},
            ).start()

        Ways(self.at).each(first, last, put, self.back)

    def arrived(self, first, last):
        for g in range(first, last):
            here = self.target.at[pl.ds(8 * (g - self.first), 8)]
            pltpu.make_async_copy(here, here, self.sems.at[1 + g]).wait()

    def sent(self):
        count = 8 * (self.last - self.first)
        here = self.target.at[pl.ds(0, count - 1 if self.first == 0 else count)]
        pltpu.make_async_copy(here, here, self.sems.at[0]).wait()

    def wait(self):
        self.arrived(self.first, self.last)
        self.sent()


OUT = ((0, 4), (4, 5), (5, 8))
HOME = ((0, 5), (5, 8))


def part_shape(span, rows):
    return jax.ShapeDtypeStruct((8 * (span[1] - span[0]),) + rows.shape[1:], rows.dtype)


def params(collective, **more):
    return pltpu.CompilerParams(collective_id=collective, has_side_effects=True, **more)


class PairSum:
    def __init__(self, mine, theirs, sems, cut):
        self.mine, self.theirs, self.sems, self.cut = mine, theirs, sems, cut
        self.count = mine.shape[1] // cut

    def copy(self, n):
        cols = pl.ds(n * self.cut, self.cut)
        return pltpu.make_async_remote_copy(
            src_ref=self.mine.at[:, cols],
            dst_ref=self.theirs.at[:, cols],
            send_sem=self.sems.at[0, n],
            recv_sem=self.sems.at[1, n],
            device_id={"head": 1 - lax.axis_index("head")},
        )


def experts_kernel(
    gated_ref,
    weights_ref,
    layer_ref,
    table_ref,
    position_ref,
    grads_refs,
    grad_rows_ref,
    gate_up_ref,
    down_ref,
    grad_out_ref,
    home_ref,
    res_ref,
    gate_up_grad_ref,
    down_grad_ref,
    shared_ref,
    back_ref,
    right_ref,
    resid_ref,
    normed_ref,
    scale_ref,
    rows_ref,
    grads_here,
    mine,
    theirs,
    slot_in,
    grad_slots,
    theirs_x,
    theirs_y,
    sums,
    wide_grad,
    weights,
    load_sems,
    pair_sems,
    out_sems,
    send,
    home_send,
    home_recv,
    sems,
):
    me, at = coordinates()
    head = lax.axis_index("head")
    sibling = {"head": 1 - head}
    names = ("recv", "fwd_send", "fwd_recv", "kept", "given_send", "given_recv")
    names += ("x_send", "x_recv", "y_send", "y_recv")
    sem = {name: sems.at[n] for n, name in enumerate(names)}
    announce(me, True)
    shared_hidden = right_ref.shape[1] // 3
    tokens, model = layer_ref.shape
    inner = gated_ref.shape[1]
    loads = []
    for n, cols in enumerate((pl.ds(0, inner), pl.ds(inner, 3 * shared_hidden))):
        loads.append(
            pltpu.make_async_copy(weights_ref.at[:, cols], weights.at[:, cols], load_sems.at[n])
        )
        loads[n].start()
    norm_ref = table_ref.at[5:6, 0:model]
    wide_grad[...] = jnp.zeros_like(wide_grad)
    down_grad_ref[...] = jnp.zeros_like(down_grad_ref)
    ways = Ways(at)
    await_all(True)
    out = Spread(at, me, grad_rows_ref, grads_here, out_sems, *OUT[2], False)

    def group(c):
        return pl.ds(pl.multiple_of(c * 8, 8), 8)

    def given(c, source=None):
        there = grad_slots.at[group(c), head]
        return pltpu.make_async_remote_copy(
            src_ref=there if source is None else source,
            dst_ref=there,
            send_sem=sem["given_send"].at[c],
            recv_sem=sem["given_recv"].at[c],
            device_id=sibling,
        )

    def kept(c, source=None):
        there = grad_slots.at[group(c), head]
        return pltpu.make_async_copy(there if source is None else source, there, sem["kept"].at[c])

    def forward(c):
        return pltpu.make_async_remote_copy(
            src_ref=slot_in.at[group(c), head],
            dst_ref=slot_in.at[group(c), head],
            send_sem=sem["fwd_send"].at[c],
            recv_sem=sem["fwd_recv"].at[c],
            device_id=sibling,
        )

    def swap(c, source, target, name):
        return pltpu.make_async_remote_copy(
            src_ref=source.at[group(c), 1 - head],
            dst_ref=target.at[group(c)],
            send_sem=sem[name + "_send"].at[c],
            recv_sem=sem[name + "_recv"].at[c],
            device_id=sibling,
        )

    for (first, last), grads_ref in zip(OUT, grads_refs):
        for c in range(first, last):
            source = grads_ref.at[pl.ds(8 * (c - first), 8)]
            kept(c, source).start()
            given(c, source).start()

    out.start()

    cut = 256
    pair = PairSum(mine, theirs, pair_sems, cut)
    loads[0].wait()
    gated = gated_ref[...]
    for n in range(pair.count):
        rows = slice(n * cut, (n + 1) * cut)
        mine[:, rows] = dot_nt(gated, weights[rows, 0:inner])
        pair.copy(n).start()
    loads[1].wait()
    both = slice(inner, inner + 2 * shared_hidden)
    less = slice(inner + 2 * shared_hidden, inner + 3 * shared_hidden)
    shared_grad_hid = dot_nn(grad_out_ref[...], weights[:, less])
    square = jnp.zeros((tokens, 1), jnp.float32)
    for n in range(pair.count):
        rows = slice(n * cut, (n + 1) * cut)
        pair.copy(n).wait()
        resid = layer_ref[:, rows].astype(jnp.float32) + (mine[:, rows] + theirs[:, rows])
        resid_ref[:, rows] = resid
        square = square + jnp.sum(resid * resid, axis=1, keepdims=True)
    scale = lax.rsqrt(square / model + EPSILON)
    scale_ref[...] = jnp.broadcast_to(scale, scale_ref.shape)
    for n in range(pair.count):
        rows = slice(n * cut, (n + 1) * cut)
        normed_ref[:, rows] = low(resid_ref[:, rows] * scale * norm_ref[:, rows])
    resid_ref.flush()
    normed_ref.flush()
    ready(position_ref)
    normed = normed_ref[...]
    slots, step = rows_ref.shape[1], 16

    @pl.loop(0, rows_ref.shape[0] // step)
    def _(i):
        here = pl.ds(pl.multiple_of(i * step, step), step)
        chosen = chosen_slots(position_ref[here, :], slots)
        rows_ref[here] = low(dot_nn(low(chosen), normed)).reshape(step, slots, model)

    own = pltpu.make_async_copy(rows_ref.at[me], slot_in.at[0, head], sem["recv"].at[0])
    own.start()

    def put(k, target):
        pltpu.make_async_remote_copy(
            src_ref=rows_ref.at[target],
            dst_ref=slot_in.at[k, head],
            send_sem=send,
            recv_sem=sem["recv"].at[k // 8],
            device_id={"seq": target},
        ).start()

    ways.each(0, 8, put)

    hidden = down_ref.shape[0]
    width = down_ref.shape[1]

    def nt(left, right):
        return lax.dot_general(
            left, right, (((1,), (1,)), ((), ())), preferred_element_type=jnp.float32
        )

    def tn(left, right):
        return lax.dot_general(
            left, right, (((0,), (0,)), ((), ())), preferred_element_type=jnp.float32
        )

    gate_up = dot_nn(normed, weights[:, both])
    gate, up = gate_up[:, :shared_hidden], gate_up[:, shared_hidden:]
    act, slope = silu_parts(gate)
    hid = low(act * up)
    right_ref[:, 2 * shared_hidden :] = hid
    right_ref[:, 0:shared_hidden] = low(shared_grad_hid * up * slope)
    right_ref[:, shared_hidden : 2 * shared_hidden] = low(shared_grad_hid * act)
    grads = right_ref[:, 0 : 2 * shared_hidden]
    for c in range(0, width, 256):
        rows = slice(c, c + 256)
        shared_ref[:, rows] = dot_nt(hid, weights[rows, less])
        back_ref[:, rows] = dot_nt(grads, weights[rows, both])
    for ref in (shared_ref, back_ref, right_ref):
        ref.flush()
    ready(gate_up_ref, down_ref)

    @pl.loop(0, 10)
    def _(i):
        @pl.when(i < 8)
        def _():
            c = i
            pltpu.make_async_copy(
                rows_ref.at[group(c)], slot_in.at[group(c), head], sem["recv"].at[c]
            ).wait()
            forward(c).start()

        for late in range(*OUT[2]):

            @pl.when(i == late - 2)
            def _():
                out.arrived(late, late + 1)
                source = grads_here.at[pl.ds(8 * (late - OUT[2][0]), 8)]
                kept(late, source).start()
                given(late, source).start()

        @pl.when((i >= 1) & (i < 9))
        def _():
            c = i - 1
            forward(c).wait()
            kept(c).wait()
            given(c).wait()
            rows = slot_in[group(c)].reshape(256, width)
            grads = grad_slots[group(c)].reshape(256, width)
            both = jnp.dot(rows, gate_up_ref[...], preferred_element_type=jnp.float32)
            gate, up = both[:, :hidden], both[:, hidden:]
            sig = jax.nn.sigmoid(gate)
            act = gate * sig
            hid = (act * up).astype(jnp.bfloat16)
            grad_hid = nt(grads, down_ref[...])
            grad_gate = grad_hid * up * (sig * (1.0 + gate * (1.0 - sig)))
            grad_both = jnp.concatenate([grad_gate, grad_hid * act], axis=1).astype(jnp.bfloat16)
            wide_grad[...] += tn(rows, grad_both)
            down_grad_ref[...] += tn(hid, grads)
            back = nt(grad_both, gate_up_ref[...]).astype(jnp.bfloat16)
            slot_in[group(c)] = back.reshape(8, 2, 16, width)
            res = jnp.dot(hid, down_ref[...], preferred_element_type=jnp.float32)
            grad_slots[group(c)] = res.astype(jnp.bfloat16).reshape(8, 2, 16, width)
            swap(c, slot_in, theirs_x, "x").start()
            swap(c, grad_slots, theirs_y, "y").start()

        @pl.when(i >= 2)
        def _():
            c = i - 2
            swap(c, slot_in, theirs_x, "x").wait()

            def add(k):
                total = slot_in[k, head].astype(jnp.float32) + theirs_x[k].astype(jnp.float32)
                sums[k] = total.astype(sums.dtype)

            def put_home(k, source):
                add(k)
                pltpu.make_async_remote_copy(
                    src_ref=sums.at[k],
                    dst_ref=home_ref.at[me],
                    send_sem=home_send,
                    recv_sem=home_recv,
                    device_id={"seq": source},
                ).start()

            @pl.when(c == 0)
            def _():
                add(0)
                pltpu.make_async_copy(sums.at[0], home_ref.at[me], home_recv).start()

            ways.each(c, c + 1, put_home, back=True)
            swap(c, grad_slots, theirs_y, "y").wait()

            @pl.loop(0, 8)
            def _(n):
                j = c * 8 + n
                total = grad_slots[j, head].astype(jnp.float32) + theirs_y[j].astype(jnp.float32)
                res_ref[j] = total.astype(res_ref.dtype)

    out.sent()
    tiles = hidden // 128
    for tile in range(tiles):
        for which in range(2):
            start = which * hidden + tile * 128
            gate_up_grad_ref[pl.ds(tile * 2 + which, width, stride=2 * tiles), :] = wide_grad[
                :, start : start + 128
            ]
    some = pl.ds(0, 63)
    pltpu.make_async_copy(rows_ref.at[some], rows_ref.at[some], send).wait()
    pltpu.make_async_copy(sums.at[some], sums.at[some], home_send).wait()
    pltpu.make_async_copy(sums, home_ref, home_recv).wait()


def experts(
    gated, weights, layer_in, table, position, grads, grad_rows, gate_up, down, grad_out, slots, collective
):
    tokens, model = layer_in.shape
    shared_hidden = (weights.shape[1] - gated.shape[1]) // 3
    hidden, width = down.shape
    half, bf16 = (position.shape[0], slots, model), jnp.bfloat16
    whole = (half[0], 2) + half[1:]
    vmem, hbm = pl.BlockSpec(memory_space=pltpu.VMEM), pl.BlockSpec(memory_space=pl.ANY)
    home, res, wide, down_grad, *shared = call(
        experts_kernel,
        out_shape=[
            jax.ShapeDtypeStruct(half, bf16),
            jax.ShapeDtypeStruct(half, bf16),
            jax.ShapeDtypeStruct((width * 2 * hidden // 128, 128), jnp.float32),
            jax.ShapeDtypeStruct((hidden, width), jnp.float32),
            jax.ShapeDtypeStruct((tokens, width), jnp.float32),
            jax.ShapeDtypeStruct((tokens, width), jnp.float32),
            jax.ShapeDtypeStruct((tokens, 3 * shared_hidden), bf16),
            jax.ShapeDtypeStruct((tokens, model), jnp.float32),
            jax.ShapeDtypeStruct((tokens, model), bf16),
            jax.ShapeDtypeStruct((tokens, 128), jnp.float32),
        ],
        in_specs=[Lazy, hbm, Lazy, vmem, Lazy, [hbm] * len(grads), hbm, Lazy, Lazy, Lazy],
        out_specs=[hbm] + [vmem] * 3 + [Eager] * 5 + [vmem],
        scratch_shapes=[
            pltpu.VMEM(half, bf16),
            pltpu.VMEM(part_shape(OUT[2], grad_rows).shape, bf16),
            pltpu.VMEM((tokens, model), jnp.float32),
            pltpu.VMEM((tokens, model), jnp.float32),
            pltpu.VMEM(whole, bf16),
            pltpu.VMEM(whole, bf16),
            pltpu.VMEM(half, bf16),
            pltpu.VMEM(half, bf16),
            pltpu.VMEM(half, bf16),
            pltpu.VMEM((width, 2 * hidden), jnp.float32),
            pltpu.VMEM(weights.shape, bf16),
            pltpu.SemaphoreType.DMA((2,)),
            pltpu.SemaphoreType.DMA((2, model // 256)),
            pltpu.SemaphoreType.DMA((9,)),
            pltpu.SemaphoreType.DMA,
            pltpu.SemaphoreType.DMA,
            pltpu.SemaphoreType.DMA,
            pltpu.SemaphoreType.DMA((10, 8)),
        ],
        compiler_params=params(collective, vmem_limit_bytes=VMEM),
        name="experts",
    )(gated, weights, layer_in, table, position, grads, grad_rows, gate_up, down, grad_out)
    return home, res, wide, down_grad, *shared


class Scan:
    def __init__(self, reverse, at, me, x_ref, out_ref, got, made, sems):
        self.reverse, self.at, self.me = reverse, at, me
        self.x_ref, self.out_ref, self.got, self.made = x_ref, out_ref, got, made
        self.send, self.recv, self.back_send, self.back_recv = [sems.at[n] for n in range(4)]

    def spread(self, source, target_ref, send, recv):
        def put(_, target):
            pltpu.make_async_remote_copy(
                src_ref=source.at[target],
                dst_ref=target_ref.at[self.me],
                send_sem=send,
                recv_sem=recv,
                device_id={"seq": target},
            ).start()

        Ways(self.at).each(0, 8, put)

    def begin(self):
        self.got[self.me] = self.x_ref[self.me]
        self.spread(self.x_ref, self.got, self.send, self.recv)

    def middle(self):
        some = pl.ds(0, 63)
        x_ref, got, made = self.x_ref, self.got, self.made
        pltpu.make_async_copy(x_ref.at[some], x_ref.at[some], self.send).wait()
        pltpu.make_async_copy(got.at[some], got.at[some], self.recv).wait()
        heads, width = made.shape[1:]
        number = lax.broadcasted_iota(jnp.int32, (heads, width), 0) + heads * self.me
        chosen = number // 64 == lax.broadcasted_iota(jnp.int32, (heads, width), 1)

        def step(k, state):
            at_k = 63 - k if self.reverse else k
            made[at_k] = state
            rows = got[at_k].astype(jnp.float32)
            row = jnp.sum(rows[heads:], axis=0, keepdims=True)
            decay = jnp.sum(jnp.where(chosen, row, 0.0), axis=1, keepdims=True)
            return decay * state + rows[:heads]

        lax.fori_loop(0, 64, step, jnp.zeros((heads, width), jnp.float32), unroll=8)
        self.out_ref[self.me] = made[self.me]
        self.spread(made, self.out_ref, self.back_send, self.back_recv)

    def end(self):
        some = pl.ds(0, 63)
        made = self.made
        pltpu.make_async_copy(made.at[some], made.at[some], self.back_send).wait()
        pltpu.make_async_copy(made.at[some], made.at[some], self.back_recv).wait()


def scan_rows(states, decay):
    decays = [part.astype(jnp.float32) for part in split(decay, 3)]
    decays = jnp.concatenate(decays + [jnp.zeros((5, decay.shape[1]), jnp.float32)], axis=0)
    decays = jnp.broadcast_to(decays[None], (states.shape[0],) + decays.shape)
    return low(jnp.concatenate([states, decays], axis=1))


class Small:
    def __init__(self, at, me, x_ref, out_ref, got, sems):
        self.at, self.me = at, me
        self.x_ref, self.out_ref, self.got = x_ref, out_ref, got
        self.send, self.recv, self.back_send, self.back_recv = [sems.at[n] for n in range(4)]

    def begin(self):
        self.got[self.me] = self.x_ref[self.me]

        def put(_, target):
            pltpu.make_async_remote_copy(
                src_ref=self.x_ref.at[target],
                dst_ref=self.got.at[self.me],
                send_sem=self.send,
                recv_sem=self.recv,
                device_id={"seq": target},
            ).start()

        Ways(self.at).each(0, 8, put)

    def middle(self):
        some = pl.ds(0, 63)
        x_ref, got, out_ref, me = self.x_ref, self.got, self.out_ref, self.me
        pltpu.make_async_copy(x_ref.at[some], x_ref.at[some], self.send).wait()
        pltpu.make_async_copy(got.at[some], got.at[some], self.recv).wait()
        out_ref[me] = lax.fori_loop(1, 64, lambda k, total: total + got[k], got[0], unroll=9)

        def put(_, target):
            pltpu.make_async_remote_copy(
                src_ref=out_ref.at[me],
                dst_ref=out_ref.at[me],
                send_sem=self.back_send,
                recv_sem=self.back_recv,
                device_id={"seq": target},
            ).start()

        Ways(self.at).each(0, 8, put)

    def end(self):
        some = pl.ds(0, 63)
        got = self.got
        pltpu.make_async_copy(got.at[some], got.at[some], self.back_send).wait()
        pltpu.make_async_copy(got.at[some], got.at[some], self.back_recv).wait()


class Scatter:
    def __init__(self, at, plan, lefts, rights, out_ref, buf, rest, send, recv):
        self.at, self.plan, self.lefts, self.rights = at, plan, lefts, rights
        self.out_ref, self.buf, self.rest, self.send, self.recv = out_ref, buf, rest, send, recv
        self.third, self.half = parts_of(buf.shape[4])
        self.copies = {}

    def spans(self, p):
        start, third, half = p * self.third, self.third, self.half
        return pl.ds(start, half), pl.ds(start + half, third - half)

    def product(self, p):
        buf = self.buf
        rows = buf.shape[3]
        for which, other, first, start, length in self.plan[p]:
            left, right = self.lefts[which], self.rights[other]
            ready(left, right)

            @pl.loop(0, 4)
            def _(x):
                across = pl.ds(pl.multiple_of(x * 16 * rows, 128), 16 * rows)
                total = lax.dot_general(
                    left[:, across],
                    right[:, first : first + length],
                    (((0,), (0,)), ((), ())),
                    preferred_element_type=jnp.float32,
                )
                total = total.reshape(4, 4, rows, length).astype(jnp.bfloat16)
                buf[x, :, :, :, start : start + length] = total

    def send_to(self, phase, p, by, value, cols, slot, kind):
        order = ORDERS[p]
        axis = order[phase]
        lead = (slice(None),) * phase
        copy = pltpu.make_async_remote_copy(
            src_ref=self.buf.at[region(self.at, order, phase, value, cols)],
            dst_ref=self.rest[phase].at[(slot,) + lead + (slice(None), cols)],
            send_sem=self.send.at[phase, p, kind],
            recv_sem=self.recv.at[phase, p, kind],
            device_id={"seq": seq_of(moved(self.at, axis, by))},
        )
        copy.start()
        self.copies[phase, p, kind] = copy

    def added(self, phase, p, value, cols, slots):
        order, buf, room = ORDERS[p], self.buf, self.rest[phase]

        @pl.loop(0, 4**phase)
        def _(i):
            free = ((), (i,), (i // 4, i % 4))[phase]
            index = list(region(self.at, order, phase, value, cols))
            for n, axis in enumerate(sorted(order[:phase])):
                index[axis] = free[n]
            index = tuple(index)
            total = buf[index].astype(jnp.float32)
            for slot in slots:
                total = total + room[(slot,) + free + (slice(None), cols)].astype(jnp.float32)
            if phase == 0 and len(slots) == 2:
                self.out_ref[:, cols] = total
            else:
                buf[index] = total.astype(jnp.bfloat16)

    def first(self, phase, p):
        self.first_far(phase, p)
        self.first_near(phase, p)

    def first_far(self, phase, p):
        c = self.at[ORDERS[p][phase]]
        low, high = self.spans(p)
        self.send_to(phase, p, 1, (c + 2) % 4, low, 2, 0)
        self.send_to(phase, p, 3, (c + 2) % 4, high, 2, 1)

    def first_near(self, phase, p):
        c = self.at[ORDERS[p][phase]]
        low, high = self.spans(p)
        self.send_to(phase, p, 1, (c + 1) % 4, high, 0, 2)
        self.send_to(phase, p, 3, (c + 3) % 4, low, 1, 3)

    def second(self, phase, p):
        c = self.at[ORDERS[p][phase]]
        low, high = self.spans(p)
        self.copies[phase, p, 0].wait_recv()
        self.added(phase, p, (c + 1) % 4, low, (2,))
        self.send_to(phase, p, 1, (c + 1) % 4, low, 0, 4)
        self.copies[phase, p, 1].wait_recv()
        self.added(phase, p, (c + 3) % 4, high, (2,))
        self.send_to(phase, p, 3, (c + 3) % 4, high, 1, 5)

    def third_step(self, phase, p):
        c = self.at[ORDERS[p][phase]]
        low, high = self.spans(p)
        self.copies[phase, p, 2].wait_recv()
        self.copies[phase, p, 5].wait_recv()
        self.added(phase, p, c, high, (0, 1))
        self.copies[phase, p, 3].wait_recv()
        self.copies[phase, p, 4].wait_recv()
        self.added(phase, p, c, low, (0, 1))

    def finish(self, phase):
        for p in range(3):
            self.third_step(phase, p)
            if phase > 0:
                self.first(phase - 1, p)

    def end(self):
        for copy in self.copies.values():
            copy.wait_send()


def scatter_shapes(rows, columns):
    return [
        pltpu.VMEM((4, 4, 4, rows, columns), jnp.bfloat16),
        [pltpu.VMEM((3,) + (4,) * phase + (rows, columns), jnp.bfloat16) for phase in range(3)],
        pltpu.SemaphoreType.DMA((3, 3, 6)),
        pltpu.SemaphoreType.DMA((3, 3, 6)),
    ]


def dot_nn(left, right):
    return jnp.dot(left, right, preferred_element_type=jnp.float32)


def dot_nt(left, right):
    return lax.dot_general(
        left, right, (((1,), (1,)), ((), ())), preferred_element_type=jnp.float32
    )


def dot_tn(left, right):
    return lax.dot_general(
        left, right, (((0,), (0,)), ((), ())), preferred_element_type=jnp.float32
    )


def low(value):
    return value.astype(jnp.bfloat16)


def split(value, count):
    parts = []
    for _ in range(count):
        parts.append(low(value))
        value = value - parts[-1].astype(jnp.float32)
    return parts


def dot_split(left, right, count, dot=dot_nn):
    return sum(dot(left, part) for part in split(right, count))


def split_dot(left, right, count):
    return sum(dot_nn(part, right) for part in split(left, count))


def dot_three(left, right, dot=dot_nn):
    high, less = split(left, 2)
    other_high, other_less = split(right, 2)
    return dot(high, other_high) + dot(less, other_high) + dot(high, other_less)


def head_spread(lanes, width, size):
    head = lax.broadcasted_iota(jnp.int32, (lanes, width), 0)
    column = lax.broadcasted_iota(jnp.int32, (lanes, width), 1)
    return low(jnp.where(head == column // size, 1.0, 0.0))


def head_gather(lanes, width, size):
    head = lax.broadcasted_iota(jnp.int32, (width, lanes), 1)
    column = lax.broadcasted_iota(jnp.int32, (width, lanes), 0)
    return low(jnp.where(head == column // size, 1.0, 0.0))


def triangle(rows, keep):
    first = lax.broadcasted_iota(jnp.int32, (rows, rows), 0)
    second = lax.broadcasted_iota(jnp.int32, (rows, rows), 1)
    return keep(first, second)


def silu_parts(value):
    sig = jax.nn.sigmoid(value)
    return value * sig, sig * (1.0 + value * (1.0 - sig))


def mixer_back_kernel(
    lefts,
    rights,
    home_ref,
    position_ref,
    add_ref,
    resid_ref,
    scale_ref,
    weights_ref,
    z_ref,
    gate_scale_ref,
    y_ref,
    x_ref,
    bc_ref,
    conv_ref,
    pre_ref,
    step_raw_ref,
    table_ref,
    start_ref,
    res_ref,
    mixer_out_ref,
    gate_up_ref,
    down_ref,
    grads_ref,
    taps_grad_ref,
    heads_grad_ref,
    results_ref,
    grad_resid_ref,
    norm_grad_ref,
    gain_grad_ref,
    weights,
    grad_mix,
    dy_ref,
    stat,
    stat_theirs,
    message,
    back,
    got,
    made,
    decayed,
    q,
    spread,
    cum_rows,
    scores,
    acc,
    ext,
    mine,
    theirs,
    shared_out,
    shared_scratch,
    mix_scratch,
    scan_sems,
    sems,
    home_sems,
    load_sem,
    pair_sems,
    stat_sems,
):
    me, at = coordinates()
    head = lax.axis_index("head")
    tokens, width = x_ref.shape
    model = resid_ref.shape[1]
    size = start_ref.shape[1]
    lanes = step_raw_ref.shape[1]
    each = width // 64
    mid = tokens // 2
    cut = 384
    numbers_ref, taps_ref = table_ref.at[8:16, 0:lanes], table_ref
    norm_ref, gain_ref = table_ref.at[5:6, 0:model], table_ref.at[6:7, 0:width]
    announce(me, True)
    added = pltpu.make_async_copy(add_ref, q, load_sem.at[1])
    added.start()
    load = pltpu.make_async_copy(weights_ref.at[:, pl.ds(0, width)], weights, load_sem.at[0])
    load.start()
    normed_second, grad_out = lefts
    normed_gate, shared_right = rights
    third = width // 3
    plan = [((n // 2, 0, n * third, n * third, third),) for n in range(3)]
    shared = Scatter(at, plan, lefts, [shared_right], shared_out, *shared_scratch)
    plan = [((0, 0, n * third, n * third, third),) for n in range(3)]
    mix = Scatter(at, plan, [grad_mix], [normed_gate], mixer_out_ref, *mix_scratch)
    scan = Scan(True, at, me, message, back, got, made, scan_sems)
    results = Spread(at, me, res_ref, results_ref, home_sems, *HOME[0], True)

    gate_cut = 256
    pair = PairSum(q, decayed, pair_sems, gate_cut)
    added.wait()
    ready(home_ref, position_ref)
    slots, step = home_ref.shape[1], 16

    @pl.loop(0, home_ref.shape[0] // step)
    def _(i):
        here = pl.ds(pl.multiple_of(i * step, step), step)
        chosen = low(chosen_slots(position_ref[here, :], slots))
        q[...] += dot_tn(chosen, home_ref[here].reshape(step * slots, model))

    await_all(True)
    for n in range(pair.count):
        pair.copy(n).start()
    results.start(HOME[0][0], HOME[0][0] + 1)
    for p in range(3):
        shared.product(p)
        shared.first(2, p)
    scale = scale_ref[:, 0:1]
    inner_sum = jnp.zeros((tokens, 1), jnp.float32)
    for n in range(pair.count):
        cols = slice(n * gate_cut, (n + 1) * gate_cut)
        pair.copy(n).wait()
        grad = q[:, cols] + decayed[:, cols]
        q[:, cols] = grad
        resid = resid_ref[:, cols]
        norm_grad_ref[:, cols] = jnp.sum(grad * resid * scale, axis=0, keepdims=True)
        inner_sum = inner_sum + jnp.sum(resid * norm_ref[:, cols] * grad, axis=1, keepdims=True)
    pull = scale * scale * scale * (inner_sum / model)
    for n in range(pair.count):
        cols = slice(n * gate_cut, (n + 1) * gate_cut)
        grad = scale * norm_ref[:, cols] * q[:, cols] - resid_ref[:, cols] * pull
        grad = grad_out[:, cols].astype(jnp.float32) + grad
        grad_resid_ref[:, cols] = grad
        grad_mix[:, cols] = low(grad)
    grad_resid_ref.flush()

    load.wait()
    gate_scale = gate_scale_ref[:, 0:1]
    dots = jnp.zeros((tokens, 1), jnp.float32)
    for c in range(0, width, cut):
        cols = slice(c, c + cut)
        grad = dot_nn(grad_mix[...], weights[:, cols])
        z = z_ref[:, cols]
        gated = y_ref[:, cols] * (z * jax.nn.sigmoid(z))
        gain_grad_ref[:, cols] = jnp.sum(grad * gated * gate_scale, axis=0, keepdims=True)
        weighted = grad * gain_ref[:, cols]
        dy_ref[:, cols] = weighted
        dots = dots + jnp.sum(weighted * gated, axis=1, keepdims=True)
    stat[...] = jnp.broadcast_to(dots, stat.shape)
    stat_swap = pltpu.make_async_remote_copy(
        src_ref=stat,
        dst_ref=stat_theirs,
        send_sem=stat_sems.at[0],
        recv_sem=stat_sems.at[1],
        device_id={"head": 1 - head},
    )
    stat_swap.start()
    for p in range(3):
        mix.product(p)
        mix.first(2, p)
    for p in range(3):
        shared.second(2, p)
    stat_swap.wait()
    dots = (stat[...] + stat_theirs[...])[:, 0:1]
    pull = gate_scale * gate_scale * gate_scale * (dots / (2 * width))
    for c in range(0, width, cut):
        cols = slice(c, c + cut)
        z, y = z_ref[:, cols], y_ref[:, cols]
        act, slope = silu_parts(z)
        grad = gate_scale * dy_ref[:, cols] - y * act * pull
        dy_ref[:, cols] = grad * act
        grads_ref[:, cols] = low(grad * y * slope)

    rate = numbers_ref[0:1, :]
    step_raw = step_raw_ref[...]
    step = jax.nn.softplus(step_raw)
    earlier = low(triangle(tokens, lambda t, s: jnp.where(t >= s, 1.0, 0.0)))
    cum = dot_split(earlier, -step * rate, 3)
    cum_rows[...] = cum.T
    tail = cum[tokens - 1 : tokens, :]
    rest_decay = jnp.exp(tail - cum)
    weight = rest_decay * step
    spreader = head_spread(lanes, width, 64)
    gatherer = head_gather(lanes, width, 64)
    spread[...] = split_dot(jnp.exp(cum), spreader, 2)
    held_full, read_full = bc_ref[:, :size], bc_ref[:, size:]
    held, read = low(held_full), low(read_full)

    for c in range(0, width, cut):
        part = dy_ref[:, c : c + cut] * spread[:, c : c + cut]
        decayed[:, c : c + cut] = part
        made_rows = dot_three(part, read_full, dot_tn)
        made_rows = made_rows.reshape(cut // each, each, size)
        message[c // each : (c + cut) // each] = scan_rows(made_rows, jnp.exp(tail))
    scan.begin()
    for p in range(3):
        mix.second(2, p)
    shared.finish(2)
    scan.middle()

    spread[...] = split_dot(step, spreader, 2)
    blocks = ((0, 0), (0, 1), (1, 1))
    for n, (s, t) in enumerate(blocks):
        scores[n] = dot_nt(held[s * mid : (s + 1) * mid], read[t * mid : (t + 1) * mid])
    acc[...] = jnp.zeros_like(acc)
    causal = triangle(mid, lambda s, t: s <= t)
    ready(x_ref)
    second_head = lax.broadcasted_iota(jnp.int32, (tokens, 128), 1) >= 64

    @pl.loop(0, width // 128)
    def _(i):
        here = pl.ds(pl.multiple_of(i * 128, 128), 128)
        dy, dy_less = split(dy_ref[:, here], 2)
        stepped = x_ref[:, here] * spread[:, here]
        results = []
        for which in range(2):
            row = cum_rows[pl.ds(2 * i + which, 1), :]
            column = jnp.broadcast_to(row, (128, tokens)).T
            mask = second_head if which else jnp.logical_not(second_head)
            values, values_less = split(jnp.where(mask, stepped, 0.0), 2)
            total = [None, None]
            for n, (s, t) in enumerate(blocks):
                gap = row[:, t * mid : (t + 1) * mid] - column[s * mid : (s + 1) * mid]
                decay = jnp.exp(gap)
                if s == t:
                    decay = jnp.where(causal, decay, 0.0)
                later = dy[t * mid : (t + 1) * mid]
                first, later_less = values[s * mid : (s + 1) * mid], dy_less[t * mid : (t + 1) * mid]
                pairs = dot_nt(first, later) + dot_nt(first, later_less)
                pairs = pairs + dot_nt(values_less[s * mid : (s + 1) * mid], later)
                acc[n] += decay * pairs
                part = dot_nn(low(decay * scores[n]), later)
                total[s] = part if total[s] is None else total[s] + part
            results.append(total)
        for s in range(2):
            rows = slice(s * mid, (s + 1) * mid)
            q[rows, here] = jnp.where(second_head[rows], results[1][s], results[0][s])

    for p in range(3):
        shared.second(1, p)
    shared.finish(1)
    mix.finish(2)
    results.start(HOME[0][0] + 1, HOME[0][0] + 2)
    scan.end()

    skip = split_dot(jnp.broadcast_to(numbers_ref[1:2, :], (8, lanes)), spreader, 2)[0:1, :]
    grad_weight = grad_step = rows_sum = jnp.zeros((tokens, lanes), jnp.float32)
    skip_grad = jnp.zeros((8, lanes), jnp.float32)
    state_dot = jnp.zeros((lanes, size), jnp.float32)
    held_parts = held_full[:mid], held_full[mid:]
    read_parts = read_full[:mid], read_full[mid:]
    grad_held = dot_three(acc[0], read_parts[0]) + dot_three(acc[1], read_parts[1])
    grad_held = jnp.concatenate([grad_held, dot_three(acc[2], read_parts[1])], axis=0)
    grad_read = dot_three(acc[1], held_parts[0], dot_tn) + dot_three(acc[2], held_parts[1], dot_tn)
    grad_read = jnp.concatenate([dot_three(acc[0], held_parts[0], dot_tn), grad_read], axis=0)
    for c in range(0, width, cut):
        here = slice(c, c + cut)
        x, dy, inner = x_ref[:, here], dy_ref[:, here], q[:, here]
        after = back[c // each : (c + cut) // each].reshape(cut, size)
        start = start_ref[here, :]
        gather = gatherer[here, :]
        weights = split_dot(weight, spreader[:, here], 2)
        through = dot_nt(held, low(after))
        grad_x = inner * spread[:, here] + skip[:, here] * dy + weights * through
        grad_step = grad_step + split_dot(x * inner, gather, 2)
        grad_weight = grad_weight + split_dot(x * through, gather, 2)
        rows_sum = rows_sum + split_dot(dy * (y_ref[:, here] - skip[:, here] * x), gather, 2)
        pairs = jnp.sum(dy * x, axis=0, keepdims=True)
        skip_grad = skip_grad + split_dot(jnp.broadcast_to(pairs, (8, cut)), gather, 2)
        state_dot = state_dot + dot_split(gather, after * start, 2, dot_tn)
        grad_held = grad_held + dot_three(weights * x, after)
        grad_read = grad_read + dot_three(decayed[:, here], start)
        ext[0:tokens, here] = grad_x * silu_parts(conv_ref[:, here])[1]
        if c == cut:
            for p in range(3):
                shared.second(0, p)
            for p in range(3):
                mix.second(1, p)
            results.start(HOME[0][0] + 2, HOME[0][0] + 3)
    mine[:, :size] = grad_held
    mine[:, size:] = grad_read
    swap = pltpu.make_async_remote_copy(
        src_ref=mine,
        dst_ref=theirs,
        send_sem=sems.at[0],
        recv_sem=sems.at[1],
        device_id={"head": 1 - head},
    )
    swap.start()
    mix.finish(1)
    results.start(HOME[0][0] + 3, HOME[0][0] + 4)

    ones = jnp.ones((8, size), jnp.bfloat16)
    state_grad = dot_split(ones, state_dot, 2, dot_nt)[0:1, :]
    used = grad_weight * weight
    tail_grad = jnp.sum(used, axis=0, keepdims=True) + jnp.exp(tail) * state_grad
    grad_cum = rows_sum - step * grad_step - used
    last = lax.broadcasted_iota(jnp.int32, (tokens, lanes), 0) == tokens - 1
    grad_cum = grad_cum + jnp.where(last, tail_grad, 0.0)
    later = low(triangle(tokens, lambda t, s: jnp.where(t <= s, 1.0, 0.0)))
    grad_log = dot_split(later, grad_cum, 3)
    grad_step = grad_step + grad_weight * rest_decay - rate * grad_log
    grad_raw = grad_step * jax.nn.sigmoid(step_raw)
    heads_grad_ref[...] = jnp.zeros_like(heads_grad_ref)
    heads_grad_ref[0:1, :] = skip_grad[0:1, :]
    heads_grad_ref[1:2, :] = -jnp.sum(step * grad_log, axis=0, keepdims=True)
    heads_grad_ref[2:3, :] = jnp.sum(grad_raw, axis=0, keepdims=True)

    channels = width + 2 * size
    grads_ref[:, width + channels : width + channels + lanes] = low(grad_raw)
    swap.wait()
    ext[0:tokens, width:channels] = (mine[...] + theirs[...]) * silu_parts(
        conv_ref[:, width:channels]
    )[1]
    edge = pltpu.make_async_remote_copy(
        src_ref=ext.at[pl.ds(0, 8)],
        dst_ref=ext.at[pl.ds(tokens, 8)],
        send_sem=sems.at[2],
        recv_sem=sems.at[3],
        device_id={"seq": (me + 63) % 64},
    )
    edge.start()
    shared.finish(0)
    for p in range(3):
        mix.second(0, p)
    results.start(HOME[0][0] + 4, HOME[0][1])
    edge.wait()
    there = jnp.where(me == 63, 0.0, 1.0)
    ext[tokens : tokens + 8, :] = ext[tokens : tokens + 8, :] * there
    taps_grad_ref[...] = jnp.zeros_like(taps_grad_ref)
    ready(pre_ref)

    @pl.loop(0, channels // 256)
    def _(i):
        here = pl.ds(pl.multiple_of(i * 256, 256), 256)
        grad = ext[0:tokens, here]
        total = jnp.zeros_like(grad)
        for j in range(4):
            total = total + taps_ref[j : j + 1, here] * ext[3 - j : 3 - j + tokens, here]
            products = grad * pre_ref[5 + j : 5 + j + tokens, here]
            taps_grad_ref[j : j + 1, here] = jnp.sum(products, axis=0, keepdims=True)
        grads_ref[:, pl.ds(pl.multiple_of(width + i * 256, 256), 256)] = low(total)

    mix.finish(0)
    hidden = down_ref.shape[1]
    for n in range(2):
        gate_up_ref[:, n, :] = shared_out[:, n * hidden : (n + 1) * hidden]
    down_ref[...] = shared_out[:, 2 * hidden :]
    shared.end()
    mix.end()
    results.wait()


def mixer_back(
    lefts,
    rights,
    home,
    position,
    add,
    resid,
    scale,
    weights,
    z,
    gate_scale,
    y,
    x,
    bc,
    conv,
    pre,
    step_raw,
    table,
    start,
    res,
    collective,
):
    tokens, model = resid.shape
    rows = model // 64
    width = x.shape[1]
    hidden = rights[1].shape[1] // 3
    size, lanes = start.shape[1], step_raw.shape[1]
    each, channels, mid = width // 64, width + 2 * size, tokens // 2
    f32, bf16 = jnp.float32, jnp.bfloat16
    vmem, hbm = pl.BlockSpec(memory_space=pltpu.VMEM), pl.BlockSpec(memory_space=pl.ANY)
    return call(
        mixer_back_kernel,
        out_shape=[
            jax.ShapeDtypeStruct((rows, width), f32),
            jax.ShapeDtypeStruct((rows, 2, hidden), f32),
            jax.ShapeDtypeStruct((rows, hidden), f32),
            jax.ShapeDtypeStruct((tokens, width + channels + lanes), bf16),
            jax.ShapeDtypeStruct((8, channels), f32),
            jax.ShapeDtypeStruct((8, lanes), f32),
            part_shape(HOME[0], res),
            jax.ShapeDtypeStruct((tokens, model), f32),
            jax.ShapeDtypeStruct((1, model), f32),
            jax.ShapeDtypeStruct((1, width), f32),
        ],
        in_specs=[[Lazy] * len(lefts), [Lazy] * len(rights)]
        + [Lazy, Lazy, hbm, Lazy, Lazy, hbm]
        + [Lazy] * 4
        + [vmem, Lazy, Lazy, vmem, vmem, Lazy, hbm],
        out_specs=[vmem] * 6 + [hbm, Eager, vmem, vmem],
        scratch_shapes=[
            pltpu.VMEM((model, width), bf16),
            pltpu.VMEM((tokens, model), bf16),
            pltpu.VMEM((tokens, width), f32),
            pltpu.VMEM((tokens, 128), f32),
            pltpu.VMEM((tokens, 128), f32),
            pltpu.VMEM((64, each + 8, size), bf16),
            pltpu.VMEM((64, each, size), f32),
            pltpu.VMEM((64, each + 8, size), bf16),
            pltpu.VMEM((64, each, size), f32),
            pltpu.VMEM((tokens, width), f32),
            pltpu.VMEM((tokens, width), f32),
            pltpu.VMEM((tokens, width), f32),
            pltpu.VMEM((lanes, tokens), f32),
            pltpu.VMEM((3, mid, mid), f32),
            pltpu.VMEM((3, mid, mid), f32),
            pltpu.VMEM((tokens + 8, channels), f32),
            pltpu.VMEM((tokens, 2 * size), f32),
            pltpu.VMEM((tokens, 2 * size), f32),
            pltpu.VMEM((rows, 3 * hidden), f32),
            scatter_shapes(rows, 3 * hidden),
            scatter_shapes(rows, width),
            pltpu.SemaphoreType.DMA((4,)),
            pltpu.SemaphoreType.DMA((4,)),
            pltpu.SemaphoreType.DMA((9,)),
            pltpu.SemaphoreType.DMA((2,)),
            pltpu.SemaphoreType.DMA((2, model // 256)),
            pltpu.SemaphoreType.DMA((2,)),
        ],
        compiler_params=params(collective, vmem_limit_bytes=VMEM),
        name="mixer_back",
    )(
        lefts, rights, home, position, add, resid, scale, weights, z, gate_scale, y, x, bc, conv,
        pre, step_raw, table, start, res,
    )


def input_back_kernel(
    plan,
    left,
    right,
    weights_ref,
    resid_ref,
    table_ref,
    grad_ref,
    res_ref,
    near_refs,
    position_ref,
    weight_ref,
    shared_ref,
    block_ref,
    taps_ref,
    heads_ref,
    norm_ref,
    gate_gain_ref,
    mixer_in_ref,
    state_ref,
    step_ref,
    input_ref,
    layer_ref,
    norm_first_out,
    norm_second_out,
    gate_gain_out,
    conv_main_out,
    conv_state_out,
    heads_outs,
    weights,
    mine,
    theirs,
    theirs_mix,
    home,
    named,
    weighed,
    small,
    small_got,
    small_out,
    out_ref,
    buf,
    rest,
    send,
    recv,
    small_sems,
    sems,
    home_sems,
    mix_sems,
):
    me, at = coordinates()
    head = lax.axis_index("head")
    tokens, model = resid_ref.shape
    columns = right.shape[1]
    gain_ref = table_ref.at[4:5, 0:model]
    load = pltpu.make_async_copy(weights_ref, weights, sems.at[0])
    load.start()
    announce(me, True)
    sums = Scatter(at, plan, [left], [right], out_ref, buf, rest, send, recv)
    totals = Small(at, me, small, small_out, small_got, small_sems)
    results = Spread(at, me, res_ref, home, home_sems, *HOME[1], True)
    for p in range(3):
        sums.product(p)
        if p == 0:
            await_all(True)
            results.start(HOME[1][0], HOME[1][0] + 1)
        sums.first(2, p)
    load.wait()

    start = columns - 384
    other = pl.multiple_of(start + 128 * (1 - head), 128)
    cut = 256
    swaps = []
    for c in range(0, model, cut):
        rows = slice(c, c + cut)
        total = dot_nt(right[...], weights[rows, :])
        total = total - dot_nt(right[:, pl.ds(other, 128)], weights[rows, pl.ds(other, 128)])
        mine[:, rows] = total
        swap = pltpu.make_async_remote_copy(
            src_ref=mine.at[:, pl.ds(c, cut)],
            dst_ref=theirs.at[:, pl.ds(c, cut)],
            send_sem=sems.at[1 + c // cut],
            recv_sem=sems.at[1 + (model + c) // cut],
            device_id={"head": 1 - head},
        )
        swap.start()
        swaps.append(swap)
    for p in range(3):
        sums.second(2, p)
    square = jnp.zeros((tokens, 1), jnp.float32)
    inner = jnp.zeros((tokens, 1), jnp.float32)
    for n, c in enumerate(range(0, model, cut)):
        rows = slice(c, c + cut)
        swaps[n].wait()
        grad = mine[:, rows] + theirs[:, rows]
        mine[:, rows] = grad
        resid = resid_ref[:, rows].astype(jnp.float32)
        square = square + jnp.sum(resid * resid, axis=1, keepdims=True)
        inner = inner + jnp.sum(resid * gain_ref[:, rows] * grad, axis=1, keepdims=True)
    scale = lax.rsqrt(square / model + EPSILON)
    pull = scale * scale * scale * (inner / model)
    tiles, inner_tiles = model // 128, gate_gain_ref.shape[1] // 128
    channel_tiles = taps_ref.shape[1] // 128
    small[...] = jnp.zeros_like(small)

    def put_small(row, value):
        small[row // 8, row % 8 : row % 8 + 1, :] = value

    for tile in range(tiles):
        put_small(tiles + tile, norm_ref[:, tile * 128 : (tile + 1) * 128])
    for tile in range(inner_tiles):
        put_small(2 * tiles + tile, gate_gain_ref[:, tile * 128 : (tile + 1) * 128])
    taps_row = 2 * tiles + inner_tiles
    for tap in range(4):
        for tile in range(channel_tiles):
            row = taps_row + tap * channel_tiles + tile
            put_small(row, taps_ref[tap : tap + 1, tile * 128 : (tile + 1) * 128])
    heads_row = taps_row + 4 * channel_tiles
    for n in range(3):
        put_small(heads_row + n, heads_ref[n : n + 1, :])
    for c in range(0, model, cut):
        rows = slice(c, c + cut)
        grad = mine[:, rows]
        resid = resid_ref[:, rows].astype(jnp.float32)
        input_ref[:, rows] = grad_ref[:, rows] + scale * gain_ref[:, rows] * grad - resid * pull
        gain_grad = jnp.sum(grad * resid * scale, axis=0, keepdims=True)
        for tile in range(c // 128, (c + cut) // 128):
            at_tile = tile * 128 - c
            put_small(tile, gain_grad[:, at_tile : at_tile + 128])
    totals.begin()
    results.start(HOME[1][0] + 1, HOME[1][0] + 2)
    input_ref.flush()
    mine[...] = shared_ref[...]
    slots = home.shape[1]

    def mix(span, rows_ref):
        @pl.loop(*span)
        def _(g):
            for n, (_, expert) in enumerate(Ways(at).group(g)):
                named[n : n + 1, :] = position_ref[pl.ds(expert, 1), :]
                weighed[n : n + 1, :] = weight_ref[pl.ds(expert, 1), :]
            chosen = chosen_slots(named[...], slots)
            weighted = chosen.reshape(8, slots, -1) * weighed[...][:, None, :]
            high, less = split(weighted.reshape(chosen.shape), 2)
            here = pl.ds(pl.multiple_of((g - span[0]) * 8, 8), 8)
            rows = rows_ref[here].reshape(8 * slots, model)
            mine[...] += dot_tn(high, rows) + dot_tn(less, rows)

    ready(position_ref, weight_ref, *near_refs)
    for span, near_ref in zip(HOME, near_refs):
        mix(span, near_ref)
    first = HOME[1][0]
    sums.finish(2)
    for p in range(3):
        sums.second(1, p)
    results.start(first + 2, HOME[1][1])
    totals.middle()
    sums.finish(1)
    results.arrived(first, first + 2)
    mix((first, first + 2), home)
    for p in range(3):
        sums.second(0, p)
    results.arrived(first + 2, HOME[1][1])
    mix((first + 2, HOME[1][1]), home.at[pl.ds(16, home.shape[0] - 16)])
    pair = PairSum(mine, theirs_mix, mix_sems, cut)
    for n in range(pair.count):
        pair.copy(n).start()
    sums.finish(0)
    for n in range(pair.count):
        cols = slice(n * cut, (n + 1) * cut)
        pair.copy(n).wait()
        layer_ref[:, cols] = low(block_ref[:, cols] + (mine[:, cols] + theirs_mix[:, cols]))
    totals.end()

    def get_small(row):
        return small_out[row // 8, row % 8 : row % 8 + 1, :]

    for tile in range(tiles):
        norm_first_out[tile : tile + 1, :] = get_small(tile)
        norm_second_out[tile : tile + 1, :] = get_small(tiles + tile)
    for tile in range(inner_tiles):
        gate_gain_out[tile : tile + 1, :] = get_small(2 * tiles + tile)
    for tap in range(4):
        for tile in range(channel_tiles):
            value = get_small(taps_row + tap * channel_tiles + tile)
            if tile < inner_tiles:
                conv_main_out[tap : tap + 1, tile * 128 : (tile + 1) * 128] = value
            else:
                start = (tile - inner_tiles) * 128
                conv_state_out[tap : tap + 1, start : start + 128] = value
    for n, heads_out in enumerate(heads_outs):
        heads_out[...] = get_small(heads_row + n)[:, : heads_out.shape[1]]
    results.sent()
    inner = mixer_in_ref.shape[2]
    for n in range(2):
        mixer_in_ref[:, n, :] = out_ref[:, n * inner : (n + 1) * inner]
    wide = 2 * inner + state_ref.shape[1]
    state_ref[...] = out_ref[:, 2 * inner : wide]
    step_ref[...] = out_ref[:, wide : wide + 128][:, : step_ref.shape[1]]
    sums.end()


def input_back(
    left,
    right,
    plan,
    weights,
    resid,
    table,
    grad,
    res,
    near,
    position,
    weight,
    shared,
    block,
    taps,
    heads,
    norm,
    gate_gain,
    heads_dev,
    collective,
):
    tokens, model = resid.shape
    columns = right.shape[1]
    rows = model // 64
    inner, channels = gate_gain.shape[1], taps.shape[1]
    f32 = jnp.float32
    vmem, hbm = pl.BlockSpec(memory_space=pltpu.VMEM), pl.BlockSpec(memory_space=pl.ANY)
    return call(
        functools.partial(input_back_kernel, plan),
        out_shape=[
            jax.ShapeDtypeStruct((rows, 2, inner), f32),
            jax.ShapeDtypeStruct((rows, channels - inner), f32),
            jax.ShapeDtypeStruct((rows, heads_dev), f32),
            jax.ShapeDtypeStruct((tokens, model), f32),
            jax.ShapeDtypeStruct((tokens, model), jnp.bfloat16),
            jax.ShapeDtypeStruct((model // 128, 128), f32),
            jax.ShapeDtypeStruct((model // 128, 128), f32),
            jax.ShapeDtypeStruct((inner // 128, 128), f32),
            jax.ShapeDtypeStruct((4, inner), f32),
            jax.ShapeDtypeStruct((4, channels - inner), f32),
            [jax.ShapeDtypeStruct((1, heads_dev), f32)] * 3,
        ],
        in_specs=[Lazy, Lazy, hbm, Lazy, vmem, Lazy] + [hbm, [Lazy] * len(near)] + [Lazy] * 8,
        out_specs=[vmem] * 3 + [Eager] * 2 + [vmem] * 5 + [[vmem] * 3],
        scratch_shapes=[
            pltpu.VMEM(weights.shape, weights.dtype),
            pltpu.VMEM((tokens, model), f32),
            pltpu.VMEM((tokens, model), f32),
            pltpu.VMEM((tokens, model), f32),
            pltpu.VMEM(part_shape(HOME[1], res).shape, res.dtype),
            pltpu.VMEM((8, tokens), f32),
            pltpu.VMEM((8, tokens), f32),
            pltpu.VMEM((64, 8, 128), f32),
            pltpu.VMEM((64, 8, 128), f32),
            pltpu.VMEM((64, 8, 128), f32),
            pltpu.VMEM((rows, columns), f32),
        ]
        + scatter_shapes(rows, columns)
        + [pltpu.SemaphoreType.DMA((4,)), pltpu.SemaphoreType.DMA((1 + 2 * model // 256,))]
        + [pltpu.SemaphoreType.DMA((9,)), pltpu.SemaphoreType.DMA((2, model // 256))],
        compiler_params=params(collective, vmem_limit_bytes=VMEM),
        name="input_back",
    )(
        left, right, weights, resid, table, grad, res, near, position, weight, shared, block,
        taps, heads, norm, gate_gain,
    )


class Gather:
    def __init__(self, at, x_ref, out_ref, send, recv, local_sem):
        self.at, self.x_ref, self.out_ref, self.send, self.recv = at, x_ref, out_ref, send, recv
        self.third, self.half = parts_of(out_ref.shape[4])
        if x_ref is not None:
            self.own = pltpu.make_async_copy(x_ref, out_ref.at[at[0], at[1], at[2]], local_sem)
        self.copies = {}

    def put(self, source, here, phase, p, kind, by):
        copy = pltpu.make_async_remote_copy(
            src_ref=source,
            dst_ref=self.out_ref.at[here],
            send_sem=self.send.at[phase, p, kind],
            recv_sem=self.recv.at[phase, p, kind],
            device_id={"seq": seq_of(moved(self.at, ORDERS[p][phase], by))},
        )
        copy.start()
        self.copies[phase, p, kind] = copy

    def first(self, phase):
        if phase == 1:
            self.own.wait()
        if phase == 0:
            self.own.start()
        elif (phase - 1, 0, 2) in self.copies:
            self.arrived(phase - 1)
        for p, order in enumerate(ORDERS):
            cols = pl.ds(p * self.third, self.third)
            here = region(self.at, order, phase, self.at[order[phase]], cols)
            source = self.x_ref.at[:, cols] if phase == 0 else self.out_ref.at[here]
            for kind, by in enumerate((1, 3)):
                self.put(source, here, phase, p, kind, by)

    def second(self, phase):
        for p, order in enumerate(ORDERS):
            for kind, by in enumerate((1, 3)):
                start, length = p * self.third, self.half
                if kind:
                    start, length = start + self.half, self.third - self.half
                there = region(
                    self.at, order, phase, (self.at[order[phase]] - by) % 4, pl.ds(start, length)
                )
                self.copies[phase, p, kind].wait_recv()
                self.put(self.out_ref.at[there], there, phase, p, 2 + kind, by)

    def arrived(self, phase):
        for p in range(3):
            for kind in (2, 3):
                self.copies[phase, p, kind].wait_recv()

    def end(self):
        for copy in self.copies.values():
            copy.wait_send()


def gather_shapes():
    return [
        pltpu.SemaphoreType.DMA((3, 3, 4)),
        pltpu.SemaphoreType.DMA((3, 3, 4)),
        pltpu.SemaphoreType.DMA,
    ]


def slot_tables(routes_ref, weights_ref, position_ref, weight_ref):
    experts, tokens = position_ref.shape
    expert = lax.broadcasted_iota(jnp.int32, (experts, tokens), 0)
    named = jnp.zeros((experts, tokens), jnp.float32)
    weight = jnp.zeros((experts, tokens), jnp.float32)
    for k in range(routes_ref.shape[0]):
        hit = expert == routes_ref[k : k + 1, :]
        named = named + jnp.where(hit, 1.0, 0.0)
        weight = weight + jnp.where(hit, weights_ref[k : k + 1, :], 0.0)
    earlier = low(triangle(tokens, lambda t, s: jnp.where(t < s, 1.0, 0.0)))
    position_ref[...] = jnp.where(named > 0.0, dot_nn(low(named), earlier), -1.0)
    weight_ref[...] = weight


def chosen_slots(position, slots):
    count, tokens = position.shape
    number = lax.broadcasted_iota(jnp.int32, (count, slots, tokens), 1)
    number = (number + slots * lax.axis_index("head")).astype(jnp.float32)
    return jnp.where(position[:, None, :] == number, 1.0, 0.0).reshape(count * slots, tokens)


def gather_kernel(
    early_refs,
    late_refs,
    wide_in,
    layer_ref,
    routes_ref,
    weights_ref,
    grads_ref,
    vectors,
    out_ref,
    late_out,
    before_ref,
    position_ref,
    weight_ref,
    rows,
    slots_ref,
    table_ref,
    wide_ref,
    x_ref,
    late_ref,
    send,
    recv,
    local_sem,
    late_send,
    late_recv,
    late_sem,
    sems,
    out_sems,
):
    me, at = coordinates()
    announce(me, False)
    def beside(target, sources):
        column = 0
        for source in sources:
            value = source[...]
            if value.ndim == 3:
                value = value.astype(jnp.float32)
                halves = [low(value[:, n, :]) for n in range(2)]
            else:
                halves = [value]
            for half in halves:
                target[:, column : column + half.shape[1]] = half
                column = column + half.shape[1]

    rows_step = x_ref.shape[1] - 128
    x_ref[:, rows_step:] = jnp.zeros((x_ref.shape[0], 128), x_ref.dtype)
    beside(x_ref, early_refs)
    beside(late_ref, late_refs)
    gather = Gather(at, x_ref, out_ref, send, recv, local_sem)
    late = Gather(at, late_ref, late_out, late_send, late_recv, late_sem)
    conv_main, conv_state, gains, numbers = vectors
    width, heads = conv_main.shape[1], numbers[0].shape[1]
    table_ref[...] = jnp.zeros_like(table_ref)
    table_ref[0:4, 0:width] = conv_main[...]
    table_ref[0:4, width:] = conv_state[...]
    for n, gain in enumerate(gains):
        for tile in range(gain.shape[0]):
            table_ref[4 + n : 5 + n, tile * 128 : (tile + 1) * 128] = gain[tile : tile + 1, :]
    for n, number in enumerate(numbers):
        table_ref[8 + n : 9 + n, 0:heads] = number[...]
    slot_tables(routes_ref, weights_ref, position_ref, weight_ref)
    grads = grads_ref[...]
    slots, step = rows.shape[1], 16

    @pl.loop(0, rows.shape[0] // step)
    def _(i):
        here = pl.ds(pl.multiple_of(i * step, step), step)
        chosen = chosen_slots(position_ref[here, :], slots)
        weighted = chosen.reshape(step, slots, -1) * weight_ref[here, :][:, None, :]
        scale = jnp.sum(weighted.reshape(chosen.shape), axis=1, keepdims=True)
        rows[here] = low(dot_nn(low(chosen), grads) * scale).reshape(step, slots, -1)

    await_all(False)
    gather.first(0)
    late.first(0)
    edge = pltpu.make_async_remote_copy(
        src_ref=layer_ref.at[pl.ds(layer_ref.shape[0] - 16, 16)],
        dst_ref=before_ref,
        send_sem=sems.at[0],
        recv_sem=sems.at[1],
        device_id={"seq": (me + 1) % 64},
    )
    edge.start()
    out = Spread(at, me, rows, slots_ref, out_sems, *OUT[0], False)
    gather.second(0)
    late.second(0)
    out.start(0, 1)
    gather.first(1)
    late.first(1)
    out.start(1, 2)
    gather.second(1)
    late.second(1)
    out.start(2, 3)
    gather.first(2)
    gather.second(2)
    out.start(3, OUT[0][1])
    ready(wide_in)
    hidden = wide_in.shape[2]

    @pl.loop(0, wide_in.shape[0] // 64)
    def _(i):
        here = pl.ds(pl.multiple_of(i * 64, 64), 64)
        value = wide_in[here].astype(jnp.float32)
        for n in range(2):
            wide_ref[here, n * hidden : (n + 1) * hidden] = low(value[:, n, :])

    late.arrived(1)
    late.end()
    gather.arrived(2)
    edge.wait()
    gather.end()
    out.wait()


def gather_rows(
    early, late, wide, layer_in, routes, route_weights, grads, vectors, experts, slots, collective
):
    rows = early[0].shape[0]
    bf16 = early[0].dtype
    count = lambda arrays: sum(array.size // rows for array in arrays)
    columns = -(-count(early) // 128) * 128
    channels = vectors[0].shape[1] + vectors[1].shape[1]
    tokens, model = grads.shape
    grad_rows = jax.ShapeDtypeStruct((experts, slots, model), grads.dtype)
    hbm, vmem = pl.BlockSpec(memory_space=pl.ANY), pl.BlockSpec(memory_space=pltpu.VMEM)
    return call(
        gather_kernel,
        out_shape=[
            jax.ShapeDtypeStruct((4, 4, 4, rows, columns), bf16),
            jax.ShapeDtypeStruct((4, 4, 4, rows, count(late)), bf16),
            jax.ShapeDtypeStruct((16, model), layer_in.dtype),
            jax.ShapeDtypeStruct((experts, tokens), jnp.float32),
            jax.ShapeDtypeStruct((experts, tokens), jnp.float32),
            grad_rows,
            part_shape(OUT[0], grad_rows),
            jax.ShapeDtypeStruct((16, channels), jnp.float32),
            jax.ShapeDtypeStruct((wide.shape[0], 2 * wide.shape[2]), bf16),
        ],
        in_specs=[[vmem] * len(early), [vmem] * len(late), Lazy, hbm, vmem, vmem, Lazy, [vmem, vmem, [vmem] * 3, [vmem] * 3]],
        out_specs=[hbm, hbm, hbm, vmem, vmem, vmem, hbm, vmem, vmem],
        scratch_shapes=[pltpu.VMEM((rows, columns), bf16), pltpu.VMEM((rows, count(late)), bf16)]
        + gather_shapes()
        + gather_shapes() + [pltpu.SemaphoreType.DMA((2,))]
        + [pltpu.SemaphoreType.DMA((9,))],
        compiler_params=params(collective, vmem_limit_bytes=VMEM),
        name="gather_rows",
    )(early, late, wide, layer_in, routes.T, route_weights.T, grads, vectors)


def mixer_kernel(
    layer_ref,
    edge_ref,
    table_ref,
    weights_ref,
    _,
    rows_ref,
    normed_ref,
    z_ref,
    x_ref,
    bc_ref,
    conv_ref,
    pre_ref,
    step_raw_ref,
    start_ref,
    y_ref,
    gated_ref,
    scale_ref,
    gathered_ref,
    slots_ref,
    weights,
    normed,
    message,
    got,
    made,
    spread,
    cum_rows,
    scores,
    mine,
    theirs,
    load_sems,
    scan_sems,
    pair_sems,
    send,
    recv,
    slot_sems,
):
    me, at = coordinates()
    head = lax.axis_index("head")
    tokens, model = layer_ref.shape
    width = x_ref.shape[1]
    size = bc_ref.shape[1] // 2
    lanes = step_raw_ref.shape[1]
    each = width // 64
    mid = tokens // 2
    cut = 384
    norm_ref, gain_ref = table_ref.at[4:5, 0:model], table_ref.at[6:7, 0:width]
    numbers_ref, taps_ref = table_ref.at[8:16, 0:lanes], table_ref

    def load(n):
        cols = pl.ds(pl.multiple_of(n * cut, 128), cut)
        return pltpu.make_async_copy(weights_ref.at[:, cols], weights.at[:, cols], load_sems.at[n])

    for n in (8, 4, 5, 6, 7, 0, 1, 2, 3):
        load(n).start()
    announce(me, True)
    gather = Gather(at, None, gathered_ref, send, recv, None)

    def norm(rows):
        rows = rows.astype(jnp.float32)
        scale = lax.rsqrt(jnp.mean(rows * rows, axis=1, keepdims=True) + EPSILON)
        return low(rows * scale * norm_ref[...])

    before = norm(edge_ref[...]).astype(jnp.float32) * jnp.where(me == 0, 0.0, 1.0)
    normed[0:16, :] = low(before)
    normed[16 : 16 + tokens, :] = norm(layer_ref[...])
    normed_ref[...] = normed[16 : 16 + tokens, :]
    normed_ref.flush()
    await_all(True)
    gather.first(2)

    def conv(cols):
        total = jnp.zeros((tokens, cols.size), jnp.float32)
        for j in range(4):
            total = total + taps_ref[j : j + 1, cols] * pre_ref[5 + j : 5 + j + tokens, cols]
        conv_ref[:, cols] = total
        return total * jax.nn.sigmoid(total)

    load(8).wait()
    last = dot_nn(normed[...], weights[:, 8 * cut : 9 * cut])
    cols = pl.ds(width, 2 * size)
    pre_ref[:, cols] = last[8:, : 2 * size]
    bc_ref[...] = conv(cols)
    bc_ref.flush()
    step_raw = last[16:, 2 * size :] + numbers_ref[2:3, :]
    step_raw_ref[...] = step_raw
    step = jax.nn.softplus(step_raw)
    earlier = low(triangle(tokens, lambda t, s: jnp.where(t >= s, 1.0, 0.0)))
    cum = dot_split(earlier, -step * numbers_ref[0:1, :], 3)
    cum_rows[...] = cum.T
    tail = cum[tokens - 1 : tokens, :]
    spreader = head_spread(lanes, width, 64)
    spread[...] = split_dot(jnp.exp(tail - cum) * step, spreader, 2)
    held, read = bc_ref[:, :size], bc_ref[:, size:]

    @pl.loop(0, 4)
    def _(i):
        load(4 + i).wait()
        from_cols = pl.ds(pl.multiple_of((4 + i) * cut, 128), cut)
        here = pl.ds(pl.multiple_of(i * cut, 128), cut)
        pre_ref[:, here] = dot_nn(normed[...], weights[:, from_cols])[8:]
        x = conv(here)
        x_ref[:, here] = x
        made_rows = dot_three(x * spread[:, here], held, dot_tn)
        made_rows = made_rows.reshape(cut // each, each, size)
        message[pl.ds(i * (cut // each), cut // each)] = scan_rows(made_rows, jnp.exp(tail))

    for ref in (x_ref, pre_ref, conv_ref):
        ref.flush()
    scan = Scan(False, at, me, message, start_ref, got, made, scan_sems)
    scan.begin()

    @pl.loop(0, 4)
    def _(i):
        load(i).wait()
        here = pl.ds(pl.multiple_of(i * cut, 128), cut)
        z_ref[:, here] = dot_nn(normed[16 : 16 + tokens, :], weights[:, here])

    z_ref.flush()
    scan.middle()
    out = Spread(at, me, rows_ref, slots_ref, slot_sems, *OUT[1], False)
    gather.second(2)
    out.start()

    spread[...] = split_dot(step, spreader, 2)
    blocks = ((0, 0), (1, 0), (1, 1))
    for n, (t, s) in enumerate(blocks):
        rows, columns = slice(t * mid, (t + 1) * mid), slice(s * mid, (s + 1) * mid)
        scores[n] = dot_three(read[rows], held[columns], dot_nt)
    causal = triangle(mid, lambda t, s: t >= s)
    second_head = lax.broadcasted_iota(jnp.int32, (tokens, 128), 1) >= 64

    @pl.loop(0, width // 128)
    def _(i):
        here = pl.ds(pl.multiple_of(i * 128, 128), 128)
        values, values_less = split(x_ref[:, here] * spread[:, here], 2)
        results = []
        for which in range(2):
            row = cum_rows[pl.ds(2 * i + which, 1), :]
            column = jnp.broadcast_to(row, (128, tokens)).T
            total = [None, None]
            for n, (t, s) in enumerate(blocks):
                columns = slice(s * mid, (s + 1) * mid)
                decay = jnp.exp(column[t * mid : (t + 1) * mid] - row[:, columns])
                if s == t:
                    decay = jnp.where(causal, decay, 0.0)
                mixing, mixing_less = split(decay * scores[n], 2)
                part = dot_nn(mixing, values[columns]) + dot_nn(mixing_less, values[columns])
                part = part + dot_nn(mixing, values_less[columns])
                total[t] = part if total[t] is None else total[t] + part
            results.append(total)
        for t in range(2):
            rows = slice(t * mid, (t + 1) * mid)
            y_ref[rows, here] = jnp.where(second_head[rows], results[1][t], results[0][t])

    scan.end()
    skip = split_dot(jnp.broadcast_to(numbers_ref[1:2, :], (8, lanes)), spreader, 2)[0:1, :]
    carry = split_dot(jnp.exp(cum), spreader, 2)
    square = jnp.zeros((tokens, 1), jnp.float32)
    for c in range(0, width, cut):
        here = slice(c, c + cut)
        start = start_ref[c // each : (c + cut) // each].reshape(cut, size)
        through = dot_three(read, start, dot_nt)
        y = y_ref[:, here] + carry[:, here] * through + skip[:, here] * x_ref[:, here]
        y_ref[:, here] = y
        z = z_ref[:, here]
        gated = y * (z * jax.nn.sigmoid(z))
        spread[:, here] = gated
        square = square + jnp.sum(gated * gated, axis=1, keepdims=True)
    y_ref.flush()
    mine[...] = jnp.broadcast_to(square, mine.shape)
    swap = pltpu.make_async_remote_copy(
        src_ref=mine,
        dst_ref=theirs,
        send_sem=pair_sems.at[0],
        recv_sem=pair_sems.at[1],
        device_id={"head": 1 - head},
    )
    swap.start()
    swap.wait()
    scale = lax.rsqrt((mine[...] + theirs[...]) / (2 * width) + EPSILON)
    scale_ref[...] = scale
    for c in range(0, width, cut):
        here = slice(c, c + cut)
        gated_ref[:, here] = low(spread[:, here] * scale[:, 0:1] * gain_ref[:, here])
    gather.arrived(2)
    gather.end()
    out.wait()


def mixer(layer_in, edge, table, weights, width, late, grad_rows, collective):
    tokens, model = layer_in.shape
    channels, lanes = table.shape[1], 128
    size = (channels - width) // 2
    each, mid = width // 64, tokens // 2
    f32, bf16 = jnp.float32, jnp.bfloat16
    vmem, hbm = pl.BlockSpec(memory_space=pltpu.VMEM), pl.BlockSpec(memory_space=pl.ANY)
    out = [
        ((tokens, model), bf16),
        ((tokens, width), f32),
        ((tokens, width), f32),
        ((tokens, 2 * size), f32),
        ((tokens, channels), f32),
        ((tokens + 8, channels), f32),
        ((tokens, lanes), f32),
        ((64, each, size), f32),
        ((tokens, width), f32),
        ((tokens, width), bf16),
        ((tokens, lanes), f32),
        (late.shape, bf16),
        (part_shape(OUT[1], grad_rows).shape, bf16),
    ]
    return call(
        mixer_kernel,
        out_shape=[jax.ShapeDtypeStruct(*shape) for shape in out],
        in_specs=[vmem, vmem, vmem, hbm, hbm, hbm],
        out_specs=[Eager] * 6 + [vmem] * 2 + [Eager] * 2 + [vmem] + [hbm] * 2,
        scratch_shapes=[
            pltpu.VMEM(weights.shape, bf16),
            pltpu.VMEM((tokens + 16, model), bf16),
            pltpu.VMEM((64, each + 8, size), bf16),
            pltpu.VMEM((64, each + 8, size), bf16),
            pltpu.VMEM((64, each, size), f32),
            pltpu.VMEM((tokens, width), f32),
            pltpu.VMEM((lanes, tokens), f32),
            pltpu.VMEM((3, mid, mid), f32),
            pltpu.VMEM((tokens, lanes), f32),
            pltpu.VMEM((tokens, lanes), f32),
            pltpu.SemaphoreType.DMA((9,)),
            pltpu.SemaphoreType.DMA((4,)),
            pltpu.SemaphoreType.DMA((2,)),
        ]
        + gather_shapes()[:2]
        + [pltpu.SemaphoreType.DMA((9,))],
        input_output_aliases={4: len(out) - 2},
        compiler_params=params(collective, vmem_limit_bytes=VMEM),
        name="mixer",
    )(layer_in, edge, table, weights, late, grad_rows)


def per_device(
    layer_in,
    norm_first,
    mixer_in,
    state_proj,
    step_proj,
    step_bias,
    conv_main,
    conv_state,
    decay_rate,
    skip_gain,
    gate_gain,
    mixer_out,
    norm_second,
    shared_gate_up,
    shared_down,
    expert_gate_up,
    expert_down,
    routes,
    route_weights,
    grad_out,
):
    tokens, model_width = layer_in.shape
    inner_dev = mixer_in.shape[2]
    state_size = state_proj.shape[1] // 2
    heads_dev = step_proj.shape[1]
    conv_taps = conv_main.shape[0]
    shared_dev = shared_down.shape[1]
    local_experts = expert_gate_up.shape[0]
    experts_all = local_experts * lax.axis_size("seq")
    choices_per = routes.shape[1]
    capacity = max(2, tokens * choices_per * 4 // (3 * experts_all))
    slots_dev = capacity // lax.axis_size("head")
    lanes = 128
    vectors = [
        conv_main,
        conv_state,
        [gain.reshape(-1, 128) for gain in (norm_first, norm_second, gate_gain)],
        [number[None] for number in (decay_rate, skip_gain, step_bias)],
    ]
    gathered, late_rows, edge, position, slot_weight, grads_out, grads_first, table, gate_up = gather_rows(
        [mixer_in, state_proj, step_proj],
        [mixer_out, shared_gate_up, shared_down],
        expert_gate_up.reshape(expert_gate_up.shape[1:]),
        layer_in,
        routes,
        route_weights,
        grad_out,
        vectors,
        experts_all,
        slots_dev,
        0,
    )
    weights_in = gathered.reshape(model_width, -1)
    (
        normed,
        gate_z,
        heads_x,
        state_both,
        conv_sum,
        pre,
        step_raw,
        state_start,
        ssd,
        normed_gate,
        gate_scale,
        gathered,
        grads_second,
    ) = mixer(
        layer_in,
        edge,
        table,
        weights_in,
        inner_dev,
        late_rows,
        grads_out,
        1,
    )
    weights_late = gathered.reshape(model_width, -1)
    (
        grad_home,
        res_sums,
        expert_gate_up_grad,
        expert_down_grad,
        shared_part,
        shared_back,
        shared_right,
        residual,
        normed_second,
        scale_second,
    ) = experts(
        normed_gate,
        weights_late,
        layer_in,
        table,
        position,
        [grads_first, grads_second],
        grads_out,
        gate_up,
        expert_down.reshape(-1, model_width),
        grad_out,
        slots_dev,
        2,
    )
    (
        mixer_out_grad,
        shared_gate_up_grad,
        shared_down_grad,
        right_grads,
        taps_grad,
        heads_grad,
        home_near,
        grad_resid,
        norm_second_grad,
        gate_gain_grad,
    ) = mixer_back(
        [normed_second, grad_out],
        [normed_gate, shared_right],
        grad_home,
        position,
        shared_back,
        residual,
        scale_second,
        weights_late,
        gate_z,
        gate_scale,
        ssd,
        heads_x,
        state_both,
        conv_sum,
        pre,
        step_raw,
        table,
        state_start.reshape(inner_dev, state_size),
        res_sums,
        3,
    )
    (
        mixer_in_grad,
        state_proj_grad,
        step_proj_grad,
        input_grad,
        layer_out,
        norm_first_sum,
        norm_second_sum,
        gate_gain_sum,
        conv_main_grad,
        conv_state_grad,
        (skip_gain_grad, decay_rate_grad, step_bias_grad),
    ) = input_back(
        normed,
        right_grads,
        tuple(((0, 0, start, start, 1152),) for start in (0, 1152, 2304)),
        weights_in,
        layer_in,
        table,
        grad_resid,
        res_sums,
        [home_near],
        position,
        slot_weight,
        shared_part,
        residual,
        taps_grad,
        heads_grad,
        norm_second_grad,
        gate_gain_grad,
        heads_dev,
        4,
    )
    (
        layer_out,
        input_grad,
        expert_gate_up_grad,
        expert_down_grad,
        mixer_in_grad,
        state_proj_grad,
        step_proj_grad,
        norm_first_sum,
        norm_second_sum,
        gate_gain_sum,
        conv_main_grad,
        conv_state_grad,
        skip_gain_grad,
        decay_rate_grad,
        step_bias_grad,
        mixer_out_grad,
        shared_gate_up_grad,
        shared_down_grad,
    ) = emit(
        [
            layer_out,
            input_grad,
            expert_gate_up_grad,
            expert_down_grad,
            mixer_in_grad,
            state_proj_grad,
            step_proj_grad,
            norm_first_sum,
            norm_second_sum,
            gate_gain_sum,
            conv_main_grad,
            conv_state_grad,
            skip_gain_grad,
            decay_rate_grad,
            step_bias_grad,
            mixer_out_grad,
            shared_gate_up_grad,
            shared_down_grad,
        ]
    )
    expert_gate_up_grad = expert_gate_up_grad.reshape(model_width, -1, 2, lanes)
    expert_gate_up_grad = expert_gate_up_grad.transpose(0, 2, 1, 3).reshape(expert_gate_up.shape)
    return (
        layer_out,
        input_grad,
        norm_first_sum.reshape(-1),
        mixer_in_grad,
        state_proj_grad,
        step_proj_grad,
        step_bias_grad.reshape(-1),
        conv_main_grad,
        conv_state_grad,
        decay_rate_grad.reshape(-1),
        skip_gain_grad.reshape(-1),
        gate_gain_sum.reshape(-1),
        mixer_out_grad,
        norm_second_sum.reshape(-1),
        shared_gate_up_grad,
        shared_down_grad,
        expert_gate_up_grad,
        expert_down_grad[None],
    )


def solution(mesh):
    placed = (
        P("seq", None),
        P(),
        P("seq", None, "head"),
        P("seq", None),
        P("seq", "head"),
        P("head"),
        P(None, "head"),
        P(),
        P("head"),
        P("head"),
        P("head"),
        P("seq", "head"),
        P(),
        P("seq", None, "head"),
        P("seq", "head"),
        P("seq", None, None, "head"),
        P("seq", "head", None),
        P("seq", None),
        P("seq", None),
        P("seq", None),
    )
    return jax.shard_map(
        per_device,
        mesh=mesh,
        in_specs=placed,
        out_specs=(
            P("seq", None),
            P("seq", None),
            P(),
            P("seq", None, "head"),
            P("seq", None),
            P("seq", "head"),
            P("head"),
            P(None, "head"),
            P(),
            P("head"),
            P("head"),
            P("head"),
            P("seq", "head"),
            P(),
            P("seq", None, "head"),
            P("seq", "head"),
            P("seq", None, None, "head"),
            P("seq", "head", None),
        ),
        check_vma=False,
    )
```

```python
import functools
import jax
import jax.numpy as jnp
from jax import lax
from jax.experimental import pallas as pl
from jax.experimental.pallas import tpu as pltpu
from jax.sharding import PartitionSpec as P

ORDERS = ((0, 1, 2), (1, 2, 0), (2, 0, 1))
VMEM = 62 << 20
EPSILON = 1e-05


def coordinates():
    me = lax.axis_index("seq")
    return me, [me // 16, (me // 4) % 4, me % 4]


def seq_of(at):
    return at[0] * 16 + at[1] * 4 + at[2]


def moved(at, axis, by):
    return [(c + by) % 4 if i == axis else c for i, c in enumerate(at)]


def announce(me, with_sibling):
    barrier = pltpu.get_barrier_semaphore()

    @pl.loop(1, 64)
    def _(k):
        pl.semaphore_signal(barrier, inc=1, device_id={"seq": lax.rem(me + k, 64)})

    if with_sibling:
        pl.semaphore_signal(barrier, inc=1, device_id={"head": 1 - lax.axis_index("head")})


def await_all(with_sibling):
    pl.semaphore_wait(pltpu.get_barrier_semaphore(), 64 if with_sibling else 63)


def parts_of(columns):
    third = columns // 3
    tiles = third // 128
    half = tiles // 2 * 128
    return third, half


def region(at, order, phase, value, cols):
    index = [None] * 3
    for i in range(3):
        if i < phase:
            index[order[i]] = slice(None)
        elif i == phase:
            index[order[i]] = value
        else:
            index[order[i]] = at[order[i]]
    return tuple(index) + (slice(None), cols)


class Ways:
    def __init__(self, at):
        self.at = at

    def group(self, g, back=False):
        x, z, y = self.at
        sign, lead = (-1, 8) if back else (1, 0)
        near, far = lax.rem(g, 4), g // 4
        xs = [lax.rem(x + lead + sign * a, 4) * 16 for a in range(4)]
        zs = [lax.rem(z + lead + sign * (near + a), 4) * 4 for a in range(4)]
        ys = [lax.rem(y + lead + sign * (far + a), 4) for a in range(4)]
        return [(g * 8 + n, xs[n % 4] + zs[n % 4] + ys[(n % 4 + n // 4 * 2) % 4]) for n in range(8)]

    def each(self, first, last, body, back=False):
        @pl.loop(first, last)
        def _(g):
            for n, (k, device) in enumerate(self.group(g, back)):
                if n == 0:
                    pl.when(k > 0)(functools.partial(body, k, device))
                else:
                    body(k, device)


class Lazy:
    def __init__(self, source, ref, sem):
        self.ref, self.copy = ref, pltpu.make_async_copy(source, ref, sem)
        self.shape, self.dtype = ref.shape, ref.dtype
        self.copy.start()

    def ready(self):
        if self.copy is not None:
            self.copy.wait()
            self.copy = None
        return self.ref

    @property
    def at(self):
        return self.ready().at

    def __getitem__(self, index):
        return self.ready()[index]


class Eager:
    def __init__(self, target, ref, sem):
        self.ref, self.copy, self.going = ref, pltpu.make_async_copy(ref, target, sem), False
        self.shape, self.dtype, self.at = ref.shape, ref.dtype, ref.at

    def __getitem__(self, index):
        return self.ref[index]

    def __setitem__(self, index, value):
        self.ref[index] = value

    def flush(self):
        if not self.going:
            self.going = True
            self.copy.start()


def ready(*refs):
    for ref in refs:
        if isinstance(ref, Lazy):
            ref.ready()


def call(kernel, out_shape, in_specs, out_specs, scratch_shapes, **options):
    def run(*args):
        leaves, tree = jax.tree.flatten(list(args))
        specs = tree.flatten_up_to(list(in_specs))
        shapes, out_tree = jax.tree.flatten(list(out_shape))
        out_kinds = out_tree.flatten_up_to(list(out_specs))
        lazy = [n for n, spec in enumerate(specs) if spec is Lazy]
        eager = [n for n, spec in enumerate(out_kinds) if spec is Eager]
        hbm = pl.BlockSpec(memory_space=pl.ANY)
        buffers = [pltpu.VMEM(leaves[n].shape, leaves[n].dtype) for n in lazy]
        buffers += [pltpu.VMEM(shapes[n].shape, shapes[n].dtype) for n in eager]
        buffers += [pltpu.SemaphoreType.DMA((max(1, len(lazy)),))]
        buffers += [pltpu.SemaphoreType.DMA((max(1, len(eager)),))]
        own = len(scratch_shapes)

        def body(*refs):
            ins, outs = list(refs[: len(leaves)]), list(refs[len(leaves) :][: len(shapes)])
            rest = refs[len(leaves) + len(shapes) :]
            more = rest[own:]
            for n, index in enumerate(lazy):
                ins[index] = Lazy(ins[index], more[n], more[-2].at[n])
            for n, index in enumerate(eager):
                outs[index] = Eager(outs[index], more[len(lazy) + n], more[-1].at[n])
            kernel(*tree.unflatten(ins), *out_tree.unflatten(outs), *rest[:own])
            for index in lazy:
                ins[index].ready()
            for index in eager:
                outs[index].flush()
            for index in eager:
                outs[index].copy.wait()

        out = pl.pallas_call(
            body,
            out_shape=shapes,
            in_specs=[hbm if spec is Lazy else spec for spec in specs],
            out_specs=[hbm if kind is Eager else kind for kind in out_kinds],
            scratch_shapes=list(scratch_shapes) + buffers,
            **options,
        )(*leaves)
        return out_tree.unflatten(out)

    return run


def emit_kernel(*refs):
    count = (len(refs) - 1) // 3
    sources, targets, buffers, sems = refs[:count], refs[count : 2 * count], refs[2 * count : -1], refs[-1]
    pieces = []
    for n in range(count):
        rows = sources[n].shape[0]
        parts = 4 if rows >= 256 else 1
        for part in range(parts):
            here = pl.ds(part * (rows // parts), rows // parts)
            place = buffers[n].at[here]
            come = pltpu.make_async_copy(sources[n].at[here], place, sems.at[0, n, part])
            go = pltpu.make_async_copy(place, targets[n].at[here], sems.at[1, n, part])
            come.start()
            pieces.append((come, go))
    for come, go in pieces:
        come.wait()
        go.start()
    for _, go in pieces:
        go.wait()


def emit(arrays):
    hbm = [pl.BlockSpec(memory_space=pl.ANY)] * len(arrays)
    return pl.pallas_call(
        emit_kernel,
        out_shape=[jax.ShapeDtypeStruct(array.shape, array.dtype) for array in arrays],
        in_specs=hbm,
        out_specs=hbm,
        scratch_shapes=[pltpu.VMEM(array.shape, array.dtype) for array in arrays]
        + [pltpu.SemaphoreType.DMA((2, len(arrays), 4))],
        compiler_params=pltpu.CompilerParams(vmem_limit_bytes=VMEM),
        name="emit",
    )(*arrays)


class Spread:
    def __init__(self, at, me, source, target, sems, first, last, back):
        self.at, self.me, self.source, self.target = at, me, source, target
        self.sems = sems
        self.first, self.last, self.back = first, last, back

    def start(self, first=None, last=None):
        first = self.first if first is None else first
        last = self.last if last is None else last
        if first == 0:
            own = self.source.at[0 if self.back else self.me]
            pltpu.make_async_copy(own, self.target.at[0], self.sems.at[1]).start()

        def put(k, device):
            pltpu.make_async_remote_copy(
                src_ref=self.source.at[k if self.back else device],
                dst_ref=self.target.at[k - 8 * self.first],
                send_sem=self.sems.at[0],
                recv_sem=self.sems.at[1 + k // 8],
                device_id={"seq": device},
            ).start()

        Ways(self.at).each(first, last, put, self.back)

    def arrived(self, first, last):
        for g in range(first, last):
            here = self.target.at[pl.ds(8 * (g - self.first), 8)]
            pltpu.make_async_copy(here, here, self.sems.at[1 + g]).wait()

    def sent(self):
        count = 8 * (self.last - self.first)
        here = self.target.at[pl.ds(0, count - 1 if self.first == 0 else count)]
        pltpu.make_async_copy(here, here, self.sems.at[0]).wait()

    def wait(self):
        self.arrived(self.first, self.last)
        self.sent()


OUT = ((0, 4), (4, 5), (5, 8))
HOME = ((0, 6), (6, 8))


def part_shape(span, rows):
    return jax.ShapeDtypeStruct((8 * (span[1] - span[0]),) + rows.shape[1:], rows.dtype)


def params(collective, **more):
    return pltpu.CompilerParams(collective_id=collective, has_side_effects=True, **more)


class PairSum:
    def __init__(self, mine, theirs, sems, cut):
        self.mine, self.theirs, self.sems, self.cut = mine, theirs, sems, cut
        self.count = mine.shape[1] // cut

    def copy(self, n):
        cols = pl.ds(n * self.cut, self.cut)
        return pltpu.make_async_remote_copy(
            src_ref=self.mine.at[:, cols],
            dst_ref=self.theirs.at[:, cols],
            send_sem=self.sems.at[0, n],
            recv_sem=self.sems.at[1, n],
            device_id={"head": 1 - lax.axis_index("head")},
        )


def experts_kernel(
    gated_ref,
    weights_ref,
    layer_ref,
    table_ref,
    position_ref,
    grads_refs,
    grad_rows_ref,
    gate_up_ref,
    down_ref,
    grad_out_ref,
    home_ref,
    res_ref,
    gate_up_grad_ref,
    down_grad_ref,
    shared_ref,
    back_ref,
    right_ref,
    resid_ref,
    normed_ref,
    scale_ref,
    rows_ref,
    grads_here,
    mine,
    theirs,
    slot_in,
    grad_slots,
    theirs_x,
    theirs_y,
    sums,
    wide_grad,
    weights,
    load_sems,
    pair_sems,
    out_sems,
    send,
    home_send,
    home_recv,
    sems,
):
    me, at = coordinates()
    head = lax.axis_index("head")
    sibling = {"head": 1 - head}
    names = ("recv", "fwd_send", "fwd_recv", "kept", "given_send", "given_recv")
    names += ("x_send", "x_recv", "y_send", "y_recv")
    sem = {name: sems.at[n] for n, name in enumerate(names)}
    announce(me, True)
    shared_hidden = right_ref.shape[1] // 3
    tokens, model = layer_ref.shape
    inner = gated_ref.shape[1]
    loads = []
    for n, cols in enumerate((pl.ds(0, inner), pl.ds(inner, 3 * shared_hidden))):
        loads.append(
            pltpu.make_async_copy(weights_ref.at[:, cols], weights.at[:, cols], load_sems.at[n])
        )
        loads[n].start()
    norm_ref = table_ref.at[5:6, 0:model]
    wide_grad[...] = jnp.zeros_like(wide_grad)
    down_grad_ref[...] = jnp.zeros_like(down_grad_ref)
    ways = Ways(at)
    await_all(True)
    out = Spread(at, me, grad_rows_ref, grads_here, out_sems, *OUT[2], False)

    def group(c):
        return pl.ds(pl.multiple_of(c * 8, 8), 8)

    def given(c, source=None):
        there = grad_slots.at[group(c), head]
        return pltpu.make_async_remote_copy(
            src_ref=there if source is None else source,
            dst_ref=there,
            send_sem=sem["given_send"].at[c],
            recv_sem=sem["given_recv"].at[c],
            device_id=sibling,
        )

    def kept(c, source=None):
        there = grad_slots.at[group(c), head]
        return pltpu.make_async_copy(there if source is None else source, there, sem["kept"].at[c])

    def forward(c):
        return pltpu.make_async_remote_copy(
            src_ref=slot_in.at[group(c), head],
            dst_ref=slot_in.at[group(c), head],
            send_sem=sem["fwd_send"].at[c],
            recv_sem=sem["fwd_recv"].at[c],
            device_id=sibling,
        )

    def swap(c, source, target, name):
        return pltpu.make_async_remote_copy(
            src_ref=source.at[group(c), 1 - head],
            dst_ref=target.at[group(c)],
            send_sem=sem[name + "_send"].at[c],
            recv_sem=sem[name + "_recv"].at[c],
            device_id=sibling,
        )

    for (first, last), grads_ref in zip(OUT, grads_refs):
        for c in range(first, last):
            source = grads_ref.at[pl.ds(8 * (c - first), 8)]
            kept(c, source).start()
            given(c, source).start()

    out.start()

    cut = 256
    pair = PairSum(mine, theirs, pair_sems, cut)
    loads[0].wait()
    gated = gated_ref[...]
    for n in range(pair.count):
        rows = slice(n * cut, (n + 1) * cut)
        mine[:, rows] = dot_nt(gated, weights[rows, 0:inner])
        pair.copy(n).start()
    loads[1].wait()
    both = slice(inner, inner + 2 * shared_hidden)
    less = slice(inner + 2 * shared_hidden, inner + 3 * shared_hidden)
    shared_grad_hid = dot_nn(grad_out_ref[...], weights[:, less])
    square = jnp.zeros((tokens, 1), jnp.float32)
    for n in range(pair.count):
        rows = slice(n * cut, (n + 1) * cut)
        pair.copy(n).wait()
        resid = layer_ref[:, rows].astype(jnp.float32) + (mine[:, rows] + theirs[:, rows])
        resid_ref[:, rows] = resid
        square = square + jnp.sum(resid * resid, axis=1, keepdims=True)
    scale = lax.rsqrt(square / model + EPSILON)
    scale_ref[...] = jnp.broadcast_to(scale, scale_ref.shape)
    for n in range(pair.count):
        rows = slice(n * cut, (n + 1) * cut)
        normed_ref[:, rows] = low(resid_ref[:, rows] * scale * norm_ref[:, rows])
    resid_ref.flush()
    normed_ref.flush()
    ready(position_ref)
    normed = normed_ref[...]
    slots, step = rows_ref.shape[1], 16

    @pl.loop(0, rows_ref.shape[0] // step)
    def _(i):
        here = pl.ds(pl.multiple_of(i * step, step), step)
        chosen = chosen_slots(position_ref[here, :], slots)
        rows_ref[here] = low(dot_nn(low(chosen), normed)).reshape(step, slots, model)

    own = pltpu.make_async_copy(rows_ref.at[me], slot_in.at[0, head], sem["recv"].at[0])
    own.start()

    def put(k, target):
        pltpu.make_async_remote_copy(
            src_ref=rows_ref.at[target],
            dst_ref=slot_in.at[k, head],
            send_sem=send,
            recv_sem=sem["recv"].at[k // 8],
            device_id={"seq": target},
        ).start()

    ways.each(0, 8, put)

    hidden = down_ref.shape[0]
    width = down_ref.shape[1]

    def nt(left, right):
        return lax.dot_general(
            left, right, (((1,), (1,)), ((), ())), preferred_element_type=jnp.float32
        )

    def tn(left, right):
        return lax.dot_general(
            left, right, (((0,), (0,)), ((), ())), preferred_element_type=jnp.float32
        )

    gate_up = dot_nn(normed, weights[:, both])
    gate, up = gate_up[:, :shared_hidden], gate_up[:, shared_hidden:]
    act, slope = silu_parts(gate)
    hid = low(act * up)
    right_ref[:, 2 * shared_hidden :] = hid
    right_ref[:, 0:shared_hidden] = low(shared_grad_hid * up * slope)
    right_ref[:, shared_hidden : 2 * shared_hidden] = low(shared_grad_hid * act)
    grads = right_ref[:, 0 : 2 * shared_hidden]
    for c in range(0, width, 256):
        rows = slice(c, c + 256)
        shared_ref[:, rows] = dot_nt(hid, weights[rows, less])
        back_ref[:, rows] = dot_nt(grads, weights[rows, both])
    for ref in (shared_ref, back_ref, right_ref):
        ref.flush()
    ready(gate_up_ref, down_ref)

    @pl.loop(0, 10)
    def _(i):
        @pl.when(i < 8)
        def _():
            c = i
            pltpu.make_async_copy(
                rows_ref.at[group(c)], slot_in.at[group(c), head], sem["recv"].at[c]
            ).wait()
            forward(c).start()

        for late in range(*OUT[2]):

            @pl.when(i == late - 2)
            def _():
                out.arrived(late, late + 1)
                source = grads_here.at[pl.ds(8 * (late - OUT[2][0]), 8)]
                kept(late, source).start()
                given(late, source).start()

        @pl.when((i >= 1) & (i < 9))
        def _():
            c = i - 1
            forward(c).wait()
            kept(c).wait()
            given(c).wait()
            rows = slot_in[group(c)].reshape(256, width)
            grads = grad_slots[group(c)].reshape(256, width)
            both = jnp.dot(rows, gate_up_ref[...], preferred_element_type=jnp.float32)
            gate, up = both[:, :hidden], both[:, hidden:]
            sig = jax.nn.sigmoid(gate)
            act = gate * sig
            hid = (act * up).astype(jnp.bfloat16)
            grad_hid = nt(grads, down_ref[...])
            grad_gate = grad_hid * up * (sig * (1.0 + gate * (1.0 - sig)))
            grad_both = jnp.concatenate([grad_gate, grad_hid * act], axis=1).astype(jnp.bfloat16)
            wide_grad[...] += tn(rows, grad_both)
            down_grad_ref[...] += tn(hid, grads)
            back = nt(grad_both, gate_up_ref[...]).astype(jnp.bfloat16)
            slot_in[group(c)] = back.reshape(8, 2, 16, width)
            res = jnp.dot(hid, down_ref[...], preferred_element_type=jnp.float32)
            grad_slots[group(c)] = res.astype(jnp.bfloat16).reshape(8, 2, 16, width)
            swap(c, slot_in, theirs_x, "x").start()
            swap(c, grad_slots, theirs_y, "y").start()

        @pl.when(i >= 2)
        def _():
            c = i - 2
            swap(c, slot_in, theirs_x, "x").wait()

            def add(k):
                total = slot_in[k, head].astype(jnp.float32) + theirs_x[k].astype(jnp.float32)
                sums[k] = total.astype(sums.dtype)

            def put_home(k, source):
                add(k)
                pltpu.make_async_remote_copy(
                    src_ref=sums.at[k],
                    dst_ref=home_ref.at[me],
                    send_sem=home_send,
                    recv_sem=home_recv,
                    device_id={"seq": source},
                ).start()

            @pl.when(c == 0)
            def _():
                add(0)
                pltpu.make_async_copy(sums.at[0], home_ref.at[me], home_recv).start()

            ways.each(c, c + 1, put_home, back=True)
            swap(c, grad_slots, theirs_y, "y").wait()

            @pl.loop(0, 8)
            def _(n):
                j = c * 8 + n
                total = grad_slots[j, head].astype(jnp.float32) + theirs_y[j].astype(jnp.float32)
                res_ref[j] = total.astype(res_ref.dtype)

    out.sent()
    tiles = hidden // 128
    for tile in range(tiles):
        for which in range(2):
            start = which * hidden + tile * 128
            gate_up_grad_ref[pl.ds(tile * 2 + which, width, stride=2 * tiles), :] = wide_grad[
                :, start : start + 128
            ]
    some = pl.ds(0, 63)
    pltpu.make_async_copy(rows_ref.at[some], rows_ref.at[some], send).wait()
    pltpu.make_async_copy(sums.at[some], sums.at[some], home_send).wait()
    pltpu.make_async_copy(sums, home_ref, home_recv).wait()


def experts(
    gated, weights, layer_in, table, position, grads, grad_rows, gate_up, down, grad_out, slots, collective
):
    tokens, model = layer_in.shape
    shared_hidden = (weights.shape[1] - gated.shape[1]) // 3
    hidden, width = down.shape
    half, bf16 = (position.shape[0], slots, model), jnp.bfloat16
    whole = (half[0], 2) + half[1:]
    vmem, hbm = pl.BlockSpec(memory_space=pltpu.VMEM), pl.BlockSpec(memory_space=pl.ANY)
    home, res, wide, down_grad, *shared = call(
        experts_kernel,
        out_shape=[
            jax.ShapeDtypeStruct(half, bf16),
            jax.ShapeDtypeStruct(half, bf16),
            jax.ShapeDtypeStruct((width * 2 * hidden // 128, 128), jnp.float32),
            jax.ShapeDtypeStruct((hidden, width), jnp.float32),
            jax.ShapeDtypeStruct((tokens, width), jnp.float32),
            jax.ShapeDtypeStruct((tokens, width), jnp.float32),
            jax.ShapeDtypeStruct((tokens, 3 * shared_hidden), bf16),
            jax.ShapeDtypeStruct((tokens, model), jnp.float32),
            jax.ShapeDtypeStruct((tokens, model), bf16),
            jax.ShapeDtypeStruct((tokens, 128), jnp.float32),
        ],
        in_specs=[Lazy, hbm, Lazy, vmem, Lazy, [hbm] * len(grads), hbm, Lazy, Lazy, Lazy],
        out_specs=[hbm] + [vmem] * 3 + [Eager] * 5 + [vmem],
        scratch_shapes=[
            pltpu.VMEM(half, bf16),
            pltpu.VMEM(part_shape(OUT[2], grad_rows).shape, bf16),
            pltpu.VMEM((tokens, model), jnp.float32),
            pltpu.VMEM((tokens, model), jnp.float32),
            pltpu.VMEM(whole, bf16),
            pltpu.VMEM(whole, bf16),
            pltpu.VMEM(half, bf16),
            pltpu.VMEM(half, bf16),
            pltpu.VMEM(half, bf16),
            pltpu.VMEM((width, 2 * hidden), jnp.float32),
            pltpu.VMEM(weights.shape, bf16),
            pltpu.SemaphoreType.DMA((2,)),
            pltpu.SemaphoreType.DMA((2, model // 256)),
            pltpu.SemaphoreType.DMA((9,)),
            pltpu.SemaphoreType.DMA,
            pltpu.SemaphoreType.DMA,
            pltpu.SemaphoreType.DMA,
            pltpu.SemaphoreType.DMA((10, 8)),
        ],
        compiler_params=params(collective, vmem_limit_bytes=VMEM),
        name="experts",
    )(gated, weights, layer_in, table, position, grads, grad_rows, gate_up, down, grad_out)
    return home, res, wide, down_grad, *shared


class Scan:
    def __init__(self, reverse, at, me, x_ref, out_ref, got, made, sems):
        self.reverse, self.at, self.me = reverse, at, me
        self.x_ref, self.out_ref, self.got, self.made = x_ref, out_ref, got, made
        self.send, self.recv, self.back_send, self.back_recv = [sems.at[n] for n in range(4)]

    def spread(self, source, target_ref, send, recv):
        def put(_, target):
            pltpu.make_async_remote_copy(
                src_ref=source.at[target],
                dst_ref=target_ref.at[self.me],
                send_sem=send,
                recv_sem=recv,
                device_id={"seq": target},
            ).start()

        Ways(self.at).each(0, 8, put)

    def begin(self):
        self.got[self.me] = self.x_ref[self.me]
        self.spread(self.x_ref, self.got, self.send, self.recv)

    def middle(self):
        some = pl.ds(0, 63)
        x_ref, got, made = self.x_ref, self.got, self.made
        pltpu.make_async_copy(x_ref.at[some], x_ref.at[some], self.send).wait()
        pltpu.make_async_copy(got.at[some], got.at[some], self.recv).wait()
        heads, width = made.shape[1:]
        number = lax.broadcasted_iota(jnp.int32, (heads, width), 0) + heads * self.me
        chosen = number // 64 == lax.broadcasted_iota(jnp.int32, (heads, width), 1)

        def step(k, state):
            at_k = 63 - k if self.reverse else k
            made[at_k] = state
            rows = got[at_k].astype(jnp.float32)
            row = jnp.sum(rows[heads:], axis=0, keepdims=True)
            decay = jnp.sum(jnp.where(chosen, row, 0.0), axis=1, keepdims=True)
            return decay * state + rows[:heads]

        lax.fori_loop(0, 64, step, jnp.zeros((heads, width), jnp.float32), unroll=8)
        self.out_ref[self.me] = made[self.me]
        self.spread(made, self.out_ref, self.back_send, self.back_recv)

    def end(self):
        some = pl.ds(0, 63)
        made = self.made
        pltpu.make_async_copy(made.at[some], made.at[some], self.back_send).wait()
        pltpu.make_async_copy(made.at[some], made.at[some], self.back_recv).wait()


def scan_rows(states, decay):
    decays = [part.astype(jnp.float32) for part in split(decay, 3)]
    decays = jnp.concatenate(decays + [jnp.zeros((5, decay.shape[1]), jnp.float32)], axis=0)
    decays = jnp.broadcast_to(decays[None], (states.shape[0],) + decays.shape)
    return low(jnp.concatenate([states, decays], axis=1))


class Small:
    def __init__(self, at, me, x_ref, out_ref, got, sems):
        self.at, self.me = at, me
        self.x_ref, self.out_ref, self.got = x_ref, out_ref, got
        self.send, self.recv, self.back_send, self.back_recv = [sems.at[n] for n in range(4)]

    def begin(self):
        self.got[self.me] = self.x_ref[self.me]

        def put(_, target):
            pltpu.make_async_remote_copy(
                src_ref=self.x_ref.at[target],
                dst_ref=self.got.at[self.me],
                send_sem=self.send,
                recv_sem=self.recv,
                device_id={"seq": target},
            ).start()

        Ways(self.at).each(0, 8, put)

    def middle(self):
        some = pl.ds(0, 63)
        x_ref, got, out_ref, me = self.x_ref, self.got, self.out_ref, self.me
        pltpu.make_async_copy(x_ref.at[some], x_ref.at[some], self.send).wait()
        pltpu.make_async_copy(got.at[some], got.at[some], self.recv).wait()
        out_ref[me] = lax.fori_loop(1, 64, lambda k, total: total + got[k], got[0], unroll=9)

        def put(_, target):
            pltpu.make_async_remote_copy(
                src_ref=out_ref.at[me],
                dst_ref=out_ref.at[me],
                send_sem=self.back_send,
                recv_sem=self.back_recv,
                device_id={"seq": target},
            ).start()

        Ways(self.at).each(0, 8, put)

    def end(self):
        some = pl.ds(0, 63)
        got = self.got
        pltpu.make_async_copy(got.at[some], got.at[some], self.back_send).wait()
        pltpu.make_async_copy(got.at[some], got.at[some], self.back_recv).wait()


class Scatter:
    def __init__(self, at, plan, lefts, rights, out_ref, buf, rest, send, recv):
        self.at, self.plan, self.lefts, self.rights = at, plan, lefts, rights
        self.out_ref, self.buf, self.rest, self.send, self.recv = out_ref, buf, rest, send, recv
        self.third, self.half = parts_of(buf.shape[4])
        self.copies = {}

    def spans(self, p):
        start, third, half = p * self.third, self.third, self.half
        return pl.ds(start, half), pl.ds(start + half, third - half)

    def product(self, p):
        buf = self.buf
        rows = buf.shape[3]
        for which, other, first, start, length in self.plan[p]:
            left, right = self.lefts[which], self.rights[other]
            ready(left, right)

            @pl.loop(0, 4)
            def _(x):
                across = pl.ds(pl.multiple_of(x * 16 * rows, 128), 16 * rows)
                total = lax.dot_general(
                    left[:, across],
                    right[:, first : first + length],
                    (((0,), (0,)), ((), ())),
                    preferred_element_type=jnp.float32,
                )
                total = total.reshape(4, 4, rows, length).astype(jnp.bfloat16)
                buf[x, :, :, :, start : start + length] = total

    def send_to(self, phase, p, by, value, cols, slot, kind):
        order = ORDERS[p]
        axis = order[phase]
        lead = (slice(None),) * phase
        copy = pltpu.make_async_remote_copy(
            src_ref=self.buf.at[region(self.at, order, phase, value, cols)],
            dst_ref=self.rest[phase].at[(slot,) + lead + (slice(None), cols)],
            send_sem=self.send.at[phase, p, kind],
            recv_sem=self.recv.at[phase, p, kind],
            device_id={"seq": seq_of(moved(self.at, axis, by))},
        )
        copy.start()
        self.copies[phase, p, kind] = copy

    def added(self, phase, p, value, cols, slots):
        order, buf, room = ORDERS[p], self.buf, self.rest[phase]

        @pl.loop(0, 4**phase)
        def _(i):
            free = ((), (i,), (i // 4, i % 4))[phase]
            index = list(region(self.at, order, phase, value, cols))
            for n, axis in enumerate(sorted(order[:phase])):
                index[axis] = free[n]
            index = tuple(index)
            total = buf[index].astype(jnp.float32)
            for slot in slots:
                total = total + room[(slot,) + free + (slice(None), cols)].astype(jnp.float32)
            if phase == 0 and len(slots) == 2:
                self.out_ref[:, cols] = total
            else:
                buf[index] = total.astype(jnp.bfloat16)

    def first(self, phase, p):
        self.first_far(phase, p)
        self.first_near(phase, p)

    def first_far(self, phase, p):
        c = self.at[ORDERS[p][phase]]
        low, high = self.spans(p)
        self.send_to(phase, p, 1, (c + 2) % 4, low, 2, 0)
        self.send_to(phase, p, 3, (c + 2) % 4, high, 2, 1)

    def first_near(self, phase, p):
        c = self.at[ORDERS[p][phase]]
        low, high = self.spans(p)
        self.send_to(phase, p, 1, (c + 1) % 4, high, 0, 2)
        self.send_to(phase, p, 3, (c + 3) % 4, low, 1, 3)

    def second(self, phase, p):
        c = self.at[ORDERS[p][phase]]
        low, high = self.spans(p)
        self.copies[phase, p, 0].wait_recv()
        self.added(phase, p, (c + 1) % 4, low, (2,))
        self.send_to(phase, p, 1, (c + 1) % 4, low, 0, 4)
        self.copies[phase, p, 1].wait_recv()
        self.added(phase, p, (c + 3) % 4, high, (2,))
        self.send_to(phase, p, 3, (c + 3) % 4, high, 1, 5)

    def third_step(self, phase, p):
        c = self.at[ORDERS[p][phase]]
        low, high = self.spans(p)
        self.copies[phase, p, 2].wait_recv()
        self.copies[phase, p, 5].wait_recv()
        self.added(phase, p, c, high, (0, 1))
        self.copies[phase, p, 3].wait_recv()
        self.copies[phase, p, 4].wait_recv()
        self.added(phase, p, c, low, (0, 1))

    def finish(self, phase):
        for p in range(3):
            self.third_step(phase, p)
            if phase > 0:
                self.first(phase - 1, p)

    def end(self):
        for copy in self.copies.values():
            copy.wait_send()


def scatter_shapes(rows, columns):
    return [
        pltpu.VMEM((4, 4, 4, rows, columns), jnp.bfloat16),
        [pltpu.VMEM((3,) + (4,) * phase + (rows, columns), jnp.bfloat16) for phase in range(3)],
        pltpu.SemaphoreType.DMA((3, 3, 6)),
        pltpu.SemaphoreType.DMA((3, 3, 6)),
    ]


def dot_nn(left, right):
    return jnp.dot(left, right, preferred_element_type=jnp.float32)


def dot_nt(left, right):
    return lax.dot_general(
        left, right, (((1,), (1,)), ((), ())), preferred_element_type=jnp.float32
    )


def dot_tn(left, right):
    return lax.dot_general(
        left, right, (((0,), (0,)), ((), ())), preferred_element_type=jnp.float32
    )


def low(value):
    return value.astype(jnp.bfloat16)


def split(value, count):
    parts = []
    for _ in range(count):
        parts.append(low(value))
        value = value - parts[-1].astype(jnp.float32)
    return parts


def dot_split(left, right, count, dot=dot_nn):
    return sum(dot(left, part) for part in split(right, count))


def split_dot(left, right, count):
    return sum(dot_nn(part, right) for part in split(left, count))


def dot_three(left, right, dot=dot_nn):
    high, less = split(left, 2)
    other_high, other_less = split(right, 2)
    return dot(high, other_high) + dot(less, other_high) + dot(high, other_less)


def head_spread(lanes, width, size):
    head = lax.broadcasted_iota(jnp.int32, (lanes, width), 0)
    column = lax.broadcasted_iota(jnp.int32, (lanes, width), 1)
    return low(jnp.where(head == column // size, 1.0, 0.0))


def head_gather(lanes, width, size):
    head = lax.broadcasted_iota(jnp.int32, (width, lanes), 1)
    column = lax.broadcasted_iota(jnp.int32, (width, lanes), 0)
    return low(jnp.where(head == column // size, 1.0, 0.0))


def triangle(rows, keep):
    first = lax.broadcasted_iota(jnp.int32, (rows, rows), 0)
    second = lax.broadcasted_iota(jnp.int32, (rows, rows), 1)
    return keep(first, second)


def silu_parts(value):
    sig = jax.nn.sigmoid(value)
    return value * sig, sig * (1.0 + value * (1.0 - sig))


def mixer_back_kernel(
    lefts,
    rights,
    home_ref,
    position_ref,
    add_ref,
    resid_ref,
    scale_ref,
    weights_ref,
    z_ref,
    gate_scale_ref,
    y_ref,
    x_ref,
    bc_ref,
    conv_ref,
    pre_ref,
    step_raw_ref,
    table_ref,
    start_ref,
    res_ref,
    mixer_out_ref,
    gate_up_ref,
    down_ref,
    grads_ref,
    taps_grad_ref,
    heads_grad_ref,
    results_ref,
    grad_resid_ref,
    norm_grad_ref,
    gain_grad_ref,
    weights,
    grad_mix,
    dy_ref,
    stat,
    stat_theirs,
    message,
    back,
    got,
    made,
    decayed,
    q,
    spread,
    cum_rows,
    scores,
    acc,
    ext,
    mine,
    theirs,
    shared_out,
    shared_scratch,
    mix_scratch,
    scan_sems,
    sems,
    home_sems,
    load_sem,
    pair_sems,
    stat_sems,
):
    me, at = coordinates()
    head = lax.axis_index("head")
    tokens, width = x_ref.shape
    model = resid_ref.shape[1]
    size = start_ref.shape[1]
    lanes = step_raw_ref.shape[1]
    each = width // 64
    mid = tokens // 2
    cut = 384
    numbers_ref, taps_ref = table_ref.at[8:16, 0:lanes], table_ref
    norm_ref, gain_ref = table_ref.at[5:6, 0:model], table_ref.at[6:7, 0:width]
    announce(me, True)
    added = pltpu.make_async_copy(add_ref, q, load_sem.at[1])
    added.start()
    load = pltpu.make_async_copy(weights_ref.at[:, pl.ds(0, width)], weights, load_sem.at[0])
    load.start()
    normed_second, grad_out = lefts
    normed_gate, shared_right = rights
    third = width // 3
    plan = [((n // 2, 0, n * third, n * third, third),) for n in range(3)]
    shared = Scatter(at, plan, lefts, [shared_right], shared_out, *shared_scratch)
    plan = [((0, 0, n * third, n * third, third),) for n in range(3)]
    mix = Scatter(at, plan, [grad_mix], [normed_gate], mixer_out_ref, *mix_scratch)
    scan = Scan(True, at, me, message, back, got, made, scan_sems)
    results = Spread(at, me, res_ref, results_ref, home_sems, *HOME[0], True)

    gate_cut = 256
    pair = PairSum(q, decayed, pair_sems, gate_cut)
    added.wait()
    ready(home_ref, position_ref)
    slots, step = home_ref.shape[1], 16

    @pl.loop(0, home_ref.shape[0] // step)
    def _(i):
        here = pl.ds(pl.multiple_of(i * step, step), step)
        chosen = low(chosen_slots(position_ref[here, :], slots))
        q[...] += dot_tn(chosen, home_ref[here].reshape(step * slots, model))

    await_all(True)
    for n in range(pair.count):
        pair.copy(n).start()
    results.start(HOME[0][0], HOME[0][0] + 1)
    for p in range(3):
        shared.product(p)
        shared.first(2, p)
    scale = scale_ref[:, 0:1]
    inner_sum = jnp.zeros((tokens, 1), jnp.float32)
    for n in range(pair.count):
        cols = slice(n * gate_cut, (n + 1) * gate_cut)
        pair.copy(n).wait()
        grad = q[:, cols] + decayed[:, cols]
        q[:, cols] = grad
        resid = resid_ref[:, cols]
        norm_grad_ref[:, cols] = jnp.sum(grad * resid * scale, axis=0, keepdims=True)
        inner_sum = inner_sum + jnp.sum(resid * norm_ref[:, cols] * grad, axis=1, keepdims=True)
    pull = scale * scale * scale * (inner_sum / model)
    for n in range(pair.count):
        cols = slice(n * gate_cut, (n + 1) * gate_cut)
        grad = scale * norm_ref[:, cols] * q[:, cols] - resid_ref[:, cols] * pull
        grad = grad_out[:, cols].astype(jnp.float32) + grad
        grad_resid_ref[:, cols] = grad
        grad_mix[:, cols] = low(grad)
    grad_resid_ref.flush()

    load.wait()
    gate_scale = gate_scale_ref[:, 0:1]
    dots = jnp.zeros((tokens, 1), jnp.float32)
    for c in range(0, width, cut):
        cols = slice(c, c + cut)
        grad = dot_nn(grad_mix[...], weights[:, cols])
        z = z_ref[:, cols]
        gated = y_ref[:, cols] * (z * jax.nn.sigmoid(z))
        gain_grad_ref[:, cols] = jnp.sum(grad * gated * gate_scale, axis=0, keepdims=True)
        weighted = grad * gain_ref[:, cols]
        dy_ref[:, cols] = weighted
        dots = dots + jnp.sum(weighted * gated, axis=1, keepdims=True)
    stat[...] = jnp.broadcast_to(dots, stat.shape)
    stat_swap = pltpu.make_async_remote_copy(
        src_ref=stat,
        dst_ref=stat_theirs,
        send_sem=stat_sems.at[0],
        recv_sem=stat_sems.at[1],
        device_id={"head": 1 - head},
    )
    stat_swap.start()
    for p in range(3):
        mix.product(p)
        mix.first(2, p)
    for p in range(3):
        shared.second(2, p)
    stat_swap.wait()
    dots = (stat[...] + stat_theirs[...])[:, 0:1]
    pull = gate_scale * gate_scale * gate_scale * (dots / (2 * width))
    for c in range(0, width, cut):
        cols = slice(c, c + cut)
        z, y = z_ref[:, cols], y_ref[:, cols]
        act, slope = silu_parts(z)
        grad = gate_scale * dy_ref[:, cols] - y * act * pull
        dy_ref[:, cols] = grad * act
        grads_ref[:, cols] = low(grad * y * slope)

    rate = numbers_ref[0:1, :]
    step_raw = step_raw_ref[...]
    step = jax.nn.softplus(step_raw)
    earlier = low(triangle(tokens, lambda t, s: jnp.where(t >= s, 1.0, 0.0)))
    cum = dot_split(earlier, -step * rate, 3)
    cum_rows[...] = cum.T
    tail = cum[tokens - 1 : tokens, :]
    rest_decay = jnp.exp(tail - cum)
    weight = rest_decay * step
    spreader = head_spread(lanes, width, 64)
    gatherer = head_gather(lanes, width, 64)
    spread[...] = split_dot(jnp.exp(cum), spreader, 2)
    held_full, read_full = bc_ref[:, :size], bc_ref[:, size:]
    held, read = low(held_full), low(read_full)

    for c in range(0, width, cut):
        part = dy_ref[:, c : c + cut] * spread[:, c : c + cut]
        decayed[:, c : c + cut] = part
        made_rows = dot_three(part, read_full, dot_tn)
        made_rows = made_rows.reshape(cut // each, each, size)
        message[c // each : (c + cut) // each] = scan_rows(made_rows, jnp.exp(tail))
    scan.begin()
    for p in range(3):
        mix.second(2, p)
    shared.finish(2)
    scan.middle()

    spread[...] = split_dot(step, spreader, 2)
    blocks = ((0, 0), (0, 1), (1, 1))
    for n, (s, t) in enumerate(blocks):
        scores[n] = dot_nt(held[s * mid : (s + 1) * mid], read[t * mid : (t + 1) * mid])
    acc[...] = jnp.zeros_like(acc)
    causal = triangle(mid, lambda s, t: s <= t)
    ready(x_ref)
    second_head = lax.broadcasted_iota(jnp.int32, (tokens, 128), 1) >= 64

    @pl.loop(0, width // 128)
    def _(i):
        here = pl.ds(pl.multiple_of(i * 128, 128), 128)
        dy, dy_less = split(dy_ref[:, here], 2)
        stepped = x_ref[:, here] * spread[:, here]
        results = []
        for which in range(2):
            row = cum_rows[pl.ds(2 * i + which, 1), :]
            column = jnp.broadcast_to(row, (128, tokens)).T
            mask = second_head if which else jnp.logical_not(second_head)
            values, values_less = split(jnp.where(mask, stepped, 0.0), 2)
            total = [None, None]
            for n, (s, t) in enumerate(blocks):
                gap = row[:, t * mid : (t + 1) * mid] - column[s * mid : (s + 1) * mid]
                decay = jnp.exp(gap)
                if s == t:
                    decay = jnp.where(causal, decay, 0.0)
                later = dy[t * mid : (t + 1) * mid]
                first, later_less = values[s * mid : (s + 1) * mid], dy_less[t * mid : (t + 1) * mid]
                pairs = dot_nt(first, later) + dot_nt(first, later_less)
                pairs = pairs + dot_nt(values_less[s * mid : (s + 1) * mid], later)
                acc[n] += decay * pairs
                part = dot_nn(low(decay * scores[n]), later)
                total[s] = part if total[s] is None else total[s] + part
            results.append(total)
        for s in range(2):
            rows = slice(s * mid, (s + 1) * mid)
            q[rows, here] = jnp.where(second_head[rows], results[1][s], results[0][s])

    for p in range(3):
        shared.second(1, p)
    shared.finish(1)
    mix.finish(2)
    results.start(HOME[0][0] + 1, HOME[0][0] + 2)
    scan.end()

    skip = split_dot(jnp.broadcast_to(numbers_ref[1:2, :], (8, lanes)), spreader, 2)[0:1, :]
    grad_weight = grad_step = rows_sum = jnp.zeros((tokens, lanes), jnp.float32)
    skip_grad = jnp.zeros((8, lanes), jnp.float32)
    state_dot = jnp.zeros((lanes, size), jnp.float32)
    held_parts = held_full[:mid], held_full[mid:]
    read_parts = read_full[:mid], read_full[mid:]
    grad_held = dot_three(acc[0], read_parts[0]) + dot_three(acc[1], read_parts[1])
    grad_held = jnp.concatenate([grad_held, dot_three(acc[2], read_parts[1])], axis=0)
    grad_read = dot_three(acc[1], held_parts[0], dot_tn) + dot_three(acc[2], held_parts[1], dot_tn)
    grad_read = jnp.concatenate([dot_three(acc[0], held_parts[0], dot_tn), grad_read], axis=0)
    for c in range(0, width, cut):
        here = slice(c, c + cut)
        x, dy, inner = x_ref[:, here], dy_ref[:, here], q[:, here]
        after = back[c // each : (c + cut) // each].reshape(cut, size)
        start = start_ref[here, :]
        gather = gatherer[here, :]
        weights = split_dot(weight, spreader[:, here], 2)
        through = dot_nt(held, low(after))
        grad_x = inner * spread[:, here] + skip[:, here] * dy + weights * through
        grad_step = grad_step + split_dot(x * inner, gather, 2)
        grad_weight = grad_weight + split_dot(x * through, gather, 2)
        rows_sum = rows_sum + split_dot(dy * (y_ref[:, here] - skip[:, here] * x), gather, 2)
        pairs = jnp.sum(dy * x, axis=0, keepdims=True)
        skip_grad = skip_grad + split_dot(jnp.broadcast_to(pairs, (8, cut)), gather, 2)
        state_dot = state_dot + dot_split(gather, after * start, 2, dot_tn)
        grad_held = grad_held + dot_three(weights * x, after)
        grad_read = grad_read + dot_three(decayed[:, here], start)
        ext[0:tokens, here] = grad_x * silu_parts(conv_ref[:, here])[1]
        if c == cut:
            for p in range(3):
                shared.second(0, p)
            for p in range(3):
                mix.second(1, p)
            results.start(HOME[0][0] + 2, HOME[0][0] + 3)
    mine[:, :size] = grad_held
    mine[:, size:] = grad_read
    swap = pltpu.make_async_remote_copy(
        src_ref=mine,
        dst_ref=theirs,
        send_sem=sems.at[0],
        recv_sem=sems.at[1],
        device_id={"head": 1 - head},
    )
    swap.start()
    mix.finish(1)
    results.start(HOME[0][0] + 3, HOME[0][0] + 4)

    ones = jnp.ones((8, size), jnp.bfloat16)
    state_grad = dot_split(ones, state_dot, 2, dot_nt)[0:1, :]
    used = grad_weight * weight
    tail_grad = jnp.sum(used, axis=0, keepdims=True) + jnp.exp(tail) * state_grad
    grad_cum = rows_sum - step * grad_step - used
    last = lax.broadcasted_iota(jnp.int32, (tokens, lanes), 0) == tokens - 1
    grad_cum = grad_cum + jnp.where(last, tail_grad, 0.0)
    later = low(triangle(tokens, lambda t, s: jnp.where(t <= s, 1.0, 0.0)))
    grad_log = dot_split(later, grad_cum, 3)
    grad_step = grad_step + grad_weight * rest_decay - rate * grad_log
    grad_raw = grad_step * jax.nn.sigmoid(step_raw)
    heads_grad_ref[...] = jnp.zeros_like(heads_grad_ref)
    heads_grad_ref[0:1, :] = skip_grad[0:1, :]
    heads_grad_ref[1:2, :] = -jnp.sum(step * grad_log, axis=0, keepdims=True)
    heads_grad_ref[2:3, :] = jnp.sum(grad_raw, axis=0, keepdims=True)

    channels = width + 2 * size
    grads_ref[:, width + channels : width + channels + lanes] = low(grad_raw)
    swap.wait()
    ext[0:tokens, width:channels] = (mine[...] + theirs[...]) * silu_parts(
        conv_ref[:, width:channels]
    )[1]
    edge = pltpu.make_async_remote_copy(
        src_ref=ext.at[pl.ds(0, 8)],
        dst_ref=ext.at[pl.ds(tokens, 8)],
        send_sem=sems.at[2],
        recv_sem=sems.at[3],
        device_id={"seq": (me + 63) % 64},
    )
    edge.start()
    shared.finish(0)
    for p in range(3):
        mix.second(0, p)
    results.start(HOME[0][0] + 4, HOME[0][1])
    edge.wait()
    there = jnp.where(me == 63, 0.0, 1.0)
    ext[tokens : tokens + 8, :] = ext[tokens : tokens + 8, :] * there
    taps_grad_ref[...] = jnp.zeros_like(taps_grad_ref)
    ready(pre_ref)

    @pl.loop(0, channels // 256)
    def _(i):
        here = pl.ds(pl.multiple_of(i * 256, 256), 256)
        grad = ext[0:tokens, here]
        total = jnp.zeros_like(grad)
        for j in range(4):
            total = total + taps_ref[j : j + 1, here] * ext[3 - j : 3 - j + tokens, here]
            products = grad * pre_ref[5 + j : 5 + j + tokens, here]
            taps_grad_ref[j : j + 1, here] = jnp.sum(products, axis=0, keepdims=True)
        grads_ref[:, pl.ds(pl.multiple_of(width + i * 256, 256), 256)] = low(total)

    mix.finish(0)
    hidden = down_ref.shape[1]
    for n in range(2):
        gate_up_ref[:, n, :] = shared_out[:, n * hidden : (n + 1) * hidden]
    down_ref[...] = shared_out[:, 2 * hidden :]
    shared.end()
    mix.end()
    results.wait()


def mixer_back(
    lefts,
    rights,
    home,
    position,
    add,
    resid,
    scale,
    weights,
    z,
    gate_scale,
    y,
    x,
    bc,
    conv,
    pre,
    step_raw,
    table,
    start,
    res,
    collective,
):
    tokens, model = resid.shape
    rows = model // 64
    width = x.shape[1]
    hidden = rights[1].shape[1] // 3
    size, lanes = start.shape[1], step_raw.shape[1]
    each, channels, mid = width // 64, width + 2 * size, tokens // 2
    f32, bf16 = jnp.float32, jnp.bfloat16
    vmem, hbm = pl.BlockSpec(memory_space=pltpu.VMEM), pl.BlockSpec(memory_space=pl.ANY)
    return call(
        mixer_back_kernel,
        out_shape=[
            jax.ShapeDtypeStruct((rows, width), f32),
            jax.ShapeDtypeStruct((rows, 2, hidden), f32),
            jax.ShapeDtypeStruct((rows, hidden), f32),
            jax.ShapeDtypeStruct((tokens, width + channels + lanes), bf16),
            jax.ShapeDtypeStruct((8, channels), f32),
            jax.ShapeDtypeStruct((8, lanes), f32),
            part_shape(HOME[0], res),
            jax.ShapeDtypeStruct((tokens, model), f32),
            jax.ShapeDtypeStruct((1, model), f32),
            jax.ShapeDtypeStruct((1, width), f32),
        ],
        in_specs=[[Lazy] * len(lefts), [Lazy] * len(rights)]
        + [Lazy, Lazy, hbm, Lazy, Lazy, hbm]
        + [Lazy] * 4
        + [vmem, Lazy, Lazy, vmem, vmem, Lazy, hbm],
        out_specs=[vmem] * 6 + [hbm, Eager, vmem, vmem],
        scratch_shapes=[
            pltpu.VMEM((model, width), bf16),
            pltpu.VMEM((tokens, model), bf16),
            pltpu.VMEM((tokens, width), f32),
            pltpu.VMEM((tokens, 128), f32),
            pltpu.VMEM((tokens, 128), f32),
            pltpu.VMEM((64, each + 8, size), bf16),
            pltpu.VMEM((64, each, size), f32),
            pltpu.VMEM((64, each + 8, size), bf16),
            pltpu.VMEM((64, each, size), f32),
            pltpu.VMEM((tokens, width), f32),
            pltpu.VMEM((tokens, width), f32),
            pltpu.VMEM((tokens, width), f32),
            pltpu.VMEM((lanes, tokens), f32),
            pltpu.VMEM((3, mid, mid), f32),
            pltpu.VMEM((3, mid, mid), f32),
            pltpu.VMEM((tokens + 8, channels), f32),
            pltpu.VMEM((tokens, 2 * size), f32),
            pltpu.VMEM((tokens, 2 * size), f32),
            pltpu.VMEM((rows, 3 * hidden), f32),
            scatter_shapes(rows, 3 * hidden),
            scatter_shapes(rows, width),
            pltpu.SemaphoreType.DMA((4,)),
            pltpu.SemaphoreType.DMA((4,)),
            pltpu.SemaphoreType.DMA((9,)),
            pltpu.SemaphoreType.DMA((2,)),
            pltpu.SemaphoreType.DMA((2, model // 256)),
            pltpu.SemaphoreType.DMA((2,)),
        ],
        compiler_params=params(collective, vmem_limit_bytes=VMEM),
        name="mixer_back",
    )(
        lefts, rights, home, position, add, resid, scale, weights, z, gate_scale, y, x, bc, conv,
        pre, step_raw, table, start, res,
    )


def input_back_kernel(
    plan,
    left,
    right,
    weights_ref,
    resid_ref,
    table_ref,
    grad_ref,
    res_ref,
    near_refs,
    position_ref,
    weight_ref,
    shared_ref,
    block_ref,
    taps_ref,
    heads_ref,
    norm_ref,
    gate_gain_ref,
    mixer_in_ref,
    state_ref,
    step_ref,
    input_ref,
    layer_ref,
    norm_first_out,
    norm_second_out,
    gate_gain_out,
    conv_main_out,
    conv_state_out,
    heads_outs,
    weights,
    mine,
    theirs,
    theirs_mix,
    home,
    named,
    weighed,
    small,
    small_got,
    small_out,
    out_ref,
    buf,
    rest,
    send,
    recv,
    small_sems,
    sems,
    home_sems,
    mix_sems,
):
    me, at = coordinates()
    head = lax.axis_index("head")
    tokens, model = resid_ref.shape
    columns = right.shape[1]
    gain_ref = table_ref.at[4:5, 0:model]
    load = pltpu.make_async_copy(weights_ref, weights, sems.at[0])
    load.start()
    announce(me, True)
    sums = Scatter(at, plan, [left], [right], out_ref, buf, rest, send, recv)
    totals = Small(at, me, small, small_out, small_got, small_sems)
    results = Spread(at, me, res_ref, home, home_sems, *HOME[1], True)
    for p in range(3):
        sums.product(p)
        if p == 0:
            await_all(True)
            results.start(HOME[1][0], HOME[1][0] + 1)
        sums.first(2, p)
    load.wait()

    start = columns - 384
    other = pl.multiple_of(start + 128 * (1 - head), 128)
    cut = 256
    swaps = []
    for c in range(0, model, cut):
        rows = slice(c, c + cut)
        total = dot_nt(right[...], weights[rows, :])
        total = total - dot_nt(right[:, pl.ds(other, 128)], weights[rows, pl.ds(other, 128)])
        mine[:, rows] = total
        swap = pltpu.make_async_remote_copy(
            src_ref=mine.at[:, pl.ds(c, cut)],
            dst_ref=theirs.at[:, pl.ds(c, cut)],
            send_sem=sems.at[1 + c // cut],
            recv_sem=sems.at[1 + (model + c) // cut],
            device_id={"head": 1 - head},
        )
        swap.start()
        swaps.append(swap)
    for p in range(3):
        sums.second(2, p)
    square = jnp.zeros((tokens, 1), jnp.float32)
    inner = jnp.zeros((tokens, 1), jnp.float32)
    for n, c in enumerate(range(0, model, cut)):
        rows = slice(c, c + cut)
        swaps[n].wait()
        grad = mine[:, rows] + theirs[:, rows]
        mine[:, rows] = grad
        resid = resid_ref[:, rows].astype(jnp.float32)
        square = square + jnp.sum(resid * resid, axis=1, keepdims=True)
        inner = inner + jnp.sum(resid * gain_ref[:, rows] * grad, axis=1, keepdims=True)
    scale = lax.rsqrt(square / model + EPSILON)
    pull = scale * scale * scale * (inner / model)
    tiles, inner_tiles = model // 128, gate_gain_ref.shape[1] // 128
    channel_tiles = taps_ref.shape[1] // 128
    small[...] = jnp.zeros_like(small)

    def put_small(row, value):
        small[row // 8, row % 8 : row % 8 + 1, :] = value

    for tile in range(tiles):
        put_small(tiles + tile, norm_ref[:, tile * 128 : (tile + 1) * 128])
    for tile in range(inner_tiles):
        put_small(2 * tiles + tile, gate_gain_ref[:, tile * 128 : (tile + 1) * 128])
    taps_row = 2 * tiles + inner_tiles
    for tap in range(4):
        for tile in range(channel_tiles):
            row = taps_row + tap * channel_tiles + tile
            put_small(row, taps_ref[tap : tap + 1, tile * 128 : (tile + 1) * 128])
    heads_row = taps_row + 4 * channel_tiles
    for n in range(3):
        put_small(heads_row + n, heads_ref[n : n + 1, :])
    for c in range(0, model, cut):
        rows = slice(c, c + cut)
        grad = mine[:, rows]
        resid = resid_ref[:, rows].astype(jnp.float32)
        input_ref[:, rows] = grad_ref[:, rows] + scale * gain_ref[:, rows] * grad - resid * pull
        gain_grad = jnp.sum(grad * resid * scale, axis=0, keepdims=True)
        for tile in range(c // 128, (c + cut) // 128):
            at_tile = tile * 128 - c
            put_small(tile, gain_grad[:, at_tile : at_tile + 128])
    totals.begin()
    results.start(HOME[1][0] + 1, HOME[1][0] + 2)
    input_ref.flush()
    mine[...] = shared_ref[...]
    slots = home.shape[1]

    def mix(span, rows_ref):
        @pl.loop(*span)
        def _(g):
            for n, (_, expert) in enumerate(Ways(at).group(g)):
                named[n : n + 1, :] = position_ref[pl.ds(expert, 1), :]
                weighed[n : n + 1, :] = weight_ref[pl.ds(expert, 1), :]
            chosen = chosen_slots(named[...], slots)
            weighted = chosen.reshape(8, slots, -1) * weighed[...][:, None, :]
            high, less = split(weighted.reshape(chosen.shape), 2)
            here = pl.ds(pl.multiple_of((g - span[0]) * 8, 8), 8)
            rows = rows_ref[here].reshape(8 * slots, model)
            mine[...] += dot_tn(high, rows) + dot_tn(less, rows)

    ready(position_ref, weight_ref, *near_refs)
    for span, near_ref in zip(HOME, near_refs):
        mix(span, near_ref)
    sums.finish(2)
    for p in range(3):
        sums.second(1, p)
    totals.middle()
    sums.finish(1)
    results.arrived(*HOME[1])
    mix(HOME[1], home)
    for p in range(3):
        sums.second(0, p)
    pair = PairSum(mine, theirs_mix, mix_sems, cut)
    for n in range(pair.count):
        pair.copy(n).start()
    sums.finish(0)
    for n in range(pair.count):
        cols = slice(n * cut, (n + 1) * cut)
        pair.copy(n).wait()
        layer_ref[:, cols] = low(block_ref[:, cols] + (mine[:, cols] + theirs_mix[:, cols]))
    totals.end()

    def get_small(row):
        return small_out[row // 8, row % 8 : row % 8 + 1, :]

    for tile in range(tiles):
        norm_first_out[tile : tile + 1, :] = get_small(tile)
        norm_second_out[tile : tile + 1, :] = get_small(tiles + tile)
    for tile in range(inner_tiles):
        gate_gain_out[tile : tile + 1, :] = get_small(2 * tiles + tile)
    for tap in range(4):
        for tile in range(channel_tiles):
            value = get_small(taps_row + tap * channel_tiles + tile)
            if tile < inner_tiles:
                conv_main_out[tap : tap + 1, tile * 128 : (tile + 1) * 128] = value
            else:
                start = (tile - inner_tiles) * 128
                conv_state_out[tap : tap + 1, start : start + 128] = value
    for n, heads_out in enumerate(heads_outs):
        heads_out[...] = get_small(heads_row + n)[:, : heads_out.shape[1]]
    results.sent()
    inner = mixer_in_ref.shape[2]
    for n in range(2):
        mixer_in_ref[:, n, :] = out_ref[:, n * inner : (n + 1) * inner]
    wide = 2 * inner + state_ref.shape[1]
    state_ref[...] = out_ref[:, 2 * inner : wide]
    step_ref[...] = out_ref[:, wide : wide + 128][:, : step_ref.shape[1]]
    sums.end()


def input_back(
    left,
    right,
    plan,
    weights,
    resid,
    table,
    grad,
    res,
    near,
    position,
    weight,
    shared,
    block,
    taps,
    heads,
    norm,
    gate_gain,
    heads_dev,
    collective,
):
    tokens, model = resid.shape
    columns = right.shape[1]
    rows = model // 64
    inner, channels = gate_gain.shape[1], taps.shape[1]
    f32 = jnp.float32
    vmem, hbm = pl.BlockSpec(memory_space=pltpu.VMEM), pl.BlockSpec(memory_space=pl.ANY)
    return call(
        functools.partial(input_back_kernel, plan),
        out_shape=[
            jax.ShapeDtypeStruct((rows, 2, inner), f32),
            jax.ShapeDtypeStruct((rows, channels - inner), f32),
            jax.ShapeDtypeStruct((rows, heads_dev), f32),
            jax.ShapeDtypeStruct((tokens, model), f32),
            jax.ShapeDtypeStruct((tokens, model), jnp.bfloat16),
            jax.ShapeDtypeStruct((model // 128, 128), f32),
            jax.ShapeDtypeStruct((model // 128, 128), f32),
            jax.ShapeDtypeStruct((inner // 128, 128), f32),
            jax.ShapeDtypeStruct((4, inner), f32),
            jax.ShapeDtypeStruct((4, channels - inner), f32),
            [jax.ShapeDtypeStruct((1, heads_dev), f32)] * 3,
        ],
        in_specs=[Lazy, Lazy, hbm, Lazy, vmem, Lazy] + [hbm, [Lazy] * len(near)] + [Lazy] * 8,
        out_specs=[vmem] * 3 + [Eager] * 2 + [vmem] * 5 + [[vmem] * 3],
        scratch_shapes=[
            pltpu.VMEM(weights.shape, weights.dtype),
            pltpu.VMEM((tokens, model), f32),
            pltpu.VMEM((tokens, model), f32),
            pltpu.VMEM((tokens, model), f32),
            pltpu.VMEM(part_shape(HOME[1], res).shape, res.dtype),
            pltpu.VMEM((8, tokens), f32),
            pltpu.VMEM((8, tokens), f32),
            pltpu.VMEM((64, 8, 128), f32),
            pltpu.VMEM((64, 8, 128), f32),
            pltpu.VMEM((64, 8, 128), f32),
            pltpu.VMEM((rows, columns), f32),
        ]
        + scatter_shapes(rows, columns)
        + [pltpu.SemaphoreType.DMA((4,)), pltpu.SemaphoreType.DMA((1 + 2 * model // 256,))]
        + [pltpu.SemaphoreType.DMA((9,)), pltpu.SemaphoreType.DMA((2, model // 256))],
        compiler_params=params(collective, vmem_limit_bytes=VMEM),
        name="input_back",
    )(
        left, right, weights, resid, table, grad, res, near, position, weight, shared, block,
        taps, heads, norm, gate_gain,
    )


class Gather:
    def __init__(self, at, x_ref, out_ref, send, recv, local_sem):
        self.at, self.x_ref, self.out_ref, self.send, self.recv = at, x_ref, out_ref, send, recv
        self.third, self.half = parts_of(out_ref.shape[4])
        if x_ref is not None:
            self.own = pltpu.make_async_copy(x_ref, out_ref.at[at[0], at[1], at[2]], local_sem)
        self.copies = {}

    def put(self, source, here, phase, p, kind, by):
        copy = pltpu.make_async_remote_copy(
            src_ref=source,
            dst_ref=self.out_ref.at[here],
            send_sem=self.send.at[phase, p, kind],
            recv_sem=self.recv.at[phase, p, kind],
            device_id={"seq": seq_of(moved(self.at, ORDERS[p][phase], by))},
        )
        copy.start()
        self.copies[phase, p, kind] = copy

    def first(self, phase):
        if phase == 1:
            self.own.wait()
        if phase == 0:
            self.own.start()
        elif (phase - 1, 0, 2) in self.copies:
            self.arrived(phase - 1)
        for p, order in enumerate(ORDERS):
            cols = pl.ds(p * self.third, self.third)
            here = region(self.at, order, phase, self.at[order[phase]], cols)
            source = self.x_ref.at[:, cols] if phase == 0 else self.out_ref.at[here]
            for kind, by in enumerate((1, 3)):
                self.put(source, here, phase, p, kind, by)

    def second(self, phase):
        for p, order in enumerate(ORDERS):
            for kind, by in enumerate((1, 3)):
                start, length = p * self.third, self.half
                if kind:
                    start, length = start + self.half, self.third - self.half
                there = region(
                    self.at, order, phase, (self.at[order[phase]] - by) % 4, pl.ds(start, length)
                )
                self.copies[phase, p, kind].wait_recv()
                self.put(self.out_ref.at[there], there, phase, p, 2 + kind, by)

    def arrived(self, phase):
        for p in range(3):
            for kind in (2, 3):
                self.copies[phase, p, kind].wait_recv()

    def end(self):
        for copy in self.copies.values():
            copy.wait_send()


def gather_shapes():
    return [
        pltpu.SemaphoreType.DMA((3, 3, 4)),
        pltpu.SemaphoreType.DMA((3, 3, 4)),
        pltpu.SemaphoreType.DMA,
    ]


def slot_tables(routes_ref, weights_ref, position_ref, weight_ref):
    experts, tokens = position_ref.shape
    expert = lax.broadcasted_iota(jnp.int32, (experts, tokens), 0)
    named = jnp.zeros((experts, tokens), jnp.float32)
    weight = jnp.zeros((experts, tokens), jnp.float32)
    for k in range(routes_ref.shape[0]):
        hit = expert == routes_ref[k : k + 1, :]
        named = named + jnp.where(hit, 1.0, 0.0)
        weight = weight + jnp.where(hit, weights_ref[k : k + 1, :], 0.0)
    earlier = low(triangle(tokens, lambda t, s: jnp.where(t < s, 1.0, 0.0)))
    position_ref[...] = jnp.where(named > 0.0, dot_nn(low(named), earlier), -1.0)
    weight_ref[...] = weight


def chosen_slots(position, slots):
    count, tokens = position.shape
    number = lax.broadcasted_iota(jnp.int32, (count, slots, tokens), 1)
    number = (number + slots * lax.axis_index("head")).astype(jnp.float32)
    return jnp.where(position[:, None, :] == number, 1.0, 0.0).reshape(count * slots, tokens)


def gather_kernel(
    early_refs,
    late_refs,
    wide_in,
    layer_ref,
    routes_ref,
    weights_ref,
    grads_ref,
    vectors,
    out_ref,
    late_out,
    before_ref,
    position_ref,
    weight_ref,
    rows,
    slots_ref,
    table_ref,
    wide_ref,
    x_ref,
    late_ref,
    send,
    recv,
    local_sem,
    late_send,
    late_recv,
    late_sem,
    sems,
    out_sems,
):
    me, at = coordinates()
    announce(me, False)
    def beside(target, sources):
        column = 0
        for source in sources:
            value = source[...]
            if value.ndim == 3:
                value = value.astype(jnp.float32)
                halves = [low(value[:, n, :]) for n in range(2)]
            else:
                halves = [value]
            for half in halves:
                target[:, column : column + half.shape[1]] = half
                column = column + half.shape[1]

    rows_step = x_ref.shape[1] - 128
    x_ref[:, rows_step:] = jnp.zeros((x_ref.shape[0], 128), x_ref.dtype)
    beside(x_ref, early_refs)
    beside(late_ref, late_refs)
    gather = Gather(at, x_ref, out_ref, send, recv, local_sem)
    late = Gather(at, late_ref, late_out, late_send, late_recv, late_sem)
    conv_main, conv_state, gains, numbers = vectors
    width, heads = conv_main.shape[1], numbers[0].shape[1]
    table_ref[...] = jnp.zeros_like(table_ref)
    table_ref[0:4, 0:width] = conv_main[...]
    table_ref[0:4, width:] = conv_state[...]
    for n, gain in enumerate(gains):
        for tile in range(gain.shape[0]):
            table_ref[4 + n : 5 + n, tile * 128 : (tile + 1) * 128] = gain[tile : tile + 1, :]
    for n, number in enumerate(numbers):
        table_ref[8 + n : 9 + n, 0:heads] = number[...]
    slot_tables(routes_ref, weights_ref, position_ref, weight_ref)
    grads = grads_ref[...]
    slots, step = rows.shape[1], 16

    @pl.loop(0, rows.shape[0] // step)
    def _(i):
        here = pl.ds(pl.multiple_of(i * step, step), step)
        chosen = chosen_slots(position_ref[here, :], slots)
        weighted = chosen.reshape(step, slots, -1) * weight_ref[here, :][:, None, :]
        scale = jnp.sum(weighted.reshape(chosen.shape), axis=1, keepdims=True)
        rows[here] = low(dot_nn(low(chosen), grads) * scale).reshape(step, slots, -1)

    await_all(False)
    gather.first(0)
    late.first(0)
    edge = pltpu.make_async_remote_copy(
        src_ref=layer_ref.at[pl.ds(layer_ref.shape[0] - 16, 16)],
        dst_ref=before_ref,
        send_sem=sems.at[0],
        recv_sem=sems.at[1],
        device_id={"seq": (me + 1) % 64},
    )
    edge.start()
    out = Spread(at, me, rows, slots_ref, out_sems, *OUT[0], False)
    gather.second(0)
    late.second(0)
    out.start(0, 1)
    gather.first(1)
    late.first(1)
    out.start(1, 2)
    gather.second(1)
    late.second(1)
    out.start(2, 3)
    gather.first(2)
    gather.second(2)
    out.start(3, OUT[0][1])
    ready(wide_in)
    hidden = wide_in.shape[2]

    @pl.loop(0, wide_in.shape[0] // 64)
    def _(i):
        here = pl.ds(pl.multiple_of(i * 64, 64), 64)
        value = wide_in[here].astype(jnp.float32)
        for n in range(2):
            wide_ref[here, n * hidden : (n + 1) * hidden] = low(value[:, n, :])

    late.arrived(1)
    late.end()
    gather.arrived(2)
    edge.wait()
    gather.end()
    out.wait()


def gather_rows(
    early, late, wide, layer_in, routes, route_weights, grads, vectors, experts, slots, collective
):
    rows = early[0].shape[0]
    bf16 = early[0].dtype
    count = lambda arrays: sum(array.size // rows for array in arrays)
    columns = -(-count(early) // 128) * 128
    channels = vectors[0].shape[1] + vectors[1].shape[1]
    tokens, model = grads.shape
    grad_rows = jax.ShapeDtypeStruct((experts, slots, model), grads.dtype)
    hbm, vmem = pl.BlockSpec(memory_space=pl.ANY), pl.BlockSpec(memory_space=pltpu.VMEM)
    return call(
        gather_kernel,
        out_shape=[
            jax.ShapeDtypeStruct((4, 4, 4, rows, columns), bf16),
            jax.ShapeDtypeStruct((4, 4, 4, rows, count(late)), bf16),
            jax.ShapeDtypeStruct((16, model), layer_in.dtype),
            jax.ShapeDtypeStruct((experts, tokens), jnp.float32),
            jax.ShapeDtypeStruct((experts, tokens), jnp.float32),
            grad_rows,
            part_shape(OUT[0], grad_rows),
            jax.ShapeDtypeStruct((16, channels), jnp.float32),
            jax.ShapeDtypeStruct((wide.shape[0], 2 * wide.shape[2]), bf16),
        ],
        in_specs=[[vmem] * len(early), [vmem] * len(late), Lazy, hbm, vmem, vmem, Lazy, [vmem, vmem, [vmem] * 3, [vmem] * 3]],
        out_specs=[hbm, hbm, hbm, vmem, vmem, vmem, hbm, vmem, vmem],
        scratch_shapes=[pltpu.VMEM((rows, columns), bf16), pltpu.VMEM((rows, count(late)), bf16)]
        + gather_shapes()
        + gather_shapes() + [pltpu.SemaphoreType.DMA((2,))]
        + [pltpu.SemaphoreType.DMA((9,))],
        compiler_params=params(collective, vmem_limit_bytes=VMEM),
        name="gather_rows",
    )(early, late, wide, layer_in, routes.T, route_weights.T, grads, vectors)


def mixer_kernel(
    layer_ref,
    edge_ref,
    table_ref,
    weights_ref,
    _,
    rows_ref,
    normed_ref,
    z_ref,
    x_ref,
    bc_ref,
    conv_ref,
    pre_ref,
    step_raw_ref,
    start_ref,
    y_ref,
    gated_ref,
    scale_ref,
    gathered_ref,
    slots_ref,
    weights,
    normed,
    message,
    got,
    made,
    spread,
    cum_rows,
    scores,
    mine,
    theirs,
    load_sems,
    scan_sems,
    pair_sems,
    send,
    recv,
    slot_sems,
):
    me, at = coordinates()
    head = lax.axis_index("head")
    tokens, model = layer_ref.shape
    width = x_ref.shape[1]
    size = bc_ref.shape[1] // 2
    lanes = step_raw_ref.shape[1]
    each = width // 64
    mid = tokens // 2
    cut = 384
    norm_ref, gain_ref = table_ref.at[4:5, 0:model], table_ref.at[6:7, 0:width]
    numbers_ref, taps_ref = table_ref.at[8:16, 0:lanes], table_ref

    def load(n):
        cols = pl.ds(pl.multiple_of(n * cut, 128), cut)
        return pltpu.make_async_copy(weights_ref.at[:, cols], weights.at[:, cols], load_sems.at[n])

    for n in (8, 4, 5, 6, 7, 0, 1, 2, 3):
        load(n).start()
    announce(me, True)
    gather = Gather(at, None, gathered_ref, send, recv, None)

    def norm(rows):
        rows = rows.astype(jnp.float32)
        scale = lax.rsqrt(jnp.mean(rows * rows, axis=1, keepdims=True) + EPSILON)
        return low(rows * scale * norm_ref[...])

    before = norm(edge_ref[...]).astype(jnp.float32) * jnp.where(me == 0, 0.0, 1.0)
    normed[0:16, :] = low(before)
    normed[16 : 16 + tokens, :] = norm(layer_ref[...])
    normed_ref[...] = normed[16 : 16 + tokens, :]
    normed_ref.flush()
    await_all(True)
    gather.first(2)

    def conv(cols):
        total = jnp.zeros((tokens, cols.size), jnp.float32)
        for j in range(4):
            total = total + taps_ref[j : j + 1, cols] * pre_ref[5 + j : 5 + j + tokens, cols]
        conv_ref[:, cols] = total
        return total * jax.nn.sigmoid(total)

    load(8).wait()
    last = dot_nn(normed[...], weights[:, 8 * cut : 9 * cut])
    cols = pl.ds(width, 2 * size)
    pre_ref[:, cols] = last[8:, : 2 * size]
    bc_ref[...] = conv(cols)
    bc_ref.flush()
    step_raw = last[16:, 2 * size :] + numbers_ref[2:3, :]
    step_raw_ref[...] = step_raw
    step = jax.nn.softplus(step_raw)
    earlier = low(triangle(tokens, lambda t, s: jnp.where(t >= s, 1.0, 0.0)))
    cum = dot_split(earlier, -step * numbers_ref[0:1, :], 3)
    cum_rows[...] = cum.T
    tail = cum[tokens - 1 : tokens, :]
    spreader = head_spread(lanes, width, 64)
    spread[...] = split_dot(jnp.exp(tail - cum) * step, spreader, 2)
    held, read = bc_ref[:, :size], bc_ref[:, size:]

    @pl.loop(0, 4)
    def _(i):
        load(4 + i).wait()
        from_cols = pl.ds(pl.multiple_of((4 + i) * cut, 128), cut)
        here = pl.ds(pl.multiple_of(i * cut, 128), cut)
        pre_ref[:, here] = dot_nn(normed[...], weights[:, from_cols])[8:]
        x = conv(here)
        x_ref[:, here] = x
        made_rows = dot_three(x * spread[:, here], held, dot_tn)
        made_rows = made_rows.reshape(cut // each, each, size)
        message[pl.ds(i * (cut // each), cut // each)] = scan_rows(made_rows, jnp.exp(tail))

    for ref in (x_ref, pre_ref, conv_ref):
        ref.flush()
    scan = Scan(False, at, me, message, start_ref, got, made, scan_sems)
    scan.begin()

    @pl.loop(0, 4)
    def _(i):
        load(i).wait()
        here = pl.ds(pl.multiple_of(i * cut, 128), cut)
        z_ref[:, here] = dot_nn(normed[16 : 16 + tokens, :], weights[:, here])

    z_ref.flush()
    scan.middle()
    out = Spread(at, me, rows_ref, slots_ref, slot_sems, *OUT[1], False)
    gather.second(2)
    out.start()

    spread[...] = split_dot(step, spreader, 2)
    blocks = ((0, 0), (1, 0), (1, 1))
    for n, (t, s) in enumerate(blocks):
        rows, columns = slice(t * mid, (t + 1) * mid), slice(s * mid, (s + 1) * mid)
        scores[n] = dot_three(read[rows], held[columns], dot_nt)
    causal = triangle(mid, lambda t, s: t >= s)
    second_head = lax.broadcasted_iota(jnp.int32, (tokens, 128), 1) >= 64

    @pl.loop(0, width // 128)
    def _(i):
        here = pl.ds(pl.multiple_of(i * 128, 128), 128)
        values, values_less = split(x_ref[:, here] * spread[:, here], 2)
        results = []
        for which in range(2):
            row = cum_rows[pl.ds(2 * i + which, 1), :]
            column = jnp.broadcast_to(row, (128, tokens)).T
            total = [None, None]
            for n, (t, s) in enumerate(blocks):
                columns = slice(s * mid, (s + 1) * mid)
                decay = jnp.exp(column[t * mid : (t + 1) * mid] - row[:, columns])
                if s == t:
                    decay = jnp.where(causal, decay, 0.0)
                mixing, mixing_less = split(decay * scores[n], 2)
                part = dot_nn(mixing, values[columns]) + dot_nn(mixing_less, values[columns])
                part = part + dot_nn(mixing, values_less[columns])
                total[t] = part if total[t] is None else total[t] + part
            results.append(total)
        for t in range(2):
            rows = slice(t * mid, (t + 1) * mid)
            y_ref[rows, here] = jnp.where(second_head[rows], results[1][t], results[0][t])

    scan.end()
    skip = split_dot(jnp.broadcast_to(numbers_ref[1:2, :], (8, lanes)), spreader, 2)[0:1, :]
    carry = split_dot(jnp.exp(cum), spreader, 2)
    square = jnp.zeros((tokens, 1), jnp.float32)
    for c in range(0, width, cut):
        here = slice(c, c + cut)
        start = start_ref[c // each : (c + cut) // each].reshape(cut, size)
        through = dot_three(read, start, dot_nt)
        y = y_ref[:, here] + carry[:, here] * through + skip[:, here] * x_ref[:, here]
        y_ref[:, here] = y
        z = z_ref[:, here]
        gated = y * (z * jax.nn.sigmoid(z))
        spread[:, here] = gated
        square = square + jnp.sum(gated * gated, axis=1, keepdims=True)
    y_ref.flush()
    mine[...] = jnp.broadcast_to(square, mine.shape)
    swap = pltpu.make_async_remote_copy(
        src_ref=mine,
        dst_ref=theirs,
        send_sem=pair_sems.at[0],
        recv_sem=pair_sems.at[1],
        device_id={"head": 1 - head},
    )
    swap.start()
    swap.wait()
    scale = lax.rsqrt((mine[...] + theirs[...]) / (2 * width) + EPSILON)
    scale_ref[...] = scale
    for c in range(0, width, cut):
        here = slice(c, c + cut)
        gated_ref[:, here] = low(spread[:, here] * scale[:, 0:1] * gain_ref[:, here])
    gather.arrived(2)
    gather.end()
    out.wait()


def mixer(layer_in, edge, table, weights, width, late, grad_rows, collective):
    tokens, model = layer_in.shape
    channels, lanes = table.shape[1], 128
    size = (channels - width) // 2
    each, mid = width // 64, tokens // 2
    f32, bf16 = jnp.float32, jnp.bfloat16
    vmem, hbm = pl.BlockSpec(memory_space=pltpu.VMEM), pl.BlockSpec(memory_space=pl.ANY)
    out = [
        ((tokens, model), bf16),
        ((tokens, width), f32),
        ((tokens, width), f32),
        ((tokens, 2 * size), f32),
        ((tokens, channels), f32),
        ((tokens + 8, channels), f32),
        ((tokens, lanes), f32),
        ((64, each, size), f32),
        ((tokens, width), f32),
        ((tokens, width), bf16),
        ((tokens, lanes), f32),
        (late.shape, bf16),
        (part_shape(OUT[1], grad_rows).shape, bf16),
    ]
    return call(
        mixer_kernel,
        out_shape=[jax.ShapeDtypeStruct(*shape) for shape in out],
        in_specs=[vmem, vmem, vmem, hbm, hbm, hbm],
        out_specs=[Eager] * 6 + [vmem] * 2 + [Eager] * 2 + [vmem] + [hbm] * 2,
        scratch_shapes=[
            pltpu.VMEM(weights.shape, bf16),
            pltpu.VMEM((tokens + 16, model), bf16),
            pltpu.VMEM((64, each + 8, size), bf16),
            pltpu.VMEM((64, each + 8, size), bf16),
            pltpu.VMEM((64, each, size), f32),
            pltpu.VMEM((tokens, width), f32),
            pltpu.VMEM((lanes, tokens), f32),
            pltpu.VMEM((3, mid, mid), f32),
            pltpu.VMEM((tokens, lanes), f32),
            pltpu.VMEM((tokens, lanes), f32),
            pltpu.SemaphoreType.DMA((9,)),
            pltpu.SemaphoreType.DMA((4,)),
            pltpu.SemaphoreType.DMA((2,)),
        ]
        + gather_shapes()[:2]
        + [pltpu.SemaphoreType.DMA((9,))],
        input_output_aliases={4: len(out) - 2},
        compiler_params=params(collective, vmem_limit_bytes=VMEM),
        name="mixer",
    )(layer_in, edge, table, weights, late, grad_rows)


def per_device(
    layer_in,
    norm_first,
    mixer_in,
    state_proj,
    step_proj,
    step_bias,
    conv_main,
    conv_state,
    decay_rate,
    skip_gain,
    gate_gain,
    mixer_out,
    norm_second,
    shared_gate_up,
    shared_down,
    expert_gate_up,
    expert_down,
    routes,
    route_weights,
    grad_out,
):
    tokens, model_width = layer_in.shape
    inner_dev = mixer_in.shape[2]
    state_size = state_proj.shape[1] // 2
    heads_dev = step_proj.shape[1]
    conv_taps = conv_main.shape[0]
    shared_dev = shared_down.shape[1]
    local_experts = expert_gate_up.shape[0]
    experts_all = local_experts * lax.axis_size("seq")
    choices_per = routes.shape[1]
    capacity = max(2, tokens * choices_per * 4 // (3 * experts_all))
    slots_dev = capacity // lax.axis_size("head")
    lanes = 128
    vectors = [
        conv_main,
        conv_state,
        [gain.reshape(-1, 128) for gain in (norm_first, norm_second, gate_gain)],
        [number[None] for number in (decay_rate, skip_gain, step_bias)],
    ]
    gathered, late_rows, edge, position, slot_weight, grads_out, grads_first, table, gate_up = gather_rows(
        [mixer_in, state_proj, step_proj],
        [mixer_out, shared_gate_up, shared_down],
        expert_gate_up.reshape(expert_gate_up.shape[1:]),
        layer_in,
        routes,
        route_weights,
        grad_out,
        vectors,
        experts_all,
        slots_dev,
        0,
    )
    weights_in = gathered.reshape(model_width, -1)
    (
        normed,
        gate_z,
        heads_x,
        state_both,
        conv_sum,
        pre,
        step_raw,
        state_start,
        ssd,
        normed_gate,
        gate_scale,
        gathered,
        grads_second,
    ) = mixer(
        layer_in,
        edge,
        table,
        weights_in,
        inner_dev,
        late_rows,
        grads_out,
        1,
    )
    weights_late = gathered.reshape(model_width, -1)
    (
        grad_home,
        res_sums,
        expert_gate_up_grad,
        expert_down_grad,
        shared_part,
        shared_back,
        shared_right,
        residual,
        normed_second,
        scale_second,
    ) = experts(
        normed_gate,
        weights_late,
        layer_in,
        table,
        position,
        [grads_first, grads_second],
        grads_out,
        gate_up,
        expert_down.reshape(-1, model_width),
        grad_out,
        slots_dev,
        2,
    )
    (
        mixer_out_grad,
        shared_gate_up_grad,
        shared_down_grad,
        right_grads,
        taps_grad,
        heads_grad,
        home_near,
        grad_resid,
        norm_second_grad,
        gate_gain_grad,
    ) = mixer_back(
        [normed_second, grad_out],
        [normed_gate, shared_right],
        grad_home,
        position,
        shared_back,
        residual,
        scale_second,
        weights_late,
        gate_z,
        gate_scale,
        ssd,
        heads_x,
        state_both,
        conv_sum,
        pre,
        step_raw,
        table,
        state_start.reshape(inner_dev, state_size),
        res_sums,
        3,
    )
    (
        mixer_in_grad,
        state_proj_grad,
        step_proj_grad,
        input_grad,
        layer_out,
        norm_first_sum,
        norm_second_sum,
        gate_gain_sum,
        conv_main_grad,
        conv_state_grad,
        (skip_gain_grad, decay_rate_grad, step_bias_grad),
    ) = input_back(
        normed,
        right_grads,
        tuple(((0, 0, start, start, 1152),) for start in (0, 1152, 2304)),
        weights_in,
        layer_in,
        table,
        grad_resid,
        res_sums,
        [home_near],
        position,
        slot_weight,
        shared_part,
        residual,
        taps_grad,
        heads_grad,
        norm_second_grad,
        gate_gain_grad,
        heads_dev,
        4,
    )
    (
        layer_out,
        input_grad,
        expert_gate_up_grad,
        expert_down_grad,
        mixer_in_grad,
        state_proj_grad,
        step_proj_grad,
        norm_first_sum,
        norm_second_sum,
        gate_gain_sum,
        conv_main_grad,
        conv_state_grad,
        skip_gain_grad,
        decay_rate_grad,
        step_bias_grad,
        mixer_out_grad,
        shared_gate_up_grad,
        shared_down_grad,
    ) = emit(
        [
            layer_out,
            input_grad,
            expert_gate_up_grad,
            expert_down_grad,
            mixer_in_grad,
            state_proj_grad,
            step_proj_grad,
            norm_first_sum,
            norm_second_sum,
            gate_gain_sum,
            conv_main_grad,
            conv_state_grad,
            skip_gain_grad,
            decay_rate_grad,
            step_bias_grad,
            mixer_out_grad,
            shared_gate_up_grad,
            shared_down_grad,
        ]
    )
    expert_gate_up_grad = expert_gate_up_grad.reshape(model_width, -1, 2, lanes)
    expert_gate_up_grad = expert_gate_up_grad.transpose(0, 2, 1, 3).reshape(expert_gate_up.shape)
    return (
        layer_out,
        input_grad,
        norm_first_sum.reshape(-1),
        mixer_in_grad,
        state_proj_grad,
        step_proj_grad,
        step_bias_grad.reshape(-1),
        conv_main_grad,
        conv_state_grad,
        decay_rate_grad.reshape(-1),
        skip_gain_grad.reshape(-1),
        gate_gain_sum.reshape(-1),
        mixer_out_grad,
        norm_second_sum.reshape(-1),
        shared_gate_up_grad,
        shared_down_grad,
        expert_gate_up_grad,
        expert_down_grad[None],
    )


def solution(mesh):
    placed = (
        P("seq", None),
        P(),
        P("seq", None, "head"),
        P("seq", None),
        P("seq", "head"),
        P("head"),
        P(None, "head"),
        P(),
        P("head"),
        P("head"),
        P("head"),
        P("seq", "head"),
        P(),
        P("seq", None, "head"),
        P("seq", "head"),
        P("seq", None, None, "head"),
        P("seq", "head", None),
        P("seq", None),
        P("seq", None),
        P("seq", None),
    )
    return jax.shard_map(
        per_device,
        mesh=mesh,
        in_specs=placed,
        out_specs=(
            P("seq", None),
            P("seq", None),
            P(),
            P("seq", None, "head"),
            P("seq", None),
            P("seq", "head"),
            P("head"),
            P(None, "head"),
            P(),
            P("head"),
            P("head"),
            P("head"),
            P("seq", "head"),
            P(),
            P("seq", None, "head"),
            P("seq", "head"),
            P("seq", None, None, "head"),
            P("seq", "head", None),
        ),
        check_vma=False,
    )
```
